128 devices in a mesh: dp: 4 (over z_hi, core), context: 8 (over x, z_lo), experts: 4 (over y).
Axes of the slice: x: 4, y: 4, z: 4 (z_hi: 2, z_lo: 2; z = z_hi * 2 + z_lo), core: 2. Of those that a mesh axis runs over, the one named last changes fastest.
Arguments:
- hidden_in: bfloat16 [12, 1024, 2048], P('dp', 'context'), may hold values from -6 to 6
- segments: int32 [12, 1024], P('dp'), may hold values from 0 to 2, as said below
- attn_gain: bfloat16 [2048], replicated, may hold values from 0.5 to 1.5
- query_gain: bfloat16 [128], replicated, may hold values from 0.5 to 1.5
- key_gain: bfloat16 [128], replicated, may hold values from 0.5 to 1.5
- w_query: bfloat16 [2048, 4096], P(None, 'experts'), may hold values from -0.125 to 0.125
- key_weight_matrix: bfloat16 [2048, 512], P(None, 'experts'), may hold values from -0.125 to 0.125
- value_weight_matrix: bfloat16 [2048, 512], P(None, 'experts'), may hold values from -0.125 to 0.125
- w_out: bfloat16 [2048, 4096], P(None, 'experts'), may hold values from -1.5 to 1.5
- moe_gain: bfloat16 [2048], replicated, may hold values from 0.5 to 1.5
- expert_ids: int32 [12, 1024, 8], P('dp', ('context', 'experts')), may hold values from 0 to 15, as said below
- gate_values: float32 [12, 1024, 8], P('dp', ('context', 'experts')), may hold values from 0.06 to 0.2
- capacity: int32 [16], replicated, may hold values from 24 to 48, as said below
- w_gate: bfloat16 [16, 2048, 768], P(('dp', 'experts')), may hold values from -0.125 to 0.125
- w_up: bfloat16 [16, 2048, 768], P(('dp', 'experts')), may hold values from -0.125 to 0.125
- w_down: bfloat16 [16, 2048, 768], P(('dp', 'experts')), may hold values from -0.875 to 0.875
- cotangent: bfloat16 [12, 1024, 2048], P('dp', ('context', 'experts')), may hold values from -6 to 6
Outputs:
- layer_out: float32 [12, 1024, 2048], P('dp', ('context', 'experts'))
- input_grad: float32 [12, 1024, 2048], P('dp', ('context', 'experts'))
- attn_gain_grad: float32 [2048], replicated
- query_gain_grad: float32 [128], replicated
- key_gain_grad: float32 [128], replicated
- w_query_grad: float32 [2048, 4096], P(('dp', 'context'), 'experts')
- w_key_grad: float32 [2048, 512], P(('dp', 'context'), 'experts')
- w_value_grad: float32 [2048, 512], P(('dp', 'context'), 'experts')
- w_out_grad: float32 [2048, 4096], P(('dp', 'context'), 'experts')
- moe_gain_grad: float32 [2048], replicated
- gate_grad: float32 [12, 1024, 8], P('dp', ('context', 'experts'))
- w_gate_grad: float32 [16, 2048, 768], P(('dp', 'experts'), 'context')
- w_up_grad: float32 [16, 2048, 768], P(('dp', 'experts'), 'context')
- w_down_grad: float32 [16, 2048, 768], P(('dp', 'experts'), 'context')
- head_clip_scale: float32 [32], P('experts')
The draws below stay inside these ranges and needn't reach their ends.
Inputs may be any that keep to these rules, and one draw needn't show every extreme that they name: `segments`: in each sequence the document numbers never fall and take the values 0, 1, 2; document 1 starts within the first 128 positions and ends within the last 128 positions. `expert_ids`: each token names 8 different experts in increasing order; one expert is named by every token. The expert that every token names has capacity 48; some other expert has capacity 48 // 2.
All inputs are finite; a program needn't handle non-finite values.
Results may differ from the reference program's by a relative error of at most 0.028.
Values may be sent and summed in bfloat16 or wider, within the bound.
A program may use at most 192 MiB of HBM per device.

```python
import math
import jax
import jax.numpy as jnp
from jax import lax

MODEL_DIM = 2048
QUERY_HEADS = 32
KEY_VALUE_HEADS = 4
HEAD_SIZE = 128
FF = 768
TOPK = 8
LEN = 1024
SEQS = 3
EXPERTS = 16
BATCH = 12
CH = 128
MT = 32
CAP = 48


def popular(key):
    return jax.random.randint(jax.random.fold_in(key, 11), (), 0, EXPERTS)


def draw_segments(key, part):
    key = jax.random.fold_in(key, 1)
    first = jax.random.randint(jax.random.fold_in(key, 2), (BATCH, 1), 1, CH)
    last = jax.random.randint(jax.random.fold_in(key, 3), (BATCH, 1), 1, CH)
    position = jnp.arange(LEN, dtype=jnp.int32)[None, :]
    return ((position >= first).astype(jnp.int32) + (position >= LEN - last).astype(jnp.int32)).astype(jnp.int32)


def draw_expert_ids(key, part):
    favored = popular(key)
    key = jax.random.fold_in(key, 4)
    lean = jax.random.randint(jax.random.fold_in(key, 5), (EXPERTS,), 0, 32768)
    lean = jnp.where(jnp.arange(EXPERTS) == favored, 262144, lean)
    noise = jax.random.randint(jax.random.fold_in(key, 6), (BATCH, LEN, EXPERTS), 0, 65536)
    ranking = (noise + lean[None, None, :]) * EXPERTS + jnp.arange(EXPERTS, dtype=jnp.int32)[None, None, :]
    picked = lax.top_k(ranking, TOPK)[1]
    return jnp.sort(picked, axis=-1).astype(jnp.int32)


def draw_capacity(key, part):
    favored = popular(key)
    key = jax.random.fold_in(key, 8)
    lowest = max(1, CAP // 2)
    values = jax.random.randint(key, (EXPERTS,), lowest, CAP + 1)
    neighbour = (favored + 1) % EXPERTS
    values = jnp.where(jnp.arange(EXPERTS) == neighbour, lowest, values)
    return jnp.where(jnp.arange(EXPERTS) == favored, CAP, values).astype(jnp.int32)


def levels(key, extent, cuts, smallest, high):
    def one(dim, parts):
        heights = jax.random.uniform(jax.random.fold_in(jax.random.fold_in(key, 6), dim), (parts,), jnp.float32, smallest / len(cuts), high / len(cuts))
        return jnp.repeat(jnp.exp(heights), extent[dim] // parts).reshape((-1,) + (1,) * (len(extent) - dim - 1))

    gain = one(*cuts[0])
    for cut in cuts[1:]:
        gain = gain * one(*cut)
    return gain


def gaussian(own_key, shape, deviation, most, split=(), held_as=jnp.bfloat16):
    array = deviation * jax.random.normal(own_key, shape, jnp.float32)
    if split:
        array = array * levels(own_key, shape, split, -0.22, 0.18)
    return jnp.clip(array, -most, most).astype(held_as)


def setup_inputs(seed: int = 0) -> dict:
    key_list = jax.random.split(jax.random.key(seed), 18)
    return {
        "hidden_in": gaussian(key_list[0], (BATCH, LEN, MODEL_DIM), 1.0, 6.0, ((0, 4), (1, 8))),
        "segments": draw_segments(jax.random.fold_in(key_list[17], 71), 0),
        "attn_gain": jnp.clip(1.0 + 0.1 * jax.random.normal(key_list[2], (MODEL_DIM,), jnp.float32), 0.5, 1.5).astype(jnp.bfloat16),
        "query_gain": jnp.clip(1.0 + 0.1 * jax.random.normal(key_list[3], (HEAD_SIZE,), jnp.float32), 0.5, 1.5).astype(jnp.bfloat16),
        "key_gain": jnp.clip(1.0 + 0.1 * jax.random.normal(key_list[4], (HEAD_SIZE,), jnp.float32), 0.5, 1.5).astype(jnp.bfloat16),
        "w_query": gaussian(key_list[5], (MODEL_DIM, QUERY_HEADS * HEAD_SIZE), MODEL_DIM ** -0.5, 0.125, ((1, 4),)),
        "key_weight_matrix": gaussian(key_list[6], (MODEL_DIM, KEY_VALUE_HEADS * HEAD_SIZE), MODEL_DIM ** -0.5, 0.125, ((1, 4),)),
        "value_weight_matrix": gaussian(key_list[7], (MODEL_DIM, KEY_VALUE_HEADS * HEAD_SIZE), MODEL_DIM ** -0.5, 0.125, ((1, 4),)),
        "w_out": gaussian(key_list[8], (MODEL_DIM, QUERY_HEADS * HEAD_SIZE), (max(1, QUERY_HEADS * HEAD_SIZE // 256)) ** -0.5, 1.5, ((1, 4),)),
        "moe_gain": jnp.clip(1.0 + 0.1 * jax.random.normal(key_list[9], (MODEL_DIM,), jnp.float32), 0.5, 1.5).astype(jnp.bfloat16),
        "expert_ids": draw_expert_ids(jax.random.fold_in(key_list[17], 71), 0),
        "gate_values": jnp.clip(jnp.exp(math.log(0.2) - 1.2039728 * jax.random.uniform(key_list[11], (BATCH, LEN, TOPK), jnp.float32) ** levels(key_list[11], (BATCH, LEN, TOPK), ((0, 4), (1, 32)), -0.2, 0.2)), 0.06, 0.2),
        "capacity": draw_capacity(jax.random.fold_in(key_list[17], 71), 0),
        "w_gate": gaussian(key_list[13], (EXPERTS, MODEL_DIM, FF), MODEL_DIM ** -0.5, 0.125, ((0, 16),)),
        "w_up": gaussian(key_list[14], (EXPERTS, MODEL_DIM, FF), MODEL_DIM ** -0.5, 0.125, ((0, 16),)),
        "w_down": gaussian(key_list[15], (EXPERTS, MODEL_DIM, FF), (max(1, FF // 16)) ** -0.5, 0.875, ((0, 16),)),
        "cotangent": gaussian(key_list[16], (BATCH, LEN, MODEL_DIM), 1.0, 6.0, ((0, 4), (1, 32))),
    }


epsilon = 1e-06
rope_base = 1000000.0
clip_limit = 1.0
masked_value = -1e+30
highest_logit = lax.Precision.HIGHEST

@jax.custom_vjp
def reduced_precise(v):
    return lax.optimization_barrier(v.astype(jnp.bfloat16)).astype(jnp.float32)

@jax.custom_vjp
def reduced_backward(v):
    return v

def low_keep(v):
    return (reduced_precise(v), None)

def low_pass(kept, grad):
    return (grad,)

def back_keep(v):
    return (v, None)

def back_low(kept, grad):
    return (reduced_precise(grad),)
reduced_precise.defvjp(low_keep, low_pass)
reduced_backward.defvjp(back_keep, back_low)

def rms_scale(values, factor):
    return values * lax.rsqrt(lax.optimization_barrier(jnp.mean(values * values, axis=-1, keepdims=True)) + epsilon) * factor

def turn(values):
    middle = values.shape[-1] // 2
    return jnp.concatenate([-values[..., middle:], values[..., :middle]], axis=-1)

def rotary(offset, amount):
    inverse = 1.0 / rope_base ** (jnp.arange(0, HEAD_SIZE, 2, dtype=jnp.float32) / HEAD_SIZE)
    position = (offset + jnp.arange(amount, dtype=jnp.int32)).astype(jnp.float32)
    angle = position[:, None] * inverse[None, :]
    angle = jnp.concatenate([angle, angle], axis=-1)
    return (jnp.cos(angle), jnp.sin(angle))

def attend_one(normalized_input, seg_row, w_query, key_weight_matrix, value_weight_matrix, query_gain, key_gain):
    span_length = normalized_input.shape[0]
    cosine_table, sine_table = rotary(0, span_length)
    cosine_table = cosine_table[:, None, :]
    sine_table = sine_table[:, None, :]
    query_raw = reduced_backward(jnp.dot(normalized_input, w_query, precision=highest_logit)).reshape(span_length, QUERY_HEADS, HEAD_SIZE)
    unclipped_key = reduced_backward(jnp.dot(normalized_input, key_weight_matrix, precision=highest_logit)).reshape(span_length, KEY_VALUE_HEADS, HEAD_SIZE)
    value_reduced = reduced_precise(reduced_backward(jnp.dot(normalized_input, value_weight_matrix, precision=highest_logit))).reshape(span_length, KEY_VALUE_HEADS, HEAD_SIZE)
    query_normed = rms_scale(query_raw, query_gain)
    query_rot = reduced_precise(query_normed * cosine_table + turn(query_normed) * sine_table)
    key_normed = rms_scale(unclipped_key, key_gain)
    key_rot = reduced_precise(key_normed * cosine_table + turn(key_normed) * sine_table)
    repeat_factor = QUERY_HEADS // KEY_VALUE_HEADS
    key_full = jnp.repeat(key_rot, repeat_factor, axis=1)
    value_full = jnp.repeat(value_reduced, repeat_factor, axis=1)
    score = reduced_backward(jnp.einsum('qhd,khd->hqk', query_rot, key_full, precision=highest_logit) * HEAD_SIZE ** (-0.5))
    position = jnp.arange(span_length, dtype=jnp.int32)
    allowed = (seg_row[:, None] == seg_row[None, :]) & (position[None, :] <= position[:, None])
    masked = jnp.where(allowed[None, :, :], score, masked_value)
    row_peak = lax.optimization_barrier(jnp.max(masked, axis=-1, keepdims=True))
    log_total = row_peak + jnp.log(lax.optimization_barrier(jnp.sum(jnp.exp(masked - row_peak), axis=-1, keepdims=True)))
    probability = reduced_precise(jnp.exp(masked - log_total))
    mixed_heads = jnp.einsum('hqk,khd->qhd', probability, value_full, precision=highest_logit)
    return (reduced_precise(reduced_backward(mixed_heads)).reshape(span_length, QUERY_HEADS * HEAD_SIZE), lax.optimization_barrier(jnp.max(masked, axis=(1, 2))))

def layer(hidden_in, attn_gain, query_gain, key_gain, w_query, key_weight_matrix, value_weight_matrix, w_out, moe_gain, gate_values, w_gate, w_up, w_down, segments, expert_ids, capacity):
    normalized_input = reduced_precise(rms_scale(hidden_in, attn_gain))

    def attend_step(carried, member):
        return (carried, attend_one(member[0], member[1], w_query, key_weight_matrix, value_weight_matrix, query_gain, key_gain))
    carried_end, outputs = lax.scan(jax.checkpoint(attend_step), jnp.float32(0.0), (normalized_input, segments))
    mixed_heads, head_peaks = outputs
    branch = reduced_backward(jnp.einsum('blk,dk->bld', mixed_heads, w_out, precision=highest_logit))
    after_attn = hidden_in + branch
    moe_in = reduced_precise(rms_scale(after_attn, moe_gain))
    seq_groups = BATCH // SEQS
    blocks = LEN // MT
    per_block = SEQS * MT

    def regroup(values):
        tail = values.shape[2:]
        values = values.reshape((seq_groups, SEQS, blocks, MT) + tail)
        return jnp.swapaxes(values, 1, 2).reshape((seq_groups * blocks, per_block) + tail)
    moe_groups = regroup(moe_in)
    id_groups = regroup(expert_ids)
    gate_groups = regroup(gate_values)
    choose = (id_groups[..., None] == jnp.arange(EXPERTS, dtype=jnp.int32)).astype(jnp.int32)
    chosen = lax.optimization_barrier(jnp.sum(choose, axis=2))
    before = jnp.cumsum(chosen, axis=1) - chosen
    kept = (chosen > 0) & (before < capacity[None, None, :])
    share = lax.optimization_barrier(jnp.sum(gate_groups[..., None] * choose.astype(jnp.float32), axis=2))
    slot_index = jnp.arange(CAP, dtype=jnp.int32)

    def expert_step(running, member):
        gate_weight, up_weight, down_weight, kept_rows, before_rows, share_rows = member
        table = (kept_rows[:, None, :] & (before_rows[:, None, :] == slot_index[None, :, None])).astype(jnp.float32)
        rows_in = reduced_backward(jnp.einsum('gcn,gnd->gcd', table, moe_groups, precision=highest_logit))
        gate_pre = reduced_backward(jnp.einsum('gcd,df->gcf', rows_in, gate_weight, precision=highest_logit))
        up_pre = reduced_backward(jnp.einsum('gcd,df->gcf', rows_in, up_weight, precision=highest_logit))
        activation = reduced_precise(jax.nn.silu(gate_pre) * up_pre)
        produced = reduced_precise(reduced_backward(jnp.einsum('gcf,df->gcd', activation, down_weight, precision=highest_logit)))
        slot_share = jnp.einsum('gcn,gn->gc', table, share_rows, precision=highest_logit)
        added = jnp.einsum('gcn,gcd->gnd', table, produced * slot_share[..., None], precision=highest_logit)
        return (running + added, None)
    members = (w_gate, w_up, w_down, jnp.moveaxis(kept, 2, 0), jnp.moveaxis(before, 2, 0), jnp.moveaxis(share, 2, 0))
    moe_total, unused = lax.scan(jax.checkpoint(expert_step), jnp.zeros_like(moe_groups), members)
    moe_out = jnp.swapaxes(moe_total.reshape(seq_groups, blocks, SEQS, MT, MODEL_DIM), 1, 2).reshape(BATCH, LEN, MODEL_DIM)
    return (after_attn + moe_out, lax.optimization_barrier(jnp.max(head_peaks, axis=0)))

def reference(hidden_in, segments, attn_gain, query_gain, key_gain, w_query, key_weight_matrix, value_weight_matrix, w_out, moe_gain, expert_ids, gate_values, capacity, w_gate, w_up, w_down, cotangent):

    def forward(inputs, gain_a, gain_q, gain_k, weight_q, weight_k, weight_v, weight_o, gain_m, gates_in, weight_g, weight_u, weight_d):
        return layer(inputs, gain_a, gain_q, gain_k, weight_q, weight_k, weight_v, weight_o, gain_m, gates_in, weight_g, weight_u, weight_d, segments, expert_ids, capacity)
    primals = (hidden_in.astype(jnp.float32), attn_gain.astype(jnp.float32), query_gain.astype(jnp.float32), key_gain.astype(jnp.float32), w_query.astype(jnp.float32), key_weight_matrix.astype(jnp.float32), value_weight_matrix.astype(jnp.float32), w_out.astype(jnp.float32), moe_gain.astype(jnp.float32), gate_values.astype(jnp.float32), w_gate.astype(jnp.float32), w_up.astype(jnp.float32), w_down.astype(jnp.float32))
    layer_out, pullback, peaks = jax.vjp(forward, *primals, has_aux=True)
    grads = pullback(cotangent.astype(jnp.float32))
    head_clip_scale = clip_limit / jnp.maximum(peaks, clip_limit)
    return (layer_out, grads[0], grads[1], grads[2], grads[3], grads[4], grads[5], grads[6], grads[7], grads[8], grads[9], grads[10], grads[11], grads[12], head_clip_scale)
```

```python
import functools
import itertools

import jax
import jax.numpy as jnp
from jax import lax
from jax.experimental import pallas as pl
from jax.experimental.pallas import tpu as pltpu
from jax.sharding import PartitionSpec as P

HEAD_SIZE = 128
MESH = pl.DeviceIdType.MESH
VMEM = pl.BlockSpec(memory_space=pltpu.VMEM)


epsilon = 1e-06
rope_base = 1000000.0
clip_limit = 1.0
masked_value = -1e30


def rms_scale(values, factor):
    return values * lax.rsqrt(jnp.mean(values * values, axis=-1, keepdims=True) + epsilon) * factor


def rms_back(gradient, values, factor):
    inverse = lax.rsqrt(jnp.mean(values * values, axis=-1, keepdims=True) + epsilon)
    normal = values * inverse
    scaled = gradient * factor
    result = inverse * (scaled - normal * jnp.mean(scaled * normal, axis=-1, keepdims=True))
    return (result, jnp.sum(gradient * normal, axis=tuple(range(values.ndim - 1))))


def turn(values):
    middle = values.shape[-1] // 2
    return jnp.concatenate([-values[..., middle:], values[..., :middle]], axis=-1)


def turn_back(values):
    middle = values.shape[-1] // 2
    return jnp.concatenate([values[..., middle:], -values[..., :middle]], axis=-1)


def rotary(offset, amount):
    inverse = 1.0 / rope_base ** (jnp.arange(0, HEAD_SIZE, 2, dtype=jnp.float32) / HEAD_SIZE)
    position = (offset + jnp.arange(amount, dtype=jnp.int32)).astype(jnp.float32)
    angle = position[:, None] * inverse[None, :]
    angle = jnp.concatenate([angle, angle], axis=-1)
    return (jnp.cos(angle), jnp.sin(angle))


def contract_last(left, right):
    return lax.dot_general(
        left, right, (((1,), (1,)), ((), ())), preferred_element_type=jnp.float32
    )


def contract_first(left, right):
    return lax.dot_general(
        left, right, (((0,), (0,)), ((), ())), preferred_element_type=jnp.float32
    )


class Place:
    def __init__(self):
        dp = lax.axis_index("dp")
        context = lax.axis_index("context")
        self.dp, self.context, self.y = dp, context, lax.axis_index("experts")
        self.core, self.z_hi = lax.rem(dp, 2), dp // 2
        self.x, self.z_lo = context // 2, lax.rem(context, 2)
        self.z = self.z_hi * 2 + self.z_lo

    def at(self, x=None, y=None, z=None, core=None):
        x = self.x if x is None else x
        y = self.y if y is None else y
        z = self.z if z is None else z
        core = self.core if core is None else core
        return (z // 2 * 2 + core, x * 2 + lax.rem(z, 2), y)

    def x_by(self, step):
        return lax.rem(self.x + step, 4)

    def y_by(self, step):
        return lax.rem(self.y + step, 4)

    def z_by(self, step):
        return lax.rem(self.z + step, 4)


class Net:
    def __init__(self, send, recv):
        self.send, self.recv, self.copies = send, recv, []

    def copy(self, src, dst, device):
        spot = len(self.copies)
        made = pltpu.make_async_remote_copy(
            src_ref=src,
            dst_ref=dst,
            send_sem=self.send.at[spot],
            recv_sem=self.recv.at[spot],
            device_id=device,
            device_id_type=MESH,
        )
        made.start()
        self.copies.append(made)
        return made

    def finish(self):
        for made in self.copies:
            made.wait_send()


def greet(devices):
    barrier = pltpu.get_barrier_semaphore()
    for device in devices:
        pl.semaphore_signal(barrier, inc=1, device_id=device, device_id_type=MESH)
    pl.semaphore_wait(barrier, len(devices))


def add_into(target, parts, block=32):
    rows = target.shape[-2]
    block = min(block, rows)
    for lead in itertools.product(*[range(size) for size in target.shape[:-2]]):

        def body(step, carry, lead=lead):
            spot = lead + (pl.ds(pl.multiple_of(step * block, block), block),)
            total = parts[0][spot].astype(jnp.float32)
            for part in parts[1:]:
                total = total + part[spot].astype(jnp.float32)
            target[spot] = total.astype(target.dtype)
            return carry

        lax.fori_loop(0, rows // block, body, 0)


def ring_reduce(net, plus, minus, own, slots, target):
    first_plus = net.copy(own(2, 0), slots.at[0], plus)
    first_minus = net.copy(own(2, 1), slots.at[2], minus)
    side_plus = net.copy(own(1, 1), slots.at[1], plus)
    side_minus = net.copy(own(3, 0), slots.at[3], minus)
    yield
    first_plus.wait_recv()
    add_into(slots.at[0], [slots.at[0], own(1, 0)])
    last_plus = net.copy(slots.at[0], slots.at[4], plus)
    first_minus.wait_recv()
    add_into(slots.at[2], [slots.at[2], own(3, 1)])
    last_minus = net.copy(slots.at[2], slots.at[5], minus)
    yield
    side_minus.wait_recv()
    last_plus.wait_recv()
    add_into(target(0), [own(0, 0), slots.at[3], slots.at[4]])
    side_plus.wait_recv()
    last_minus.wait_recv()
    add_into(target(1), [own(0, 1), slots.at[1], slots.at[5]])


def expert_x_first(net, me, source, slots, middle, other, out):
    ring = ring_reduce(
        net,
        me.at(x=me.x_by(1)),
        me.at(x=me.x_by(3)),
        lambda step, half: source.at[me.x_by(step), half],
        slots,
        lambda half: middle.at[half],
    )
    yield from ring
    across = net.copy(middle.at[1 - me.z_lo], other, me.at(z=me.z + 1 - 2 * me.z_lo))
    yield
    across.wait_recv()
    add_into(out, [middle.at[me.z_lo], other])


def expert_z_first(net, me, source, other, middle, slots, out):
    across = net.copy(source.at[:, 1 - me.z_lo], other, me.at(z=me.z + 1 - 2 * me.z_lo))
    yield
    across.wait_recv()
    add_into(middle, [source.at[:, me.z_lo], other])
    half_rows = middle.shape[1] // 2
    yield from ring_reduce(
        net,
        me.at(x=me.x_by(1)),
        me.at(x=me.x_by(3)),
        lambda step, half: middle.at[me.x_by(step), pl.ds(half * half_rows, half_rows)],
        slots,
        lambda half: out.at[pl.ds(half * half_rows, half_rows)],
    )


def core_pair(net, me, source, other, middle):
    across = net.copy(source.at[:, 1 - me.core], other, me.at(core=1 - me.core))
    yield
    across.wait_recv()
    add_into(middle, [source.at[:, me.core], other])


def dense_x_first(net, me, source, other, middle, slots, corner, last, out):
    yield from core_pair(net, me, source, other, middle)
    yield from ring_reduce(
        net,
        me.at(x=me.x_by(1)),
        me.at(x=me.x_by(3)),
        lambda step, half: middle.at[half, me.x_by(step)],
        slots,
        lambda half: corner.at[half],
    )
    half_rows = corner.shape[2] // 2
    yield from ring_reduce(
        net,
        me.at(z=me.z_by(1)),
        me.at(z=me.z_by(3)),
        lambda step, half: corner.at[
            me.z_by(step) // 2, lax.rem(me.z_by(step), 2), pl.ds(half * half_rows, half_rows)
        ],
        last,
        lambda half: out.at[pl.ds(half * half_rows, half_rows)],
    )


def dense_z_first(net, me, source, other, middle, slots, corner, last, out):
    yield from core_pair(net, me, source, other, middle)
    yield from ring_reduce(
        net,
        me.at(z=me.z_by(1)),
        me.at(z=me.z_by(3)),
        lambda step, half: middle.at[
            me.z_by(step) // 2, pl.ds(half * 2, 2), lax.rem(me.z_by(step), 2)
        ],
        slots,
        lambda half: corner.at[pl.ds(half * 2, 2)],
    )
    half_rows = corner.shape[1] // 2
    yield from ring_reduce(
        net,
        me.at(x=me.x_by(1)),
        me.at(x=me.x_by(3)),
        lambda step, half: corner.at[me.x_by(step), pl.ds(half * half_rows, half_rows)],
        last,
        lambda half: out.at[pl.ds(half * half_rows, half_rows)],
    )


def in_turn(tasks):
    tasks = list(tasks)
    while tasks:
        for task in list(tasks):
            if next(task, "end") == "end":
                tasks.remove(task)


def reduce_kernel(counts, *refs):
    refs = list(refs)

    def take(number):
        taken = refs[:number]
        del refs[:number]
        return taken

    gate, up, down, query, key_value, out_w = take(6)
    gate_out, up_out, down_out, query_out, key_value_out, out_w_out = take(6)
    scratch = [take(count) for count in counts]
    send, recv = take(2)
    me = Place()
    greet(
        [
            me.at(x=me.x_by(1)),
            me.at(x=me.x_by(3)),
            me.at(z=me.z_by(1)),
            me.at(z=me.z_by(3)),
            me.at(core=1 - me.core),
        ]
    )
    net = Net(send, recv)
    in_turn(
        [
            dense_z_first(net, me, out_w, *scratch[5], out_w_out),
            dense_x_first(net, me, query, *scratch[3], query_out),
            dense_x_first(net, me, key_value, *scratch[4], key_value_out),
            expert_z_first(net, me, down, *scratch[2], down_out),
            expert_x_first(net, me, gate, *scratch[0], gate_out),
            expert_x_first(net, me, up, *scratch[1], up_out),
        ]
    )
    net.finish()


def reduce_weights(gate, up, down, query, key_value, out_w):
    low = jnp.bfloat16
    x_first = [
        pltpu.VMEM((6, 256, 768), low),
        pltpu.VMEM((2, 256, 768), low),
        pltpu.VMEM((256, 768), low),
    ]
    z_first = [
        pltpu.VMEM((4, 256, 768), low),
        pltpu.VMEM((4, 256, 768), low),
        pltpu.VMEM((6, 128, 768), low),
    ]

    def dense(columns, x_first):
        return [
            pltpu.VMEM((2, 4, 2, 64, columns), low),
            pltpu.VMEM((2, 4, 2, 64, columns), low),
            pltpu.VMEM((6, 2, 64, columns), low),
            pltpu.VMEM((2, 2, 64, columns) if x_first else (4, 64, columns), low),
            pltpu.VMEM((6, 32, columns), low),
        ]

    groups = [x_first, x_first, z_first, dense(1024, True), dense(256, True), dense(1024, False)]
    copies = 64
    return pl.pallas_call(
        functools.partial(reduce_kernel, [len(group) for group in groups]),
        out_shape=[
            jax.ShapeDtypeStruct((256, 768), jnp.float32),
            jax.ShapeDtypeStruct((256, 768), jnp.float32),
            jax.ShapeDtypeStruct((256, 768), jnp.float32),
            jax.ShapeDtypeStruct((64, 1024), jnp.float32),
            jax.ShapeDtypeStruct((64, 256), jnp.float32),
            jax.ShapeDtypeStruct((64, 1024), jnp.float32),
        ],
        in_specs=[VMEM] * 6,
        out_specs=[VMEM] * 6,
        scratch_shapes=[one for group in groups for one in group]
        + [pltpu.SemaphoreType.DMA((copies,)), pltpu.SemaphoreType.DMA((copies,))],
        compiler_params=pltpu.CompilerParams(
            collective_id=0, has_side_effects=True, vmem_limit_bytes=56 << 20
        ),
        name="reduce_weights",
    )(
        gate.reshape(4, 2, 256, 768),
        up.reshape(4, 2, 256, 768),
        down.reshape(4, 2, 256, 768),
        query.reshape(2, 2, 4, 2, 64, 1024),
        key_value.reshape(2, 2, 4, 2, 64, 256),
        out_w.reshape(2, 2, 4, 2, 64, 1024),
    )


def shards(
    hidden_in,
    segments,
    attn_gain,
    query_gain,
    key_gain,
    w_query,
    key_weight_matrix,
    value_weight_matrix,
    w_out,
    moe_gain,
    expert_ids,
    gate_values,
    capacity,
    w_gate,
    w_up,
    w_down,
    cotangent,
):
    seqs_local, rows_ctx, model_width = hidden_in.shape
    seq_length = segments.shape[1]
    expert_span = lax.axis_size("experts")
    ctx_index = lax.axis_index("context")
    own_index = lax.axis_index("experts")
    own_rows = rows_ctx // expert_span
    head_count = w_query.shape[1] // HEAD_SIZE
    kv_count = key_weight_matrix.shape[1] // HEAD_SIZE
    per_group = head_count // kv_count
    score_scale = HEAD_SIZE ** (-0.5)
    token_count = seqs_local * rows_ctx
    inputs = hidden_in.astype(jnp.float32)
    gain_attn = attn_gain.astype(jnp.float32)
    gain_query = query_gain.astype(jnp.float32)
    gain_key = key_gain.astype(jnp.float32)
    gain_moe = moe_gain.astype(jnp.float32)
    normalized_input = rms_scale(inputs, gain_attn).astype(jnp.bfloat16)
    normed_flat = normalized_input.reshape(token_count, model_width)
    query_raw = jnp.dot(normed_flat, w_query, preferred_element_type=jnp.float32).reshape(
        seqs_local, rows_ctx, head_count, HEAD_SIZE
    )
    unclipped_key = jnp.dot(
        normed_flat, key_weight_matrix, preferred_element_type=jnp.float32
    ).reshape(seqs_local, rows_ctx, kv_count, HEAD_SIZE)
    value_reduced = (
        jnp.dot(normed_flat, value_weight_matrix, preferred_element_type=jnp.float32)
        .astype(jnp.bfloat16)
        .reshape(seqs_local, rows_ctx, kv_count, HEAD_SIZE)
    )
    cosine_table, sine_table = rotary(ctx_index * rows_ctx, rows_ctx)
    cosine_table = cosine_table[None, :, None, :]
    sine_table = sine_table[None, :, None, :]
    query_normed = rms_scale(query_raw, gain_query)
    query_rot = (query_normed * cosine_table + turn(query_normed) * sine_table).astype(jnp.bfloat16)
    key_normed = rms_scale(unclipped_key, gain_key)
    key_rot = (key_normed * cosine_table + turn(key_normed) * sine_table).astype(jnp.bfloat16)
    keys_all, values_all = (
        lax.all_gather(key_rot, "context", axis=1, tiled=True),
        lax.all_gather(value_reduced, "context", axis=1, tiled=True),
    )
    query_group = query_rot.reshape(seqs_local, rows_ctx, kv_count, per_group, HEAD_SIZE)
    seg_query = lax.dynamic_slice_in_dim(segments, ctx_index * rows_ctx, rows_ctx, 1)
    query_spot = ctx_index * rows_ctx + jnp.arange(rows_ctx, dtype=jnp.int32)
    key_spot = jnp.arange(seq_length, dtype=jnp.int32)
    allowed = (seg_query[:, :, None] == segments[:, None, :]) & (
        key_spot[None, None, :] <= query_spot[None, :, None]
    )
    allowed = allowed[:, None, :, None, :]

    def masked_scores():
        raw_score = (
            jnp.einsum(
                "sqhgd,skhd->shqgk", query_group, keys_all, preferred_element_type=jnp.float32
            )
            * score_scale
        )
        return jnp.where(allowed, raw_score, masked_value)

    masked = masked_scores()
    row_peak = jnp.max(masked, axis=-1, keepdims=True)
    log_total = row_peak + jnp.log(jnp.sum(jnp.exp(masked - row_peak), axis=-1, keepdims=True))
    head_peak = jnp.max(masked, axis=(0, 2, 4)).reshape(head_count)
    prob_low = jnp.exp(masked - log_total).astype(jnp.bfloat16)
    mixed_heads = jnp.einsum(
        "shqgk,skhd->sqhgd", prob_low, values_all, preferred_element_type=jnp.float32
    )
    mixed_low = mixed_heads.astype(jnp.bfloat16).reshape(token_count, head_count * HEAD_SIZE)
    branch_part = contract_last(mixed_low, w_out)
    branch = lax.psum_scatter(
        branch_part.reshape(seqs_local, rows_ctx, model_width).astype(jnp.bfloat16),
        "experts",
        scatter_dimension=1,
        tiled=True,
    ).astype(jnp.float32)
    own_inputs = lax.dynamic_slice_in_dim(inputs, own_index * own_rows, own_rows, 1)
    after_attn = own_inputs + branch
    peak_all = lax.pmax(head_peak, ("dp", "context"))
    head_clip_scale = clip_limit / jnp.maximum(peak_all, clip_limit)
    moe_in = rms_scale(after_attn, gain_moe).astype(jnp.bfloat16)
    pair_tokens = seqs_local * own_rows
    expert_total = capacity.shape[0]
    top_count = expert_ids.shape[2]
    slot_count = pair_tokens * top_count // expert_total
    moe_rows = moe_in.reshape(pair_tokens, model_width)
    routes = expert_ids.reshape(pair_tokens, top_count)
    choose = (
        routes[:, :, None] == jnp.arange(expert_total, dtype=jnp.int32)[None, None, :]
    ).astype(jnp.float32)
    chosen = jnp.sum(choose, axis=1).astype(jnp.int32)
    before = jnp.cumsum(chosen, axis=0) - chosen
    kept = (chosen > 0) & (before < capacity[None, :])
    share = jnp.sum(gate_values.reshape(pair_tokens, top_count)[:, :, None] * choose, axis=1)
    table_mask = kept.T[:, None, :] & (
        before.T[:, None, :] == jnp.arange(slot_count, dtype=jnp.int32)[None, :, None]
    )
    table = table_mask.astype(jnp.bfloat16)
    send_rows = jnp.einsum(
        "ecn,nd->ecd", table, moe_rows, preferred_element_type=jnp.float32
    ).astype(jnp.bfloat16)
    local_rows = lax.all_to_all(
        send_rows, ("dp", "experts"), split_axis=0, concat_axis=1, tiled=True
    )
    gate_pre = jnp.einsum("erd,edf->erf", local_rows, w_gate, preferred_element_type=jnp.float32)
    up_pre = jnp.einsum("erd,edf->erf", local_rows, w_up, preferred_element_type=jnp.float32)
    sigmoid_gate = jax.nn.sigmoid(gate_pre)
    silu_gate = gate_pre * sigmoid_gate
    activation = (silu_gate * up_pre).astype(jnp.bfloat16)
    produced = jnp.einsum(
        "erf,edf->erd", activation, w_down, preferred_element_type=jnp.float32
    ).astype(jnp.bfloat16)
    returned = lax.all_to_all(produced, ("dp", "experts"), split_axis=1, concat_axis=0, tiled=True)
    per_expert = jnp.einsum("ecn,ecd->ned", table, returned, preferred_element_type=jnp.float32)
    moe_out = jnp.sum(share[:, :, None] * per_expert, axis=1)
    layer_out = after_attn + moe_out.reshape(seqs_local, own_rows, model_width)
    out_grad = cotangent.astype(jnp.float32)
    cot_rows = cotangent.reshape(pair_tokens, model_width)
    dots = jnp.sum(per_expert * out_grad.reshape(pair_tokens, 1, model_width), axis=2)
    gate_grad = jnp.sum(choose * dots[:, None, :], axis=2).reshape(seqs_local, own_rows, top_count)
    slot_share = jnp.sum(table.astype(jnp.float32) * share.T[:, None, :], axis=2)
    slot_rows = jnp.einsum("ecn,nd->ecd", table, cot_rows, preferred_element_type=jnp.float32)
    grad_send = (slot_rows * slot_share[:, :, None]).astype(jnp.bfloat16)
    grad_rows = lax.all_to_all(
        grad_send, ("dp", "experts"), split_axis=0, concat_axis=1, tiled=True
    )
    act_back = jnp.einsum("erd,edf->erf", grad_rows, w_down, preferred_element_type=jnp.float32)
    gate_back = (act_back * up_pre * sigmoid_gate * (1.0 + gate_pre * (1.0 - sigmoid_gate))).astype(
        jnp.bfloat16
    )
    up_back = (act_back * silu_gate).astype(jnp.bfloat16)
    row_back = jnp.einsum("erf,edf->erd", gate_back, w_gate, preferred_element_type=jnp.float32)
    row_back = (
        row_back + jnp.einsum("erf,edf->erd", up_back, w_up, preferred_element_type=jnp.float32)
    ).astype(jnp.bfloat16)
    back_rows = lax.all_to_all(row_back, ("dp", "experts"), split_axis=1, concat_axis=0, tiled=True)
    moe_in_grad = jnp.einsum(
        "ecn,ecd->nd", table, back_rows, preferred_element_type=jnp.float32
    ).reshape(seqs_local, own_rows, model_width)
    full_gate = jnp.einsum(
        "erd,erf->edf", local_rows, gate_back, preferred_element_type=jnp.float32
    )
    full_up = jnp.einsum("erd,erf->edf", local_rows, up_back, preferred_element_type=jnp.float32)
    full_down = jnp.einsum(
        "erd,erf->edf", grad_rows, activation, preferred_element_type=jnp.float32
    )
    moe_part, moe_gain_part = rms_back(moe_in_grad, after_attn, gain_moe)
    after_grad = out_grad + moe_part
    branch_grad = lax.all_gather(after_grad.astype(jnp.bfloat16), "experts", axis=1, tiled=True)
    branch_flat = branch_grad.reshape(token_count, model_width)
    heads_grad = jnp.dot(branch_flat, w_out, preferred_element_type=jnp.float32).astype(
        jnp.bfloat16
    )
    w_out_part = contract_first(branch_flat, mixed_low)
    heads_group = heads_grad.reshape(seqs_local, rows_ctx, kv_count, per_group, HEAD_SIZE)
    again_prob = jnp.exp(masked_scores() - log_total)
    again_low = again_prob.astype(jnp.bfloat16)
    prob_grad = jnp.einsum(
        "sqhgd,skhd->shqgk", heads_group, values_all, preferred_element_type=jnp.float32
    )
    delta = jnp.sum(again_prob * prob_grad, axis=-1, keepdims=True)
    score_grad = (again_prob * (prob_grad - delta)).astype(jnp.bfloat16)
    query_rot_grad = (
        jnp.einsum("shqgk,skhd->sqhgd", score_grad, keys_all, preferred_element_type=jnp.float32)
        * score_scale
    )
    key_part = (
        jnp.einsum("shqgk,sqhgd->skhd", score_grad, query_group, preferred_element_type=jnp.float32)
        * score_scale
    )
    value_part = jnp.einsum(
        "shqgk,sqhgd->skhd", again_low, heads_group, preferred_element_type=jnp.float32
    )
    key_rot_grad, value_grad = (
        lax.psum_scatter(
            key_part.astype(jnp.bfloat16), "context", scatter_dimension=1, tiled=True
        ).astype(jnp.float32),
        lax.psum_scatter(
            value_part.astype(jnp.bfloat16), "context", scatter_dimension=1, tiled=True
        ).astype(jnp.float32),
    )

    def rope_back(gradient):
        return gradient * cosine_table + turn_back(gradient * sine_table)

    query_normed_grad = rope_back(
        query_rot_grad.reshape(seqs_local, rows_ctx, head_count, HEAD_SIZE)
    )
    query_grad, query_gain_part = rms_back(query_normed_grad, query_raw, gain_query)
    key_grad, key_gain_part = rms_back(rope_back(key_rot_grad), unclipped_key, gain_key)
    query_low = query_grad.astype(jnp.bfloat16).reshape(token_count, head_count * HEAD_SIZE)
    key_low = key_grad.astype(jnp.bfloat16).reshape(token_count, kv_count * HEAD_SIZE)
    value_back = value_grad.astype(jnp.bfloat16).reshape(token_count, kv_count * HEAD_SIZE)
    normed_grad = (
        contract_last(query_low, w_query)
        + contract_last(key_low, key_weight_matrix)
        + contract_last(value_back, value_weight_matrix)
    )
    w_query_part = contract_first(normed_flat, query_low)
    w_key_part = contract_first(normed_flat, key_low)
    w_value_part = contract_first(normed_flat, value_back)
    own_normed_grad = lax.psum_scatter(
        normed_grad.reshape(seqs_local, rows_ctx, model_width).astype(jnp.bfloat16),
        "experts",
        scatter_dimension=1,
        tiled=True,
    ).astype(jnp.float32)
    input_part, attn_gain_part = rms_back(own_normed_grad, own_inputs, gain_attn)
    input_grad = after_grad + input_part
    key_value_part = jnp.concatenate([w_key_part, w_value_part], axis=1)
    w_gate_grad, w_up_grad, w_down_grad, w_query_grad, w_key_value_grad, w_out_grad = (
        reduce_weights(
            full_gate.astype(jnp.bfloat16),
            full_up.astype(jnp.bfloat16),
            full_down.astype(jnp.bfloat16),
            w_query_part.astype(jnp.bfloat16),
            key_value_part.astype(jnp.bfloat16),
            w_out_part.astype(jnp.bfloat16),
        )
    )
    w_key_grad, w_value_grad = w_key_value_grad[:, :128], w_key_value_grad[:, 128:]
    w_gate_grad, w_up_grad, w_down_grad = w_gate_grad[None], w_up_grad[None], w_down_grad[None]
    attn_gain_grad, query_gain_grad, key_gain_grad, moe_gain_grad = lax.psum(
        (attn_gain_part, query_gain_part, key_gain_part, moe_gain_part),
        ("dp", "context", "experts"),
    )
    return (
        layer_out,
        input_grad,
        attn_gain_grad,
        query_gain_grad,
        key_gain_grad,
        w_query_grad,
        w_key_grad,
        w_value_grad,
        w_out_grad,
        moe_gain_grad,
        gate_grad,
        w_gate_grad,
        w_up_grad,
        w_down_grad,
        head_clip_scale,
    )


def solution(mesh):
    in_specs = (
        P("dp", "context", None),
        P("dp", None),
        P(),
        P(),
        P(),
        P(None, "experts"),
        P(None, "experts"),
        P(None, "experts"),
        P(None, "experts"),
        P(),
        P("dp", ("context", "experts"), None),
        P("dp", ("context", "experts"), None),
        P(),
        P(("dp", "experts"), None, None),
        P(("dp", "experts"), None, None),
        P(("dp", "experts"), None, None),
        P("dp", ("context", "experts"), None),
    )
    out_specs = (
        P("dp", ("context", "experts"), None),
        P("dp", ("context", "experts"), None),
        P(),
        P(),
        P(),
        P(("dp", "context"), "experts"),
        P(("dp", "context"), "experts"),
        P(("dp", "context"), "experts"),
        P(("dp", "context"), "experts"),
        P(),
        P("dp", ("context", "experts"), None),
        P(("dp", "experts"), "context", None),
        P(("dp", "experts"), "context", None),
        P(("dp", "experts"), "context", None),
        P("experts"),
    )
    return jax.shard_map(shards, mesh=mesh, in_specs=in_specs, out_specs=out_specs, check_vma=False)
```

```python
import functools
import itertools

import jax
import jax.numpy as jnp
from jax import lax
from jax.experimental import pallas as pl
from jax.experimental.pallas import tpu as pltpu
from jax.sharding import PartitionSpec as P

HEAD_SIZE = 128
MESH = pl.DeviceIdType.MESH
VMEM = pl.BlockSpec(memory_space=pltpu.VMEM)


epsilon = 1e-06
rope_base = 1000000.0
clip_limit = 1.0
masked_value = -1e30


def rms_scale(values, factor):
    return values * lax.rsqrt(jnp.mean(values * values, axis=-1, keepdims=True) + epsilon) * factor


def rms_back(gradient, values, factor):
    inverse = lax.rsqrt(jnp.mean(values * values, axis=-1, keepdims=True) + epsilon)
    normal = values * inverse
    scaled = gradient * factor
    result = inverse * (scaled - normal * jnp.mean(scaled * normal, axis=-1, keepdims=True))
    return (result, jnp.sum(gradient * normal, axis=tuple(range(values.ndim - 1))))


def turn(values):
    middle = values.shape[-1] // 2
    return jnp.concatenate([-values[..., middle:], values[..., :middle]], axis=-1)


def turn_back(values):
    middle = values.shape[-1] // 2
    return jnp.concatenate([values[..., middle:], -values[..., :middle]], axis=-1)


def rotary(offset, amount):
    inverse = 1.0 / rope_base ** (jnp.arange(0, HEAD_SIZE, 2, dtype=jnp.float32) / HEAD_SIZE)
    position = (offset + jnp.arange(amount, dtype=jnp.int32)).astype(jnp.float32)
    angle = position[:, None] * inverse[None, :]
    angle = jnp.concatenate([angle, angle], axis=-1)
    return (jnp.cos(angle), jnp.sin(angle))


def contract_last(left, right):
    return lax.dot_general(
        left, right, (((1,), (1,)), ((), ())), preferred_element_type=jnp.float32
    )


def contract_first(left, right):
    return lax.dot_general(
        left, right, (((0,), (0,)), ((), ())), preferred_element_type=jnp.float32
    )


class Place:
    def __init__(self):
        dp = lax.axis_index("dp")
        context = lax.axis_index("context")
        self.dp, self.context, self.y = dp, context, lax.axis_index("experts")
        self.core, self.z_hi = lax.rem(dp, 2), dp // 2
        self.x, self.z_lo = context // 2, lax.rem(context, 2)
        self.z = self.z_hi * 2 + self.z_lo

    def at(self, x=None, y=None, z=None, core=None):
        x = self.x if x is None else x
        y = self.y if y is None else y
        z = self.z if z is None else z
        core = self.core if core is None else core
        return (z // 2 * 2 + core, x * 2 + lax.rem(z, 2), y)

    def x_by(self, step):
        return lax.rem(self.x + step, 4)

    def y_by(self, step):
        return lax.rem(self.y + step, 4)

    def z_by(self, step):
        return lax.rem(self.z + step, 4)


class Net:
    def __init__(self, send, recv):
        self.send, self.recv, self.copies = send, recv, []

    def copy(self, src, dst, device):
        spot = len(self.copies)
        made = pltpu.make_async_remote_copy(
            src_ref=src,
            dst_ref=dst,
            send_sem=self.send.at[spot],
            recv_sem=self.recv.at[spot],
            device_id=device,
            device_id_type=MESH,
        )
        made.start()
        self.copies.append(made)
        return made

    def sent(self, made):
        made.wait_send()
        self.copies = [None if one is made else one for one in self.copies]

    def finish(self):
        for made in self.copies:
            if made is not None:
                made.wait_send()


def greet(devices):
    barrier = pltpu.get_barrier_semaphore()
    for device in devices:
        pl.semaphore_signal(barrier, inc=1, device_id=device, device_id_type=MESH)
    pl.semaphore_wait(barrier, len(devices))


def add_into(target, parts, block=32):
    rows = target.shape[-2]
    block = min(block, rows)
    for lead in itertools.product(*[range(size) for size in target.shape[:-2]]):

        def body(step, carry, lead=lead):
            spot = lead + (pl.ds(pl.multiple_of(step * block, block), block),)
            total = parts[0][spot].astype(jnp.float32)
            for part in parts[1:]:
                total = total + part[spot].astype(jnp.float32)
            target[spot] = total.astype(target.dtype)
            return carry

        lax.fori_loop(0, rows // block, body, 0)


def ring_reduce(net, plus, minus, own, slots, target):
    first_plus = net.copy(own(2, 0), slots.at[0], plus)
    first_minus = net.copy(own(2, 1), slots.at[2], minus)
    side_plus = net.copy(own(1, 1), slots.at[1], plus)
    side_minus = net.copy(own(3, 0), slots.at[3], minus)
    yield
    first_plus.wait_recv()
    add_into(slots.at[0], [slots.at[0], own(1, 0)])
    last_plus = net.copy(slots.at[0], slots.at[4], plus)
    first_minus.wait_recv()
    add_into(slots.at[2], [slots.at[2], own(3, 1)])
    last_minus = net.copy(slots.at[2], slots.at[5], minus)
    yield
    side_minus.wait_recv()
    last_plus.wait_recv()
    add_into(target(0), [own(0, 0), slots.at[3], slots.at[4]])
    side_plus.wait_recv()
    last_minus.wait_recv()
    add_into(target(1), [own(0, 1), slots.at[1], slots.at[5]])


def expert_x_first(net, me, source, slots, middle, other, out):
    ring = ring_reduce(
        net,
        me.at(x=me.x_by(1)),
        me.at(x=me.x_by(3)),
        lambda step, half: source.at[me.x_by(step), half],
        slots,
        lambda half: middle.at[half],
    )
    yield from ring
    across = net.copy(middle.at[1 - me.z_lo], other, me.at(z=me.z + 1 - 2 * me.z_lo))
    yield
    across.wait_recv()
    add_into(out, [middle.at[me.z_lo], other])


def expert_z_first(net, me, source, other, middle, slots, out):
    across = net.copy(source.at[:, 1 - me.z_lo], other, me.at(z=me.z + 1 - 2 * me.z_lo))
    yield
    across.wait_recv()
    add_into(middle, [source.at[:, me.z_lo], other])
    half_rows = middle.shape[1] // 2
    yield from ring_reduce(
        net,
        me.at(x=me.x_by(1)),
        me.at(x=me.x_by(3)),
        lambda step, half: middle.at[me.x_by(step), pl.ds(half * half_rows, half_rows)],
        slots,
        lambda half: out.at[pl.ds(half * half_rows, half_rows)],
    )


def core_pair(net, me, source, other, middle):
    across = net.copy(source.at[:, 1 - me.core], other, me.at(core=1 - me.core))
    yield
    across.wait_recv()
    add_into(middle, [source.at[:, me.core], other])


def dense_x_first(net, me, source, other, middle, slots, corner, last, out):
    yield from core_pair(net, me, source, other, middle)
    yield from ring_reduce(
        net,
        me.at(x=me.x_by(1)),
        me.at(x=me.x_by(3)),
        lambda step, half: middle.at[half, me.x_by(step)],
        slots,
        lambda half: corner.at[half],
    )
    half_rows = corner.shape[2] // 2
    yield from ring_reduce(
        net,
        me.at(z=me.z_by(1)),
        me.at(z=me.z_by(3)),
        lambda step, half: corner.at[
            me.z_by(step) // 2, lax.rem(me.z_by(step), 2), pl.ds(half * half_rows, half_rows)
        ],
        last,
        lambda half: out.at[pl.ds(half * half_rows, half_rows)],
    )


def dense_z_first(net, me, source, other, middle, slots, corner, last, out):
    yield from core_pair(net, me, source, other, middle)
    yield from ring_reduce(
        net,
        me.at(z=me.z_by(1)),
        me.at(z=me.z_by(3)),
        lambda step, half: middle.at[
            me.z_by(step) // 2, pl.ds(half * 2, 2), lax.rem(me.z_by(step), 2)
        ],
        slots,
        lambda half: corner.at[pl.ds(half * 2, 2)],
    )
    half_rows = corner.shape[1] // 2
    yield from ring_reduce(
        net,
        me.at(x=me.x_by(1)),
        me.at(x=me.x_by(3)),
        lambda step, half: corner.at[me.x_by(step), pl.ds(half * half_rows, half_rows)],
        last,
        lambda half: out.at[pl.ds(half * half_rows, half_rows)],
    )


def all_sum(net, devices, spot, own, slots, most):
    slots[spot] = own[...]
    sent = [net.copy(own, slots.at[spot], device) for device in devices]
    yield
    for made in sent:
        made.wait_recv()
    count = slots.shape[0]
    total = slots[0]
    peak = slots[0, most:]
    for step in range(1, count):
        total = total + slots[step]
        peak = jnp.maximum(peak, slots[step, most:])
    for made in sent:
        net.sent(made)
    own[:most] = total[:most]
    own[most:] = peak


def all_small(net, me, small, working, by_core, by_x, by_z, by_y, out):
    working[...] = small[...]
    yield from all_sum(net, [me.at(core=1 - me.core)], me.core, working, by_core, 40)
    yield from all_sum(net, [me.at(x=me.x_by(s)) for s in (1, 2, 3)], me.x, working, by_x, 40)
    yield from all_sum(net, [me.at(z=me.z_by(s)) for s in (1, 2, 3)], me.z, working, by_z, 40)
    out[40:] = working[40:]
    yield from all_sum(net, [me.at(y=me.y_by(s)) for s in (1, 2, 3)], me.y, working, by_y, 40)
    out[:40] = working[:40]


def peers(me):
    offsets = [(a, b) for a in (2, 3, 0, 1) for b in (1, 3, 2, 0) if a or b]
    return [(a, b) + peer(me, a, b) for a, b in offsets]


def peer(me, a, b):
    z = me.z if a < 2 else lax.rem(me.z + 2, 4)
    core = me.core if a % 2 == 0 else 1 - me.core
    y = me.y_by(b)
    return z // 2 * 2 + core, y, me.at(z=z, core=core, y=y)


def bring_home(net, me, produced, home, table, after, out):
    sent = []
    for a, b, dp, y, device in peers(me):
        sent.append(net.copy(produced.at[dp, y], home.at[me.dp, me.y], device))
    home[me.dp, me.y] = produced[me.dp, me.y]
    for step in range(5):
        yield
    for made in sent:
        made.wait_recv()
    gather_rows(
        table,
        home,
        lambda columns, total: out.__setitem__(
            (slice(None), columns), after[:, columns] + total
        ),
    )


def gather_rows(table, home, store):
    def body(step, carry):
        columns = pl.ds(pl.multiple_of(step * 256, 256), 256)
        rows = home[:, :, :, columns].reshape(768, 256)
        total = contract_first(table[...], rows)
        store(columns, total[:96])
        return carry

    lax.fori_loop(0, home.shape[3] // 256, body, 0)


def in_turn(tasks):
    tasks = list(tasks)
    while tasks:
        for task in list(tasks):
            if next(task, "end") == "end":
                tasks.remove(task)


def reduce_kernel(counts, *refs):
    refs = list(refs)

    def take(number):
        taken = refs[:number]
        del refs[:number]
        return taken

    gate, up, down, query, key_value, out_w, small, produced, table, after = take(10)
    gate_out, up_out, down_out, query_out, key_value_out, out_w_out, small_out, layer = take(8)
    scratch = [take(count) for count in counts]
    send, recv = take(2)
    me = Place()
    greet(
        [
            me.at(x=me.x_by(1)),
            me.at(x=me.x_by(3)),
            me.at(z=me.z_by(1)),
            me.at(z=me.z_by(3)),
            me.at(x=me.x_by(2)),
            me.at(z=me.z_by(2)),
        ]
        + [one[4] for one in peers(me) if one[:2] != (2, 0)]
    )
    net = Net(send, recv)
    in_turn(
        [
            all_small(net, me, small, *scratch[6], small_out),
            dense_z_first(net, me, out_w, *scratch[5], out_w_out),
            dense_x_first(net, me, query, *scratch[3], query_out),
            dense_x_first(net, me, key_value, *scratch[4], key_value_out),
            expert_z_first(net, me, down, *scratch[2], down_out),
            expert_x_first(net, me, gate, *scratch[0], gate_out),
            expert_x_first(net, me, up, *scratch[1], up_out),
            bring_home(net, me, produced, *scratch[7], table, after, layer),
        ]
    )
    net.finish()


def reduce_weights(gate, up, down, query, key_value, out_w, small, produced, table, after):
    low = jnp.bfloat16
    x_first = [
        pltpu.VMEM((6, 256, 768), low),
        pltpu.VMEM((2, 256, 768), low),
        pltpu.VMEM((256, 768), low),
    ]
    z_first = [
        pltpu.VMEM((4, 256, 768), low),
        pltpu.VMEM((4, 256, 768), low),
        pltpu.VMEM((6, 128, 768), low),
    ]

    def dense(columns, x_first):
        return [
            pltpu.VMEM((2, 4, 2, 64, columns), low),
            pltpu.VMEM((2, 4, 2, 64, columns), low),
            pltpu.VMEM((6, 2, 64, columns), low),
            pltpu.VMEM((2, 2, 64, columns) if x_first else (4, 64, columns), low),
            pltpu.VMEM((6, 32, columns), low),
        ]

    smalls = [pltpu.VMEM(small.shape, jnp.float32)] + [
        pltpu.VMEM((count,) + small.shape, jnp.float32) for count in (2, 4, 4, 4)
    ]
    groups = [x_first, x_first, z_first, dense(1024, True), dense(256, True), dense(1024, False)]
    groups += [smalls, [pltpu.VMEM((4, 4, 48, 2048), low)]]
    copies = 90
    return pl.pallas_call(
        functools.partial(reduce_kernel, [len(group) for group in groups]),
        out_shape=[
            jax.ShapeDtypeStruct((256, 768), jnp.float32),
            jax.ShapeDtypeStruct((256, 768), jnp.float32),
            jax.ShapeDtypeStruct((256, 768), jnp.float32),
            jax.ShapeDtypeStruct((64, 1024), jnp.float32),
            jax.ShapeDtypeStruct((64, 256), jnp.float32),
            jax.ShapeDtypeStruct((64, 1024), jnp.float32),
            jax.ShapeDtypeStruct(small.shape, jnp.float32),
            jax.ShapeDtypeStruct(after.shape, jnp.float32),
        ],
        in_specs=[VMEM] * 10,
        out_specs=[VMEM] * 8,
        scratch_shapes=[one for group in groups for one in group]
        + [pltpu.SemaphoreType.DMA((copies,)), pltpu.SemaphoreType.DMA((copies,))],
        compiler_params=pltpu.CompilerParams(
            collective_id=0, has_side_effects=True, vmem_limit_bytes=56 << 20
        ),
        name="reduce_weights",
    )(
        gate.reshape(4, 2, 256, 768),
        up.reshape(4, 2, 256, 768),
        down.reshape(4, 2, 256, 768),
        query.reshape(2, 2, 4, 2, 64, 1024),
        key_value.reshape(2, 2, 4, 2, 64, 256),
        out_w.reshape(2, 2, 4, 2, 64, 1024),
        small,
        produced,
        table,
        after,
    )


def moe_kernel(
    after,
    cotangent,
    gain,
    ids,
    gates,
    capacity,
    w_gate,
    w_up,
    w_down,
    after_grad,
    gain_part,
    gate_grad,
    produced,
    table,
    full_gate,
    full_up,
    full_down,
    rows,
    sending,
    sending_grad,
    info,
    info_in,
    local,
    grads,
    act,
    gate_back,
    up_back,
    back,
    home,
    dots,
    dots_in,
    send,
    recv,
):
    low, full = jnp.bfloat16, jnp.float32
    me = Place()
    greet([one[4] for one in peers(me)])
    net = Net(send, recv)

    expert = lax.broadcasted_iota(jnp.int32, (16, 128), 0)
    chosen = jnp.zeros((16, 128), full)
    share = jnp.zeros((16, 128), full)
    for k in range(8):
        named = ids[k : k + 1, :] == expert
        chosen = chosen + jnp.where(named, 1.0, 0.0)
        share = share + jnp.where(named, gates[k : k + 1, :], 0.0)
    earlier = lax.broadcasted_iota(jnp.int32, (128, 128), 0) < lax.broadcasted_iota(
        jnp.int32, (128, 128), 1
    )
    before = jnp.dot(
        chosen.astype(low), jnp.where(earlier, 1.0, 0.0).astype(low), preferred_element_type=full
    )
    slot = jnp.where((chosen > 0.0) & (before < capacity[...]), before, -1.0)
    spot = lax.broadcasted_iota(jnp.int32, (48, 128), 0).astype(full)
    for e in range(16):
        mask = jnp.where(slot[e : e + 1, :] == spot, 1.0, 0.0)
        table[e * 48 : e * 48 + 48, :] = mask.astype(low)
        info[e // 4, e % 4] = jnp.concatenate(
            [slot[e : e + 1, :], share[e : e + 1, :], jnp.zeros((6, 128), full)], axis=0
        )

    def dispatch(sender):
        for a, b, dp, y, device in peers(me):
            if b == 1:
                rest = table[pl.ds(pl.multiple_of(dp * 192, 192), 192), :]
                columns = 512
                for step in range(2048 // columns):
                    run = slice(step * columns, (step + 1) * columns)
                    picked = jnp.dot(rest, rows[:, run], preferred_element_type=full)
                    sender[dp, :, :, run] = picked.astype(low).reshape(4, 48, columns)
            yield a, b, dp, y, device

    told, came, grad_came = {}, {}, {}
    for a, b, dp, y, device in peers(me):
        told[a, b] = net.copy(info.at[dp, y], info_in.at[me.dp, me.y], device)
    info_in[me.dp, me.y] = info[me.dp, me.y]
    values = after[...]
    inverse = lax.rsqrt(jnp.mean(values * values, axis=-1, keepdims=True) + epsilon)
    rows[96:, :] = jnp.zeros((32, 2048), low)
    rows[:96, :] = (values * inverse * gain[...]).astype(low)
    for a, b, dp, y, device in dispatch(sending):
        came[a, b] = net.copy(sending.at[dp, y], local.at[me.dp, me.y], device)
    local[me.dp, me.y] = sending[me.dp, me.y]
    rows[:96, :] = cotangent[...]
    for a, b, dp, y, device in dispatch(sending_grad):
        grad_came[a, b] = net.copy(sending_grad.at[dp, y], grads.at[me.dp, me.y], device)
    grads[me.dp, me.y] = sending_grad[me.dp, me.y]

    back_came, dots_came = {}, {}
    for a in (0, 1, 2, 3):
        group = peer(me, a, 0)[0]
        for b in range(4):
            if a or b:
                told[a, b].wait_recv()
                came[a, b].wait_recv()
                grad_came[a, b].wait_recv()
        masks, shares = [], []
        for y in range(4):
            mask = info_in[group, y, 0:1, :] == spot
            masks.append(mask)
            shares.append(
                jnp.sum(jnp.where(mask, info_in[group, y, 1:2, :], 0.0), axis=1, keepdims=True)
            )
        shared = jnp.concatenate(shares, axis=0)

        def inner(step, carry, group=group, shared=shared):
            columns = pl.ds(pl.multiple_of(step * 256, 256), 256)
            entered = local[group].reshape(192, 2048)
            gate_pre = jnp.dot(entered, w_gate[:, columns], preferred_element_type=full)
            up_pre = jnp.dot(entered, w_up[:, columns], preferred_element_type=full)
            scaled = (grads[group].reshape(192, 2048).astype(full) * shared).astype(low)
            act_back = jnp.dot(scaled, w_down[:, columns], preferred_element_type=full)
            sigmoid = 1.0 / (1.0 + jnp.exp(-gate_pre))
            silu = gate_pre * sigmoid
            act[group, :, columns] = (silu * up_pre).astype(low)
            gate_back[group, :, columns] = (
                act_back * up_pre * sigmoid * (1.0 + gate_pre * (1.0 - sigmoid))
            ).astype(low)
            up_back[group, :, columns] = (act_back * silu).astype(low)
            return carry

        lax.fori_loop(0, 3, inner, 0)

        def outer(step, dot, group=group, shared=shared):
            columns = pl.ds(pl.multiple_of(step * 256, 256), 256)
            made = contract_last(act[group], w_down[columns, :]).astype(low).astype(full)
            produced[group, :, :, columns] = (made * shared).astype(low).reshape(4, 48, 256)
            incoming = grads[group, :, :, columns].reshape(192, 256).astype(full)
            dot = dot + jnp.sum(made * incoming, axis=1, keepdims=True)
            grads[group, :, :, columns] = (incoming * shared).astype(low).reshape(4, 48, 256)
            row_back = contract_last(gate_back[group], w_gate[columns, :]) + contract_last(
                up_back[group], w_up[columns, :]
            )
            back[group, :, :, columns] = row_back.astype(low).reshape(4, 48, 256)
            return dot

        dot = lax.fori_loop(0, 8, outer, jnp.zeros((192, 1), full))
        for y in range(4):
            line = jnp.sum(
                jnp.where(masks[y], dot[y * 48 : y * 48 + 48], 0.0), axis=0, keepdims=True
            )
            dots[group, y] = jnp.broadcast_to(line, (8, 128))
        for b in (2, 1, 3, 0):
            if a or b:
                dp, y, device = peer(me, a, b)
                back_came[a, b] = net.copy(back.at[dp, y], home.at[me.dp, me.y], device)
                dots_came[a, b] = net.copy(dots.at[dp, y], dots_in.at[me.dp, me.y], device)
    home[me.dp, me.y] = back[me.dp, me.y]
    dots_in[me.dp, me.y] = dots[me.dp, me.y]

    def weigh(step, carry):
        columns = pl.ds(pl.multiple_of(step * 256, 256), 256)
        entered = local[:, :, :, columns].reshape(768, 256)
        full_gate[columns, :] = contract_first(entered, gate_back[...].reshape(768, 768)).astype(low)
        full_up[columns, :] = contract_first(entered, up_back[...].reshape(768, 768)).astype(low)
        incoming = grads[:, :, :, columns].reshape(768, 256)
        full_down[columns, :] = contract_first(incoming, act[...].reshape(768, 768)).astype(low)
        return carry

    lax.fori_loop(0, 8, weigh, 0)

    for a, b, *_ in peers(me):
        back_came[a, b].wait_recv()
        dots_came[a, b].wait_recv()
    chosen_dots = [jnp.zeros((1, 128), full) for k in range(8)]
    for e in range(16):
        line = dots_in[e // 4, e % 4, 0:1, :]
        for k in range(8):
            chosen_dots[k] = chosen_dots[k] + jnp.where(ids[k : k + 1, :] == e, line, 0.0)
    gate_grad[...] = jnp.concatenate(chosen_dots, axis=0)

    def keep(columns, total):
        after_grad[:, columns] = total

    gather_rows(table, home, keep)
    gradient = after_grad[...]
    values = after[...]
    inverse = lax.rsqrt(jnp.mean(values * values, axis=-1, keepdims=True) + epsilon)
    normal = values * inverse
    gain_part[...] = jnp.sum(gradient * normal, axis=0, keepdims=True)
    scaled = gradient * gain[...]
    mean = jnp.mean(scaled * normal, axis=-1, keepdims=True)
    after_grad[...] = cotangent[...].astype(full) + inverse * (scaled - normal * mean)
    net.finish()


def moe(after, cotangent, gain, ids, gates, capacity, w_gate, w_up, w_down):
    low, full = jnp.bfloat16, jnp.float32
    copies = 75
    shape = jax.ShapeDtypeStruct
    return pl.pallas_call(
        moe_kernel,
        out_shape=[
            shape((96, 2048), full),
            shape((1, 2048), full),
            shape((8, 128), full),
            shape((4, 4, 48, 2048), low),
            shape((768, 128), low),
            shape((2048, 768), low),
            shape((2048, 768), low),
            shape((2048, 768), low),
        ],
        in_specs=[VMEM] * 9,
        out_specs=[VMEM] * 8,
        scratch_shapes=[
            pltpu.VMEM((128, 2048), low),
            pltpu.VMEM((4, 4, 48, 2048), low),
            pltpu.VMEM((4, 4, 48, 2048), low),
            pltpu.VMEM((4, 4, 8, 128), full),
            pltpu.VMEM((4, 4, 8, 128), full),
            pltpu.VMEM((4, 4, 48, 2048), low),
            pltpu.VMEM((4, 4, 48, 2048), low),
            pltpu.VMEM((4, 192, 768), low),
            pltpu.VMEM((4, 192, 768), low),
            pltpu.VMEM((4, 192, 768), low),
            pltpu.VMEM((4, 4, 48, 2048), low),
            pltpu.VMEM((4, 4, 48, 2048), low),
            pltpu.VMEM((4, 4, 8, 128), full),
            pltpu.VMEM((4, 4, 8, 128), full),
            pltpu.SemaphoreType.DMA((copies,)),
            pltpu.SemaphoreType.DMA((copies,)),
        ],
        compiler_params=pltpu.CompilerParams(
            collective_id=1, has_side_effects=True, vmem_limit_bytes=60 << 20
        ),
        name="moe",
    )(after, cotangent, gain, ids, gates, capacity, w_gate, w_up, w_down)


def shards(
    hidden_in,
    segments,
    attn_gain,
    query_gain,
    key_gain,
    w_query,
    key_weight_matrix,
    value_weight_matrix,
    w_out,
    moe_gain,
    expert_ids,
    gate_values,
    capacity,
    w_gate,
    w_up,
    w_down,
    cotangent,
):
    seqs_local, rows_ctx, model_width = hidden_in.shape
    seq_length = segments.shape[1]
    expert_span = lax.axis_size("experts")
    ctx_index = lax.axis_index("context")
    own_index = lax.axis_index("experts")
    own_rows = rows_ctx // expert_span
    head_count = w_query.shape[1] // HEAD_SIZE
    kv_count = key_weight_matrix.shape[1] // HEAD_SIZE
    per_group = head_count // kv_count
    score_scale = HEAD_SIZE ** (-0.5)
    token_count = seqs_local * rows_ctx
    inputs = hidden_in.astype(jnp.float32)
    gain_attn = attn_gain.astype(jnp.float32)
    gain_query = query_gain.astype(jnp.float32)
    gain_key = key_gain.astype(jnp.float32)
    gain_moe = moe_gain.astype(jnp.float32)
    normalized_input = rms_scale(inputs, gain_attn).astype(jnp.bfloat16)
    normed_flat = normalized_input.reshape(token_count, model_width)
    query_raw = jnp.dot(normed_flat, w_query, preferred_element_type=jnp.float32).reshape(
        seqs_local, rows_ctx, head_count, HEAD_SIZE
    )
    unclipped_key = jnp.dot(
        normed_flat, key_weight_matrix, preferred_element_type=jnp.float32
    ).reshape(seqs_local, rows_ctx, kv_count, HEAD_SIZE)
    value_reduced = (
        jnp.dot(normed_flat, value_weight_matrix, preferred_element_type=jnp.float32)
        .astype(jnp.bfloat16)
        .reshape(seqs_local, rows_ctx, kv_count, HEAD_SIZE)
    )
    cosine_table, sine_table = rotary(ctx_index * rows_ctx, rows_ctx)
    cosine_table = cosine_table[None, :, None, :]
    sine_table = sine_table[None, :, None, :]
    query_normed = rms_scale(query_raw, gain_query)
    query_rot = (query_normed * cosine_table + turn(query_normed) * sine_table).astype(jnp.bfloat16)
    key_normed = rms_scale(unclipped_key, gain_key)
    key_rot = (key_normed * cosine_table + turn(key_normed) * sine_table).astype(jnp.bfloat16)
    keys_all, values_all = (
        lax.all_gather(key_rot, "context", axis=1, tiled=True),
        lax.all_gather(value_reduced, "context", axis=1, tiled=True),
    )
    query_group = query_rot.reshape(seqs_local, rows_ctx, kv_count, per_group, HEAD_SIZE)
    seg_query = lax.dynamic_slice_in_dim(segments, ctx_index * rows_ctx, rows_ctx, 1)
    query_spot = ctx_index * rows_ctx + jnp.arange(rows_ctx, dtype=jnp.int32)
    key_spot = jnp.arange(seq_length, dtype=jnp.int32)
    allowed = (seg_query[:, :, None] == segments[:, None, :]) & (
        key_spot[None, None, :] <= query_spot[None, :, None]
    )
    allowed = allowed[:, None, :, None, :]

    def masked_scores():
        raw_score = (
            jnp.einsum(
                "sqhgd,skhd->shqgk", query_group, keys_all, preferred_element_type=jnp.float32
            )
            * score_scale
        )
        return jnp.where(allowed, raw_score, masked_value)

    masked = masked_scores()
    row_peak = jnp.max(masked, axis=-1, keepdims=True)
    log_total = row_peak + jnp.log(jnp.sum(jnp.exp(masked - row_peak), axis=-1, keepdims=True))
    head_peak = jnp.max(masked, axis=(0, 2, 4)).reshape(head_count)
    prob_low = jnp.exp(masked - log_total).astype(jnp.bfloat16)
    mixed_heads = jnp.einsum(
        "shqgk,skhd->sqhgd", prob_low, values_all, preferred_element_type=jnp.float32
    )
    mixed_low = mixed_heads.astype(jnp.bfloat16).reshape(token_count, head_count * HEAD_SIZE)
    branch_part = contract_last(mixed_low, w_out)
    branch = lax.psum_scatter(
        branch_part.reshape(seqs_local, rows_ctx, model_width).astype(jnp.bfloat16),
        "experts",
        scatter_dimension=1,
        tiled=True,
    ).astype(jnp.float32)
    own_inputs = lax.dynamic_slice_in_dim(inputs, own_index * own_rows, own_rows, 1)
    after_attn = own_inputs + branch
    pair_tokens = seqs_local * own_rows
    top_count = expert_ids.shape[2]
    token_lanes = ((0, 0), (0, 128 - pair_tokens))
    ids = jnp.pad(expert_ids.reshape(pair_tokens, top_count).T, token_lanes, constant_values=-1)
    gates = jnp.pad(gate_values.reshape(pair_tokens, top_count).T, token_lanes)
    after_flat = after_attn.reshape(pair_tokens, model_width)
    after_grad, moe_gain_part, gate_grad, produced, table, full_gate, full_up, full_down = moe(
        after_flat,
        cotangent.reshape(pair_tokens, model_width),
        gain_moe[None],
        ids,
        gates,
        jnp.broadcast_to(capacity.astype(jnp.float32)[:, None], (capacity.shape[0], 128)),
        w_gate[0],
        w_up[0],
        w_down[0],
    )
    after_grad = after_grad.reshape(seqs_local, own_rows, model_width)
    gate_grad = gate_grad[:, :pair_tokens].T.reshape(seqs_local, own_rows, top_count)
    branch_grad = lax.all_gather(after_grad.astype(jnp.bfloat16), "experts", axis=1, tiled=True)
    branch_flat = branch_grad.reshape(token_count, model_width)
    heads_grad = jnp.dot(branch_flat, w_out, preferred_element_type=jnp.float32).astype(
        jnp.bfloat16
    )
    w_out_part = contract_first(branch_flat, mixed_low)
    heads_group = heads_grad.reshape(seqs_local, rows_ctx, kv_count, per_group, HEAD_SIZE)
    again_prob = jnp.exp(masked_scores() - log_total)
    again_low = again_prob.astype(jnp.bfloat16)
    prob_grad = jnp.einsum(
        "sqhgd,skhd->shqgk", heads_group, values_all, preferred_element_type=jnp.float32
    )
    delta = jnp.sum(again_prob * prob_grad, axis=-1, keepdims=True)
    score_grad = (again_prob * (prob_grad - delta)).astype(jnp.bfloat16)
    query_rot_grad = (
        jnp.einsum("shqgk,skhd->sqhgd", score_grad, keys_all, preferred_element_type=jnp.float32)
        * score_scale
    )
    key_part = (
        jnp.einsum("shqgk,sqhgd->skhd", score_grad, query_group, preferred_element_type=jnp.float32)
        * score_scale
    )
    value_part = jnp.einsum(
        "shqgk,sqhgd->skhd", again_low, heads_group, preferred_element_type=jnp.float32
    )
    key_rot_grad, value_grad = (
        lax.psum_scatter(
            key_part.astype(jnp.bfloat16), "context", scatter_dimension=1, tiled=True
        ).astype(jnp.float32),
        lax.psum_scatter(
            value_part.astype(jnp.bfloat16), "context", scatter_dimension=1, tiled=True
        ).astype(jnp.float32),
    )

    def rope_back(gradient):
        return gradient * cosine_table + turn_back(gradient * sine_table)

    query_normed_grad = rope_back(
        query_rot_grad.reshape(seqs_local, rows_ctx, head_count, HEAD_SIZE)
    )
    query_grad, query_gain_part = rms_back(query_normed_grad, query_raw, gain_query)
    key_grad, key_gain_part = rms_back(rope_back(key_rot_grad), unclipped_key, gain_key)
    query_low = query_grad.astype(jnp.bfloat16).reshape(token_count, head_count * HEAD_SIZE)
    key_low = key_grad.astype(jnp.bfloat16).reshape(token_count, kv_count * HEAD_SIZE)
    value_back = value_grad.astype(jnp.bfloat16).reshape(token_count, kv_count * HEAD_SIZE)
    normed_grad = (
        contract_last(query_low, w_query)
        + contract_last(key_low, key_weight_matrix)
        + contract_last(value_back, value_weight_matrix)
    )
    w_query_part = contract_first(normed_flat, query_low)
    w_key_part = contract_first(normed_flat, key_low)
    w_value_part = contract_first(normed_flat, value_back)
    own_normed_grad = lax.psum_scatter(
        normed_grad.reshape(seqs_local, rows_ctx, model_width).astype(jnp.bfloat16),
        "experts",
        scatter_dimension=1,
        tiled=True,
    ).astype(jnp.float32)
    input_part, attn_gain_part = rms_back(own_normed_grad, own_inputs, gain_attn)
    input_grad = after_grad + input_part
    key_value_part = jnp.concatenate([w_key_part, w_value_part], axis=1)
    small = jnp.concatenate(
        [
            attn_gain_part.reshape(16, 128),
            moe_gain_part.reshape(16, 128),
            query_gain_part[None],
            key_gain_part[None],
            jnp.zeros((6, 128), jnp.float32),
            jnp.broadcast_to(head_peak[:, None], (head_count, 128)),
        ],
        axis=0,
    )
    (
        w_gate_grad,
        w_up_grad,
        w_down_grad,
        w_query_grad,
        w_key_value_grad,
        w_out_grad,
        small,
        layer_out,
    ) = reduce_weights(
        full_gate,
        full_up,
        full_down,
        w_query_part.astype(jnp.bfloat16),
        key_value_part.astype(jnp.bfloat16),
        w_out_part.astype(jnp.bfloat16),
        small,
        produced,
        table,
        after_flat,
    )
    layer_out = layer_out.reshape(seqs_local, own_rows, model_width)
    w_key_grad, w_value_grad = w_key_value_grad[:, :128], w_key_value_grad[:, 128:]
    w_gate_grad, w_up_grad, w_down_grad = w_gate_grad[None], w_up_grad[None], w_down_grad[None]
    attn_gain_grad = small[:16].reshape(model_width)
    moe_gain_grad = small[16:32].reshape(model_width)
    query_gain_grad, key_gain_grad = small[32], small[33]
    head_clip_scale = clip_limit / jnp.maximum(small[40:, 0], clip_limit)
    return (
        layer_out,
        input_grad,
        attn_gain_grad,
        query_gain_grad,
        key_gain_grad,
        w_query_grad,
        w_key_grad,
        w_value_grad,
        w_out_grad,
        moe_gain_grad,
        gate_grad,
        w_gate_grad,
        w_up_grad,
        w_down_grad,
        head_clip_scale,
    )


def solution(mesh):
    in_specs = (
        P("dp", "context", None),
        P("dp", None),
        P(),
        P(),
        P(),
        P(None, "experts"),
        P(None, "experts"),
        P(None, "experts"),
        P(None, "experts"),
        P(),
        P("dp", ("context", "experts"), None),
        P("dp", ("context", "experts"), None),
        P(),
        P(("dp", "experts"), None, None),
        P(("dp", "experts"), None, None),
        P(("dp", "experts"), None, None),
        P("dp", ("context", "experts"), None),
    )
    out_specs = (
        P("dp", ("context", "experts"), None),
        P("dp", ("context", "experts"), None),
        P(),
        P(),
        P(),
        P(("dp", "context"), "experts"),
        P(("dp", "context"), "experts"),
        P(("dp", "context"), "experts"),
        P(("dp", "context"), "experts"),
        P(),
        P("dp", ("context", "experts"), None),
        P(("dp", "experts"), "context", None),
        P(("dp", "experts"), "context", None),
        P(("dp", "experts"), "context", None),
        P("experts"),
    )
    return jax.shard_map(shards, mesh=mesh, in_specs=in_specs, out_specs=out_specs, check_vma=False)
```

```python
import functools
import itertools
import types

import jax
import jax.numpy as jnp
from jax import lax
from jax.experimental import pallas as pl
from jax.experimental.pallas import tpu as pltpu
from jax.sharding import PartitionSpec as P

HEAD_SIZE = 128
MESH = pl.DeviceIdType.MESH
VMEM = pl.BlockSpec(memory_space=pltpu.VMEM)
ANY = pl.BlockSpec(memory_space=pl.ANY)


epsilon = 1e-06
rope_base = 1000000.0
clip_limit = 1.0
masked_value = -1e30


def rms_scale(values, factor):
    return values * lax.rsqrt(jnp.mean(values * values, axis=-1, keepdims=True) + epsilon) * factor


def turn(values):
    middle = values.shape[-1] // 2
    return jnp.concatenate([-values[..., middle:], values[..., :middle]], axis=-1)


def rotary(offset, amount):
    inverse = 1.0 / rope_base ** (jnp.arange(0, HEAD_SIZE, 2, dtype=jnp.float32) / HEAD_SIZE)
    position = (offset + jnp.arange(amount, dtype=jnp.int32)).astype(jnp.float32)
    angle = position[:, None] * inverse[None, :]
    angle = jnp.concatenate([angle, angle], axis=-1)
    return (jnp.cos(angle), jnp.sin(angle))


def contract_last(left, right):
    return lax.dot_general(
        left, right, (((1,), (1,)), ((), ())), preferred_element_type=jnp.float32
    )


def contract_first(left, right):
    return lax.dot_general(
        left, right, (((0,), (0,)), ((), ())), preferred_element_type=jnp.float32
    )


class Place:
    def __init__(self):
        dp = lax.axis_index("dp")
        context = lax.axis_index("context")
        self.dp, self.context, self.y = dp, context, lax.axis_index("experts")
        self.core, self.z_hi = lax.rem(dp, 2), dp // 2
        self.x, self.z_lo = context // 2, lax.rem(context, 2)
        self.z = self.z_hi * 2 + self.z_lo

    def at(self, x=None, y=None, z=None, core=None):
        x = self.x if x is None else x
        y = self.y if y is None else y
        z = self.z if z is None else z
        core = self.core if core is None else core
        return (z // 2 * 2 + core, x * 2 + lax.rem(z, 2), y)

    def x_by(self, step):
        return lax.rem(self.x + step, 4)

    def y_by(self, step):
        return lax.rem(self.y + step, 4)

    def z_by(self, step):
        return lax.rem(self.z + step, 4)


class Net:
    def __init__(self, send, recv, here=None):
        self.send, self.recv, self.copies = send, recv, []
        self.here, self.loads = here, 0

    def copy(self, src, dst, device):
        spot = len(self.copies)
        made = pltpu.make_async_remote_copy(
            src_ref=src,
            dst_ref=dst,
            send_sem=self.send.at[spot],
            recv_sem=self.recv.at[spot],
            device_id=device,
            device_id_type=MESH,
        )
        made.start()
        self.copies.append(made)
        return made

    def load(self, src, dst):
        made = pltpu.make_async_copy(src, dst, self.here.at[self.loads])
        self.loads += 1
        made.start()
        return made

    def sent(self, made):
        made.wait_send()
        self.copies = [None if one is made else one for one in self.copies]

    def finish(self):
        for made in self.copies:
            if made is not None:
                made.wait_send()


def greet(devices):
    barrier = pltpu.get_barrier_semaphore()
    for device in devices:
        pl.semaphore_signal(barrier, inc=1, device_id=device, device_id_type=MESH)
    pl.semaphore_wait(barrier, len(devices))


def add_into(target, parts, block=32):
    rows = target.shape[-2]
    block = min(block, rows)
    for lead in itertools.product(*[range(size) for size in target.shape[:-2]]):

        def body(step, carry, lead=lead):
            spot = lead + (pl.ds(pl.multiple_of(step * block, block), block),)
            total = parts[0][spot].astype(jnp.float32)
            for part in parts[1:]:
                total = total + part[spot].astype(jnp.float32)
            target[spot] = total.astype(target.dtype)
            return carry

        lax.fori_loop(0, rows // block, body, 0)


def ring_reduce(net, plus, minus, own, slots, target, held=None):
    held = own if held is None else held
    first_plus = net.copy(own(2, 0), slots.at[0], plus)
    first_minus = net.copy(own(2, 1), slots.at[2], minus)
    side_plus = net.copy(own(1, 1), slots.at[1], plus)
    side_minus = net.copy(own(3, 0), slots.at[3], minus)
    yield
    first_plus.wait_recv()
    add_into(slots.at[0], [slots.at[0], held(1, 0)])
    last_plus = net.copy(slots.at[0], slots.at[4], plus)
    first_minus.wait_recv()
    add_into(slots.at[2], [slots.at[2], held(3, 1)])
    last_minus = net.copy(slots.at[2], slots.at[5], minus)
    yield
    side_minus.wait_recv()
    last_plus.wait_recv()
    add_into(target(0), [held(0, 0), slots.at[3], slots.at[4]])
    side_plus.wait_recv()
    last_minus.wait_recv()
    add_into(target(1), [held(0, 1), slots.at[1], slots.at[5]])


def x_first(net, me, source, slots, middle, other, out, held=None):
    staged = None
    if held is not None:
        order = {(1, 0): 0, (3, 1): 1, (0, 0): 2, (0, 1): 3}
        loads = [
            net.load(source.at[me.x_by(step), half], held.at[spot])
            for (step, half), spot in order.items()
        ]

        def staged(step, half):
            return held.at[order[step, half]]

    ring = ring_reduce(
        net,
        me.at(x=me.x_by(1)),
        me.at(x=me.x_by(3)),
        lambda step, half: source.at[me.x_by(step), half],
        slots,
        lambda half: middle.at[half],
        staged,
    )
    next(ring)
    yield
    if held is not None:
        for load in loads:
            load.wait()
    yield from ring
    across = net.copy(middle.at[1 - me.z_lo], other, me.at(z=me.z + 1 - 2 * me.z_lo))
    yield
    across.wait_recv()
    add_into(out, [middle.at[me.z_lo], other])


def z_first(net, me, source, other, middle, slots, out):
    across = net.copy(source.at[:, 1 - me.z_lo], other, me.at(z=me.z + 1 - 2 * me.z_lo))
    load = net.load(source.at[:, me.z_lo], middle)
    yield
    load.wait()
    across.wait_recv()
    add_into(middle, [middle, other])
    half_rows = middle.shape[1] // 2
    yield from ring_reduce(
        net,
        me.at(x=me.x_by(1)),
        me.at(x=me.x_by(3)),
        lambda step, half: middle.at[me.x_by(step), pl.ds(half * half_rows, half_rows)],
        slots,
        lambda half: out.at[pl.ds(half * half_rows, half_rows)],
    )


def core_pair(net, me, sending, other, middle):
    across = net.copy(sending, other, me.at(core=1 - me.core))
    yield
    net.sent(across)
    across.wait_recv()
    add_into(middle, [middle, other])


def dense_x_first(net, me, sending, other, middle, slots, corner, last, out):
    yield from core_pair(net, me, sending, other, middle)
    yield from ring_reduce(
        net,
        me.at(x=me.x_by(1)),
        me.at(x=me.x_by(3)),
        lambda step, half: middle.at[half, me.x_by(step)],
        slots,
        lambda half: corner.at[half],
    )
    half_rows = corner.shape[2] // 2
    yield from ring_reduce(
        net,
        me.at(z=me.z_by(1)),
        me.at(z=me.z_by(3)),
        lambda step, half: corner.at[
            me.z_by(step) // 2, lax.rem(me.z_by(step), 2), pl.ds(half * half_rows, half_rows)
        ],
        last,
        lambda half: out.at[pl.ds(half * half_rows, half_rows)],
    )


def dense_z_first(net, me, sending, other, middle, slots, corner, last, out):
    yield from core_pair(net, me, sending, other, middle)
    yield from ring_reduce(
        net,
        me.at(z=me.z_by(1)),
        me.at(z=me.z_by(3)),
        lambda step, half: middle.at[
            me.z_by(step) // 2, pl.ds(half * 2, 2), lax.rem(me.z_by(step), 2)
        ],
        slots,
        lambda half: corner.at[pl.ds(half * 2, 2)],
    )
    half_rows = corner.shape[1] // 2
    yield from ring_reduce(
        net,
        me.at(x=me.x_by(1)),
        me.at(x=me.x_by(3)),
        lambda step, half: corner.at[me.x_by(step), pl.ds(half * half_rows, half_rows)],
        last,
        lambda half: out.at[pl.ds(half * half_rows, half_rows)],
    )


def all_sum(net, devices, spot, own, slots, most):
    slots[spot] = own[...]
    sent = [net.copy(own, slots.at[spot], device) for device in devices]
    yield
    for made in sent:
        made.wait_recv()
    count = slots.shape[0]
    total = slots[0]
    peak = slots[0, most:]
    for step in range(1, count):
        total = total + slots[step]
        peak = jnp.maximum(peak, slots[step, most:])
    for made in sent:
        net.sent(made)
    own[:most] = total[:most]
    own[most:] = peak


def all_small(net, me, working, by_core, by_x, by_z, by_y, out):
    yield from all_sum(net, [me.at(core=1 - me.core)], me.core, working, by_core, 40)
    yield from all_sum(net, [me.at(x=me.x_by(s)) for s in (1, 2, 3)], me.x, working, by_x, 40)
    yield from all_sum(net, [me.at(z=me.z_by(s)) for s in (1, 2, 3)], me.z, working, by_z, 40)
    out[40:] = working[40:]
    yield from all_sum(net, [me.at(y=me.y_by(s)) for s in (1, 2, 3)], me.y, working, by_y, 40)
    out[:40] = working[:40]


def peers(me):
    offsets = [(a, b) for a in (2, 3, 0, 1) for b in (1, 3, 2, 0) if a or b]
    return [(a, b) + peer(me, a, b) for a, b in offsets]


def peer(me, a, b):
    z = me.z if a < 2 else lax.rem(me.z + 2, 4)
    core = me.core if a % 2 == 0 else 1 - me.core
    y = me.y_by(b)
    return z // 2 * 2 + core, y, me.at(z=z, core=core, y=y)


def gather_rows(table, home, store):
    def body(step, carry):
        columns = pl.ds(pl.multiple_of(step * 256, 256), 256)
        rows = home[:, :, :, columns].reshape(768, 256)
        total = contract_first(table[...], rows)
        store(columns, total[:96])
        return carry

    lax.fori_loop(0, home.shape[3] // 256, body, 0)


def turned(values):
    return pltpu.roll(values, 64, 1)


def column_of(row):
    eye = lax.broadcasted_iota(jnp.int32, (128, 128), 0) == lax.broadcasted_iota(
        jnp.int32, (128, 128), 1
    )
    return jnp.sum(jnp.where(eye, row, 0.0), axis=1, keepdims=True)


def norm_back(gradient, raw, gain):
    inverse = lax.rsqrt(jnp.mean(raw * raw, axis=-1, keepdims=True) + epsilon)
    normal = raw * inverse
    scaled = gradient * gain
    result = inverse * (scaled - normal * jnp.mean(scaled * normal, axis=-1, keepdims=True))
    return result, jnp.sum(gradient * normal, axis=0, keepdims=True)


def back_kernel(names, *refs):
    r = types.SimpleNamespace(**dict(zip(names, refs, strict=True)))
    low, full = jnp.bfloat16, jnp.float32
    score_scale = HEAD_SIZE ** (-0.5)
    me = Place()
    greet(
        [
            me.at(x=me.x_by(1)),
            me.at(x=me.x_by(3)),
            me.at(z=me.z_by(1)),
            me.at(z=me.z_by(3)),
            me.at(x=me.x_by(2)),
        ]
        + [one[4] for one in peers(me)]
    )
    net = Net(r.send, r.recv, r.here)

    branch, whole = r.branch, r.whole
    above, below = me.at(y=me.y_by(1)), me.at(y=me.y_by(3))
    to_above = net.copy(branch, whole.at[:, me.y], above)
    to_below = net.copy(branch, whole.at[:, me.y], below)
    own_branch = net.load(branch, whole.at[:, me.y])
    weight = r.weight
    load_out = net.load(r.w_out, weight)
    gate = x_first(
        net, me, r.gate, r.gate_slots, r.gate_middle, r.gate_other,
        r.gate_out, r.gate_held,
    )
    up = x_first(
        net, me, r.up, r.up_slots, r.up_middle, r.up_other,
        r.up_out, r.up_held,
    )
    down = z_first(
        net, me, r.down, r.down_other, r.down_middle, r.down_slots,
        r.down_out,
    )
    for task in (gate, up, down):
        next(task)

    hidden, inverse = r.hidden, r.inverse
    for s in range(3):
        rows = slice(s * 128, s * 128 + 128)
        values = hidden[rows, :].astype(full)
        root = lax.rsqrt(jnp.mean(values * values, axis=-1, keepdims=True) + epsilon)
        inverse[rows, :] = jnp.broadcast_to(root, (128, 128))

    first, second = pl.ds(0, 1024), pl.ds(1024, 1024)
    to_above.wait_recv()
    passed = whole.at[:, me.y_by(3), :, first]
    far_above = net.copy(passed, passed, above)
    to_below.wait_recv()
    passed = whole.at[:, me.y_by(1), :, second]
    far_below = net.copy(passed, passed, below)
    own_branch.wait()
    load_out.wait()
    far_above.wait_recv()
    far_below.wait_recv()

    heads_grad, mixed = r.heads_grad, r.mixed

    def heads_step(step, carry):
        columns = pl.ds(pl.multiple_of(step * 256, 256), 256)
        heads_grad[:, columns] = jnp.dot(
            whole[...].reshape(384, 2048), weight[:, columns], preferred_element_type=full
        ).astype(low)
        return carry

    lax.fori_loop(0, 4, heads_step, 0)
    load_query = net.load(r.w_query, weight)

    produced, home, table = r.produced, r.home, r.table
    mine = pl.ds(pl.multiple_of(me.dp * 192 + me.y * 48, 16), 48)
    home_came = [
        net.copy(produced.at[dp, y], home.at[mine], device) for a, b, dp, y, device in peers(me)
    ]
    home_own = net.load(produced.at[me.dp, me.y], home.at[mine])

    query, query_raw, pair = r.query, r.query_raw, r.pair
    cosine, sine = r.cosine, r.sine
    gain_query, gain_key = r.gain_query, r.gain_key
    bias, key_sum, value_sum = r.bias, r.key_sum, r.value_sum
    pair_grad, gain_part = r.pair_grad, r.gain_part
    gain_part[...] = jnp.zeros((8, 128), full)

    def rope_back(gradient):
        return gradient * cosine[...] + turned(gradient) * sine[...]

    def attend(s):
        here = pl.ds(s * 128, 128)
        spot = me.context * 128 + lax.broadcasted_iota(jnp.int32, (128, 1024), 0)
        allowed = (column_of(r.seg_query[s]) == r.seg_key[s]) & (
            lax.broadcasted_iota(jnp.int32, (128, 1024), 1) <= spot
        )
        bias[...] = jnp.where(allowed, 0.0, masked_value)
        key_sum[...] = jnp.zeros_like(key_sum)
        value_sum[...] = jnp.zeros_like(value_sum)

        def two_heads(step, carry):
            columns = pl.ds(pl.multiple_of(step * 256, 256), 256)

            def stacked(ref):
                both = ref[here, columns]
                return jnp.concatenate([both[:, :128], both[:, 128:]], axis=0)

            q, d = stacked(query), stacked(heads_grad)
            keys, values = pair[0, s], pair[1, s]
            lines = r.log_sum
            logs = jnp.concatenate(
                [column_of(lines[s * 8 + step * 2]), column_of(lines[s * 8 + step * 2 + 1])], axis=0
            )
            score = contract_last(q, keys) * score_scale
            score = score + jnp.concatenate([bias[...], bias[...]], axis=0)
            prob = jnp.exp(score - logs)
            prob_grad = contract_last(d, values)
            delta = jnp.sum(prob * prob_grad, axis=-1, keepdims=True)
            score_grad = (prob * (prob_grad - delta)).astype(low)
            value_sum[...] += contract_first(prob.astype(low), d)
            key_sum[...] += contract_first(score_grad, q)
            turned_grad = jnp.dot(score_grad, keys, preferred_element_type=full) * score_scale
            for half in range(2):
                run = pl.ds(pl.multiple_of(step * 256 + half * 128, 128), 128)
                grad, part = norm_back(
                    rope_back(turned_grad[half * 128 : half * 128 + 128]),
                    query_raw[here, run],
                    gain_query[...],
                )
                heads_grad[here, run] = grad.astype(low)
                gain_part[0:1, :] += part
            return carry

        lax.fori_loop(0, 4, two_heads, 0)
        pair_grad[:, :, 0, s] = (key_sum[...] * score_scale).astype(low).reshape(4, 2, 128, 128)
        pair_grad[:, :, 1, s] = value_sum[...].astype(low).reshape(4, 2, 128, 128)

    attend(0)
    attend(1)
    next(gate)
    next(up)
    attend(2)
    pairs = x_first(
        net, me, pair_grad, r.pair_slots, r.pair_middle, r.pair_other,
        r.pair_out,
    )
    next(pairs)

    query_low = heads_grad
    gain_attn = r.gain_attn

    def normed(columns):
        values = hidden[:, columns].astype(full)
        return (values * inverse[:, 0:1] * gain_attn[:, columns]).astype(low)

    def whole_part(columns):
        return whole[:, :, :, columns].reshape(384, 256)

    def weigh(core, left, right, target):
        def body(step, carry):
            z_hi, part = step // 2, lax.rem(step, 2)
            columns = pl.ds(pl.multiple_of((z_hi * 2 + core) * 512 + part * 256, 256), 256)
            made = contract_first(left(columns), right[...]).astype(low)
            target[z_hi, pl.ds(part * 2, 2)] = made.reshape(2, 2, 64, right.shape[1])
            return carry

        lax.fori_loop(0, 4, body, 0)

    def dense(order, left, right, sending, other, middle, *more):
        weigh(1 - me.core, left, right, sending)
        task = order(net, me, sending, other, middle, *more)
        next(task)
        weigh(me.core, left, right, middle)
        return task

    out_w = dense(
        dense_z_first, whole_part, mixed, r.sending, r.out_w_other, r.out_w_middle, r.out_w_slots, r.out_w_corner,
        r.out_w_last, r.out_w_out,
    )
    next(pairs)
    next(down)
    next(out_w)
    query_w = dense(
        dense_x_first, normed, query_low, r.sending, r.query_w_other, r.query_w_middle, r.query_w_slots, r.query_w_corner,
        r.query_w_last, r.query_w_out,
    )
    next(pairs)
    next(gate)
    next(up)

    pair_out, key_raw, pair_low = r.pair_out, r.key_raw, r.pair_low
    next(pairs, None)
    for s in range(3):
        rows = slice(s * 128, s * 128 + 128)
        grad, part = norm_back(rope_back(pair_out[0, s]), key_raw[rows, :], gain_key[...])
        gain_part[1:2, :] += part
        pair_low[rows, :128] = grad.astype(low)
        pair_low[rows, 128:] = pair_out[1, s].astype(low)

    load_query.wait()
    net.sent(far_above)
    net.sent(far_below)
    small = r.small
    normed_part = r.normed_part

    def normed_step(step, carry):
        columns = pl.ds(pl.multiple_of(step * 256, 256), 256)
        made = contract_last(query_low[...], weight[columns, :])
        made = made + contract_last(pair_low[:, :128], r.w_key[columns, :])
        made = made + contract_last(pair_low[:, 128:], r.w_value[columns, :])
        normal = hidden[:, columns].astype(full) * inverse[:, 0:1]
        normed_part[:, columns] = jnp.sum(made * normal, axis=0, keepdims=True)
        whole[:, :, :, columns] = made.astype(low).reshape(3, 4, 32, 256)
        return carry

    lax.fori_loop(0, 8, normed_step, 0)
    normed_out = r.normed_out
    normed_sum = ring_reduce(
        net,
        above,
        below,
        lambda step, half: whole.at[:, me.y_by(step), :, pl.ds(half * 1024, 1024)],
        r.normed_slots,
        lambda half: normed_out.at[:, :, pl.ds(half * 1024, 1024)],
    )
    next(normed_sum)
    for step in range(16):
        run = slice(step * 128, step * 128 + 128)
        small[step : step + 1, :] = normed_part[:, run]
        small[16 + step : 17 + step, :] = r.moe_gain_part[:, run]
    small[32:40, :] = gain_part[...]
    small[40:, :] = r.peaks[...]
    smalls = all_small(
        net, me, small, r.by_core, r.by_x, r.by_z, r.by_y, r.small_out
    )
    next(smalls)
    pair_w = dense(
        dense_x_first, normed, pair_low, r.pair_sending, r.pair_w_other, r.pair_w_middle, r.pair_w_slots, r.pair_w_corner,
        r.pair_w_last, r.pair_w_out,
    )
    next(query_w)
    next(smalls)

    def rest(*tasks):
        for task in tasks:
            next(task, None)

    rest(normed_sum, out_w, pair_w, smalls, gate, up, down, query_w)

    next(normed_sum, None)
    for s in range(3):
        rows = pl.ds(pl.multiple_of(s * 128 + me.y * 32, 32), 32)
        grad, _ = norm_back(normed_out[s], hidden[rows, :].astype(full), gain_attn[...])
        normed_out[s] = grad

    rest(out_w, pair_w, smalls, down, gate, up, query_w)
    rest(pair_w, out_w, smalls, query_w)

    for made in home_came:
        made.wait_recv()
    home_own.wait()
    home_loads = [
        net.load(home.at[:, pl.ds(half * 1024, 1024)], weight.at[pl.ds(half * 768, 768)])
        for half in range(2)
    ]
    rest(pair_w, out_w, smalls, query_w, gate, up, down)
    moe_out = r.moe_out
    for half in range(2):
        home_loads[half].wait()

        def gather(step, carry, half=half):
            columns = pl.ds(pl.multiple_of(step * 256, 256), 256)
            total = contract_first(table[...], weight[half * 768 : half * 768 + 768, columns])
            moe_out[:, pl.ds(pl.multiple_of(half * 1024 + step * 256, 256), 256)] = total[:96]
            return carry

        lax.fori_loop(0, 4, gather, 0)
    tasks = [pair_w, out_w, smalls, query_w, gate, up, down]
    while tasks:
        for task in list(tasks):
            if next(task, "end") == "end":
                tasks.remove(task)
    net.finish()


def dense_slots(columns, corner):
    low = jnp.bfloat16
    return [
        pltpu.VMEM((2, 4, 2, 64, columns), low),
        pltpu.VMEM((2, 4, 2, 64, columns), low),
        pltpu.VMEM((6, 2, 64, columns), low),
        pltpu.VMEM(corner + (64, columns), low),
        pltpu.VMEM((6, 32, columns), low),
    ]


def back(far, near):
    low, full = jnp.bfloat16, jnp.float32
    outs = dict(
        gate_out=(256, 768),
        up_out=(256, 768),
        down_out=(256, 768),
        query_w_out=(64, 1024),
        pair_w_out=(64, 256),
        out_w_out=(64, 1024),
        small_out=(48, 128),
        normed_out=(3, 32, 2048),
        moe_out=(96, 2048),
    )
    scratch = dict(
        whole=pltpu.VMEM((3, 4, 32, 2048), low),
        weight=pltpu.VMEM((2048, 1024), low),
        inverse=pltpu.VMEM((384, 128), full),
        heads_grad=pltpu.VMEM((384, 1024), low),
        bias=pltpu.VMEM((128, 1024), full),
        key_sum=pltpu.VMEM((1024, 128), full),
        value_sum=pltpu.VMEM((1024, 128), full),
        pair_grad=pltpu.VMEM((4, 2, 2, 3, 128, 128), low),
        pair_slots=pltpu.VMEM((6, 2, 3, 128, 128), low),
        pair_middle=pltpu.VMEM((2, 2, 3, 128, 128), low),
        pair_other=pltpu.VMEM((2, 3, 128, 128), low),
        pair_out=pltpu.VMEM((2, 3, 128, 128), full),
        pair_low=pltpu.VMEM((384, 256), low),
        gain_part=pltpu.VMEM((8, 128), full),
        normed_part=pltpu.VMEM((1, 2048), full),
        normed_slots=pltpu.VMEM((6, 3, 32, 1024), low),
        small=pltpu.VMEM((48, 128), full),
        by_core=pltpu.VMEM((2, 48, 128), full),
        by_x=pltpu.VMEM((4, 48, 128), full),
        by_z=pltpu.VMEM((4, 48, 128), full),
        by_y=pltpu.VMEM((4, 48, 128), full),
        down_other=pltpu.VMEM((4, 256, 768), low),
        down_middle=pltpu.VMEM((4, 256, 768), low),
        down_slots=pltpu.VMEM((6, 128, 768), low),
        gate_slots=pltpu.VMEM((6, 256, 768), low),
        gate_middle=pltpu.VMEM((2, 256, 768), low),
        gate_other=pltpu.VMEM((256, 768), low),
        gate_held=pltpu.VMEM((4, 256, 768), low),
        up_slots=pltpu.VMEM((6, 256, 768), low),
        up_middle=pltpu.VMEM((2, 256, 768), low),
        up_other=pltpu.VMEM((256, 768), low),
        up_held=pltpu.VMEM((4, 256, 768), low),
        sending=pltpu.VMEM((2, 4, 2, 64, 1024), low),
        pair_sending=pltpu.VMEM((2, 4, 2, 64, 256), low),
        query_w_other=None,
        query_w_middle=None,
        query_w_slots=None,
        query_w_corner=None,
        query_w_last=None,
        pair_w_other=None,
        pair_w_middle=None,
        pair_w_slots=None,
        pair_w_corner=None,
        pair_w_last=None,
        out_w_other=None,
        out_w_middle=None,
        out_w_slots=None,
        out_w_corner=None,
        out_w_last=None,
        send=pltpu.SemaphoreType.DMA((104,)),
        recv=pltpu.SemaphoreType.DMA((104,)),
        here=pltpu.SemaphoreType.DMA((20,)),
    )
    dense = dense_slots(1024, (2, 2)) + dense_slots(256, (2, 2)) + dense_slots(1024, (4,))
    scratch = {name: one or dense.pop(0) for name, one in scratch.items()}
    names = list(far) + list(near) + list(outs) + list(dict(home=0)) + list(scratch)
    results = pl.pallas_call(
        functools.partial(back_kernel, names),
        out_shape=[jax.ShapeDtypeStruct(size, full) for size in outs.values()]
        + [jax.ShapeDtypeStruct((768, 2048), low)],
        in_specs=[ANY] * len(far) + [VMEM] * len(near),
        out_specs=[VMEM] * len(outs) + [ANY],
        scratch_shapes=list(scratch.values()),
        compiler_params=pltpu.CompilerParams(
            collective_id=0, has_side_effects=True, vmem_limit_bytes=62 << 20
        ),
        name="back",
    )(*far.values(), *near.values())
    return types.SimpleNamespace(**dict(zip(outs, results[:-1], strict=True)))


def moe_kernel(
    after,
    cotangent,
    gain,
    ids,
    gates,
    capacity,
    w_gate,
    w_up,
    w_down,
    after_grad,
    gain_part,
    gate_grad,
    produced,
    table,
    full_gate,
    full_up,
    full_down,
    rows,
    sending,
    sending_grad,
    info,
    info_in,
    local,
    grads,
    act,
    gate_back,
    up_back,
    back,
    home,
    dots,
    dots_in,
    send,
    recv,
):
    low, full = jnp.bfloat16, jnp.float32
    me = Place()
    greet([one[4] for one in peers(me)])
    net = Net(send, recv)

    expert = lax.broadcasted_iota(jnp.int32, (16, 128), 0)
    chosen = jnp.zeros((16, 128), full)
    share = jnp.zeros((16, 128), full)
    for k in range(8):
        named = ids[k : k + 1, :] == expert
        chosen = chosen + jnp.where(named, 1.0, 0.0)
        share = share + jnp.where(named, gates[k : k + 1, :], 0.0)
    earlier = lax.broadcasted_iota(jnp.int32, (128, 128), 0) < lax.broadcasted_iota(
        jnp.int32, (128, 128), 1
    )
    before = jnp.dot(
        chosen.astype(low), jnp.where(earlier, 1.0, 0.0).astype(low), preferred_element_type=full
    )
    slot = jnp.where((chosen > 0.0) & (before < capacity[...]), before, -1.0)
    spot = lax.broadcasted_iota(jnp.int32, (48, 128), 0).astype(full)
    for e in range(16):
        mask = jnp.where(slot[e : e + 1, :] == spot, 1.0, 0.0)
        table[e * 48 : e * 48 + 48, :] = mask.astype(low)
        info[e // 4, e % 4] = jnp.concatenate(
            [slot[e : e + 1, :], share[e : e + 1, :], jnp.zeros((6, 128), full)], axis=0
        )

    def dispatch(sender):
        for a, b, dp, y, device in peers(me):
            if b == 1:
                rest = table[pl.ds(pl.multiple_of(dp * 192, 192), 192), :]
                columns = 512
                for step in range(2048 // columns):
                    run = slice(step * columns, (step + 1) * columns)
                    picked = jnp.dot(rest, rows[:, run], preferred_element_type=full)
                    sender[dp, :, :, run] = picked.astype(low).reshape(4, 48, columns)
            yield a, b, dp, y, device

    told, came, grad_came = {}, {}, {}
    for a, b, dp, y, device in peers(me):
        told[a, b] = net.copy(info.at[dp, y], info_in.at[me.dp, me.y], device)
    info_in[me.dp, me.y] = info[me.dp, me.y]
    values = after[...]
    inverse = lax.rsqrt(jnp.mean(values * values, axis=-1, keepdims=True) + epsilon)
    rows[96:, :] = jnp.zeros((32, 2048), low)
    rows[:96, :] = (values * inverse * gain[...]).astype(low)
    for a, b, dp, y, device in dispatch(sending):
        came[a, b] = net.copy(sending.at[dp, y], local.at[me.dp, me.y], device)
    local[me.dp, me.y] = sending[me.dp, me.y]
    rows[:96, :] = cotangent[...]
    for a, b, dp, y, device in dispatch(sending_grad):
        grad_came[a, b] = net.copy(sending_grad.at[dp, y], grads.at[me.dp, me.y], device)
    grads[me.dp, me.y] = sending_grad[me.dp, me.y]

    back_came, dots_came = {}, {}
    for a in (0, 1, 2, 3):
        group = peer(me, a, 0)[0]
        for b in range(4):
            if a or b:
                told[a, b].wait_recv()
                came[a, b].wait_recv()
                grad_came[a, b].wait_recv()
        masks, shares = [], []
        for y in range(4):
            mask = info_in[group, y, 0:1, :] == spot
            masks.append(mask)
            shares.append(
                jnp.sum(jnp.where(mask, info_in[group, y, 1:2, :], 0.0), axis=1, keepdims=True)
            )
        shared = jnp.concatenate(shares, axis=0)

        def inner(step, carry, group=group, shared=shared):
            columns = pl.ds(pl.multiple_of(step * 256, 256), 256)
            entered = local[group].reshape(192, 2048)
            gate_pre = jnp.dot(entered, w_gate[:, columns], preferred_element_type=full)
            up_pre = jnp.dot(entered, w_up[:, columns], preferred_element_type=full)
            scaled = (grads[group].reshape(192, 2048).astype(full) * shared).astype(low)
            act_back = jnp.dot(scaled, w_down[:, columns], preferred_element_type=full)
            sigmoid = 1.0 / (1.0 + jnp.exp(-gate_pre))
            silu = gate_pre * sigmoid
            act[group, :, columns] = (silu * up_pre).astype(low)
            gate_back[group, :, columns] = (
                act_back * up_pre * sigmoid * (1.0 + gate_pre * (1.0 - sigmoid))
            ).astype(low)
            up_back[group, :, columns] = (act_back * silu).astype(low)
            return carry

        lax.fori_loop(0, 3, inner, 0)

        def outer(step, dot, group=group, shared=shared):
            columns = pl.ds(pl.multiple_of(step * 256, 256), 256)
            made = contract_last(act[group], w_down[columns, :]).astype(low).astype(full)
            produced[group, :, :, columns] = (made * shared).astype(low).reshape(4, 48, 256)
            incoming = grads[group, :, :, columns].reshape(192, 256).astype(full)
            dot = dot + jnp.sum(made * incoming, axis=1, keepdims=True)
            grads[group, :, :, columns] = (incoming * shared).astype(low).reshape(4, 48, 256)
            row_back = contract_last(gate_back[group], w_gate[columns, :]) + contract_last(
                up_back[group], w_up[columns, :]
            )
            back[group, :, :, columns] = row_back.astype(low).reshape(4, 48, 256)
            return dot

        dot = lax.fori_loop(0, 8, outer, jnp.zeros((192, 1), full))
        for y in range(4):
            line = jnp.sum(
                jnp.where(masks[y], dot[y * 48 : y * 48 + 48], 0.0), axis=0, keepdims=True
            )
            dots[group, y] = jnp.broadcast_to(line, (8, 128))
        for b in (2, 1, 3, 0):
            if a or b:
                dp, y, device = peer(me, a, b)
                back_came[a, b] = net.copy(back.at[dp, y], home.at[me.dp, me.y], device)
                dots_came[a, b] = net.copy(dots.at[dp, y], dots_in.at[me.dp, me.y], device)
    home[me.dp, me.y] = back[me.dp, me.y]
    dots_in[me.dp, me.y] = dots[me.dp, me.y]

    def weigh(step, carry):
        columns = pl.ds(pl.multiple_of(step * 256, 256), 256)
        entered = local[:, :, :, columns].reshape(768, 256)
        full_gate[columns, :] = contract_first(entered, gate_back[...].reshape(768, 768)).astype(low)
        full_up[columns, :] = contract_first(entered, up_back[...].reshape(768, 768)).astype(low)
        incoming = grads[:, :, :, columns].reshape(768, 256)
        full_down[columns, :] = contract_first(incoming, act[...].reshape(768, 768)).astype(low)
        return carry

    lax.fori_loop(0, 8, weigh, 0)

    for a, b, *_ in peers(me):
        back_came[a, b].wait_recv()
        dots_came[a, b].wait_recv()
    chosen_dots = [jnp.zeros((1, 128), full) for k in range(8)]
    for e in range(16):
        line = dots_in[e // 4, e % 4, 0:1, :]
        for k in range(8):
            chosen_dots[k] = chosen_dots[k] + jnp.where(ids[k : k + 1, :] == e, line, 0.0)
    gate_grad[...] = jnp.concatenate(chosen_dots, axis=0)

    def keep(columns, total):
        after_grad[:, columns] = total

    gather_rows(table, home, keep)
    gradient = after_grad[...]
    values = after[...]
    inverse = lax.rsqrt(jnp.mean(values * values, axis=-1, keepdims=True) + epsilon)
    normal = values * inverse
    gain_part[...] = jnp.sum(gradient * normal, axis=0, keepdims=True)
    scaled = gradient * gain[...]
    mean = jnp.mean(scaled * normal, axis=-1, keepdims=True)
    after_grad[...] = cotangent[...].astype(full) + inverse * (scaled - normal * mean)
    net.finish()


def moe(after, cotangent, gain, ids, gates, capacity, w_gate, w_up, w_down):
    low, full = jnp.bfloat16, jnp.float32
    copies = 75
    shape = jax.ShapeDtypeStruct
    return pl.pallas_call(
        moe_kernel,
        out_shape=[
            shape((96, 2048), full),
            shape((1, 2048), full),
            shape((8, 128), full),
            shape((4, 4, 48, 2048), low),
            shape((768, 128), low),
            shape((2048, 768), low),
            shape((2048, 768), low),
            shape((2048, 768), low),
        ],
        in_specs=[VMEM] * 9,
        out_specs=[VMEM] * 8,
        scratch_shapes=[
            pltpu.VMEM((128, 2048), low),
            pltpu.VMEM((4, 4, 48, 2048), low),
            pltpu.VMEM((4, 4, 48, 2048), low),
            pltpu.VMEM((4, 4, 8, 128), full),
            pltpu.VMEM((4, 4, 8, 128), full),
            pltpu.VMEM((4, 4, 48, 2048), low),
            pltpu.VMEM((4, 4, 48, 2048), low),
            pltpu.VMEM((4, 192, 768), low),
            pltpu.VMEM((4, 192, 768), low),
            pltpu.VMEM((4, 192, 768), low),
            pltpu.VMEM((4, 4, 48, 2048), low),
            pltpu.VMEM((4, 4, 48, 2048), low),
            pltpu.VMEM((4, 4, 8, 128), full),
            pltpu.VMEM((4, 4, 8, 128), full),
            pltpu.SemaphoreType.DMA((copies,)),
            pltpu.SemaphoreType.DMA((copies,)),
        ],
        compiler_params=pltpu.CompilerParams(
            collective_id=1, has_side_effects=True, vmem_limit_bytes=60 << 20
        ),
        name="moe",
    )(after, cotangent, gain, ids, gates, capacity, w_gate, w_up, w_down)


def shards(
    hidden_in,
    segments,
    attn_gain,
    query_gain,
    key_gain,
    w_query,
    key_weight_matrix,
    value_weight_matrix,
    w_out,
    moe_gain,
    expert_ids,
    gate_values,
    capacity,
    w_gate,
    w_up,
    w_down,
    cotangent,
):
    seqs_local, rows_ctx, model_width = hidden_in.shape
    seq_length = segments.shape[1]
    expert_span = lax.axis_size("experts")
    ctx_index = lax.axis_index("context")
    own_index = lax.axis_index("experts")
    own_rows = rows_ctx // expert_span
    head_count = w_query.shape[1] // HEAD_SIZE
    kv_count = key_weight_matrix.shape[1] // HEAD_SIZE
    per_group = head_count // kv_count
    score_scale = HEAD_SIZE ** (-0.5)
    token_count = seqs_local * rows_ctx
    inputs = hidden_in.astype(jnp.float32)
    gain_attn = attn_gain.astype(jnp.float32)
    gain_query = query_gain.astype(jnp.float32)
    gain_key = key_gain.astype(jnp.float32)
    gain_moe = moe_gain.astype(jnp.float32)
    normalized_input = rms_scale(inputs, gain_attn).astype(jnp.bfloat16)
    normed_flat = normalized_input.reshape(token_count, model_width)
    query_raw = jnp.dot(normed_flat, w_query, preferred_element_type=jnp.float32).reshape(
        seqs_local, rows_ctx, head_count, HEAD_SIZE
    )
    unclipped_key = jnp.dot(
        normed_flat, key_weight_matrix, preferred_element_type=jnp.float32
    ).reshape(seqs_local, rows_ctx, kv_count, HEAD_SIZE)
    value_reduced = (
        jnp.dot(normed_flat, value_weight_matrix, preferred_element_type=jnp.float32)
        .astype(jnp.bfloat16)
        .reshape(seqs_local, rows_ctx, kv_count, HEAD_SIZE)
    )
    cosine_table, sine_table = rotary(ctx_index * rows_ctx, rows_ctx)
    cosine_table = cosine_table[None, :, None, :]
    sine_table = sine_table[None, :, None, :]
    query_normed = rms_scale(query_raw, gain_query)
    query_rot = (query_normed * cosine_table + turn(query_normed) * sine_table).astype(jnp.bfloat16)
    key_normed = rms_scale(unclipped_key, gain_key)
    key_rot = (key_normed * cosine_table + turn(key_normed) * sine_table).astype(jnp.bfloat16)
    keys_all, values_all = (
        lax.all_gather(key_rot, "context", axis=1, tiled=True),
        lax.all_gather(value_reduced, "context", axis=1, tiled=True),
    )
    query_group = query_rot.reshape(seqs_local, rows_ctx, kv_count, per_group, HEAD_SIZE)
    seg_query = lax.dynamic_slice_in_dim(segments, ctx_index * rows_ctx, rows_ctx, 1)
    seg_float_query = seg_query.astype(jnp.float32)
    query_spot = ctx_index * rows_ctx + jnp.arange(rows_ctx, dtype=jnp.int32)
    key_spot = jnp.arange(seq_length, dtype=jnp.int32)
    allowed = (seg_query[:, :, None] == segments[:, None, :]) & (
        key_spot[None, None, :] <= query_spot[None, :, None]
    )
    allowed = allowed[:, None, :, None, :]

    def masked_scores():
        raw_score = (
            jnp.einsum(
                "sqhgd,skhd->shqgk", query_group, keys_all, preferred_element_type=jnp.float32
            )
            * score_scale
        )
        return jnp.where(allowed, raw_score, masked_value)

    masked = masked_scores()
    row_peak = jnp.max(masked, axis=-1, keepdims=True)
    log_total = row_peak + jnp.log(jnp.sum(jnp.exp(masked - row_peak), axis=-1, keepdims=True))
    head_peak = jnp.max(masked, axis=(0, 2, 4)).reshape(head_count)
    prob_low = jnp.exp(masked - log_total).astype(jnp.bfloat16)
    mixed_heads = jnp.einsum(
        "shqgk,skhd->sqhgd", prob_low, values_all, preferred_element_type=jnp.float32
    )
    mixed_low = mixed_heads.astype(jnp.bfloat16).reshape(token_count, head_count * HEAD_SIZE)
    branch_part = contract_last(mixed_low, w_out)
    branch = lax.psum_scatter(
        branch_part.reshape(seqs_local, rows_ctx, model_width).astype(jnp.bfloat16),
        "experts",
        scatter_dimension=1,
        tiled=True,
    ).astype(jnp.float32)
    own_inputs = lax.dynamic_slice_in_dim(inputs, own_index * own_rows, own_rows, 1)
    after_attn = own_inputs + branch
    pair_tokens = seqs_local * own_rows
    top_count = expert_ids.shape[2]
    token_lanes = ((0, 0), (0, 128 - pair_tokens))
    ids = jnp.pad(expert_ids.reshape(pair_tokens, top_count).T, token_lanes, constant_values=-1)
    gates = jnp.pad(gate_values.reshape(pair_tokens, top_count).T, token_lanes)
    after_flat = after_attn.reshape(pair_tokens, model_width)
    after_grad, moe_gain_part, gate_grad, produced, table, full_gate, full_up, full_down = moe(
        after_flat,
        cotangent.reshape(pair_tokens, model_width),
        gain_moe[None],
        ids,
        gates,
        jnp.broadcast_to(capacity.astype(jnp.float32)[:, None], (capacity.shape[0], 128)),
        w_gate[0],
        w_up[0],
        w_down[0],
    )
    after_grad = after_grad.reshape(seqs_local, own_rows, model_width)
    gate_grad = gate_grad[:, :pair_tokens].T.reshape(seqs_local, own_rows, top_count)
    cosine_row, sine_row = cosine_table[0, :, 0], sine_table[0, :, 0]
    turn_sign = jnp.where(jnp.arange(HEAD_SIZE) < HEAD_SIZE // 2, 1.0, -1.0)
    seg_float = segments.astype(jnp.float32)
    done = back(
        dict(
            branch=after_grad.astype(jnp.bfloat16),
            w_out=w_out,
            w_query=w_query,
            gate=full_gate.reshape(4, 2, 256, 768),
            up=full_up.reshape(4, 2, 256, 768),
            down=full_down.reshape(4, 2, 256, 768),
            produced=produced,
        ),
        dict(
            w_key=key_weight_matrix,
            w_value=value_weight_matrix,
            table=table,
            hidden=hidden_in.reshape(token_count, model_width),
            mixed=mixed_low,
            query=query_rot.reshape(token_count, head_count * HEAD_SIZE),
            query_raw=query_raw.reshape(token_count, head_count * HEAD_SIZE),
            key_raw=unclipped_key.reshape(token_count, HEAD_SIZE),
            pair=jnp.stack([keys_all[:, :, 0], values_all[:, :, 0]]),
            log_sum=log_total[:, 0, :, :, 0].swapaxes(1, 2).reshape(24, 1, 128),
            seg_query=seg_float_query[:, None, :],
            seg_key=seg_float[:, None, :],
            cosine=cosine_row,
            sine=sine_row * turn_sign,
            gain_query=gain_query[None],
            gain_key=gain_key[None],
            gain_attn=gain_attn[None],
            moe_gain_part=moe_gain_part,
            peaks=jnp.broadcast_to(head_peak[:, None], (head_count, 128)),
        ),
    )
    layer_out = after_attn + done.moe_out.reshape(seqs_local, own_rows, model_width)
    input_grad = after_grad + done.normed_out
    w_key_grad, w_value_grad = done.pair_w_out[:, :128], done.pair_w_out[:, 128:]
    w_query_grad, w_out_grad = done.query_w_out, done.out_w_out
    w_gate_grad, w_up_grad, w_down_grad = (
        done.gate_out[None],
        done.up_out[None],
        done.down_out[None],
    )
    small = done.small_out
    attn_gain_grad = small[:16].reshape(model_width)
    moe_gain_grad = small[16:32].reshape(model_width)
    query_gain_grad, key_gain_grad = small[32], small[33]
    head_clip_scale = clip_limit / jnp.maximum(small[40:, 0], clip_limit)
    return (
        layer_out,
        input_grad,
        attn_gain_grad,
        query_gain_grad,
        key_gain_grad,
        w_query_grad,
        w_key_grad,
        w_value_grad,
        w_out_grad,
        moe_gain_grad,
        gate_grad,
        w_gate_grad,
        w_up_grad,
        w_down_grad,
        head_clip_scale,
    )


def solution(mesh):
    in_specs = (
        P("dp", "context", None),
        P("dp", None),
        P(),
        P(),
        P(),
        P(None, "experts"),
        P(None, "experts"),
        P(None, "experts"),
        P(None, "experts"),
        P(),
        P("dp", ("context", "experts"), None),
        P("dp", ("context", "experts"), None),
        P(),
        P(("dp", "experts"), None, None),
        P(("dp", "experts"), None, None),
        P(("dp", "experts"), None, None),
        P("dp", ("context", "experts"), None),
    )
    out_specs = (
        P("dp", ("context", "experts"), None),
        P("dp", ("context", "experts"), None),
        P(),
        P(),
        P(),
        P(("dp", "context"), "experts"),
        P(("dp", "context"), "experts"),
        P(("dp", "context"), "experts"),
        P(("dp", "context"), "experts"),
        P(),
        P("dp", ("context", "experts"), None),
        P(("dp", "experts"), "context", None),
        P(("dp", "experts"), "context", None),
        P(("dp", "experts"), "context", None),
        P("experts"),
    )
    return jax.shard_map(shards, mesh=mesh, in_specs=in_specs, out_specs=out_specs, check_vma=False)
```

```python
import functools
import itertools
import types

import jax
import jax.numpy as jnp
import numpy as np
from jax import lax
from jax.experimental import pallas as pl
from jax.experimental.pallas import tpu as pltpu
from jax.sharding import PartitionSpec as P

HEAD_SIZE = 128
MESH = pl.DeviceIdType.MESH
VMEM = pl.BlockSpec(memory_space=pltpu.VMEM)
ANY = pl.BlockSpec(memory_space=pl.ANY)
SMEM = pl.BlockSpec(memory_space=pltpu.SMEM)


epsilon = 1e-06
rope_base = 1000000.0
clip_limit = 1.0
masked_value = -1e30


def rotary():
    inverse = 1.0 / rope_base ** (np.arange(0, HEAD_SIZE, 2) / HEAD_SIZE)
    angle = np.arange(1024)[:, None] * inverse[None, :]
    cosine = np.concatenate([np.cos(angle), np.cos(angle)], axis=-1)
    sine = np.concatenate([-np.sin(angle), np.sin(angle)], axis=-1)
    shape = (8, 128, HEAD_SIZE)
    return (
        jnp.asarray(cosine.reshape(shape), jnp.float32),
        jnp.asarray(sine.reshape(shape), jnp.float32),
    )


def contract_last(left, right):
    return lax.dot_general(
        left, right, (((1,), (1,)), ((), ())), preferred_element_type=jnp.float32
    )


def contract_first(left, right):
    return lax.dot_general(
        left, right, (((0,), (0,)), ((), ())), preferred_element_type=jnp.float32
    )


class Place:
    def __init__(self):
        dp = lax.axis_index("dp")
        context = lax.axis_index("context")
        self.dp, self.context, self.y = dp, context, lax.axis_index("experts")
        self.core, self.z_hi = lax.rem(dp, 2), dp // 2
        self.x, self.z_lo = context // 2, lax.rem(context, 2)
        self.z = self.z_hi * 2 + self.z_lo

    def at(self, x=None, y=None, z=None, core=None):
        x = self.x if x is None else x
        y = self.y if y is None else y
        z = self.z if z is None else z
        core = self.core if core is None else core
        return (z // 2 * 2 + core, x * 2 + lax.rem(z, 2), y)

    def x_by(self, step):
        return lax.rem(self.x + step, 4)

    def y_by(self, step):
        return lax.rem(self.y + step, 4)

    def z_by(self, step):
        return lax.rem(self.z + step, 4)


class Net:
    def __init__(self, send, recv, here=None):
        self.send, self.recv, self.copies = send, recv, []
        self.here, self.loads = here, 0

    def copy(self, src, dst, device):
        spot = len(self.copies)
        made = pltpu.make_async_remote_copy(
            src_ref=src,
            dst_ref=dst,
            send_sem=self.send.at[spot],
            recv_sem=self.recv.at[spot],
            device_id=device,
            device_id_type=MESH,
        )
        made.start()
        self.copies.append(made)
        return made

    def load(self, src, dst):
        made = pltpu.make_async_copy(src, dst, self.here.at[self.loads])
        self.loads += 1
        made.start()
        return made

    def sent(self, made):
        made.wait_send()
        self.copies = [None if one is made else one for one in self.copies]

    def finish(self):
        for made in self.copies:
            if made is not None:
                made.wait_send()


def greet(devices):
    barrier = pltpu.get_barrier_semaphore()
    for device in devices:
        pl.semaphore_signal(barrier, inc=1, device_id=device, device_id_type=MESH)
    pl.semaphore_wait(barrier, len(devices))


def add_into(target, parts, block=32):
    rows = target.shape[-2]
    block = min(block, rows)
    for lead in itertools.product(*[range(size) for size in target.shape[:-2]]):

        def body(step, carry, lead=lead):
            spot = lead + (pl.ds(pl.multiple_of(step * block, block), block),)
            total = parts[0][spot].astype(jnp.float32)
            for part in parts[1:]:
                total = total + part[spot].astype(jnp.float32)
            target[spot] = total.astype(target.dtype)
            return carry

        lax.fori_loop(0, rows // block, body, 0)


def ring_reduce(net, plus, minus, own, slots, target, held=None):
    held = own if held is None else held
    first_plus = net.copy(own(2, 0), slots.at[0], plus)
    first_minus = net.copy(own(2, 1), slots.at[2], minus)
    side_plus = net.copy(own(1, 1), slots.at[1], plus)
    side_minus = net.copy(own(3, 0), slots.at[3], minus)
    yield
    first_plus.wait_recv()
    add_into(slots.at[0], [slots.at[0], held(1, 0)])
    last_plus = net.copy(slots.at[0], slots.at[4], plus)
    first_minus.wait_recv()
    add_into(slots.at[2], [slots.at[2], held(3, 1)])
    last_minus = net.copy(slots.at[2], slots.at[5], minus)
    yield
    side_minus.wait_recv()
    last_plus.wait_recv()
    add_into(target(0), [held(0, 0), slots.at[3], slots.at[4]])
    side_plus.wait_recv()
    last_minus.wait_recv()
    add_into(target(1), [held(0, 1), slots.at[1], slots.at[5]])


def x_first(net, me, source, slots, middle, other, out, held=None):
    staged = None
    if held is not None:
        order = {(1, 0): 0, (3, 1): 1, (0, 0): 2, (0, 1): 3}
        loads = [
            net.load(source.at[me.x_by(step), half], held.at[spot])
            for (step, half), spot in order.items()
        ]

        def staged(step, half):
            return held.at[order[step, half]]

    ring = ring_reduce(
        net,
        me.at(x=me.x_by(1)),
        me.at(x=me.x_by(3)),
        lambda step, half: source.at[me.x_by(step), half],
        slots,
        lambda half: middle.at[half],
        staged,
    )
    next(ring)
    yield
    if held is not None:
        for load in loads:
            load.wait()
    yield from ring
    across = net.copy(middle.at[1 - me.z_lo], other, me.at(z=me.z + 1 - 2 * me.z_lo))
    yield
    across.wait_recv()
    add_into(out, [middle.at[me.z_lo], other])


def z_first(net, me, source, other, middle, slots, out):
    across = net.copy(source.at[:, 1 - me.z_lo], other, me.at(z=me.z + 1 - 2 * me.z_lo))
    load = net.load(source.at[:, me.z_lo], middle)
    yield
    load.wait()
    across.wait_recv()
    add_into(middle, [middle, other])
    half_rows = middle.shape[1] // 2
    yield from ring_reduce(
        net,
        me.at(x=me.x_by(1)),
        me.at(x=me.x_by(3)),
        lambda step, half: middle.at[me.x_by(step), pl.ds(half * half_rows, half_rows)],
        slots,
        lambda half: out.at[pl.ds(half * half_rows, half_rows)],
    )


def core_pair(net, me, sending, other, middle):
    across = net.copy(sending, other, me.at(core=1 - me.core))
    yield
    net.sent(across)
    across.wait_recv()
    add_into(middle, [middle, other])


def dense_x_first(net, me, sending, other, middle, slots, corner, last, out):
    yield from core_pair(net, me, sending, other, middle)
    yield from ring_reduce(
        net,
        me.at(x=me.x_by(1)),
        me.at(x=me.x_by(3)),
        lambda step, half: middle.at[half, me.x_by(step)],
        slots,
        lambda half: corner.at[half],
    )
    half_rows = corner.shape[2] // 2
    yield from ring_reduce(
        net,
        me.at(z=me.z_by(1)),
        me.at(z=me.z_by(3)),
        lambda step, half: corner.at[
            me.z_by(step) // 2, lax.rem(me.z_by(step), 2), pl.ds(half * half_rows, half_rows)
        ],
        last,
        lambda half: out.at[pl.ds(half * half_rows, half_rows)],
    )


def dense_z_first(net, me, sending, other, middle, slots, corner, last, out):
    yield from core_pair(net, me, sending, other, middle)
    yield from ring_reduce(
        net,
        me.at(z=me.z_by(1)),
        me.at(z=me.z_by(3)),
        lambda step, half: middle.at[
            me.z_by(step) // 2, pl.ds(half * 2, 2), lax.rem(me.z_by(step), 2)
        ],
        slots,
        lambda half: corner.at[pl.ds(half * 2, 2)],
    )
    half_rows = corner.shape[1] // 2
    yield from ring_reduce(
        net,
        me.at(x=me.x_by(1)),
        me.at(x=me.x_by(3)),
        lambda step, half: corner.at[me.x_by(step), pl.ds(half * half_rows, half_rows)],
        last,
        lambda half: out.at[pl.ds(half * half_rows, half_rows)],
    )


def all_sum(net, devices, spot, own, slots, most):
    slots[spot] = own[...]
    sent = [net.copy(own, slots.at[spot], device) for device in devices]
    yield
    for made in sent:
        made.wait_recv()
    count = slots.shape[0]
    total = slots[0]
    peak = slots[0, most:]
    for step in range(1, count):
        total = total + slots[step]
        peak = jnp.maximum(peak, slots[step, most:])
    for made in sent:
        net.sent(made)
    own[:most] = total[:most]
    own[most:] = peak


def all_small(net, me, working, by_core, by_x, by_z, by_y, out):
    yield from all_sum(net, [me.at(core=1 - me.core)], me.core, working, by_core, 40)
    yield from all_sum(net, [me.at(x=me.x_by(s)) for s in (1, 2, 3)], me.x, working, by_x, 40)
    yield from all_sum(net, [me.at(z=me.z_by(s)) for s in (1, 2, 3)], me.z, working, by_z, 40)
    out[40:] = working[40:]
    yield from all_sum(net, [me.at(y=me.y_by(s)) for s in (1, 2, 3)], me.y, working, by_y, 40)
    out[:40] = working[:40]


def peers(me):
    offsets = [(a, b) for a in (2, 3, 0, 1) for b in (1, 3, 2, 0) if a or b]
    return [(a, b) + peer(me, a, b) for a, b in offsets]


def peer(me, a, b):
    z = me.z if a < 2 else lax.rem(me.z + 2, 4)
    core = me.core if a % 2 == 0 else 1 - me.core
    y = me.y_by(b)
    return z // 2 * 2 + core, y, me.at(z=z, core=core, y=y)


def gather_rows(table, home, store):
    def body(step, carry):
        columns = pl.ds(pl.multiple_of(step * 256, 256), 256)
        rows = home[:, :, :, columns].reshape(768, 256)
        total = contract_first(table[...], rows)
        store(columns, total[:96])
        return carry

    lax.fori_loop(0, home.shape[3] // 256, body, 0)


def turned(values):
    return pltpu.roll(values, 64, 1)


def column_of(row):
    eye = lax.broadcasted_iota(jnp.int32, (128, 128), 0) == lax.broadcasted_iota(
        jnp.int32, (128, 128), 1
    )
    return jnp.sum(jnp.where(eye, row, 0.0), axis=1, keepdims=True)


def norm_back(gradient, raw, gain):
    inverse = lax.rsqrt(jnp.mean(raw * raw, axis=-1, keepdims=True) + epsilon)
    normal = raw * inverse
    scaled = gradient * gain
    result = inverse * (scaled - normal * jnp.mean(scaled * normal, axis=-1, keepdims=True))
    return result, jnp.sum(gradient * normal, axis=0, keepdims=True)


def back_kernel(names, *refs):
    r = types.SimpleNamespace(**dict(zip(names, refs, strict=True)))
    low, full = jnp.bfloat16, jnp.float32
    score_scale = HEAD_SIZE ** (-0.5)
    me = Place()
    net = Net(r.send, r.recv, r.here)
    fetch = Fetch(net)
    fetch.start("hidden", r.hidden, r.hidden_held)
    greet(
        [
            me.at(x=me.x_by(1)),
            me.at(x=me.x_by(3)),
            me.at(z=me.z_by(1)),
            me.at(z=me.z_by(3)),
            me.at(x=me.x_by(2)),
        ]
        + [one[4] for one in peers(me)]
    )

    branch, whole = r.branch, r.whole
    above, below = me.at(y=me.y_by(1)), me.at(y=me.y_by(3))
    to_above = net.copy(branch, whole.at[:, me.y], above)
    to_below = net.copy(branch, whole.at[:, me.y], below)
    own_branch = net.load(branch, whole.at[:, me.y])
    weight = r.weight
    load_out = net.load(r.w_out, weight)
    gate = x_first(
        net, me, r.gate, r.gate_slots, r.gate_middle, r.gate_other,
        r.gate_out, r.gate_held,
    )
    up = x_first(
        net, me, r.up, r.up_slots, r.up_middle, r.up_other,
        r.up_out, r.up_held,
    )
    down = z_first(
        net, me, r.down, r.down_other, r.down_middle, r.down_slots,
        r.down_out,
    )
    for task in (gate, up, down):
        next(task)
    fetch.start("pair", r.pair, r.pair_held)
    fetch.start("query", r.query, r.query_held)
    fetch.start("query_raw", r.query_raw, r.query_raw_held)
    fetch.start("cosine", r.cosine.at[me.context], r.cosine_held)
    fetch.start("sine", r.sine.at[me.context], r.sine_held)
    fetch.start("mixed", r.mixed, r.mixed_held)
    fetch.start("w_key", r.w_key, r.key_weight)
    fetch.start("w_value", r.w_value, r.value_weight)

    hidden, inverse = fetch.hidden, r.inverse
    for s in range(3):
        rows = slice(s * 128, s * 128 + 128)
        values = hidden[s].astype(full)
        root = lax.rsqrt(jnp.mean(values * values, axis=-1, keepdims=True) + epsilon)
        inverse[rows, :] = jnp.broadcast_to(root, (128, 128))

    first, second = pl.ds(0, 1024), pl.ds(1024, 1024)
    to_above.wait_recv()
    passed = whole.at[:, me.y_by(3), :, first]
    far_above = net.copy(passed, passed, above)
    to_below.wait_recv()
    passed = whole.at[:, me.y_by(1), :, second]
    far_below = net.copy(passed, passed, below)
    own_branch.wait()
    load_out.wait()
    far_above.wait_recv()
    far_below.wait_recv()

    heads_grad = r.heads_grad

    def heads_step(step, carry):
        columns = pl.ds(pl.multiple_of(step * 256, 256), 256)
        heads_grad[:, columns] = jnp.dot(
            whole[...].reshape(384, 2048), weight[:, columns], preferred_element_type=full
        ).astype(low)
        return carry

    lax.fori_loop(0, 4, heads_step, 0)
    load_query = net.load(r.w_query, weight)

    produced, home, table = r.produced, r.home, r.table
    mine = pl.ds(pl.multiple_of(me.dp * 192 + me.y * 48, 16), 48)
    home_came = [
        net.copy(produced.at[dp, y], home.at[mine], device) for a, b, dp, y, device in peers(me)
    ]
    home_own = net.load(produced.at[me.dp, me.y], home.at[mine])

    query, query_raw, pair = fetch.query, fetch.query_raw, fetch.pair
    cosine, sine, mixed = fetch.cosine, fetch.sine, fetch.mixed
    gain_query, gain_key = r.head_gains[0:1, :], r.head_gains[1:2, :]
    bias, key_sum, value_sum = r.bias, r.key_sum, r.value_sum
    pair_grad, gain_part = r.pair_grad, r.gain_part
    gain_part[...] = jnp.zeros((8, 128), full)

    def rope_back(gradient):
        return gradient * cosine[...] - turned(gradient) * sine[...]

    def attend(s):
        here = pl.ds(s * 128, 128)
        bias[...] = mask_bias(me, r.segments, s)
        key_sum[...] = jnp.zeros_like(key_sum)
        value_sum[...] = jnp.zeros_like(value_sum)

        def two_heads(step, carry):
            columns = pl.ds(pl.multiple_of(step * 256, 256), 256)

            def stacked(ref):
                both = ref[here, columns]
                return jnp.concatenate([both[:, :128], both[:, 128:]], axis=0)

            q, d = stacked(query), stacked(heads_grad)
            keys, values = pair[0, s], pair[1, s]
            lines = r.log_sum
            logs = jnp.concatenate(
                [column_of(lines[s * 8 + step * 2]), column_of(lines[s * 8 + step * 2 + 1])], axis=0
            )
            score = contract_last(q, keys) * score_scale
            score = score + jnp.concatenate([bias[...], bias[...]], axis=0)
            prob = jnp.exp(score - logs)
            prob_grad = contract_last(d, values)
            delta = jnp.sum(prob * prob_grad, axis=-1, keepdims=True)
            score_grad = (prob * (prob_grad - delta)).astype(low)
            value_sum[...] += contract_first(prob.astype(low), d)
            key_sum[...] += contract_first(score_grad, q)
            turned_grad = jnp.dot(score_grad, keys, preferred_element_type=full) * score_scale
            for half in range(2):
                run = pl.ds(pl.multiple_of(step * 256 + half * 128, 128), 128)
                grad, part = norm_back(
                    rope_back(turned_grad[half * 128 : half * 128 + 128]),
                    query_raw[here, run],
                    gain_query,
                )
                heads_grad[here, run] = grad.astype(low)
                gain_part[0:1, :] += part
            return carry

        lax.fori_loop(0, 4, two_heads, 0)
        pair_grad[:, :, 0, s] = (key_sum[...] * score_scale).astype(low).reshape(4, 2, 128, 128)
        pair_grad[:, :, 1, s] = value_sum[...].astype(low).reshape(4, 2, 128, 128)

    attend(0)
    attend(1)
    next(gate)
    next(up)
    attend(2)
    pairs = x_first(
        net, me, pair_grad, r.pair_slots, r.pair_middle, r.pair_other,
        r.pair_out,
    )
    next(pairs)

    query_low = heads_grad

    def own_input(columns):
        return hidden[:, :, columns].reshape(384, 256).astype(full)

    def normed(columns):
        return (own_input(columns) * inverse[:, 0:1] * r.gains[0:1, columns]).astype(low)

    def whole_part(columns):
        return whole[:, :, :, columns].reshape(384, 256)

    def weigh(core, left, right, target):
        def body(step, carry):
            z_hi, part = step // 2, lax.rem(step, 2)
            columns = pl.ds(pl.multiple_of((z_hi * 2 + core) * 512 + part * 256, 256), 256)
            made = contract_first(left(columns), right[...]).astype(low)
            target[z_hi, pl.ds(part * 2, 2)] = made.reshape(2, 2, 64, right.shape[1])
            return carry

        lax.fori_loop(0, 4, body, 0)

    def dense(order, left, right, sending, other, middle, *more):
        weigh(1 - me.core, left, right, sending)
        task = order(net, me, sending, other, middle, *more)
        next(task)
        weigh(me.core, left, right, middle)
        return task

    out_w = dense(
        dense_z_first, whole_part, mixed, r.sending, r.out_w_other, r.out_w_middle, r.out_w_slots, r.out_w_corner,
        r.out_w_last, r.out_w_out,
    )
    next(pairs)
    next(down)
    next(out_w)
    query_w = dense(
        dense_x_first, normed, query_low, r.sending, r.query_w_other, r.query_w_middle, r.query_w_slots, r.query_w_corner,
        r.query_w_last, r.query_w_out,
    )
    next(pairs)
    next(gate)
    next(up)

    pair_out, key_raw, pair_low = r.pair_out, r.key_raw, r.pair_low
    next(pairs, None)
    for s in range(3):
        rows = slice(s * 128, s * 128 + 128)
        grad, part = norm_back(rope_back(pair_out[0, s]), key_raw[rows, :], gain_key)
        gain_part[1:2, :] += part
        pair_low[rows, :128] = grad.astype(low)
        pair_low[rows, 128:] = pair_out[1, s].astype(low)

    load_query.wait()
    net.sent(far_above)
    net.sent(far_below)
    w_key, w_value = fetch.w_key, fetch.w_value
    small = r.small
    normed_part = r.normed_part

    def normed_step(step, carry):
        columns = pl.ds(pl.multiple_of(step * 256, 256), 256)
        made = contract_last(query_low[...], weight[columns, :])
        made = made + contract_last(pair_low[:, :128], w_key[columns, :])
        made = made + contract_last(pair_low[:, 128:], w_value[columns, :])
        normal = own_input(columns) * inverse[:, 0:1]
        normed_part[:, columns] = jnp.sum(made * normal, axis=0, keepdims=True)
        whole[:, :, :, columns] = made.astype(low).reshape(3, 4, 32, 256)
        return carry

    lax.fori_loop(0, 8, normed_step, 0)
    normed_out = r.normed_out
    normed_sum = ring_reduce(
        net,
        above,
        below,
        lambda step, half: whole.at[:, me.y_by(step), :, pl.ds(half * 1024, 1024)],
        r.normed_slots,
        lambda half: normed_out.at[:, :, pl.ds(half * 1024, 1024)],
    )
    next(normed_sum)
    for step in range(16):
        run = slice(step * 128, step * 128 + 128)
        small[step : step + 1, :] = normed_part[:, run]
        small[16 + step : 17 + step, :] = r.moe_gain_part[:, run]
    small[32:40, :] = gain_part[...]
    small[40:, :] = r.peaks[...]
    smalls = all_small(
        net, me, small, r.by_core, r.by_x, r.by_z, r.by_y, r.small_out
    )
    next(smalls)
    pair_w = dense(
        dense_x_first, normed, pair_low, r.pair_sending, r.pair_w_other, r.pair_w_middle, r.pair_w_slots, r.pair_w_corner,
        r.pair_w_last, r.pair_w_out,
    )
    next(query_w)
    next(smalls)

    def rest(*tasks):
        for task in tasks:
            next(task, None)

    rest(normed_sum, out_w, pair_w, smalls, gate, up, down, query_w)

    next(normed_sum, None)
    for s in range(3):
        rows = pl.ds(pl.multiple_of(me.y * 32, 32), 32)
        grad, _ = norm_back(normed_out[s], hidden[s, rows, :].astype(full), r.gains[0:1, :])
        normed_out[s] = grad

    rest(out_w, pair_w, smalls, down, gate, up, query_w)
    rest(pair_w, out_w, smalls, query_w)

    for made in home_came:
        made.wait_recv()
    home_own.wait()
    home_loads = [
        net.load(home.at[:, pl.ds(half * 1024, 1024)], weight.at[pl.ds(half * 768, 768)])
        for half in range(2)
    ]
    rest(pair_w, out_w, smalls, query_w, gate, up, down)
    moe_out = r.moe_out
    for half in range(2):
        home_loads[half].wait()

        def gather(step, carry, half=half):
            columns = pl.ds(pl.multiple_of(step * 256, 256), 256)
            total = contract_first(table[...], weight[half * 768 : half * 768 + 768, columns])
            moe_out[:, pl.ds(pl.multiple_of(half * 1024 + step * 256, 256), 256)] = total[:96]
            return carry

        lax.fori_loop(0, 4, gather, 0)
    tasks = [pair_w, out_w, smalls, query_w, gate, up, down]
    while tasks:
        for task in list(tasks):
            if next(task, "end") == "end":
                tasks.remove(task)
    net.finish()


def dense_slots(columns, corner):
    low = jnp.bfloat16
    return [
        pltpu.VMEM((2, 4, 2, 64, columns), low),
        pltpu.VMEM((2, 4, 2, 64, columns), low),
        pltpu.VMEM((6, 2, 64, columns), low),
        pltpu.VMEM(corner + (64, columns), low),
        pltpu.VMEM((6, 32, columns), low),
    ]


def back(far, near):
    low, full = jnp.bfloat16, jnp.float32
    outs = dict(
        gate_out=(256, 768),
        up_out=(256, 768),
        down_out=(256, 768),
        query_w_out=(64, 1024),
        pair_w_out=(64, 256),
        out_w_out=(64, 1024),
        small_out=(48, 128),
        normed_out=(3, 32, 2048),
        moe_out=(96, 2048),
    )
    scratch = dict(
        hidden_held=pltpu.VMEM((3, 128, 2048), low),
        pair_held=pltpu.VMEM((2, 3, 1024, 128), low),
        query_held=pltpu.VMEM((384, 1024), low),
        query_raw_held=pltpu.VMEM((384, 1024), full),
        cosine_held=pltpu.VMEM((128, 128), full),
        sine_held=pltpu.VMEM((128, 128), full),
        mixed_held=pltpu.VMEM((384, 1024), low),
        key_weight=pltpu.VMEM((2048, 128), low),
        value_weight=pltpu.VMEM((2048, 128), low),
        whole=pltpu.VMEM((3, 4, 32, 2048), low),
        weight=pltpu.VMEM((2048, 1024), low),
        inverse=pltpu.VMEM((384, 128), full),
        heads_grad=pltpu.VMEM((384, 1024), low),
        bias=pltpu.VMEM((128, 1024), full),
        key_sum=pltpu.VMEM((1024, 128), full),
        value_sum=pltpu.VMEM((1024, 128), full),
        pair_grad=pltpu.VMEM((4, 2, 2, 3, 128, 128), low),
        pair_slots=pltpu.VMEM((6, 2, 3, 128, 128), low),
        pair_middle=pltpu.VMEM((2, 2, 3, 128, 128), low),
        pair_other=pltpu.VMEM((2, 3, 128, 128), low),
        pair_out=pltpu.VMEM((2, 3, 128, 128), full),
        pair_low=pltpu.VMEM((384, 256), low),
        gain_part=pltpu.VMEM((8, 128), full),
        normed_part=pltpu.VMEM((1, 2048), full),
        normed_slots=pltpu.VMEM((6, 3, 32, 1024), low),
        small=pltpu.VMEM((48, 128), full),
        by_core=pltpu.VMEM((2, 48, 128), full),
        by_x=pltpu.VMEM((4, 48, 128), full),
        by_z=pltpu.VMEM((4, 48, 128), full),
        by_y=pltpu.VMEM((4, 48, 128), full),
        down_other=pltpu.VMEM((4, 256, 768), low),
        down_middle=pltpu.VMEM((4, 256, 768), low),
        down_slots=pltpu.VMEM((6, 128, 768), low),
        gate_slots=pltpu.VMEM((6, 256, 768), low),
        gate_middle=pltpu.VMEM((2, 256, 768), low),
        gate_other=pltpu.VMEM((256, 768), low),
        gate_held=pltpu.VMEM((4, 256, 768), low),
        up_slots=pltpu.VMEM((6, 256, 768), low),
        up_middle=pltpu.VMEM((2, 256, 768), low),
        up_other=pltpu.VMEM((256, 768), low),
        up_held=pltpu.VMEM((4, 256, 768), low),
        sending=pltpu.VMEM((2, 4, 2, 64, 1024), low),
        pair_sending=pltpu.VMEM((2, 4, 2, 64, 256), low),
        query_w_other=None,
        query_w_middle=None,
        query_w_slots=None,
        query_w_corner=None,
        query_w_last=None,
        pair_w_other=None,
        pair_w_middle=None,
        pair_w_slots=None,
        pair_w_corner=None,
        pair_w_last=None,
        out_w_other=None,
        out_w_middle=None,
        out_w_slots=None,
        out_w_corner=None,
        out_w_last=None,
        send=pltpu.SemaphoreType.DMA((104,)),
        recv=pltpu.SemaphoreType.DMA((104,)),
        here=pltpu.SemaphoreType.DMA((28,)),
    )
    dense = dense_slots(1024, (2, 2)) + dense_slots(256, (2, 2)) + dense_slots(1024, (4,))
    scratch = {name: one or dense.pop(0) for name, one in scratch.items()}
    outs = {name: jax.ShapeDtypeStruct(size, full) for name, size in outs.items()}
    far_outs = dict(home=jax.ShapeDtypeStruct((768, 2048), low))
    return call(back_kernel, 0, far, near, outs, far_outs, scratch)


class Fetch:
    def __init__(self, net):
        self.net, self.waiting, self.held = net, {}, {}

    def start(self, name, source, target):
        self.waiting[name] = self.net.load(source, target)
        self.held[name] = target

    def __getattr__(self, name):
        if name in self.waiting:
            self.waiting.pop(name).wait()
        return self.held[name]


def token_table(ids, gates, capacity, table, info):
    low, full = jnp.bfloat16, jnp.float32
    expert = lax.broadcasted_iota(jnp.int32, (96, 128), 1)
    routes = ids[...].reshape(96, 8)
    values = gates[...].reshape(96, 8)
    chosen = jnp.zeros((96, 128), full)
    share = jnp.zeros((96, 128), full)
    limit = jnp.zeros((1, 128), full)
    for k in range(8):
        named = routes[:, k : k + 1] == expert
        chosen = chosen + jnp.where(named, 1.0, 0.0)
        share = share + jnp.where(named, values[:, k : k + 1], 0.0)
    for e in range(16):
        limit = jnp.where(expert[0:1] == e, capacity[e].astype(full), limit)
    earlier = lax.broadcasted_iota(jnp.int32, (96, 96), 1) < lax.broadcasted_iota(
        jnp.int32, (96, 96), 0
    )
    before = jnp.dot(
        jnp.where(earlier, 1.0, 0.0).astype(low), chosen.astype(low), preferred_element_type=full
    )
    slot = jnp.where((chosen > 0.0) & (before < limit), before, -1.0)
    none = jnp.full((32, 128), -1.0, full)
    slot = jnp.concatenate([slot, none], axis=0).T
    share = jnp.concatenate([share, none], axis=0).T
    spot = lax.broadcasted_iota(jnp.int32, (48, 128), 0).astype(full)
    for e in range(16):
        mask = jnp.where(slot[e : e + 1, :] == spot, 1.0, 0.0)
        table[e * 48 : e * 48 + 48, :] = mask.astype(low)
        info[e // 4, e % 4] = jnp.concatenate(
            [slot[e : e + 1, :], share[e : e + 1, :], jnp.zeros((6, 128), full)], axis=0
        )


def dispatch(me, table, rows, sender):
    for a, b, dp, y, device in peers(me):
        if b == 1:
            rest = table[pl.ds(pl.multiple_of(dp * 192, 192), 192), :]
            columns = 512
            for step in range(2048 // columns):
                run = slice(step * columns, (step + 1) * columns)
                picked = jnp.dot(rest, rows[:, run], preferred_element_type=jnp.float32)
                sender[dp, :, :, run] = picked.astype(jnp.bfloat16).reshape(4, 48, columns)
        yield a, b, dp, y, device


def moe_kernel(names, *refs):
    r = types.SimpleNamespace(**dict(zip(names, refs, strict=True)))
    low, full = jnp.bfloat16, jnp.float32
    me = Place()
    net = Net(r.send, r.recv, r.here)
    fetch = Fetch(net)
    fetch.start("w_gate", r.w_gate, r.gate_weight)
    fetch.start("w_up", r.w_up, r.up_weight)
    fetch.start("grads", r.grads, r.grads_held)
    fetch.start("w_down", r.w_down, r.down_weight)
    greet([one[4] for one in peers(me)])
    rows, sending, local, table = r.rows, r.sending, r.local, r.table
    values = r.after[...]
    inverse = lax.rsqrt(jnp.mean(values * values, axis=-1, keepdims=True) + epsilon)
    gain = r.gains[1:2, :]
    rows[96:, :] = jnp.zeros((32, 2048), low)
    rows[:96, :] = (values * inverse * gain).astype(low)
    came = {}
    for a, b, dp, y, device in dispatch(me, table, rows, sending):
        came[a, b] = net.copy(sending.at[dp, y], local.at[me.dp, me.y], device)
    local[me.dp, me.y] = sending[me.dp, me.y]

    act, gate_back, up_back, back, home = r.act, r.gate_back, r.up_back, r.back, r.home
    w_gate, w_up, grads, w_down = fetch.w_gate, fetch.w_up, fetch.grads, fetch.w_down
    spot = lax.broadcasted_iota(jnp.int32, (48, 128), 0).astype(full)
    back_came, dots_came = {}, {}
    for a in (0, 1, 2, 3):
        group = peer(me, a, 0)[0]
        for b in range(4):
            if a or b:
                came[a, b].wait_recv()
        masks, shares = [], []
        for y in range(4):
            mask = r.info_in[group, y, 0:1, :] == spot
            masks.append(mask)
            shares.append(
                jnp.sum(jnp.where(mask, r.info_in[group, y, 1:2, :], 0.0), axis=1, keepdims=True)
            )
        shared = jnp.concatenate(shares, axis=0)

        def inner(step, carry, group=group, shared=shared):
            columns = pl.ds(pl.multiple_of(step * 256, 256), 256)
            entered = local[group].reshape(192, 2048)
            gate_pre = jnp.dot(entered, w_gate[:, columns], preferred_element_type=full)
            up_pre = jnp.dot(entered, w_up[:, columns], preferred_element_type=full)
            scaled = (grads[group].reshape(192, 2048).astype(full) * shared).astype(low)
            act_back = jnp.dot(scaled, w_down[:, columns], preferred_element_type=full)
            sigmoid = 1.0 / (1.0 + jnp.exp(-gate_pre))
            silu = gate_pre * sigmoid
            act[group, :, columns] = (silu * up_pre).astype(low)
            gate_back[group, :, columns] = (
                act_back * up_pre * sigmoid * (1.0 + gate_pre * (1.0 - sigmoid))
            ).astype(low)
            up_back[group, :, columns] = (act_back * silu).astype(low)
            return carry

        lax.fori_loop(0, 3, inner, 0)

        def outer(step, dot, group=group, shared=shared):
            columns = pl.ds(pl.multiple_of(step * 256, 256), 256)
            made = contract_last(act[group], w_down[columns, :]).astype(low).astype(full)
            r.produced_held[group, :, :, columns] = (
                (made * shared).astype(low).reshape(4, 48, 256)
            )
            incoming = grads[group, :, :, columns].reshape(192, 256).astype(full)
            dot = dot + jnp.sum(made * incoming, axis=1, keepdims=True)
            grads[group, :, :, columns] = (incoming * shared).astype(low).reshape(4, 48, 256)
            row_back = contract_last(gate_back[group], w_gate[columns, :]) + contract_last(
                up_back[group], w_up[columns, :]
            )
            back[group, :, :, columns] = row_back.astype(low).reshape(4, 48, 256)
            return dot

        dot = lax.fori_loop(0, 8, outer, jnp.zeros((192, 1), full))
        for y in range(4):
            line = jnp.sum(
                jnp.where(masks[y], dot[y * 48 : y * 48 + 48], 0.0), axis=0, keepdims=True
            )
            r.dots[group, y] = jnp.broadcast_to(line, (8, 128))
        for b in (2, 1, 3, 0):
            if a or b:
                dp, y, device = peer(me, a, b)
                back_came[a, b] = net.copy(back.at[dp, y], home.at[me.dp, me.y], device)
                dots_came[a, b] = net.copy(r.dots.at[dp, y], r.dots_in.at[me.dp, me.y], device)
    home[me.dp, me.y] = back[me.dp, me.y]
    r.dots_in[me.dp, me.y] = r.dots[me.dp, me.y]
    written = [net.load(r.produced_held, r.produced)]

    def weigh(step, carry):
        columns = pl.ds(pl.multiple_of(step * 256, 256), 256)
        entered = local[:, :, :, columns].reshape(768, 256)
        r.gate_held[columns, :] = contract_first(entered, gate_back[...].reshape(768, 768)).astype(
            low
        )
        r.up_held[columns, :] = contract_first(entered, up_back[...].reshape(768, 768)).astype(low)
        incoming = grads[:, :, :, columns].reshape(768, 256)
        r.down_held[columns, :] = contract_first(incoming, act[...].reshape(768, 768)).astype(low)
        return carry

    lax.fori_loop(0, 8, weigh, 0)
    written += [
        net.load(r.gate_held, r.full_gate),
        net.load(r.up_held, r.full_up),
        net.load(r.down_held, r.full_down),
    ]

    for a, b, *_ in peers(me):
        dots_came[a, b].wait_recv()
    lines = [r.dots_in[e // 4, e % 4, 0:1, :] for e in range(16)]
    by_token = jnp.concatenate(lines + [jnp.zeros((112, 128), full)], axis=0).T[:96]
    expert = lax.broadcasted_iota(jnp.int32, (96, 128), 1)
    routes = r.ids[...].reshape(96, 8)
    picked = [
        jnp.sum(jnp.where(routes[:, k : k + 1] == expert, by_token, 0.0), axis=1, keepdims=True)
        for k in range(8)
    ]
    r.gate_grad[...] = jnp.concatenate(picked, axis=1).reshape(3, 32, 8)

    for a, b, *_ in peers(me):
        back_came[a, b].wait_recv()
    after_grad = r.after_grad

    def keep(columns, total):
        after_grad[:, columns] = total

    gather_rows(table, home, keep)
    gradient = after_grad[...]
    moe_part, gain_part = norm_back(gradient, r.after[...], gain)
    r.gain_part[...] = gain_part
    result = r.cotangent[...].reshape(96, 2048).astype(full) + moe_part
    after_grad[...] = result
    r.branch[...] = result.astype(low).reshape(3, 32, 2048)
    for one in written:
        one.wait()
    net.finish()


def moe(far, near):
    low, full = jnp.bfloat16, jnp.float32
    rows = (4, 4, 48, 2048)
    outs = dict(
        after_grad=jax.ShapeDtypeStruct((96, 2048), full),
        branch=jax.ShapeDtypeStruct((3, 32, 2048), low),
        gain_part=jax.ShapeDtypeStruct((1, 2048), full),
        gate_grad=jax.ShapeDtypeStruct((3, 32, 8), full),
    )
    far_outs = dict(
        produced=jax.ShapeDtypeStruct(rows, low),
        full_gate=jax.ShapeDtypeStruct((2048, 768), low),
        full_up=jax.ShapeDtypeStruct((2048, 768), low),
        full_down=jax.ShapeDtypeStruct((2048, 768), low),
    )
    scratch = dict(
        rows=pltpu.VMEM((128, 2048), low),
        sending=pltpu.VMEM(rows, low),
        local=pltpu.VMEM(rows, low),
        grads_held=pltpu.VMEM(rows, low),
        produced_held=pltpu.VMEM(rows, low),
        back=pltpu.VMEM(rows, low),
        home=pltpu.VMEM(rows, low),
        gate_weight=pltpu.VMEM((2048, 768), low),
        up_weight=pltpu.VMEM((2048, 768), low),
        down_weight=pltpu.VMEM((2048, 768), low),
        gate_held=pltpu.VMEM((2048, 768), low),
        up_held=pltpu.VMEM((2048, 768), low),
        down_held=pltpu.VMEM((2048, 768), low),
        act=pltpu.VMEM((4, 192, 768), low),
        gate_back=pltpu.VMEM((4, 192, 768), low),
        up_back=pltpu.VMEM((4, 192, 768), low),
        dots=pltpu.VMEM((4, 4, 8, 128), full),
        dots_in=pltpu.VMEM((4, 4, 8, 128), full),
        send=pltpu.SemaphoreType.DMA((45,)),
        recv=pltpu.SemaphoreType.DMA((45,)),
        here=pltpu.SemaphoreType.DMA((8,)),
    )
    return call(moe_kernel, 1, far, near, outs, far_outs, scratch)


def call(kernel, number, far, near, outs, far_outs, scratch):
    names = list(far) + list(near) + list(outs) + list(far_outs) + list(scratch)
    shapes = {**outs, **far_outs}
    results = pl.pallas_call(
        functools.partial(kernel, names),
        out_shape=list(shapes.values()),
        in_specs=[ANY] * len(far)
        + [SMEM if one.ndim == 1 else VMEM for one in near.values()],
        out_specs=[VMEM] * len(outs) + [ANY] * len(far_outs),
        scratch_shapes=list(scratch.values()),
        compiler_params=pltpu.CompilerParams(
            collective_id=number, has_side_effects=True, vmem_limit_bytes=62 << 20
        ),
        name=kernel.__name__,
    )(*far.values(), *near.values())
    return types.SimpleNamespace(**dict(zip(shapes, results, strict=True)))


def front_kernel(names, *refs):
    r = types.SimpleNamespace(**dict(zip(names, refs, strict=True)))
    low, full = jnp.bfloat16, jnp.float32
    score_scale = HEAD_SIZE ** (-0.5)
    me = Place()
    net = Net(r.send, r.recv, r.here)
    fetch = Fetch(net)
    fetch.start("hidden", r.hidden, r.hidden_held)
    fetch.start("w_pair", r.w_key, r.key_weight)
    fetch.start("w_value", r.w_value, r.value_weight)
    fetch.start("cosine", r.cosine.at[me.context], r.cosine_held)
    fetch.start("sine", r.sine.at[me.context], r.sine_held)
    fetch.start("w_query", r.w_query, r.query_weight)
    fetch.start("cotangent", r.cotangent, r.cotangent_held)
    fetch.start("w_out", r.w_out, r.out_weight)
    beside = me.at(z=me.z + 1 - 2 * me.z_lo)
    right, left = me.at(x=me.x_by(1)), me.at(x=me.x_by(3))
    greet([right, left, beside] + [one[4] for one in peers(me)])

    hidden, normed = fetch.hidden, r.normed
    for s in range(3):
        values = hidden[s].astype(full)
        root = lax.rsqrt(jnp.mean(values * values, axis=-1, keepdims=True) + epsilon)
        normed[s * 128 : s * 128 + 128, :] = (values * root * r.gains[0:1, :]).astype(low)

    def rope(values):
        cosine = jnp.concatenate([fetch.cosine[...]] * 3, axis=0)
        sine = jnp.concatenate([fetch.sine[...]] * 3, axis=0)
        return values * cosine + turned(values) * sine

    def head_norm(raw, gain):
        return raw * lax.rsqrt(jnp.mean(raw * raw, axis=-1, keepdims=True) + epsilon) * gain

    pair, key_raw = r.pair_held, r.key_raw
    made = jnp.dot(normed[...], fetch.w_pair[...], preferred_element_type=full)
    key_raw[...] = made
    keys = rope(head_norm(made, r.head_gains[1:2, :])).astype(low)
    values = jnp.dot(normed[...], fetch.w_value[...], preferred_element_type=full).astype(low)
    own = pl.ds(pl.multiple_of(me.context * 128, 128), 128)
    pair[0, :, own, :] = keys.reshape(3, 128, 128)
    pair[1, :, own, :] = values.reshape(3, 128, 128)

    def block(x, z_lo):
        return pl.ds(pl.multiple_of((x * 2 + z_lo) * 128, 128), 128)

    def piece(x, z_lo, half=None):
        rows = block(x, z_lo)
        return pair.at[:, :, rows, :] if half is None else pair.at[half, :, rows, :]

    def pass_on(view, device):
        return net.copy(view, view, device)

    own_z, other_z = me.z_lo, 1 - me.z_lo
    from_z = pass_on(piece(me.x, own_z), beside)
    from_left = [pass_on(piece(me.x, own_z), right)]
    from_right = [pass_on(piece(me.x, own_z), left)]

    token_table(r.ids, r.gates, r.capacity, r.table, r.info)
    arrivals = []
    for a, b, dp, y, device in peers(me):
        arrivals.append(net.copy(r.info.at[dp, y], r.info_in.at[me.dp, me.y], device))
    r.info_in[me.dp, me.y] = r.info[me.dp, me.y]
    rows = r.rows
    rows[96:, :] = jnp.zeros((32, 2048), low)
    rows[:96, :] = fetch.cotangent[...].reshape(96, 2048)
    from_z.wait_recv()
    from_left.append(pass_on(piece(me.x, other_z), right))
    from_right.append(pass_on(piece(me.x, other_z), left))
    for a, b, dp, y, device in dispatch(me, r.table, rows, r.sending):
        arrivals.append(net.copy(r.sending.at[dp, y], r.grads.at[me.dp, me.y], device))
    own_grads = net.load(r.sending.at[me.dp, me.y], r.grads.at[me.dp, me.y])

    w_query, query, query_raw = fetch.w_query, r.query_held, r.query_raw_held

    def project(step, carry):
        columns = pl.ds(pl.multiple_of(step * 256, 256), 256)
        made = jnp.dot(normed[...], w_query[:, columns], preferred_element_type=full)
        query_raw[:, columns] = made
        for half in range(2):
            run = pl.ds(pl.multiple_of(step * 256 + half * 128, 128), 128)
            one = head_norm(made[:, half * 128 : half * 128 + 128], r.head_gains[0:1, :])
            query[:, run] = rope(one).astype(low)
        return carry

    lax.fori_loop(0, 4, project, 0)
    written = [net.load(query, r.query), net.load(query_raw, r.query_raw)]
    far = [[], []]
    for spot, zs in enumerate((own_z, other_z)):
        from_left[spot].wait_recv()
        far[0].append(pass_on(piece(me.x_by(3), zs, 0), right))
        from_right[spot].wait_recv()
        far[1].append(pass_on(piece(me.x_by(1), zs, 1), left))
    for one in far[0] + far[1]:
        one.wait_recv()
    written.append(net.load(pair, r.pair))

    bias, peaks, mixed = r.bias, r.peak_rows, r.mixed_held
    peaks[...] = jnp.full((8, 1, 128), -jnp.inf, full)
    for s in range(3):
        here = pl.ds(s * 128, 128)
        bias[...] = mask_bias(me, r.segments, s)

        def two_heads(step, carry, s=s, here=here):
            columns = pl.ds(pl.multiple_of(step * 256, 256), 256)
            both = query[here, columns]
            q = jnp.concatenate([both[:, :128], both[:, 128:]], axis=0)
            score = contract_last(q, pair[0, s]) * score_scale
            score = score + jnp.concatenate([bias[...], bias[...]], axis=0)
            highest = jnp.max(score, axis=-1, keepdims=True)
            weight = jnp.exp(score - highest)
            total = jnp.sum(weight, axis=-1, keepdims=True)
            prob = (weight * (1.0 / total)).astype(low)
            logs = highest + jnp.log(total)
            heads = jnp.dot(prob, pair[1, s], preferred_element_type=full).astype(low)
            for half in range(2):
                part = slice(half * 128, half * 128 + 128)
                head = step * 2 + half
                run = pl.ds(pl.multiple_of(step * 256 + half * 128, 128), 128)
                mixed[here, run] = heads[part]
                r.log_sum[s * 8 + head] = row_of(logs[part])
                top = jnp.max(highest[part], axis=0, keepdims=True)
                peaks[head] = jnp.maximum(peaks[head], top)
            return carry

        lax.fori_loop(0, 4, two_heads, 0)
    for head in range(8):
        r.peaks[head : head + 1, :] = peaks[head]
    written.append(net.load(mixed, r.mixed))

    w_out, shares = fetch.w_out, r.shares

    def branch_step(step, carry):
        columns = pl.ds(pl.multiple_of(step * 256, 256), 256)
        made = contract_last(mixed[...], w_out[columns, :])
        shares[:, :, :, columns] = made.astype(low).reshape(3, 4, 32, 256)
        return carry

    lax.fori_loop(0, 8, branch_step, 0)
    after = r.after_sum
    ring = ring_reduce(
        net,
        me.at(y=me.y_by(1)),
        me.at(y=me.y_by(3)),
        lambda step, half: shares.at[:, me.y_by(step), :, pl.ds(half * 1024, 1024)],
        r.branch_slots,
        lambda half: after.at[:, :, pl.ds(half * 1024, 1024)],
    )
    for _ in ring:
        pass
    own_rows = pl.ds(pl.multiple_of(me.y * 32, 32), 32)
    for s in range(3):
        r.after[s * 32 : s * 32 + 32, :] = after[s] + hidden[s, own_rows, :].astype(full)
    for one in arrivals:
        one.wait_recv()
    own_grads.wait()
    for one in written:
        one.wait()
    net.finish()


def row_of(column):
    eye = lax.broadcasted_iota(jnp.int32, (128, 128), 0) == lax.broadcasted_iota(
        jnp.int32, (128, 128), 1
    )
    return jnp.sum(jnp.where(eye, column, 0.0), axis=0, keepdims=True)


def mask_bias(me, segments, s):
    spot = me.context * 128 + lax.broadcasted_iota(jnp.int32, (128, 1024), 0)
    own = segments[s : s + 1, pl.ds(pl.multiple_of(me.context * 128, 128), 128)]
    document = column_of(own.astype(jnp.float32))
    allowed = (document == segments[s : s + 1, :].astype(jnp.float32)) & (
        lax.broadcasted_iota(jnp.int32, (128, 1024), 1) <= spot
    )
    return jnp.where(allowed, 0.0, masked_value)


def front(far, near):
    low, full = jnp.bfloat16, jnp.float32
    rows = (4, 4, 48, 2048)
    outs = dict(
        key_raw=jax.ShapeDtypeStruct((384, 128), full),
        log_sum=jax.ShapeDtypeStruct((24, 1, 128), full),
        peaks=jax.ShapeDtypeStruct((8, 128), full),
        after=jax.ShapeDtypeStruct((96, 2048), full),
        table=jax.ShapeDtypeStruct((768, 128), low),
        info_in=jax.ShapeDtypeStruct((4, 4, 8, 128), full),
    )
    far_outs = dict(
        query=jax.ShapeDtypeStruct((384, 1024), low),
        query_raw=jax.ShapeDtypeStruct((384, 1024), full),
        pair=jax.ShapeDtypeStruct((2, 3, 1024, 128), low),
        mixed=jax.ShapeDtypeStruct((384, 1024), low),
        grads=jax.ShapeDtypeStruct(rows, low),
    )
    scratch = dict(
        hidden_held=pltpu.VMEM((3, 128, 2048), low),
        key_weight=pltpu.VMEM((2048, 128), low),
        value_weight=pltpu.VMEM((2048, 128), low),
        cosine_held=pltpu.VMEM((128, 128), full),
        sine_held=pltpu.VMEM((128, 128), full),
        query_weight=pltpu.VMEM((2048, 1024), low),
        cotangent_held=pltpu.VMEM((3, 32, 2048), low),
        out_weight=pltpu.VMEM((2048, 1024), low),
        normed=pltpu.VMEM((384, 2048), low),
        pair_held=pltpu.VMEM((2, 3, 1024, 128), low),
        info=pltpu.VMEM((4, 4, 8, 128), full),
        rows=pltpu.VMEM((128, 2048), low),
        sending=pltpu.VMEM(rows, low),
        query_held=pltpu.VMEM((384, 1024), low),
        query_raw_held=pltpu.VMEM((384, 1024), full),
        bias=pltpu.VMEM((128, 1024), full),
        peak_rows=pltpu.VMEM((8, 1, 128), full),
        mixed_held=pltpu.VMEM((384, 1024), low),
        shares=pltpu.VMEM((3, 4, 32, 2048), low),
        branch_slots=pltpu.VMEM((6, 3, 32, 1024), low),
        after_sum=pltpu.VMEM((3, 32, 2048), full),
        send=pltpu.SemaphoreType.DMA((46,)),
        recv=pltpu.SemaphoreType.DMA((46,)),
        here=pltpu.SemaphoreType.DMA((16,)),
    )
    return call(front_kernel, 2, far, near, outs, far_outs, scratch)


def shards(
    hidden_in,
    segments,
    attn_gain,
    query_gain,
    key_gain,
    w_query,
    key_weight_matrix,
    value_weight_matrix,
    w_out,
    moe_gain,
    expert_ids,
    gate_values,
    capacity,
    w_gate,
    w_up,
    w_down,
    cotangent,
):
    full = jnp.float32
    gains = jnp.stack([attn_gain, moe_gain]).astype(full)
    head_gains = jnp.stack([query_gain, key_gain]).astype(full)
    cosine, sine = rotary()
    first = front(
        dict(
            hidden=hidden_in,
            w_key=key_weight_matrix,
            w_value=value_weight_matrix,
            cosine=cosine,
            sine=sine,
            w_query=w_query,
            cotangent=cotangent,
            w_out=w_out,
        ),
        dict(
            gains=gains,
            head_gains=head_gains,
            segments=segments,
            ids=expert_ids,
            gates=gate_values,
            capacity=capacity,
        ),
    )
    second = moe(
        dict(w_gate=w_gate[0], w_up=w_up[0], w_down=w_down[0], grads=first.grads),
        dict(
            after=first.after,
            cotangent=cotangent,
            gains=gains,
            ids=expert_ids,
            table=first.table,
            info_in=first.info_in,
        ),
    )
    done = back(
        dict(
            branch=second.branch,
            w_out=w_out,
            w_query=w_query,
            gate=second.full_gate.reshape(4, 2, 256, 768),
            up=second.full_up.reshape(4, 2, 256, 768),
            down=second.full_down.reshape(4, 2, 256, 768),
            produced=second.produced,
            hidden=hidden_in,
            mixed=first.mixed,
            query=first.query,
            query_raw=first.query_raw,
            pair=first.pair,
            cosine=cosine,
            sine=sine,
            w_key=key_weight_matrix,
            w_value=value_weight_matrix,
        ),
        dict(
            table=first.table,
            key_raw=first.key_raw,
            log_sum=first.log_sum,
            segments=segments,
            head_gains=head_gains,
            gains=gains,
            moe_gain_part=second.gain_part,
            peaks=first.peaks,
        ),
    )
    own_shape = cotangent.shape
    layer_out = first.after.reshape(own_shape) + done.moe_out.reshape(own_shape)
    input_grad = second.after_grad.reshape(own_shape) + done.normed_out
    gate_grad = second.gate_grad
    w_key_grad, w_value_grad = done.pair_w_out[:, :128], done.pair_w_out[:, 128:]
    w_query_grad, w_out_grad = done.query_w_out, done.out_w_out
    w_gate_grad, w_up_grad, w_down_grad = (
        done.gate_out[None],
        done.up_out[None],
        done.down_out[None],
    )
    small = done.small_out
    attn_gain_grad = small[:16].reshape(2048)
    moe_gain_grad = small[16:32].reshape(2048)
    query_gain_grad, key_gain_grad = small[32], small[33]
    head_clip_scale = clip_limit / jnp.maximum(small[40:, 0], clip_limit)
    return (
        layer_out,
        input_grad,
        attn_gain_grad,
        query_gain_grad,
        key_gain_grad,
        w_query_grad,
        w_key_grad,
        w_value_grad,
        w_out_grad,
        moe_gain_grad,
        gate_grad,
        w_gate_grad,
        w_up_grad,
        w_down_grad,
        head_clip_scale,
    )


def solution(mesh):
    in_specs = (
        P("dp", "context", None),
        P("dp", None),
        P(),
        P(),
        P(),
        P(None, "experts"),
        P(None, "experts"),
        P(None, "experts"),
        P(None, "experts"),
        P(),
        P("dp", ("context", "experts"), None),
        P("dp", ("context", "experts"), None),
        P(),
        P(("dp", "experts"), None, None),
        P(("dp", "experts"), None, None),
        P(("dp", "experts"), None, None),
        P("dp", ("context", "experts"), None),
    )
    out_specs = (
        P("dp", ("context", "experts"), None),
        P("dp", ("context", "experts"), None),
        P(),
        P(),
        P(),
        P(("dp", "context"), "experts"),
        P(("dp", "context"), "experts"),
        P(("dp", "context"), "experts"),
        P(("dp", "context"), "experts"),
        P(),
        P("dp", ("context", "experts"), None),
        P(("dp", "experts"), "context", None),
        P(("dp", "experts"), "context", None),
        P(("dp", "experts"), "context", None),
        P("experts"),
    )
    return jax.shard_map(shards, mesh=mesh, in_specs=in_specs, out_specs=out_specs, check_vma=False)
```

```python
import functools
import itertools
import types

import jax
import jax.numpy as jnp
import numpy as np
from jax import lax
from jax.experimental import pallas as pl
from jax.experimental.pallas import tpu as pltpu
from jax.sharding import PartitionSpec as P

HEAD_SIZE = 128
MESH = pl.DeviceIdType.MESH
VMEM = pl.BlockSpec(memory_space=pltpu.VMEM)
ANY = pl.BlockSpec(memory_space=pl.ANY)
SMEM = pl.BlockSpec(memory_space=pltpu.SMEM)


epsilon = 1e-06
rope_base = 1000000.0
clip_limit = 1.0
masked_value = -1e30


def rotary():
    inverse = 1.0 / rope_base ** (np.arange(0, HEAD_SIZE, 2) / HEAD_SIZE)
    angle = np.arange(1024)[:, None] * inverse[None, :]
    cosine = np.concatenate([np.cos(angle), np.cos(angle)], axis=-1)
    sine = np.concatenate([-np.sin(angle), np.sin(angle)], axis=-1)
    shape = (8, 128, HEAD_SIZE)
    return (
        jnp.asarray(cosine.reshape(shape), jnp.float32),
        jnp.asarray(sine.reshape(shape), jnp.float32),
    )


def contract_last(left, right):
    return lax.dot_general(
        left, right, (((1,), (1,)), ((), ())), preferred_element_type=jnp.float32
    )


def contract_first(left, right):
    return lax.dot_general(
        left, right, (((0,), (0,)), ((), ())), preferred_element_type=jnp.float32
    )


class Place:
    def __init__(self):
        dp = lax.axis_index("dp")
        context = lax.axis_index("context")
        self.dp, self.context, self.y = dp, context, lax.axis_index("experts")
        self.core, self.z_hi = lax.rem(dp, 2), dp // 2
        self.x, self.z_lo = context // 2, lax.rem(context, 2)
        self.z = self.z_hi * 2 + self.z_lo
        self.spot = (self.core, self.z_hi, self.y)

    def at(self, x=None, y=None, z=None, core=None):
        x = self.x if x is None else x
        y = self.y if y is None else y
        z = self.z if z is None else z
        core = self.core if core is None else core
        return (z // 2 * 2 + core, x * 2 + lax.rem(z, 2), y)

    def x_by(self, step):
        return lax.rem(self.x + step, 4)

    def y_by(self, step):
        return lax.rem(self.y + step, 4)

    def z_by(self, step):
        return lax.rem(self.z + step, 4)


class Net:
    def __init__(self, send, recv, here=None):
        self.send, self.recv, self.copies = send, recv, []
        self.here, self.loads = here, 0

    def copy(self, src, dst, device):
        spot = len(self.copies)
        made = pltpu.make_async_remote_copy(
            src_ref=src,
            dst_ref=dst,
            send_sem=self.send.at[spot],
            recv_sem=self.recv.at[spot],
            device_id=device,
            device_id_type=MESH,
        )
        made.start()
        self.copies.append(made)
        return made

    def load(self, src, dst):
        made = pltpu.make_async_copy(src, dst, self.here.at[self.loads])
        self.loads += 1
        made.start()
        return made

    def sent(self, made):
        made.wait_send()
        self.copies = [None if one is made else one for one in self.copies]

    def finish(self):
        for made in self.copies:
            if made is not None:
                made.wait_send()


def greet(devices):
    barrier = pltpu.get_barrier_semaphore()
    for device in devices:
        pl.semaphore_signal(barrier, inc=1, device_id=device, device_id_type=MESH)
    return lambda: pl.semaphore_wait(barrier, len(devices))


def wide(ref):
    values = ref[...].astype(jnp.float32)
    return jnp.concatenate([values[step : step + 1] for step in range(16)], axis=1)


def add_into(target, parts, block=32):
    rows = target.shape[-2]
    block = min(block, rows)
    for lead in itertools.product(*[range(size) for size in target.shape[:-2]]):

        def body(step, carry, lead=lead):
            spot = lead + (pl.ds(pl.multiple_of(step * block, block), block),)
            total = parts[0][spot].astype(jnp.float32)
            for part in parts[1:]:
                total = total + part[spot].astype(jnp.float32)
            target[spot] = total.astype(target.dtype)
            return carry

        lax.fori_loop(0, rows // block, body, 0)


def ring_reduce(net, plus, minus, own, slots, target, held=None, begun=None):
    held = own if held is None else held
    if begun is None:
        first_plus = net.copy(own(2, 0), slots.at[0], plus)
        first_minus = net.copy(own(2, 1), slots.at[2], minus)
        side_plus = net.copy(own(1, 1), slots.at[1], plus)
        side_minus = net.copy(own(3, 0), slots.at[3], minus)
        yield
        first_plus.wait_recv()
        first_minus.wait_recv()
    else:
        load = net.load(begun, slots.at[pl.ds(0, 4)])
        yield
        load.wait()
    add_into(slots.at[0], [slots.at[0], held(1, 0)])
    last_plus = net.copy(slots.at[0], slots.at[4], plus)
    add_into(slots.at[2], [slots.at[2], held(3, 1)])
    last_minus = net.copy(slots.at[2], slots.at[5], minus)
    yield
    if begun is None:
        side_minus.wait_recv()
        side_plus.wait_recv()
    last_plus.wait_recv()
    add_into(target(0), [held(0, 0), slots.at[3], slots.at[4]])
    last_minus.wait_recv()
    add_into(target(1), [held(0, 1), slots.at[1], slots.at[5]])


def x_first(net, me, source, slots, middle, other, out, held=None, begun=None):
    staged = None
    if held is not None:
        order = {(1, 0): 0, (3, 1): 1, (0, 0): 2, (0, 1): 3}
        loads = [
            net.load(source.at[me.x_by(step), half], held.at[spot])
            for (step, half), spot in order.items()
        ]

        def staged(step, half):
            return held.at[order[step, half]]

    ring = ring_reduce(
        net,
        me.at(x=me.x_by(1)),
        me.at(x=me.x_by(3)),
        lambda step, half: source.at[me.x_by(step), half],
        slots,
        lambda half: middle.at[half],
        staged,
        begun,
    )
    next(ring)
    yield
    if held is not None:
        for load in loads:
            load.wait()
    yield from ring
    across = net.copy(middle.at[1 - me.z_lo], other, me.at(z=me.z + 1 - 2 * me.z_lo))
    yield
    across.wait_recv()
    add_into(out, [middle.at[me.z_lo], other])


def core_pair(net, me, sending, other, middle):
    across = net.copy(sending, other, me.at(core=1 - me.core))
    yield
    net.sent(across)
    across.wait_recv()
    add_into(middle, [middle, other])


def dense_x_first(net, me, sending, other, middle, slots, corner, last, out):
    yield from core_pair(net, me, sending, other, middle)
    yield from ring_reduce(
        net,
        me.at(x=me.x_by(1)),
        me.at(x=me.x_by(3)),
        lambda step, half: middle.at[half, me.x_by(step)],
        slots,
        lambda half: corner.at[half],
    )
    half_rows = corner.shape[2] // 2
    yield from ring_reduce(
        net,
        me.at(z=me.z_by(1)),
        me.at(z=me.z_by(3)),
        lambda step, half: corner.at[
            me.z_by(step) // 2, lax.rem(me.z_by(step), 2), pl.ds(half * half_rows, half_rows)
        ],
        last,
        lambda half: out.at[pl.ds(half * half_rows, half_rows)],
    )


def dense_z_first(net, me, sending, other, middle, slots, corner, last, out):
    yield from core_pair(net, me, sending, other, middle)
    yield from ring_reduce(
        net,
        me.at(z=me.z_by(1)),
        me.at(z=me.z_by(3)),
        lambda step, half: middle.at[
            me.z_by(step) // 2, pl.ds(half * 2, 2), lax.rem(me.z_by(step), 2)
        ],
        slots,
        lambda half: corner.at[pl.ds(half * 2, 2)],
    )
    half_rows = corner.shape[1] // 2
    yield from ring_reduce(
        net,
        me.at(x=me.x_by(1)),
        me.at(x=me.x_by(3)),
        lambda step, half: corner.at[me.x_by(step), pl.ds(half * half_rows, half_rows)],
        last,
        lambda half: out.at[pl.ds(half * half_rows, half_rows)],
    )


def all_sum(net, devices, spot, own, slots, most):
    slots[spot] = own[...]
    sent = [net.copy(own, slots.at[spot], device) for device in devices]
    yield
    for made in sent:
        made.wait_recv()
    count = slots.shape[0]
    total = slots[0]
    peak = slots[0, most:]
    for step in range(1, count):
        total = total + slots[step]
        peak = jnp.maximum(peak, slots[step, most:])
    for made in sent:
        net.sent(made)
    own[:most] = total[:most]
    own[most:] = peak


def all_small(net, me, working, by_core, by_x, by_z, by_y, out):
    yield from all_sum(net, [me.at(core=1 - me.core)], me.core, working, by_core, 40)
    yield from all_sum(net, [me.at(x=me.x_by(s)) for s in (1, 2, 3)], me.x, working, by_x, 40)
    yield from all_sum(net, [me.at(z=me.z_by(s)) for s in (1, 2, 3)], me.z, working, by_z, 40)
    out[40:] = working[40:]
    yield from all_sum(net, [me.at(y=me.y_by(s)) for s in (1, 2, 3)], me.y, working, by_y, 40)
    out[:40] = working[:40]


OFFSETS = [(a, b) for a in (2, 0, 3, 1) for b in (0, 1, 3, 2) if a or b]


def peer(me, a, b):
    z = me.z if a < 2 else lax.rem(me.z + 2, 4)
    core = me.core if a % 2 == 0 else 1 - me.core
    y = me.y_by(b)
    return (core, z // 2, y), me.at(z=z, core=core, y=y)


def peers(me):
    return [peer(me, a, b)[1] for a, b in OFFSETS]


def gather_rows(table, home, store):
    def body(step, carry):
        columns = pl.ds(pl.multiple_of(step * 256, 256), 256)
        rows = home[:, :, :, :, columns].reshape(768, 256)
        total = contract_first(table[...], rows)
        store(columns, total[:96])
        return carry

    lax.fori_loop(0, home.shape[4] // 256, body, 0)


def turned(values):
    return pltpu.roll(values, 64, 1)


def column_of(row):
    eye = lax.broadcasted_iota(jnp.int32, (128, 128), 0) == lax.broadcasted_iota(
        jnp.int32, (128, 128), 1
    )
    return jnp.sum(jnp.where(eye, row, 0.0), axis=1, keepdims=True)


def norm_back(gradient, raw, gain):
    inverse = lax.rsqrt(jnp.mean(raw * raw, axis=-1, keepdims=True) + epsilon)
    normal = raw * inverse
    scaled = gradient * gain
    result = inverse * (scaled - normal * jnp.mean(scaled * normal, axis=-1, keepdims=True))
    return result, jnp.sum(gradient * normal, axis=0, keepdims=True)


def back_kernel(names, *refs):
    r = types.SimpleNamespace(**dict(zip(names, refs, strict=True)))
    low, full = jnp.bfloat16, jnp.float32
    score_scale = HEAD_SIZE ** (-0.5)
    me = Place()
    net = Net(r.send, r.recv, r.here)
    fetch = Fetch(net)
    fetch.start("hidden", r.hidden, r.hidden_held)
    greeted = greet(
        [
            me.at(x=me.x_by(1)),
            me.at(x=me.x_by(3)),
            me.at(z=me.z_by(1)),
            me.at(z=me.z_by(3)),
            me.at(x=me.x_by(2)),
        ]
        + peers(me)
    )
    gains = r.gain_rows
    gains[...] = wide(r.attn_gain)
    greeted()

    branch, whole = r.branch, r.whole
    above, below = me.at(y=me.y_by(1)), me.at(y=me.y_by(3))
    to_above = net.copy(branch, whole.at[:, me.y], above)
    to_below = net.copy(branch, whole.at[:, me.y], below)
    own_branch = net.load(branch, whole.at[:, me.y])
    weight = r.weight
    load_out = net.load(r.w_out, weight)
    gate = x_first(
        net, me, r.gate, r.gate_slots, r.gate_middle, r.gate_other, r.gate_out, r.gate_held,
        r.gate_begun,
    )
    up = x_first(net, me, r.up, r.up_slots, r.up_middle, r.up_other, r.up_out, r.up_held)
    down = x_first(
        net, me, r.down, r.down_slots, r.down_middle, r.down_other, r.down_out, r.down_held
    )
    next(gate)
    next(up)
    next(gate)
    fetch.start("pair", r.pair, r.pair_held)
    fetch.start("query", r.query, r.query_held)
    fetch.start("query_raw", r.query_raw, r.query_raw_held)
    fetch.start("cosine", r.cosine.at[me.context], r.cosine_held)
    fetch.start("sine", r.sine.at[me.context], r.sine_held)
    fetch.start("mixed", r.mixed, r.mixed_held)
    fetch.start("w_key", r.w_key, r.key_weight)
    fetch.start("w_value", r.w_value, r.value_weight)

    hidden, inverse = fetch.hidden, r.inverse
    for s in range(3):
        rows = slice(s * 128, s * 128 + 128)
        values = hidden[s].astype(full)
        root = lax.rsqrt(jnp.mean(values * values, axis=-1, keepdims=True) + epsilon)
        inverse[rows, :] = jnp.broadcast_to(root, (128, 128))

    first, second = pl.ds(0, 1024), pl.ds(1024, 1024)
    to_above.wait_recv()
    passed = whole.at[:, me.y_by(3), :, first]
    far_above = net.copy(passed, passed, above)
    to_below.wait_recv()
    passed = whole.at[:, me.y_by(1), :, second]
    far_below = net.copy(passed, passed, below)
    own_branch.wait()
    load_out.wait()
    far_above.wait_recv()
    far_below.wait_recv()

    heads_grad = r.heads_grad

    def heads_step(step, carry):
        columns = pl.ds(pl.multiple_of(step * 256, 256), 256)
        heads_grad[:, columns] = jnp.dot(
            whole[...].reshape(384, 2048), weight[:, columns], preferred_element_type=full
        ).astype(low)
        return carry

    lax.fori_loop(0, 4, heads_step, 0)
    load_query = net.load(r.w_query, weight)

    produced, home, table = r.produced, r.home, r.table
    start = me.core * 384 + me.z_hi * 192 + me.y * 48
    mine = pl.ds(pl.multiple_of(start, 16), 48)
    home_came = []
    for a, b in OFFSETS:
        spot, device = peer(me, a, b)
        home_came.append(net.copy(produced.at[spot], home.at[mine], device))
    home_own = net.load(produced.at[me.spot], home.at[mine])

    query, query_raw, pair = fetch.query, fetch.query_raw, fetch.pair
    cosine, sine, mixed = fetch.cosine, fetch.sine, fetch.mixed
    gain_query, gain_key = r.query_gain[...].astype(full), r.key_gain[...].astype(full)
    bias, key_sum, value_sum = r.bias, r.key_sum, r.value_sum
    pair_grad, gain_part = r.pair_grad, r.gain_part
    gain_part[...] = jnp.zeros((8, 128), full)

    def rope_back(gradient):
        return gradient * cosine[...] - turned(gradient) * sine[...]

    def attend(s):
        here = pl.ds(s * 128, 128)
        bias[...] = mask_bias(me, r.segments, s)
        key_sum[...] = jnp.zeros_like(key_sum)
        value_sum[...] = jnp.zeros_like(value_sum)

        def two_heads(step, carry):
            columns = pl.ds(pl.multiple_of(step * 256, 256), 256)

            def stacked(ref):
                both = ref[here, columns]
                return jnp.concatenate([both[:, :128], both[:, 128:]], axis=0)

            q, d = stacked(query), stacked(heads_grad)
            keys, values = pair[0, s], pair[1, s]
            lines = r.log_sum
            logs = jnp.concatenate(
                [column_of(lines[s * 8 + step * 2]), column_of(lines[s * 8 + step * 2 + 1])], axis=0
            )
            score = contract_last(q, keys) * score_scale
            score = score + jnp.concatenate([bias[...], bias[...]], axis=0)
            prob = jnp.exp(score - logs)
            prob_grad = contract_last(d, values)
            delta = jnp.sum(prob * prob_grad, axis=-1, keepdims=True)
            score_grad = (prob * (prob_grad - delta)).astype(low)
            value_sum[...] += contract_first(prob.astype(low), d)
            key_sum[...] += contract_first(score_grad, q)
            turned_grad = jnp.dot(score_grad, keys, preferred_element_type=full) * score_scale
            for half in range(2):
                run = pl.ds(pl.multiple_of(step * 256 + half * 128, 128), 128)
                grad, part = norm_back(
                    rope_back(turned_grad[half * 128 : half * 128 + 128]),
                    query_raw[here, run],
                    gain_query,
                )
                heads_grad[here, run] = grad.astype(low)
                gain_part[0:1, :] += part
            return carry

        lax.fori_loop(0, 4, two_heads, 0)
        pair_grad[:, :, 0, s] = (key_sum[...] * score_scale).astype(low).reshape(4, 2, 128, 128)
        pair_grad[:, :, 1, s] = value_sum[...].astype(low).reshape(4, 2, 128, 128)

    attend(0)
    attend(1)
    attend(2)
    pairs = x_first(
        net, me, pair_grad, r.pair_slots, r.pair_middle, r.pair_other,
        r.pair_out,
    )
    next(pairs)
    next(gate)

    query_low = heads_grad

    def own_input(columns):
        return hidden[:, :, columns].reshape(384, 256).astype(full)

    def normed(columns):
        return (own_input(columns) * inverse[:, 0:1] * gains[:, columns]).astype(low)

    def whole_part(columns):
        return whole[:, :, :, columns].reshape(384, 256)

    def weigh(core, left, right, target):
        def body(step, carry):
            z_hi, part = step // 2, lax.rem(step, 2)
            columns = pl.ds(pl.multiple_of((z_hi * 2 + core) * 512 + part * 256, 256), 256)
            made = contract_first(left(columns), right[...]).astype(low)
            target[z_hi, pl.ds(part * 2, 2)] = made.reshape(2, 2, 64, right.shape[1])
            return carry

        lax.fori_loop(0, 4, body, 0)

    def dense(order, left, right, sending, other, middle, *more):
        weigh(1 - me.core, left, right, sending)
        task = order(net, me, sending, other, middle, *more)
        next(task)
        weigh(me.core, left, right, middle)
        return task

    out_w = dense(
        dense_z_first, whole_part, mixed, r.sending, r.out_w_other, r.out_w_middle, r.out_w_slots, r.out_w_corner,
        r.out_w_last, r.out_w_out,
    )
    next(pairs)
    next(down)
    next(out_w)
    query_w = dense(
        dense_x_first, normed, query_low, r.sending, r.query_w_other, r.query_w_middle, r.query_w_slots, r.query_w_corner,
        r.query_w_last, r.query_w_out,
    )
    next(pairs)
    next(up)
    next(query_w)

    pair_out, key_raw, pair_low = r.pair_out, r.key_raw, r.pair_low
    next(pairs, None)
    for s in range(3):
        rows = slice(s * 128, s * 128 + 128)
        grad, part = norm_back(rope_back(pair_out[0, s]), key_raw[rows, :], gain_key)
        gain_part[1:2, :] += part
        pair_low[rows, :128] = grad.astype(low)
        pair_low[rows, 128:] = pair_out[1, s].astype(low)

    load_query.wait()
    net.sent(far_above)
    net.sent(far_below)
    w_key, w_value = fetch.w_key, fetch.w_value
    small = r.small
    normed_part = r.normed_part

    def normed_step(step, carry):
        columns = pl.ds(pl.multiple_of(step * 256, 256), 256)
        made = contract_last(query_low[...], weight[columns, :])
        made = made + contract_last(pair_low[:, :128], w_key[columns, :])
        made = made + contract_last(pair_low[:, 128:], w_value[columns, :])
        normal = own_input(columns) * inverse[:, 0:1]
        normed_part[:, columns] = jnp.sum(made * normal, axis=0, keepdims=True)
        whole[:, :, :, columns] = made.astype(low).reshape(3, 4, 32, 256)
        return carry

    lax.fori_loop(0, 8, normed_step, 0)
    normed_out = r.normed_out
    normed_sum = ring_reduce(
        net,
        above,
        below,
        lambda step, half: whole.at[:, me.y_by(step), :, pl.ds(half * 1024, 1024)],
        r.normed_slots,
        lambda half: normed_out.at[:, :, pl.ds(half * 1024, 1024)],
    )
    next(normed_sum)
    for step in range(16):
        run = slice(step * 128, step * 128 + 128)
        small[step : step + 1, :] = normed_part[:, run]
        small[16 + step : 17 + step, :] = r.moe_gain_part[:, run]
    small[32:40, :] = gain_part[...]
    small[40:, :] = r.peaks[...]
    smalls = all_small(
        net, me, small, r.by_core, r.by_x, r.by_z, r.by_y, r.small_out
    )
    next(smalls)
    pair_w = dense(
        dense_x_first, normed, pair_low, r.pair_sending, r.pair_w_other, r.pair_w_middle, r.pair_w_slots, r.pair_w_corner,
        r.pair_w_last, r.pair_w_out,
    )
    next(smalls)

    def rest(*tasks):
        for task in tasks:
            next(task, None)

    rest(out_w, pair_w, smalls, normed_sum, gate, up, down, query_w)

    next(normed_sum, None)
    for s in range(3):
        rows = pl.ds(pl.multiple_of(me.y * 32, 32), 32)
        grad, _ = norm_back(normed_out[s], hidden[s, rows, :].astype(full), gains[...])
        normed_out[s] = grad

    rest(pair_w, smalls, out_w, up, down, query_w)
    rest(pair_w, smalls, out_w, query_w)

    for made in home_came:
        made.wait_recv()
    home_own.wait()
    home_loads = [
        net.load(home.at[:, pl.ds(half * 1024, 1024)], weight.at[pl.ds(half * 768, 768)])
        for half in range(2)
    ]
    rest(pair_w, smalls, out_w, query_w, down)
    moe_out = r.moe_out
    for half in range(2):
        home_loads[half].wait()

        def gather(step, carry, half=half):
            columns = pl.ds(pl.multiple_of(step * 256, 256), 256)
            total = contract_first(table[...], weight[half * 768 : half * 768 + 768, columns])
            moe_out[:, pl.ds(pl.multiple_of(half * 1024 + step * 256, 256), 256)] = total[:96]
            return carry

        lax.fori_loop(0, 4, gather, 0)
    tasks = [pair_w, out_w, smalls, query_w, gate, up, down]
    while tasks:
        for task in list(tasks):
            if next(task, "end") == "end":
                tasks.remove(task)
    net.finish()


def dense_slots(columns, corner):
    low = jnp.bfloat16
    return [
        pltpu.VMEM((2, 4, 2, 64, columns), low),
        pltpu.VMEM((2, 4, 2, 64, columns), low),
        pltpu.VMEM((6, 2, 64, columns), low),
        pltpu.VMEM(corner + (64, columns), low),
        pltpu.VMEM((6, 32, columns), low),
    ]


def back(far, near):
    low, full = jnp.bfloat16, jnp.float32
    outs = dict(
        gate_out=(256, 768),
        up_out=(256, 768),
        down_out=(256, 768),
        query_w_out=(64, 1024),
        pair_w_out=(64, 256),
        out_w_out=(64, 1024),
        small_out=(48, 128),
        normed_out=(3, 32, 2048),
        moe_out=(96, 2048),
    )
    scratch = dict(
        gain_rows=pltpu.VMEM((1, 2048), full),
        hidden_held=pltpu.VMEM((3, 128, 2048), low),
        pair_held=pltpu.VMEM((2, 3, 1024, 128), low),
        query_held=pltpu.VMEM((384, 1024), low),
        query_raw_held=pltpu.VMEM((384, 1024), full),
        cosine_held=pltpu.VMEM((128, 128), full),
        sine_held=pltpu.VMEM((128, 128), full),
        mixed_held=pltpu.VMEM((384, 1024), low),
        key_weight=pltpu.VMEM((2048, 128), low),
        value_weight=pltpu.VMEM((2048, 128), low),
        whole=pltpu.VMEM((3, 4, 32, 2048), low),
        weight=pltpu.VMEM((2048, 1024), low),
        inverse=pltpu.VMEM((384, 128), full),
        heads_grad=pltpu.VMEM((384, 1024), low),
        bias=pltpu.VMEM((128, 1024), full),
        key_sum=pltpu.VMEM((1024, 128), full),
        value_sum=pltpu.VMEM((1024, 128), full),
        pair_grad=pltpu.VMEM((4, 2, 2, 3, 128, 128), low),
        pair_slots=pltpu.VMEM((6, 2, 3, 128, 128), low),
        pair_middle=pltpu.VMEM((2, 2, 3, 128, 128), low),
        pair_other=pltpu.VMEM((2, 3, 128, 128), low),
        pair_out=pltpu.VMEM((2, 3, 128, 128), full),
        pair_low=pltpu.VMEM((384, 256), low),
        gain_part=pltpu.VMEM((8, 128), full),
        normed_part=pltpu.VMEM((1, 2048), full),
        normed_slots=pltpu.VMEM((6, 3, 32, 1024), low),
        small=pltpu.VMEM((48, 128), full),
        by_core=pltpu.VMEM((2, 48, 128), full),
        by_x=pltpu.VMEM((4, 48, 128), full),
        by_z=pltpu.VMEM((4, 48, 128), full),
        by_y=pltpu.VMEM((4, 48, 128), full),
        down_slots=pltpu.VMEM((6, 256, 768), low),
        down_middle=pltpu.VMEM((2, 256, 768), low),
        down_other=pltpu.VMEM((256, 768), low),
        down_held=pltpu.VMEM((4, 256, 768), low),
        gate_slots=pltpu.VMEM((6, 256, 768), low),
        gate_middle=pltpu.VMEM((2, 256, 768), low),
        gate_other=pltpu.VMEM((256, 768), low),
        gate_held=pltpu.VMEM((4, 256, 768), low),
        up_slots=pltpu.VMEM((6, 256, 768), low),
        up_middle=pltpu.VMEM((2, 256, 768), low),
        up_other=pltpu.VMEM((256, 768), low),
        up_held=pltpu.VMEM((4, 256, 768), low),
        sending=pltpu.VMEM((2, 4, 2, 64, 1024), low),
        pair_sending=pltpu.VMEM((2, 4, 2, 64, 256), low),
        query_w_other=None,
        query_w_middle=None,
        query_w_slots=None,
        query_w_corner=None,
        query_w_last=None,
        pair_w_other=None,
        pair_w_middle=None,
        pair_w_slots=None,
        pair_w_corner=None,
        pair_w_last=None,
        out_w_other=None,
        out_w_middle=None,
        out_w_slots=None,
        out_w_corner=None,
        out_w_last=None,
        send=pltpu.SemaphoreType.DMA((104,)),
        recv=pltpu.SemaphoreType.DMA((104,)),
        here=pltpu.SemaphoreType.DMA((34,)),
    )
    dense = dense_slots(1024, (2, 2)) + dense_slots(256, (2, 2)) + dense_slots(1024, (4,))
    scratch = {name: one or dense.pop(0) for name, one in scratch.items()}
    outs = {name: jax.ShapeDtypeStruct(size, full) for name, size in outs.items()}
    far_outs = dict(home=jax.ShapeDtypeStruct((768, 2048), low))
    return call(back_kernel, 0, far, near, outs, far_outs, scratch)


class Fetch:
    def __init__(self, net):
        self.net, self.waiting, self.held = net, {}, {}

    def start(self, name, source, target):
        self.waiting[name] = self.net.load(source, target)
        self.held[name] = target

    def __getattr__(self, name):
        if name in self.waiting:
            self.waiting.pop(name).wait()
        return self.held[name]


def token_table(ids, gates, capacity, table, info):
    low, full = jnp.bfloat16, jnp.float32
    expert = lax.broadcasted_iota(jnp.int32, (16, 32), 0)
    chosen, share = [], []
    for s in range(3):
        chosen_here = jnp.zeros((16, 32), full)
        share_here = jnp.zeros((16, 32), full)
        for k in range(8):
            named = ids[s, k : k + 1, :] == expert
            chosen_here = chosen_here + jnp.where(named, 1.0, 0.0)
            share_here = share_here + jnp.where(named, gates[s, k : k + 1, :], 0.0)
        chosen.append(chosen_here)
        share.append(share_here)
    none = jnp.zeros((16, 32), full)
    chosen = jnp.concatenate(chosen + [none], axis=1)
    share = jnp.concatenate(share + [none], axis=1)
    row = lax.broadcasted_iota(jnp.int32, (16, 128), 0)
    limit = jnp.zeros((16, 128), full)
    for e in range(16):
        limit = jnp.where(row == e, capacity[e].astype(full), limit)
    earlier = lax.broadcasted_iota(jnp.int32, (128, 128), 0) < lax.broadcasted_iota(
        jnp.int32, (128, 128), 1
    )
    before = jnp.dot(
        chosen.astype(low), jnp.where(earlier, 1.0, 0.0).astype(low), preferred_element_type=full
    )
    slot = jnp.where((chosen > 0.0) & (before < limit), before, -1.0)
    spot = lax.broadcasted_iota(jnp.int32, (48, 128), 0).astype(full)
    for place in range(16):
        core, z_hi, y = place // 8, place // 4 % 2, place % 4
        e = (z_hi * 2 + core) * 4 + y
        mask = jnp.where(slot[e : e + 1, :] == spot, 1.0, 0.0)
        table[place * 48 : place * 48 + 48, :] = mask.astype(low)
        info[core, z_hi, y] = jnp.concatenate(
            [slot[e : e + 1, :], share[e : e + 1, :], jnp.zeros((6, 128), full)], axis=0
        )


def dispatch(table, rows, sender, core):
    rest = table[pl.ds(pl.multiple_of(core * 384, 384), 384), :]
    columns = 512
    for step in range(2048 // columns):
        run = slice(step * columns, (step + 1) * columns)
        picked = jnp.dot(rest, rows[:, run], preferred_element_type=jnp.float32)
        sender[core, :, :, :, run] = picked.astype(jnp.bfloat16).reshape(2, 4, 48, columns)


def moe_kernel(names, *refs):
    r = types.SimpleNamespace(**dict(zip(names, refs, strict=True)))
    low, full = jnp.bfloat16, jnp.float32
    me = Place()
    net = Net(r.send, r.recv, r.here)
    fetch = Fetch(net)
    fetch.start("w_gate", r.w_gate, r.gate_weight)
    fetch.start("w_up", r.w_up, r.up_weight)
    fetch.start("raw", r.grads, r.raw_held)
    fetch.start("w_down", r.w_down, r.down_weight)
    greeted = greet(peers(me) + [me.at(x=me.x_by(1)), me.at(x=me.x_by(3))])
    rows, sending, local, table = r.rows, r.sending, r.local, r.table
    values = r.after[...]
    inverse = lax.rsqrt(jnp.mean(values * values, axis=-1, keepdims=True) + epsilon)
    gain = wide(r.moe_gain)
    rows[96:, :] = jnp.zeros((32, 2048), low)
    rows[:96, :] = (values * inverse * gain).astype(low)
    came = {}

    def set_out(first, second):
        for a, b in OFFSETS:
            if a in (first, second):
                spot, device = peer(me, a, b)
                came[a, b] = net.copy(sending.at[spot], local.at[me.spot], device)

    dispatch(table, rows, sending, me.core)
    greeted()
    set_out(0, 2)
    local[me.spot] = sending[me.spot]
    dispatch(table, rows, sending, 1 - me.core)

    act, gate_back, up_back, back, home = r.act, r.gate_back, r.up_back, r.back, r.home
    w_gate, w_up, grads, w_down = fetch.w_gate, fetch.w_up, r.grads_held, fetch.w_down
    fetch.raw
    spot = lax.broadcasted_iota(jnp.int32, (48, 128), 0).astype(full)
    back_came, dots_came = {}, {}
    for first in (0, 1):
        group = me.core if first == 0 else 1 - me.core
        for a in (first, first + 2):
            for b in (1, 3, 2, 0):
                if a or b:
                    came[a, b].wait_recv()
            if a == 0:
                set_out(1, 3)
        masks, shares = [], []
        for z_hi in range(2):
            for y in range(4):
                mask = r.info_in[group, z_hi, y, 0:1, :] == spot
                share = jnp.where(mask, r.info_in[group, z_hi, y, 1:2, :], 0.0)
                masks.append(mask)
                shares.append(jnp.sum(share, axis=1, keepdims=True))
        shared = jnp.concatenate(shares, axis=0)

        def inner(step, carry, group=group, shared=shared):
            columns = pl.ds(pl.multiple_of(step * 256, 256), 256)
            entered = local[group].reshape(384, 2048)
            gate_pre = jnp.dot(entered, w_gate[:, columns], preferred_element_type=full)
            up_pre = jnp.dot(entered, w_up[:, columns], preferred_element_type=full)
            act_back = jnp.dot(
                grads[group].reshape(384, 2048), w_down[:, columns], preferred_element_type=full
            )
            sigmoid = 1.0 / (1.0 + jnp.exp(-gate_pre))
            silu = gate_pre * sigmoid
            act[group, :, columns] = (silu * up_pre).astype(low)
            gate_back[group, :, columns] = (
                act_back * up_pre * sigmoid * (1.0 + gate_pre * (1.0 - sigmoid))
            ).astype(low)
            up_back[group, :, columns] = (act_back * silu).astype(low)
            return carry

        def outer(step, dot, group=group, shared=shared):
            columns = pl.ds(pl.multiple_of(step * 256, 256), 256)
            row_back = contract_last(gate_back[group], w_gate[columns, :]) + contract_last(
                up_back[group], w_up[columns, :]
            )
            back[group, :, :, :, columns] = row_back.astype(low).reshape(2, 4, 48, 256)
            return dot

        def finals(step, dot, group=group, shared=shared):
            columns = pl.ds(pl.multiple_of(step * 256, 256), 256)
            made = contract_last(act[group], w_down[columns, :]).astype(low).astype(full)
            r.produced_held[group, :, :, :, columns] = (
                (made * shared).astype(low).reshape(2, 4, 48, 256)
            )
            incoming = r.raw_held[group, :, :, :, columns].reshape(384, 256).astype(full)
            return dot + jnp.sum(made * incoming, axis=1, keepdims=True)

        def scale(step, carry, group=group, shared=shared):
            columns = pl.ds(pl.multiple_of(step * 256, 256), 256)
            incoming = r.raw_held[group, :, :, :, columns].reshape(384, 256).astype(full)
            grads[group, :, :, :, columns] = (
                (incoming * shared).astype(low).reshape(2, 4, 48, 256)
            )
            return carry

        lax.fori_loop(0, 8, scale, 0)
        lax.fori_loop(0, 3, inner, 0)
        lax.fori_loop(0, 8, outer, 0)
        for a in (first + 2, first):
            for b in (0, 1, 3, 2):
                if a or b:
                    place, device = peer(me, a, b)
                    back_came[a, b] = net.copy(back.at[place], home.at[me.spot], device)
        dot = lax.fori_loop(0, 8, finals, jnp.zeros((384, 1), full))
        for place in range(8):
            line = jnp.where(masks[place], dot[place * 48 : place * 48 + 48], 0.0)
            line = jnp.sum(line, axis=0, keepdims=True)
            r.dots[group, place // 4, place % 4] = jnp.broadcast_to(line, (8, 128))
        for a in (first + 2, first):
            for b in (0, 1, 3, 2):
                if a or b:
                    place, device = peer(me, a, b)
                    dots_came[a, b] = net.copy(r.dots.at[place], r.dots_in.at[me.spot], device)
    home[me.spot] = back[me.spot]
    r.dots_in[me.spot] = r.dots[me.spot]
    written = [net.load(r.produced_held, r.produced)]

    def weigh(left, right, target):
        def body(step, carry):
            columns = pl.ds(pl.multiple_of(step * 256, 256), 256)
            entered = left[:, :, :, :, columns].reshape(768, 256)
            target[columns, :] = contract_first(entered, right[...].reshape(768, 768)).astype(low)
            return carry

        lax.fori_loop(0, 8, body, 0)

    def chunk(step, half):
        start = (me.x_by(step) * 2 + half) * 256
        return r.gate_held.at[pl.ds(pl.multiple_of(start, 256), 256)]

    weigh(local, gate_back, r.gate_held)
    right, left = me.at(x=me.x_by(1)), me.at(x=me.x_by(3))
    round_x = [
        net.copy(chunk(2, 0), r.gate_slots.at[0], right),
        net.copy(chunk(2, 1), r.gate_slots.at[2], left),
        net.copy(chunk(1, 1), r.gate_slots.at[1], right),
        net.copy(chunk(3, 0), r.gate_slots.at[3], left),
    ]
    written.append(net.load(r.gate_held, r.full_gate))
    weigh(local, up_back, r.up_held)
    written.append(net.load(r.up_held, r.full_up))
    weigh(grads, act, r.down_held)
    written.append(net.load(r.down_held, r.full_down))

    for offset in OFFSETS:
        dots_came[offset].wait_recv()
    lines = [r.dots_in[e // 4 % 2, e // 8, e % 4, 0:1, :] for e in range(16)]
    lines = jnp.concatenate(lines, axis=0)
    expert = lax.broadcasted_iota(jnp.int32, (16, 32), 0)
    for s in range(3):
        dots = lines[:, s * 32 : s * 32 + 32]
        for k in range(8):
            named = r.ids[s, k : k + 1, :] == expert
            r.gate_grad[s, k : k + 1, :] = jnp.sum(
                jnp.where(named, dots, 0.0), axis=0, keepdims=True
            )

    for offset in OFFSETS:
        back_came[offset].wait_recv()
    after_grad = r.after_grad

    def keep(columns, total):
        after_grad[:, columns] = total

    gather_rows(table, home, keep)
    gradient = after_grad[...]
    moe_part, gain_part = norm_back(gradient, r.after[...], gain)
    r.gain_part[...] = gain_part
    result = r.cotangent[...].reshape(96, 2048).astype(full) + moe_part
    after_grad[...] = result
    r.branch[...] = result.astype(low).reshape(3, 32, 2048)
    for one in written:
        one.wait()
    for one in round_x:
        one.wait_recv()
    net.finish()


def moe(far, near):
    low, full = jnp.bfloat16, jnp.float32
    rows = (2, 2, 4, 48, 2048)
    outs = dict(
        after_grad=jax.ShapeDtypeStruct((96, 2048), full),
        branch=jax.ShapeDtypeStruct((3, 32, 2048), low),
        gain_part=jax.ShapeDtypeStruct((1, 2048), full),
        gate_grad=jax.ShapeDtypeStruct((3, 8, 32), full),
    )
    far_outs = dict(
        produced=jax.ShapeDtypeStruct(rows, low),
        full_gate=jax.ShapeDtypeStruct((2048, 768), low),
        full_up=jax.ShapeDtypeStruct((2048, 768), low),
        full_down=jax.ShapeDtypeStruct((2048, 768), low),
        gate_slots=jax.ShapeDtypeStruct((4, 256, 768), low),
    )
    scratch = dict(
        rows=pltpu.VMEM((128, 2048), low),
        sending=pltpu.VMEM(rows, low),
        local=pltpu.VMEM(rows, low),
        raw_held=pltpu.VMEM(rows, low),
        grads_held=pltpu.VMEM(rows, low),
        produced_held=pltpu.VMEM(rows, low),
        back=pltpu.VMEM(rows, low),
        home=pltpu.VMEM(rows, low),
        gate_weight=pltpu.VMEM((2048, 768), low),
        up_weight=pltpu.VMEM((2048, 768), low),
        down_weight=pltpu.VMEM((2048, 768), low),
        gate_held=pltpu.VMEM((2048, 768), low),
        up_held=pltpu.VMEM((2048, 768), low),
        down_held=pltpu.VMEM((2048, 768), low),
        act=pltpu.VMEM((2, 384, 768), low),
        gate_back=pltpu.VMEM((2, 384, 768), low),
        up_back=pltpu.VMEM((2, 384, 768), low),
        dots=pltpu.VMEM((2, 2, 4, 8, 128), full),
        dots_in=pltpu.VMEM((2, 2, 4, 8, 128), full),
        send=pltpu.SemaphoreType.DMA((49,)),
        recv=pltpu.SemaphoreType.DMA((49,)),
        here=pltpu.SemaphoreType.DMA((8,)),
    )
    return call(moe_kernel, 1, far, near, outs, far_outs, scratch)


def call(kernel, number, far, near, outs, far_outs, scratch):
    names = list(far) + list(near) + list(outs) + list(far_outs) + list(scratch)
    shapes = {**outs, **far_outs}
    results = pl.pallas_call(
        functools.partial(kernel, names),
        out_shape=list(shapes.values()),
        in_specs=[ANY] * len(far)
        + [SMEM if one.ndim == 1 else VMEM for one in near.values()],
        out_specs=[VMEM] * len(outs) + [ANY] * len(far_outs),
        scratch_shapes=list(scratch.values()),
        compiler_params=pltpu.CompilerParams(
            collective_id=number, has_side_effects=True, vmem_limit_bytes=62 << 20
        ),
        name=kernel.__name__,
    )(*far.values(), *near.values())
    return types.SimpleNamespace(**dict(zip(shapes, results, strict=True)))


def front_kernel(names, *refs):
    r = types.SimpleNamespace(**dict(zip(names, refs, strict=True)))
    low, full = jnp.bfloat16, jnp.float32
    score_scale = HEAD_SIZE ** (-0.5)
    me = Place()
    net = Net(r.send, r.recv, r.here)
    fetch = Fetch(net)
    fetch.start("hidden", r.hidden, r.hidden_held)
    fetch.start("w_pair", r.w_key, r.key_weight)
    fetch.start("w_value", r.w_value, r.value_weight)
    fetch.start("cosine", r.cosine.at[me.context], r.cosine_held)
    fetch.start("sine", r.sine.at[me.context], r.sine_held)
    fetch.start("w_query", r.w_query, r.query_weight)
    fetch.start("cotangent", r.cotangent, r.cotangent_held)
    fetch.start("w_out", r.w_out, r.out_weight)
    beside = me.at(z=me.z + 1 - 2 * me.z_lo)
    right, left = me.at(x=me.x_by(1)), me.at(x=me.x_by(3))
    greeted = greet([right, left, beside] + peers(me))
    gains = r.gain_rows
    gains[...] = wide(r.attn_gain)

    token_table(r.ids, r.gates, r.capacity, r.table, r.info)
    rows = r.rows
    rows[96:, :] = jnp.zeros((32, 2048), low)
    rows[:96, :] = fetch.cotangent[...].reshape(96, 2048)
    for core in range(2):
        dispatch(r.table, rows, r.sending, core)
    greeted()
    arrivals = []

    def set_out(first, second):
        for a, b in OFFSETS:
            if a in (first, second):
                spot, device = peer(me, a, b)
                arrivals.append(net.copy(r.info.at[spot], r.info_in.at[me.spot], device))
                arrivals.append(net.copy(r.sending.at[spot], r.grads.at[me.spot], device))

    set_out(0, 1)
    r.info_in[me.spot] = r.info[me.spot]
    own_grads = net.load(r.sending.at[me.spot], r.grads.at[me.spot])

    hidden, normed = fetch.hidden, r.normed
    for s in range(3):
        values = hidden[s].astype(full)
        root = lax.rsqrt(jnp.mean(values * values, axis=-1, keepdims=True) + epsilon)
        normed[s * 128 : s * 128 + 128, :] = (values * root * gains[...]).astype(low)

    def rope(values):
        cosine = jnp.concatenate([fetch.cosine[...]] * 3, axis=0)
        sine = jnp.concatenate([fetch.sine[...]] * 3, axis=0)
        return values * cosine + turned(values) * sine

    def head_norm(raw, gain):
        return raw * lax.rsqrt(jnp.mean(raw * raw, axis=-1, keepdims=True) + epsilon) * gain

    pair, key_raw = r.pair_held, r.key_raw
    made = jnp.dot(normed[...], fetch.w_pair[...], preferred_element_type=full)
    key_raw[...] = made
    keys = rope(head_norm(made, r.key_gain[...].astype(full))).astype(low)
    values = jnp.dot(normed[...], fetch.w_value[...], preferred_element_type=full).astype(low)
    own = pl.ds(pl.multiple_of(me.context * 128, 128), 128)
    pair[0, :, own, :] = keys.reshape(3, 128, 128)
    pair[1, :, own, :] = values.reshape(3, 128, 128)

    def block(x, z_lo):
        return pl.ds(pl.multiple_of((x * 2 + z_lo) * 128, 128), 128)

    def piece(x, z_lo, half=None):
        rows = block(x, z_lo)
        return pair.at[:, :, rows, :] if half is None else pair.at[half, :, rows, :]

    def pass_on(view, device):
        return net.copy(view, view, device)

    own_z, other_z = me.z_lo, 1 - me.z_lo
    from_z = pass_on(piece(me.x, own_z), beside)
    from_left = [pass_on(piece(me.x, own_z), right)]
    from_right = [pass_on(piece(me.x, own_z), left)]

    set_out(2, 3)

    w_query, query, query_raw = fetch.w_query, r.query_held, r.query_raw_held

    def project(step, carry):
        columns = pl.ds(pl.multiple_of(step * 256, 256), 256)
        made = jnp.dot(normed[...], w_query[:, columns], preferred_element_type=full)
        query_raw[:, columns] = made
        for half in range(2):
            run = pl.ds(pl.multiple_of(step * 256 + half * 128, 128), 128)
            one = head_norm(made[:, half * 128 : half * 128 + 128], r.query_gain[...].astype(full))
            query[:, run] = rope(one).astype(low)
        return carry

    lax.fori_loop(0, 4, project, 0)
    written = [net.load(query, r.query), net.load(query_raw, r.query_raw)]
    from_z.wait_recv()
    from_left.append(pass_on(piece(me.x, other_z), right))
    from_right.append(pass_on(piece(me.x, other_z), left))
    far = [[], []]
    for spot, zs in enumerate((own_z, other_z)):
        from_left[spot].wait_recv()
        far[0].append(pass_on(piece(me.x_by(3), zs, 0), right))
        from_right[spot].wait_recv()
        far[1].append(pass_on(piece(me.x_by(1), zs, 1), left))
    for one in far[0] + far[1]:
        one.wait_recv()
    written.append(net.load(pair, r.pair))

    bias, peaks, mixed = r.bias, r.peak_rows, r.mixed_held
    peaks[...] = jnp.full((8, 1, 128), -jnp.inf, full)
    for s in range(3):
        here = pl.ds(s * 128, 128)
        bias[...] = mask_bias(me, r.segments, s)

        def two_heads(step, carry, s=s, here=here):
            columns = pl.ds(pl.multiple_of(step * 256, 256), 256)
            both = query[here, columns]
            q = jnp.concatenate([both[:, :128], both[:, 128:]], axis=0)
            score = contract_last(q, pair[0, s]) * score_scale
            score = score + jnp.concatenate([bias[...], bias[...]], axis=0)
            highest = jnp.max(score, axis=-1, keepdims=True)
            weight = jnp.exp(score - highest)
            total = jnp.sum(weight, axis=-1, keepdims=True)
            prob = (weight * (1.0 / total)).astype(low)
            logs = highest + jnp.log(total)
            heads = jnp.dot(prob, pair[1, s], preferred_element_type=full).astype(low)
            for half in range(2):
                part = slice(half * 128, half * 128 + 128)
                head = step * 2 + half
                run = pl.ds(pl.multiple_of(step * 256 + half * 128, 128), 128)
                mixed[here, run] = heads[part]
                r.log_sum[s * 8 + head] = row_of(logs[part])
                top = jnp.max(highest[part], axis=0, keepdims=True)
                peaks[head] = jnp.maximum(peaks[head], top)
            return carry

        lax.fori_loop(0, 4, two_heads, 0)
    for head in range(8):
        r.peaks[head : head + 1, :] = peaks[head]
    written.append(net.load(mixed, r.mixed))

    w_out, shares = fetch.w_out, r.shares

    def branch_step(step, carry):
        columns = pl.ds(pl.multiple_of(step * 256, 256), 256)
        made = contract_last(mixed[...], w_out[columns, :])
        shares[:, :, :, columns] = made.astype(low).reshape(3, 4, 32, 256)
        return carry

    lax.fori_loop(0, 8, branch_step, 0)
    after = r.after_sum
    ring = ring_reduce(
        net,
        me.at(y=me.y_by(1)),
        me.at(y=me.y_by(3)),
        lambda step, half: shares.at[:, me.y_by(step), :, pl.ds(half * 1024, 1024)],
        r.branch_slots,
        lambda half: after.at[:, :, pl.ds(half * 1024, 1024)],
    )
    for _ in ring:
        pass
    own_rows = pl.ds(pl.multiple_of(me.y * 32, 32), 32)
    for s in range(3):
        r.after[s * 32 : s * 32 + 32, :] = after[s] + hidden[s, own_rows, :].astype(full)
    for one in arrivals:
        one.wait_recv()
    own_grads.wait()
    for one in written:
        one.wait()
    net.finish()


def row_of(column):
    eye = lax.broadcasted_iota(jnp.int32, (128, 128), 0) == lax.broadcasted_iota(
        jnp.int32, (128, 128), 1
    )
    return jnp.sum(jnp.where(eye, column, 0.0), axis=0, keepdims=True)


def mask_bias(me, segments, s):
    spot = me.context * 128 + lax.broadcasted_iota(jnp.int32, (128, 1024), 0)
    own = segments[s : s + 1, pl.ds(pl.multiple_of(me.context * 128, 128), 128)]
    document = column_of(own.astype(jnp.float32))
    allowed = (document == segments[s : s + 1, :].astype(jnp.float32)) & (
        lax.broadcasted_iota(jnp.int32, (128, 1024), 1) <= spot
    )
    return jnp.where(allowed, 0.0, masked_value)


def front(far, near):
    low, full = jnp.bfloat16, jnp.float32
    rows = (2, 2, 4, 48, 2048)
    outs = dict(
        key_raw=jax.ShapeDtypeStruct((384, 128), full),
        log_sum=jax.ShapeDtypeStruct((24, 1, 128), full),
        peaks=jax.ShapeDtypeStruct((8, 128), full),
        after=jax.ShapeDtypeStruct((96, 2048), full),
        table=jax.ShapeDtypeStruct((768, 128), low),
        info_in=jax.ShapeDtypeStruct((2, 2, 4, 8, 128), full),
    )
    far_outs = dict(
        query=jax.ShapeDtypeStruct((384, 1024), low),
        query_raw=jax.ShapeDtypeStruct((384, 1024), full),
        pair=jax.ShapeDtypeStruct((2, 3, 1024, 128), low),
        mixed=jax.ShapeDtypeStruct((384, 1024), low),
        grads=jax.ShapeDtypeStruct(rows, low),
    )
    scratch = dict(
        gain_rows=pltpu.VMEM((1, 2048), full),
        hidden_held=pltpu.VMEM((3, 128, 2048), low),
        key_weight=pltpu.VMEM((2048, 128), low),
        value_weight=pltpu.VMEM((2048, 128), low),
        cosine_held=pltpu.VMEM((128, 128), full),
        sine_held=pltpu.VMEM((128, 128), full),
        query_weight=pltpu.VMEM((2048, 1024), low),
        cotangent_held=pltpu.VMEM((3, 32, 2048), low),
        out_weight=pltpu.VMEM((2048, 1024), low),
        normed=pltpu.VMEM((384, 2048), low),
        pair_held=pltpu.VMEM((2, 3, 1024, 128), low),
        info=pltpu.VMEM((2, 2, 4, 8, 128), full),
        rows=pltpu.VMEM((128, 2048), low),
        sending=pltpu.VMEM(rows, low),
        query_held=pltpu.VMEM((384, 1024), low),
        query_raw_held=pltpu.VMEM((384, 1024), full),
        bias=pltpu.VMEM((128, 1024), full),
        peak_rows=pltpu.VMEM((8, 1, 128), full),
        mixed_held=pltpu.VMEM((384, 1024), low),
        shares=pltpu.VMEM((3, 4, 32, 2048), low),
        branch_slots=pltpu.VMEM((6, 3, 32, 1024), low),
        after_sum=pltpu.VMEM((3, 32, 2048), full),
        send=pltpu.SemaphoreType.DMA((46,)),
        recv=pltpu.SemaphoreType.DMA((46,)),
        here=pltpu.SemaphoreType.DMA((16,)),
    )
    return call(front_kernel, 2, far, near, outs, far_outs, scratch)


def finish_kernel(names, *refs):
    r = types.SimpleNamespace(**dict(zip(names, refs, strict=True)))
    r.layer_out[...] = r.after[...] + r.moe_out[...]
    r.input_grad[...] = r.after_grad[...] + r.normed_out[...].reshape(96, 2048)
    r.gate_w[...] = r.gate_part[...]
    r.up_w[...] = r.up_part[...]
    r.down_w[...] = r.down_part[...]
    r.query_w[...] = r.query_part[...]
    r.out_w[...] = r.out_part[...]
    r.gate_grad[...] = r.gate_grad_part[...]
    r.key_w[...] = r.pair_w[:, :128]
    r.value_w[...] = r.pair_w[:, 128:]
    r.attn_gain[...] = r.small[:16]
    r.moe_gain[...] = r.small[16:32]
    r.query_gain[...] = r.small[32:33]
    r.key_gain[...] = r.small[33:34]
    diagonal = lax.broadcasted_iota(jnp.int32, (8, 128), 0) == lax.broadcasted_iota(
        jnp.int32, (8, 128), 1
    )
    peaks = jnp.sum(jnp.where(diagonal, r.small[40:], 0.0), axis=0, keepdims=True)
    r.clip[...] = (clip_limit / jnp.maximum(peaks, clip_limit))[:, :8]


def finish(near):
    outs = dict(
        layer_out=(96, 2048),
        input_grad=(96, 2048),
        gate_w=(256, 768),
        up_w=(256, 768),
        down_w=(256, 768),
        query_w=(64, 1024),
        out_w=(64, 1024),
        gate_grad=(3, 8, 32),
        key_w=(64, 128),
        value_w=(64, 128),
        attn_gain=(16, 128),
        moe_gain=(16, 128),
        query_gain=(1, 128),
        key_gain=(1, 128),
        clip=(1, 8),
    )
    results = pl.pallas_call(
        functools.partial(finish_kernel, list(near) + list(outs)),
        out_shape=[jax.ShapeDtypeStruct(size, jnp.float32) for size in outs.values()],
        in_specs=[VMEM] * len(near),
        out_specs=[VMEM] * len(outs),
        compiler_params=pltpu.CompilerParams(vmem_limit_bytes=62 << 20),
        name="finish",
    )(*near.values())
    return types.SimpleNamespace(**dict(zip(outs, results, strict=True)))


def shards(
    hidden_in,
    segments,
    attn_gain,
    query_gain,
    key_gain,
    w_query,
    key_weight_matrix,
    value_weight_matrix,
    w_out,
    moe_gain,
    expert_ids,
    gate_values,
    capacity,
    w_gate,
    w_up,
    w_down,
    cotangent,
):
    attn_wide, moe_wide = attn_gain.reshape(16, 128), moe_gain.reshape(16, 128)
    query_row, key_row = query_gain[None], key_gain[None]
    ids, gates = expert_ids.swapaxes(1, 2), gate_values.swapaxes(1, 2)
    cosine, sine = rotary()
    first = front(
        dict(
            hidden=hidden_in,
            w_key=key_weight_matrix,
            w_value=value_weight_matrix,
            cosine=cosine,
            sine=sine,
            w_query=w_query,
            cotangent=cotangent,
            w_out=w_out,
        ),
        dict(
            attn_gain=attn_wide,
            query_gain=query_row,
            key_gain=key_row,
            segments=segments,
            ids=ids,
            gates=gates,
            capacity=capacity,
        ),
    )
    second = moe(
        dict(w_gate=w_gate[0], w_up=w_up[0], w_down=w_down[0], grads=first.grads),
        dict(
            after=first.after,
            cotangent=cotangent,
            moe_gain=moe_wide,
            ids=ids,
            table=first.table,
            info_in=first.info_in,
        ),
    )
    done = back(
        dict(
            branch=second.branch,
            w_out=w_out,
            w_query=w_query,
            gate=second.full_gate.reshape(4, 2, 256, 768),
            up=second.full_up.reshape(4, 2, 256, 768),
            down=second.full_down.reshape(4, 2, 256, 768),
            produced=second.produced,
            gate_begun=second.gate_slots,
            hidden=hidden_in,
            mixed=first.mixed,
            query=first.query,
            query_raw=first.query_raw,
            pair=first.pair,
            cosine=cosine,
            sine=sine,
            w_key=key_weight_matrix,
            w_value=value_weight_matrix,
        ),
        dict(
            table=first.table,
            key_raw=first.key_raw,
            log_sum=first.log_sum,
            segments=segments,
            attn_gain=attn_wide,
            query_gain=query_row,
            key_gain=key_row,
            moe_gain_part=second.gain_part,
            peaks=first.peaks,
        ),
    )
    last = finish(
        dict(
            after=first.after,
            moe_out=done.moe_out,
            after_grad=second.after_grad,
            normed_out=done.normed_out,
            small=done.small_out,
            pair_w=done.pair_w_out,
            gate_part=done.gate_out,
            up_part=done.up_out,
            down_part=done.down_out,
            query_part=done.query_w_out,
            out_part=done.out_w_out,
            gate_grad_part=second.gate_grad,
        )
    )
    layer_out = last.layer_out.reshape(cotangent.shape)
    input_grad = last.input_grad.reshape(cotangent.shape)
    gate_grad = last.gate_grad.swapaxes(1, 2)
    w_key_grad, w_value_grad = last.key_w, last.value_w
    w_query_grad, w_out_grad = last.query_w, last.out_w
    w_gate_grad, w_up_grad, w_down_grad = last.gate_w[None], last.up_w[None], last.down_w[None]
    attn_gain_grad, moe_gain_grad = last.attn_gain.reshape(2048), last.moe_gain.reshape(2048)
    query_gain_grad, key_gain_grad = last.query_gain.reshape(128), last.key_gain.reshape(128)
    head_clip_scale = last.clip.reshape(8)
    return (
        layer_out,
        input_grad,
        attn_gain_grad,
        query_gain_grad,
        key_gain_grad,
        w_query_grad,
        w_key_grad,
        w_value_grad,
        w_out_grad,
        moe_gain_grad,
        gate_grad,
        w_gate_grad,
        w_up_grad,
        w_down_grad,
        head_clip_scale,
    )


def solution(mesh):
    in_specs = (
        P("dp", "context", None),
        P("dp", None),
        P(),
        P(),
        P(),
        P(None, "experts"),
        P(None, "experts"),
        P(None, "experts"),
        P(None, "experts"),
        P(),
        P("dp", ("context", "experts"), None),
        P("dp", ("context", "experts"), None),
        P(),
        P(("dp", "experts"), None, None),
        P(("dp", "experts"), None, None),
        P(("dp", "experts"), None, None),
        P("dp", ("context", "experts"), None),
    )
    out_specs = (
        P("dp", ("context", "experts"), None),
        P("dp", ("context", "experts"), None),
        P(),
        P(),
        P(),
        P(("dp", "context"), "experts"),
        P(("dp", "context"), "experts"),
        P(("dp", "context"), "experts"),
        P(("dp", "context"), "experts"),
        P(),
        P("dp", ("context", "experts"), None),
        P(("dp", "experts"), "context", None),
        P(("dp", "experts"), "context", None),
        P(("dp", "experts"), "context", None),
        P("experts"),
    )
    return jax.shard_map(shards, mesh=mesh, in_specs=in_specs, out_specs=out_specs, check_vma=False)
```

```python
import functools
import itertools
import types

import jax
import jax.numpy as jnp
import numpy as np
from jax import lax
from jax.experimental import pallas as pl
from jax.experimental.pallas import tpu as pltpu
from jax.sharding import PartitionSpec as P

HEAD_SIZE = 128
MESH = pl.DeviceIdType.MESH
VMEM = pl.BlockSpec(memory_space=pltpu.VMEM)
ANY = pl.BlockSpec(memory_space=pl.ANY)
SMEM = pl.BlockSpec(memory_space=pltpu.SMEM)


epsilon = 1e-06
rope_base = 1000000.0
clip_limit = 1.0
masked_value = -1e30


def rotary():
    inverse = 1.0 / rope_base ** (np.arange(0, HEAD_SIZE, 2) / HEAD_SIZE)
    angle = np.arange(1024)[:, None] * inverse[None, :]
    cosine = np.concatenate([np.cos(angle), np.cos(angle)], axis=-1)
    sine = np.concatenate([-np.sin(angle), np.sin(angle)], axis=-1)
    shape = (8, 128, HEAD_SIZE)
    return (
        jnp.asarray(cosine.reshape(shape), jnp.float32),
        jnp.asarray(sine.reshape(shape), jnp.float32),
    )


def contract_last(left, right):
    return lax.dot_general(
        left, right, (((1,), (1,)), ((), ())), preferred_element_type=jnp.float32
    )


def contract_first(left, right):
    return lax.dot_general(
        left, right, (((0,), (0,)), ((), ())), preferred_element_type=jnp.float32
    )


class Place:
    def __init__(self):
        dp = lax.axis_index("dp")
        context = lax.axis_index("context")
        self.dp, self.context, self.y = dp, context, lax.axis_index("experts")
        self.core, self.z_hi = lax.rem(dp, 2), dp // 2
        self.x, self.z_lo = context // 2, lax.rem(context, 2)
        self.z = self.z_hi * 2 + self.z_lo
        self.spot = (self.core, self.z_hi, self.y)

    def at(self, x=None, y=None, z=None, core=None):
        x = self.x if x is None else x
        y = self.y if y is None else y
        z = self.z if z is None else z
        core = self.core if core is None else core
        return (z // 2 * 2 + core, x * 2 + lax.rem(z, 2), y)

    def x_by(self, step):
        return lax.rem(self.x + step, 4)

    def y_by(self, step):
        return lax.rem(self.y + step, 4)

    def z_by(self, step):
        return lax.rem(self.z + step, 4)


class Net:
    def __init__(self, send, recv, here=None):
        self.send, self.recv, self.copies = send, recv, []
        self.here, self.loads = here, 0

    def copy(self, src, dst, device):
        spot = len(self.copies)
        made = pltpu.make_async_remote_copy(
            src_ref=src,
            dst_ref=dst,
            send_sem=self.send.at[spot],
            recv_sem=self.recv.at[spot],
            device_id=device,
            device_id_type=MESH,
        )
        made.start()
        self.copies.append(made)
        return made

    def load(self, src, dst):
        made = pltpu.make_async_copy(src, dst, self.here.at[self.loads])
        self.loads += 1
        made.start()
        return made

    def sent(self, made):
        made.wait_send()
        self.copies = [None if one is made else one for one in self.copies]

    def finish(self):
        for made in self.copies:
            if made is not None:
                made.wait_send()


def greet(devices):
    barrier = pltpu.get_barrier_semaphore()
    for device in devices:
        pl.semaphore_signal(barrier, inc=1, device_id=device, device_id_type=MESH)
    return lambda: pl.semaphore_wait(barrier, len(devices))


def wide(ref):
    values = ref[...].astype(jnp.float32)
    return jnp.concatenate([values[step : step + 1] for step in range(16)], axis=1)


def add_into(target, parts, block=32):
    rows = target.shape[-2]
    block = min(block, rows)
    for lead in itertools.product(*[range(size) for size in target.shape[:-2]]):

        def body(step, carry, lead=lead):
            spot = lead + (pl.ds(pl.multiple_of(step * block, block), block),)
            total = parts[0][spot].astype(jnp.float32)
            for part in parts[1:]:
                total = total + part[spot].astype(jnp.float32)
            target[spot] = total.astype(target.dtype)
            return carry

        lax.fori_loop(0, rows // block, body, 0)


def ring_reduce(net, plus, minus, own, slots, target, held=None, begun=None):
    held = own if held is None else held
    done = 0 if begun is None else begun.shape[0]
    if done == 4:
        loads = [net.load(begun, slots.at[pl.ds(0, 4)])]
    elif done == 2:
        loads = [net.load(begun.at[step], slots.at[step * 2]) for step in range(2)]
    else:
        first_plus = net.copy(own(2, 0), slots.at[0], plus)
        first_minus = net.copy(own(2, 1), slots.at[2], minus)
    if done != 4:
        side_plus = net.copy(own(1, 1), slots.at[1], plus)
        side_minus = net.copy(own(3, 0), slots.at[3], minus)
    yield
    if done:
        for load in loads:
            load.wait()
    else:
        first_plus.wait_recv()
        first_minus.wait_recv()
    add_into(slots.at[0], [slots.at[0], held(1, 0)])
    last_plus = net.copy(slots.at[0], slots.at[4], plus)
    add_into(slots.at[2], [slots.at[2], held(3, 1)])
    last_minus = net.copy(slots.at[2], slots.at[5], minus)
    yield
    if done != 4:
        side_minus.wait_recv()
        side_plus.wait_recv()
    last_plus.wait_recv()
    add_into(target(0), [held(0, 0), slots.at[3], slots.at[4]])
    last_minus.wait_recv()
    add_into(target(1), [held(0, 1), slots.at[1], slots.at[5]])


def x_first(net, me, source, slots, middle, other, out, held=None, begun=None):
    staged = None
    if held is not None:
        order = {(1, 0): 0, (3, 1): 1, (0, 0): 2, (0, 1): 3}
        loads = [
            net.load(source.at[me.x_by(step), half], held.at[spot])
            for (step, half), spot in order.items()
        ]

        def staged(step, half):
            return held.at[order[step, half]]

    ring = ring_reduce(
        net,
        me.at(x=me.x_by(1)),
        me.at(x=me.x_by(3)),
        lambda step, half: source.at[me.x_by(step), half],
        slots,
        lambda half: middle.at[half],
        staged,
        begun,
    )
    next(ring)
    yield
    if held is not None:
        for load in loads:
            load.wait()
    yield from ring
    across = net.copy(middle.at[1 - me.z_lo], other, me.at(z=me.z + 1 - 2 * me.z_lo))
    yield
    across.wait_recv()
    add_into(out, [middle.at[me.z_lo], other])


def core_pair(net, me, sending, other, middle):
    across = net.copy(sending, other, me.at(core=1 - me.core))
    yield
    net.sent(across)
    across.wait_recv()
    add_into(middle, [middle, other])


def dense_x_first(net, me, sending, other, middle, slots, corner, last, out):
    yield from core_pair(net, me, sending, other, middle)
    yield from ring_reduce(
        net,
        me.at(x=me.x_by(1)),
        me.at(x=me.x_by(3)),
        lambda step, half: middle.at[half, me.x_by(step)],
        slots,
        lambda half: corner.at[half],
    )
    half_rows = corner.shape[2] // 2
    yield from ring_reduce(
        net,
        me.at(z=me.z_by(1)),
        me.at(z=me.z_by(3)),
        lambda step, half: corner.at[
            me.z_by(step) // 2, lax.rem(me.z_by(step), 2), pl.ds(half * half_rows, half_rows)
        ],
        last,
        lambda half: out.at[pl.ds(half * half_rows, half_rows)],
    )


def dense_z_first(net, me, sending, other, middle, slots, corner, last, out):
    yield from core_pair(net, me, sending, other, middle)
    yield from ring_reduce(
        net,
        me.at(z=me.z_by(1)),
        me.at(z=me.z_by(3)),
        lambda step, half: middle.at[
            me.z_by(step) // 2, pl.ds(half * 2, 2), lax.rem(me.z_by(step), 2)
        ],
        slots,
        lambda half: corner.at[pl.ds(half * 2, 2)],
    )
    half_rows = corner.shape[1] // 2
    yield from ring_reduce(
        net,
        me.at(x=me.x_by(1)),
        me.at(x=me.x_by(3)),
        lambda step, half: corner.at[me.x_by(step), pl.ds(half * half_rows, half_rows)],
        last,
        lambda half: out.at[pl.ds(half * half_rows, half_rows)],
    )


def all_sum(net, devices, spot, own, slots, most):
    slots[spot] = own[...]
    sent = [net.copy(own, slots.at[spot], device) for device in devices]
    yield
    for made in sent:
        made.wait_recv()
    count = slots.shape[0]
    total = slots[0]
    peak = slots[0, most:]
    for step in range(1, count):
        total = total + slots[step]
        peak = jnp.maximum(peak, slots[step, most:])
    for made in sent:
        net.sent(made)
    own[:most] = total[:most]
    own[most:] = peak


def all_small(net, me, working, by_core, by_x, by_z, by_y, out):
    yield from all_sum(net, [me.at(core=1 - me.core)], me.core, working, by_core, 40)
    yield from all_sum(net, [me.at(x=me.x_by(s)) for s in (1, 2, 3)], me.x, working, by_x, 40)
    yield from all_sum(net, [me.at(z=me.z_by(s)) for s in (1, 2, 3)], me.z, working, by_z, 40)
    out[40:] = working[40:]
    yield from all_sum(net, [me.at(y=me.y_by(s)) for s in (1, 2, 3)], me.y, working, by_y, 40)
    out[:40] = working[:40]


OFFSETS = [(a, b) for a in (2, 0, 3, 1) for b in (0, 1, 3, 2) if a or b]


def peer(me, a, b):
    z = me.z if a < 2 else lax.rem(me.z + 2, 4)
    core = me.core if a % 2 == 0 else 1 - me.core
    y = me.y_by(b)
    return (core, z // 2, y), me.at(z=z, core=core, y=y)


def peers(me):
    return [peer(me, a, b)[1] for a, b in OFFSETS]


def gather_rows(table, home, store):
    def body(step, carry):
        columns = pl.ds(pl.multiple_of(step * 256, 256), 256)
        rows = home[:, :, :, :, columns].reshape(768, 256)
        total = contract_first(table[...], rows)
        store(columns, total[:96])
        return carry

    lax.fori_loop(0, home.shape[4] // 256, body, 0)


def turned(values):
    return pltpu.roll(values, 64, 1)


def column_of(row):
    eye = lax.broadcasted_iota(jnp.int32, (128, 128), 0) == lax.broadcasted_iota(
        jnp.int32, (128, 128), 1
    )
    return jnp.sum(jnp.where(eye, row, 0.0), axis=1, keepdims=True)


def norm_back(gradient, raw, gain):
    inverse = lax.rsqrt(jnp.mean(raw * raw, axis=-1, keepdims=True) + epsilon)
    normal = raw * inverse
    scaled = gradient * gain
    result = inverse * (scaled - normal * jnp.mean(scaled * normal, axis=-1, keepdims=True))
    return result, jnp.sum(gradient * normal, axis=0, keepdims=True)


def back_kernel(names, *refs):
    r = types.SimpleNamespace(**dict(zip(names, refs, strict=True)))
    low, full = jnp.bfloat16, jnp.float32
    score_scale = HEAD_SIZE ** (-0.5)
    me = Place()
    net = Net(r.send, r.recv, r.here)
    fetch = Fetch(net)
    fetch.start("hidden", r.hidden, r.hidden_held)
    greeted = greet(
        [
            me.at(x=me.x_by(1)),
            me.at(x=me.x_by(3)),
            me.at(z=me.z_by(1)),
            me.at(z=me.z_by(3)),
            me.at(x=me.x_by(2)),
        ]
        + peers(me)
    )
    gains = r.gain_rows
    gains[...] = wide(r.attn_gain)
    greeted()

    branch, whole = r.branch, r.whole
    above, below = me.at(y=me.y_by(1)), me.at(y=me.y_by(3))
    to_above = net.copy(branch, whole.at[:, me.y], above)
    to_below = net.copy(branch, whole.at[:, me.y], below)
    own_branch = net.load(branch, whole.at[:, me.y])
    weight = r.weight
    load_out = net.load(r.w_out, weight)
    gate = x_first(
        net, me, r.gate, r.gate_slots, r.gate_middle, r.gate_other, r.gate_out, r.gate_held,
        r.gate_begun,
    )
    up = x_first(
        net, me, r.up, r.up_slots, r.up_middle, r.up_other, r.up_out, r.up_held, r.up_begun
    )
    down = x_first(
        net, me, r.down, r.down_slots, r.down_middle, r.down_other, r.down_out, r.down_held
    )
    next(gate)
    next(gate)
    next(up)
    produced, home, table = r.produced, r.home, r.table
    start = me.core * 384 + me.z_hi * 192 + me.y * 48
    mine = pl.ds(pl.multiple_of(start, 16), 48)
    home_came = []

    def bring_home(offsets):
        for a, b in offsets:
            spot, device = peer(me, a, b)
            home_came.append(net.copy(produced.at[spot], home.at[mine], device))

    straight = [(2, 0), (3, 0)]
    bring_home(straight)
    home_own = net.load(produced.at[me.spot], home.at[mine])
    next(up)
    fetch.start("pair", r.pair, r.pair_held)
    fetch.start("query", r.query, r.query_held)
    fetch.start("query_raw", r.query_raw, r.query_raw_held)
    fetch.start("cosine", r.cosine.at[me.context], r.cosine_held)
    fetch.start("sine", r.sine.at[me.context], r.sine_held)
    fetch.start("mixed", r.mixed, r.mixed_held)
    fetch.start("w_key", r.w_key, r.key_weight)
    fetch.start("w_value", r.w_value, r.value_weight)

    hidden, inverse = fetch.hidden, r.inverse
    for s in range(3):
        rows = slice(s * 128, s * 128 + 128)
        values = hidden[s].astype(full)
        root = lax.rsqrt(jnp.mean(values * values, axis=-1, keepdims=True) + epsilon)
        inverse[rows, :] = jnp.broadcast_to(root, (128, 128))
        for step in range(8):
            run = slice(step * 256, step * 256 + 256)
            tile = hidden[s, :, run].astype(full) * root * gains[:, run]
            r.normed[run, rows] = tile.T.astype(low)

    first, second = pl.ds(0, 1024), pl.ds(1024, 1024)
    to_above.wait_recv()
    passed = whole.at[:, me.y_by(3), :, first]
    far_above = net.copy(passed, passed, above)
    to_below.wait_recv()
    passed = whole.at[:, me.y_by(1), :, second]
    far_below = net.copy(passed, passed, below)
    own_branch.wait()
    load_out.wait()
    next(gate)
    far_above.wait_recv()
    far_below.wait_recv()

    bring_home([offset for offset in OFFSETS if offset not in straight])

    heads_grad = r.heads_grad

    def heads_step(step, carry):
        columns = pl.ds(pl.multiple_of(step * 256, 256), 256)
        heads_grad[:, columns] = jnp.dot(
            whole[...].reshape(384, 2048), weight[:, columns], preferred_element_type=full
        ).astype(low)
        return carry

    lax.fori_loop(0, 4, heads_step, 0)
    load_query = net.load(r.w_query, weight)

    query_low = heads_grad

    def own_input(columns):
        return hidden[:, :, columns].reshape(384, 256).astype(full)

    def normed(columns, right):
        return jnp.dot(r.normed[columns, :], right, preferred_element_type=full)

    def whole_part(columns):
        return whole[:, :, :, columns].reshape(384, 256)

    def branch_weight(columns, right):
        return contract_first(whole_part(columns), right)

    def weigh(core, left, right, target):
        def body(step, carry):
            z_hi, part = step // 2, lax.rem(step, 2)
            columns = pl.ds(pl.multiple_of((z_hi * 2 + core) * 512 + part * 256, 256), 256)
            made = left(columns, right[...]).astype(low)
            target[z_hi, pl.ds(part * 2, 2)] = made.reshape(2, 2, 64, right.shape[1])
            return carry

        lax.fori_loop(0, 4, body, 0)

    def dense(order, left, right, sending, other, middle, *more):
        weigh(1 - me.core, left, right, sending)
        task = order(net, me, sending, other, middle, *more)
        next(task)
        weigh(me.core, left, right, middle)
        return task

    out_w = dense(
        dense_z_first, branch_weight, fetch.mixed, r.sending, r.out_w_other, r.out_w_middle,
        r.out_w_slots, r.out_w_corner, r.out_w_last, r.out_w_out,
    )
    next(down)

    query, query_raw, pair = fetch.query, fetch.query_raw, fetch.pair
    cosine, sine = fetch.cosine, fetch.sine
    gain_query, gain_key = r.query_gain[...].astype(full), r.key_gain[...].astype(full)
    bias, key_sum, value_sum = r.bias, r.key_sum, r.value_sum
    pair_grad, gain_part = r.pair_grad, r.gain_part
    gain_part[...] = jnp.zeros((8, 128), full)

    def rope_back(gradient):
        return gradient * cosine[...] - turned(gradient) * sine[...]

    def attend(s):
        here = pl.ds(s * 128, 128)
        bias[...] = mask_bias(me, r.segments, s)
        key_sum[...] = jnp.zeros_like(key_sum)
        value_sum[...] = jnp.zeros_like(value_sum)

        def two_heads(step, carry):
            columns = pl.ds(pl.multiple_of(step * 256, 256), 256)

            def stacked(ref):
                both = ref[here, columns]
                return jnp.concatenate([both[:, :128], both[:, 128:]], axis=0)

            q, d = stacked(query), stacked(heads_grad)
            keys, values = pair[0, s], pair[1, s]
            lines = r.log_sum
            logs = jnp.concatenate(
                [column_of(lines[s * 8 + step * 2]), column_of(lines[s * 8 + step * 2 + 1])], axis=0
            )
            score = contract_last(q, keys) * score_scale
            score = score + jnp.concatenate([bias[...], bias[...]], axis=0)
            prob = jnp.exp(score - logs)
            prob_grad = contract_last(d, values)
            delta = jnp.sum(prob * prob_grad, axis=-1, keepdims=True)
            score_grad = (prob * (prob_grad - delta)).astype(low)
            value_sum[...] += contract_first(prob.astype(low), d)
            key_sum[...] += contract_first(score_grad, q)
            turned_grad = jnp.dot(score_grad, keys, preferred_element_type=full) * score_scale
            for half in range(2):
                run = pl.ds(pl.multiple_of(step * 256 + half * 128, 128), 128)
                grad, part = norm_back(
                    rope_back(turned_grad[half * 128 : half * 128 + 128]),
                    query_raw[here, run],
                    gain_query,
                )
                heads_grad[here, run] = grad.astype(low)
                gain_part[0:1, :] += part
            return carry

        lax.fori_loop(0, 4, two_heads, 0)
        pair_grad[s, :, :, 0] = (key_sum[...] * score_scale).astype(low).reshape(4, 2, 128, 128)
        pair_grad[s, :, :, 1] = value_sum[...].astype(low).reshape(4, 2, 128, 128)
        return x_first(
            net, me, pair_grad.at[s], r.pair_slots.at[s], r.pair_middle.at[s], r.pair_other.at[s],
            r.pair_out.at[s],
        )

    pairs = [attend(0)]
    next(pairs[0])
    next(out_w)
    pairs.append(attend(1))
    next(pairs[1])
    next(pairs[0])
    next(up)
    pairs.append(attend(2))
    next(pairs[2])
    next(pairs[1])
    next(pairs[0])

    query_w = dense(
        dense_x_first, normed, query_low, r.sending, r.query_w_other, r.query_w_middle,
        r.query_w_slots, r.query_w_corner, r.query_w_last, r.query_w_out,
    )
    next(pairs[2])
    next(pairs[1])
    next(query_w)
    next(pairs[2])

    load_query.wait()
    net.sent(far_above)
    net.sent(far_below)

    def query_step(step, carry):
        columns = pl.ds(pl.multiple_of(step * 256, 256), 256)
        made = contract_last(query_low[...], weight[columns, :])
        whole[:, :, :, columns] = made.astype(low).reshape(3, 4, 32, 256)
        return carry

    lax.fori_loop(0, 8, query_step, 0)
    next(down)

    pair_out, key_raw, pair_low = r.pair_out, r.key_raw, r.pair_low
    for s in range(3):
        next(pairs[s], None)
        rows = slice(s * 128, s * 128 + 128)
        grad, part = norm_back(rope_back(pair_out[s, 0]), key_raw[rows, :], gain_key)
        gain_part[1:2, :] += part
        pair_low[rows, :128] = grad.astype(low)
        pair_low[rows, 128:] = pair_out[s, 1].astype(low)

    w_key, w_value = fetch.w_key, fetch.w_value
    small = r.small
    normed_part = r.normed_part

    def normed_step(step, carry):
        columns = pl.ds(pl.multiple_of(step * 256, 256), 256)
        made = whole_part(columns).astype(full)
        made = made + contract_last(pair_low[:, :128], w_key[columns, :])
        made = made + contract_last(pair_low[:, 128:], w_value[columns, :])
        normal = own_input(columns) * inverse[:, 0:1]
        normed_part[:, columns] = jnp.sum(made * normal, axis=0, keepdims=True)
        whole[:, :, :, columns] = made.astype(low).reshape(3, 4, 32, 256)
        return carry

    lax.fori_loop(0, 8, normed_step, 0)
    normed_out = r.normed_out
    normed_sum = ring_reduce(
        net,
        above,
        below,
        lambda step, half: whole.at[:, me.y_by(step), :, pl.ds(half * 1024, 1024)],
        r.normed_slots,
        lambda half: normed_out.at[:, :, pl.ds(half * 1024, 1024)],
    )
    next(normed_sum)
    for step in range(16):
        run = slice(step * 128, step * 128 + 128)
        small[step : step + 1, :] = normed_part[:, run]
        small[16 + step : 17 + step, :] = r.moe_gain_part[:, run]
    small[32:40, :] = gain_part[...]
    small[40:, :] = r.peaks[...]
    smalls = all_small(
        net, me, small, r.by_core, r.by_x, r.by_z, r.by_y, r.small_out
    )
    pair_w = dense(
        dense_x_first, normed, pair_low, r.pair_sending, r.pair_w_other, r.pair_w_middle,
        r.pair_w_slots, r.pair_w_corner, r.pair_w_last, r.pair_w_out,
    )
    next(out_w)

    for made in home_came:
        made.wait_recv()
    home_own.wait()
    home_loads = [
        net.load(home.at[:, pl.ds(half * 1024, 1024)], weight.at[pl.ds(half * 768, 768)])
        for half in range(2)
    ]
    next(pair_w)
    next(smalls)
    moe_out = r.moe_out
    for half in range(2):
        home_loads[half].wait()

        def gather(step, carry, half=half):
            columns = pl.ds(pl.multiple_of(step * 256, 256), 256)
            total = contract_first(table[...], weight[half * 768 : half * 768 + 768, columns])
            moe_out[:, pl.ds(pl.multiple_of(half * 1024 + step * 256, 256), 256)] = total[:96]
            return carry

        lax.fori_loop(0, 4, gather, 0)

    def rest(*tasks):
        for task in tasks:
            next(task, None)

    rest(normed_sum, query_w, out_w, down, smalls)

    next(normed_sum, None)
    for s in range(3):
        rows = pl.ds(pl.multiple_of(me.y * 32, 32), 32)
        grad, _ = norm_back(normed_out[s], hidden[s, rows, :].astype(full), gains[...])
        normed_out[s] = grad

    rest(pair_w, out_w, query_w, down, smalls, gate, up)
    rest(pair_w, out_w, query_w, smalls)
    tasks = [pair_w, out_w, smalls, query_w, gate, up, down]
    while tasks:
        for task in list(tasks):
            if next(task, "end") == "end":
                tasks.remove(task)
    net.finish()


def dense_slots(columns, corner):
    low = jnp.bfloat16
    return [
        pltpu.VMEM((2, 4, 2, 64, columns), low),
        pltpu.VMEM((2, 4, 2, 64, columns), low),
        pltpu.VMEM((6, 2, 64, columns), low),
        pltpu.VMEM(corner + (64, columns), low),
        pltpu.VMEM((6, 32, columns), low),
    ]


def back(far, near):
    low, full = jnp.bfloat16, jnp.float32
    outs = dict(
        gate_out=(256, 768),
        up_out=(256, 768),
        down_out=(256, 768),
        query_w_out=(64, 1024),
        pair_w_out=(64, 256),
        out_w_out=(64, 1024),
        small_out=(48, 128),
        normed_out=(3, 32, 2048),
        moe_out=(96, 2048),
    )
    scratch = dict(
        gain_rows=pltpu.VMEM((1, 2048), full),
        hidden_held=pltpu.VMEM((3, 128, 2048), low),
        pair_held=pltpu.VMEM((2, 3, 1024, 128), low),
        query_held=pltpu.VMEM((384, 1024), low),
        query_raw_held=pltpu.VMEM((384, 1024), full),
        cosine_held=pltpu.VMEM((128, 128), full),
        sine_held=pltpu.VMEM((128, 128), full),
        mixed_held=pltpu.VMEM((384, 1024), low),
        key_weight=pltpu.VMEM((2048, 128), low),
        value_weight=pltpu.VMEM((2048, 128), low),
        whole=pltpu.VMEM((3, 4, 32, 2048), low),
        weight=pltpu.VMEM((2048, 1024), low),
        inverse=pltpu.VMEM((384, 128), full),
        normed=pltpu.VMEM((2048, 384), low),
        heads_grad=pltpu.VMEM((384, 1024), low),
        bias=pltpu.VMEM((128, 1024), full),
        key_sum=pltpu.VMEM((1024, 128), full),
        value_sum=pltpu.VMEM((1024, 128), full),
        pair_grad=pltpu.VMEM((3, 4, 2, 2, 128, 128), low),
        pair_slots=pltpu.VMEM((3, 6, 2, 128, 128), low),
        pair_middle=pltpu.VMEM((3, 2, 2, 128, 128), low),
        pair_other=pltpu.VMEM((3, 2, 128, 128), low),
        pair_out=pltpu.VMEM((3, 2, 128, 128), full),
        pair_low=pltpu.VMEM((384, 256), low),
        gain_part=pltpu.VMEM((8, 128), full),
        normed_part=pltpu.VMEM((1, 2048), full),
        normed_slots=pltpu.VMEM((6, 3, 32, 1024), low),
        small=pltpu.VMEM((48, 128), full),
        by_core=pltpu.VMEM((2, 48, 128), full),
        by_x=pltpu.VMEM((4, 48, 128), full),
        by_z=pltpu.VMEM((4, 48, 128), full),
        by_y=pltpu.VMEM((4, 48, 128), full),
        down_slots=pltpu.VMEM((6, 256, 768), low),
        down_middle=pltpu.VMEM((2, 256, 768), low),
        down_other=pltpu.VMEM((256, 768), low),
        down_held=pltpu.VMEM((4, 256, 768), low),
        gate_slots=pltpu.VMEM((6, 256, 768), low),
        gate_middle=pltpu.VMEM((2, 256, 768), low),
        gate_other=pltpu.VMEM((256, 768), low),
        gate_held=pltpu.VMEM((4, 256, 768), low),
        up_slots=pltpu.VMEM((6, 256, 768), low),
        up_middle=pltpu.VMEM((2, 256, 768), low),
        up_other=pltpu.VMEM((256, 768), low),
        up_held=pltpu.VMEM((4, 256, 768), low),
        sending=pltpu.VMEM((2, 4, 2, 64, 1024), low),
        pair_sending=pltpu.VMEM((2, 4, 2, 64, 256), low),
        query_w_other=None,
        query_w_middle=None,
        query_w_slots=None,
        query_w_corner=None,
        query_w_last=None,
        pair_w_other=None,
        pair_w_middle=None,
        pair_w_slots=None,
        pair_w_corner=None,
        pair_w_last=None,
        out_w_other=None,
        out_w_middle=None,
        out_w_slots=None,
        out_w_corner=None,
        out_w_last=None,
        send=pltpu.SemaphoreType.DMA((116,)),
        recv=pltpu.SemaphoreType.DMA((116,)),
        here=pltpu.SemaphoreType.DMA((34,)),
    )
    dense = dense_slots(1024, (2, 2)) + dense_slots(256, (2, 2)) + dense_slots(1024, (4,))
    scratch = {name: one or dense.pop(0) for name, one in scratch.items()}
    outs = {name: jax.ShapeDtypeStruct(size, full) for name, size in outs.items()}
    far_outs = dict(home=jax.ShapeDtypeStruct((768, 2048), low))
    return call(back_kernel, 0, far, near, outs, far_outs, scratch)


class Fetch:
    def __init__(self, net):
        self.net, self.waiting, self.held = net, {}, {}

    def start(self, name, source, target):
        self.waiting[name] = self.net.load(source, target)
        self.held[name] = target

    def __getattr__(self, name):
        if name in self.waiting:
            self.waiting.pop(name).wait()
        return self.held[name]


def token_table(ids, gates, capacity, table, info):
    low, full = jnp.bfloat16, jnp.float32
    expert = lax.broadcasted_iota(jnp.int32, (16, 32), 0)
    chosen, share = [], []
    for s in range(3):
        chosen_here = jnp.zeros((16, 32), full)
        share_here = jnp.zeros((16, 32), full)
        for k in range(8):
            named = ids[s, k : k + 1, :] == expert
            chosen_here = chosen_here + jnp.where(named, 1.0, 0.0)
            share_here = share_here + jnp.where(named, gates[s, k : k + 1, :], 0.0)
        chosen.append(chosen_here)
        share.append(share_here)
    none = jnp.zeros((16, 32), full)
    chosen = jnp.concatenate(chosen + [none], axis=1)
    share = jnp.concatenate(share + [none], axis=1)
    row = lax.broadcasted_iota(jnp.int32, (16, 128), 0)
    limit = jnp.zeros((16, 128), full)
    for e in range(16):
        limit = jnp.where(row == e, capacity[e].astype(full), limit)
    earlier = lax.broadcasted_iota(jnp.int32, (128, 128), 0) < lax.broadcasted_iota(
        jnp.int32, (128, 128), 1
    )
    before = jnp.dot(
        chosen.astype(low), jnp.where(earlier, 1.0, 0.0).astype(low), preferred_element_type=full
    )
    slot = jnp.where((chosen > 0.0) & (before < limit), before, -1.0)
    spot = lax.broadcasted_iota(jnp.int32, (48, 128), 0).astype(full)
    for place in range(16):
        core, z_hi, y = place // 8, place // 4 % 2, place % 4
        e = (z_hi * 2 + core) * 4 + y
        mask = jnp.where(slot[e : e + 1, :] == spot, 1.0, 0.0)
        table[place * 48 : place * 48 + 48, :] = mask.astype(low)
        info[core, z_hi, y] = jnp.concatenate(
            [slot[e : e + 1, :], share[e : e + 1, :], jnp.zeros((6, 128), full)], axis=0
        )


def dispatch(table, rows, sender, core):
    rest = table[pl.ds(pl.multiple_of(core * 384, 384), 384), :]
    columns = 512
    for step in range(2048 // columns):
        run = slice(step * columns, (step + 1) * columns)
        picked = jnp.dot(rest, rows[:, run], preferred_element_type=jnp.float32)
        sender[core, :, :, :, run] = picked.astype(jnp.bfloat16).reshape(2, 4, 48, columns)


def moe_kernel(names, *refs):
    r = types.SimpleNamespace(**dict(zip(names, refs, strict=True)))
    low, full = jnp.bfloat16, jnp.float32
    me = Place()
    net = Net(r.send, r.recv, r.here)
    fetch = Fetch(net)
    fetch.start("w_gate", r.w_gate, r.gate_weight)
    fetch.start("w_up", r.w_up, r.up_weight)
    fetch.start("raw", r.grads, r.raw_held)
    fetch.start("w_down", r.w_down, r.down_weight)
    greeted = greet(peers(me) + [me.at(x=me.x_by(1)), me.at(x=me.x_by(3))])
    rows, sending, local, table = r.rows, r.sending, r.local, r.table
    values = r.after[...]
    inverse = lax.rsqrt(jnp.mean(values * values, axis=-1, keepdims=True) + epsilon)
    gain = wide(r.moe_gain)
    rows[96:, :] = jnp.zeros((32, 2048), low)
    rows[:96, :] = (values * inverse * gain).astype(low)
    came = {}

    def set_out(first, second):
        for a, b in OFFSETS:
            if a in (first, second):
                spot, device = peer(me, a, b)
                came[a, b] = net.copy(sending.at[spot], local.at[me.spot], device)

    dispatch(table, rows, sending, me.core)
    greeted()
    set_out(0, 2)
    local[me.spot] = sending[me.spot]
    dispatch(table, rows, sending, 1 - me.core)

    act, gate_back, up_back, back, home = r.act, r.gate_back, r.up_back, r.back, r.home
    w_gate, w_up, grads, w_down = fetch.w_gate, fetch.w_up, r.grads_held, fetch.w_down
    fetch.raw
    spot = lax.broadcasted_iota(jnp.int32, (48, 128), 0).astype(full)
    back_came, dots_came, round_x, written = {}, {}, [], []
    right, left = me.at(x=me.x_by(1)), me.at(x=me.x_by(3))

    def weigh(first, group, entered, given, target):
        def body(step, carry):
            columns = pl.ds(pl.multiple_of(step * 256, 256), 256)
            made = contract_first(
                entered[group, :, :, :, columns].reshape(384, 256), given[group]
            )
            if first == 1:
                made = made + target[columns, :].astype(full)
            target[columns, :] = made.astype(low)
            return carry

        lax.fori_loop(0, 8, body, 0)

    def chunk(target, step, half):
        start = (me.x_by(step) * 2 + half) * 256
        return target.at[pl.ds(pl.multiple_of(start, 256), 256)]

    for first in (0, 1):
        group = me.core if first == 0 else 1 - me.core
        for a in (first, first + 2):
            for b in (1, 3, 2, 0):
                if a or b:
                    came[a, b].wait_recv()
            if a == 0:
                set_out(1, 3)
        masks, shares = [], []
        for z_hi in range(2):
            for y in range(4):
                mask = r.info_in[group, z_hi, y, 0:1, :] == spot
                share = jnp.where(mask, r.info_in[group, z_hi, y, 1:2, :], 0.0)
                masks.append(mask)
                shares.append(jnp.sum(share, axis=1, keepdims=True))
        shared = jnp.concatenate(shares, axis=0)

        def inner(step, carry, group=group, shared=shared):
            columns = pl.ds(pl.multiple_of(step * 256, 256), 256)
            entered = local[group].reshape(384, 2048)
            gate_pre = jnp.dot(entered, w_gate[:, columns], preferred_element_type=full)
            up_pre = jnp.dot(entered, w_up[:, columns], preferred_element_type=full)
            act_back = jnp.dot(
                grads[group].reshape(384, 2048), w_down[:, columns], preferred_element_type=full
            )
            sigmoid = 1.0 / (1.0 + jnp.exp(-gate_pre))
            silu = gate_pre * sigmoid
            act[group, :, columns] = (silu * up_pre).astype(low)
            gate_back[group, :, columns] = (
                act_back * up_pre * sigmoid * (1.0 + gate_pre * (1.0 - sigmoid))
            ).astype(low)
            up_back[group, :, columns] = (act_back * silu).astype(low)
            return carry

        def outer(step, dot, group=group, shared=shared):
            columns = pl.ds(pl.multiple_of(step * 256, 256), 256)
            row_back = contract_last(gate_back[group], w_gate[columns, :]) + contract_last(
                up_back[group], w_up[columns, :]
            )
            back[group, :, :, :, columns] = row_back.astype(low).reshape(2, 4, 48, 256)
            return dot

        def finals(step, dot, group=group, shared=shared):
            columns = pl.ds(pl.multiple_of(step * 256, 256), 256)
            made = contract_last(act[group], w_down[columns, :]).astype(low).astype(full)
            r.produced_held[group, :, :, :, columns] = (
                (made * shared).astype(low).reshape(2, 4, 48, 256)
            )
            incoming = r.raw_held[group, :, :, :, columns].reshape(384, 256).astype(full)
            return dot + jnp.sum(made * incoming, axis=1, keepdims=True)

        def scale(step, carry, group=group, shared=shared):
            columns = pl.ds(pl.multiple_of(step * 256, 256), 256)
            incoming = r.raw_held[group, :, :, :, columns].reshape(384, 256).astype(full)
            grads[group, :, :, :, columns] = (
                (incoming * shared).astype(low).reshape(2, 4, 48, 256)
            )
            return carry

        lax.fori_loop(0, 8, scale, 0)
        lax.fori_loop(0, 3, inner, 0)
        lax.fori_loop(0, 8, outer, 0)
        for a in (first + 2, first):
            for b in (0, 1, 3, 2):
                if a or b:
                    place, device = peer(me, a, b)
                    back_came[a, b] = net.copy(back.at[place], home.at[me.spot], device)
        if first == 1:
            weigh(first, group, local, gate_back, r.gate_held)
            round_x += [
                net.copy(chunk(r.gate_held, 2, 0), r.gate_slots.at[0], right),
                net.copy(chunk(r.gate_held, 2, 1), r.gate_slots.at[2], left),
                net.copy(chunk(r.gate_held, 1, 1), r.gate_slots.at[1], right),
                net.copy(chunk(r.gate_held, 3, 0), r.gate_slots.at[3], left),
            ]
            written.append(net.load(r.gate_held, r.full_gate))
            weigh(first, group, local, up_back, r.up_held)
            round_x += [
                net.copy(chunk(r.up_held, 2, 0), r.up_slots.at[0], right),
                net.copy(chunk(r.up_held, 2, 1), r.up_slots.at[1], left),
            ]
            written.append(net.load(r.up_held, r.full_up))
        dot = lax.fori_loop(0, 8, finals, jnp.zeros((384, 1), full))
        for place in range(8):
            line = jnp.where(masks[place], dot[place * 48 : place * 48 + 48], 0.0)
            line = jnp.sum(line, axis=0, keepdims=True)
            r.dots[group, place // 4, place % 4] = jnp.broadcast_to(line, (8, 128))
        for a in (first + 2, first):
            for b in (0, 1, 3, 2):
                if a or b:
                    place, device = peer(me, a, b)
                    dots_came[a, b] = net.copy(r.dots.at[place], r.dots_in.at[me.spot], device)
        if first == 0:
            weigh(first, group, local, gate_back, r.gate_held)
            weigh(first, group, local, up_back, r.up_held)
        weigh(first, group, grads, act, r.down_held)
    written.append(net.load(r.produced_held, r.produced))
    written.append(net.load(r.down_held, r.full_down))
    home[me.spot] = back[me.spot]
    r.dots_in[me.spot] = r.dots[me.spot]

    for offset in OFFSETS:
        dots_came[offset].wait_recv()
    lines = [r.dots_in[e // 4 % 2, e // 8, e % 4, 0:1, :] for e in range(16)]
    lines = jnp.concatenate(lines, axis=0)
    expert = lax.broadcasted_iota(jnp.int32, (16, 32), 0)
    for s in range(3):
        dots = lines[:, s * 32 : s * 32 + 32]
        for k in range(8):
            named = r.ids[s, k : k + 1, :] == expert
            r.gate_grad[s, k : k + 1, :] = jnp.sum(
                jnp.where(named, dots, 0.0), axis=0, keepdims=True
            )

    for offset in OFFSETS:
        back_came[offset].wait_recv()
    after_grad = r.after_grad

    def keep(columns, total):
        after_grad[:, columns] = total

    gather_rows(table, home, keep)
    gradient = after_grad[...]
    moe_part, gain_part = norm_back(gradient, r.after[...], gain)
    r.gain_part[...] = gain_part
    result = r.cotangent[...].reshape(96, 2048).astype(full) + moe_part
    after_grad[...] = result
    r.branch[...] = result.astype(low).reshape(3, 32, 2048)
    for one in written:
        one.wait()
    for one in round_x:
        one.wait_recv()
    net.finish()


def moe(far, near):
    low, full = jnp.bfloat16, jnp.float32
    rows = (2, 2, 4, 48, 2048)
    outs = dict(
        after_grad=jax.ShapeDtypeStruct((96, 2048), full),
        branch=jax.ShapeDtypeStruct((3, 32, 2048), low),
        gain_part=jax.ShapeDtypeStruct((1, 2048), full),
        gate_grad=jax.ShapeDtypeStruct((3, 8, 32), full),
    )
    far_outs = dict(
        produced=jax.ShapeDtypeStruct(rows, low),
        full_gate=jax.ShapeDtypeStruct((2048, 768), low),
        full_up=jax.ShapeDtypeStruct((2048, 768), low),
        full_down=jax.ShapeDtypeStruct((2048, 768), low),
        gate_slots=jax.ShapeDtypeStruct((4, 256, 768), low),
        up_slots=jax.ShapeDtypeStruct((2, 256, 768), low),
    )
    scratch = dict(
        rows=pltpu.VMEM((128, 2048), low),
        sending=pltpu.VMEM(rows, low),
        local=pltpu.VMEM(rows, low),
        raw_held=pltpu.VMEM(rows, low),
        grads_held=pltpu.VMEM(rows, low),
        produced_held=pltpu.VMEM(rows, low),
        back=pltpu.VMEM(rows, low),
        home=pltpu.VMEM(rows, low),
        gate_weight=pltpu.VMEM((2048, 768), low),
        up_weight=pltpu.VMEM((2048, 768), low),
        down_weight=pltpu.VMEM((2048, 768), low),
        gate_held=pltpu.VMEM((2048, 768), low),
        up_held=pltpu.VMEM((2048, 768), low),
        down_held=pltpu.VMEM((2048, 768), low),
        act=pltpu.VMEM((2, 384, 768), low),
        gate_back=pltpu.VMEM((2, 384, 768), low),
        up_back=pltpu.VMEM((2, 384, 768), low),
        dots=pltpu.VMEM((2, 2, 4, 8, 128), full),
        dots_in=pltpu.VMEM((2, 2, 4, 8, 128), full),
        send=pltpu.SemaphoreType.DMA((51,)),
        recv=pltpu.SemaphoreType.DMA((51,)),
        here=pltpu.SemaphoreType.DMA((8,)),
    )
    return call(moe_kernel, 1, far, near, outs, far_outs, scratch)


def call(kernel, number, far, near, outs, far_outs, scratch):
    names = list(far) + list(near) + list(outs) + list(far_outs) + list(scratch)
    shapes = {**outs, **far_outs}
    results = pl.pallas_call(
        functools.partial(kernel, names),
        out_shape=list(shapes.values()),
        in_specs=[ANY] * len(far)
        + [SMEM if one.ndim == 1 else VMEM for one in near.values()],
        out_specs=[VMEM] * len(outs) + [ANY] * len(far_outs),
        scratch_shapes=list(scratch.values()),
        compiler_params=pltpu.CompilerParams(
            collective_id=number, has_side_effects=True, vmem_limit_bytes=63 << 20
        ),
        name=kernel.__name__,
    )(*far.values(), *near.values())
    return types.SimpleNamespace(**dict(zip(shapes, results, strict=True)))


def front_kernel(names, *refs):
    r = types.SimpleNamespace(**dict(zip(names, refs, strict=True)))
    low, full = jnp.bfloat16, jnp.float32
    score_scale = HEAD_SIZE ** (-0.5)
    me = Place()
    net = Net(r.send, r.recv, r.here)
    fetch = Fetch(net)
    fetch.start("hidden", r.hidden, r.hidden_held)
    fetch.start("w_pair", r.w_key, r.key_weight)
    fetch.start("w_value", r.w_value, r.value_weight)
    fetch.start("cosine", r.cosine.at[me.context], r.cosine_held)
    fetch.start("sine", r.sine.at[me.context], r.sine_held)
    fetch.start("w_query", r.w_query, r.query_weight)
    fetch.start("cotangent", r.cotangent, r.cotangent_held)
    fetch.start("w_out", r.w_out, r.out_weight)
    beside = me.at(z=me.z + 1 - 2 * me.z_lo)
    right, left = me.at(x=me.x_by(1)), me.at(x=me.x_by(3))
    greeted = greet([right, left, beside] + peers(me))
    gains = r.gain_rows
    gains[...] = wide(r.attn_gain)

    token_table(r.ids, r.gates, r.capacity, r.table, r.info)
    rows = r.rows
    rows[96:, :] = jnp.zeros((32, 2048), low)
    rows[:96, :] = fetch.cotangent[...].reshape(96, 2048)
    for core in range(2):
        dispatch(r.table, rows, r.sending, core)
    greeted()
    arrivals = []

    def set_out(first, second):
        for a, b in OFFSETS:
            if a in (first, second):
                spot, device = peer(me, a, b)
                arrivals.append(net.copy(r.info.at[spot], r.info_in.at[me.spot], device))
                arrivals.append(net.copy(r.sending.at[spot], r.grads.at[me.spot], device))

    set_out(0, 1)
    r.info_in[me.spot] = r.info[me.spot]
    own_grads = net.load(r.sending.at[me.spot], r.grads.at[me.spot])

    hidden, normed = fetch.hidden, r.normed
    for s in range(3):
        values = hidden[s].astype(full)
        root = lax.rsqrt(jnp.mean(values * values, axis=-1, keepdims=True) + epsilon)
        normed[s * 128 : s * 128 + 128, :] = (values * root * gains[...]).astype(low)

    def rope(values):
        cosine = jnp.concatenate([fetch.cosine[...]] * 3, axis=0)
        sine = jnp.concatenate([fetch.sine[...]] * 3, axis=0)
        return values * cosine + turned(values) * sine

    def head_norm(raw, gain):
        return raw * lax.rsqrt(jnp.mean(raw * raw, axis=-1, keepdims=True) + epsilon) * gain

    pair, key_raw = r.pair_held, r.key_raw
    made = jnp.dot(normed[...], fetch.w_pair[...], preferred_element_type=full)
    key_raw[...] = made
    keys = rope(head_norm(made, r.key_gain[...].astype(full))).astype(low)
    values = jnp.dot(normed[...], fetch.w_value[...], preferred_element_type=full).astype(low)
    own = pl.ds(pl.multiple_of(me.context * 128, 128), 128)
    pair[0, :, own, :] = keys.reshape(3, 128, 128)
    pair[1, :, own, :] = values.reshape(3, 128, 128)

    def block(x, z_lo):
        return pl.ds(pl.multiple_of((x * 2 + z_lo) * 128, 128), 128)

    def piece(x, z_lo, half=None):
        rows = block(x, z_lo)
        return pair.at[:, :, rows, :] if half is None else pair.at[half, :, rows, :]

    def pass_on(view, device):
        return net.copy(view, view, device)

    own_z, other_z = me.z_lo, 1 - me.z_lo
    from_z = pass_on(piece(me.x, own_z), beside)
    from_left = [pass_on(piece(me.x, own_z), right)]
    from_right = [pass_on(piece(me.x, own_z), left)]

    set_out(2, 3)

    w_query, query, query_raw = fetch.w_query, r.query_held, r.query_raw_held

    def project(step, carry):
        columns = pl.ds(pl.multiple_of(step * 256, 256), 256)
        made = jnp.dot(normed[...], w_query[:, columns], preferred_element_type=full)
        query_raw[:, columns] = made
        for half in range(2):
            run = pl.ds(pl.multiple_of(step * 256 + half * 128, 128), 128)
            one = head_norm(made[:, half * 128 : half * 128 + 128], r.query_gain[...].astype(full))
            query[:, run] = rope(one).astype(low)
        return carry

    lax.fori_loop(0, 4, project, 0)
    written = [net.load(query, r.query), net.load(query_raw, r.query_raw)]
    from_z.wait_recv()
    from_left.append(pass_on(piece(me.x, other_z), right))
    from_right.append(pass_on(piece(me.x, other_z), left))
    far = [[], []]
    for spot, zs in enumerate((own_z, other_z)):
        from_left[spot].wait_recv()
        far[0].append(pass_on(piece(me.x_by(3), zs, 0), right))
        from_right[spot].wait_recv()
        far[1].append(pass_on(piece(me.x_by(1), zs, 1), left))
    for one in far[0] + far[1]:
        one.wait_recv()
    written.append(net.load(pair, r.pair))

    bias, peaks, mixed = r.bias, r.peak_rows, r.mixed_held
    peaks[...] = jnp.full((8, 1, 128), -jnp.inf, full)
    for s in range(3):
        here = pl.ds(s * 128, 128)
        bias[...] = mask_bias(me, r.segments, s)

        def two_heads(step, carry, s=s, here=here):
            columns = pl.ds(pl.multiple_of(step * 256, 256), 256)
            both = query[here, columns]
            q = jnp.concatenate([both[:, :128], both[:, 128:]], axis=0)
            score = contract_last(q, pair[0, s]) * score_scale
            score = score + jnp.concatenate([bias[...], bias[...]], axis=0)
            highest = jnp.max(score, axis=-1, keepdims=True)
            weight = jnp.exp(score - highest)
            total = jnp.sum(weight, axis=-1, keepdims=True)
            prob = (weight * (1.0 / total)).astype(low)
            logs = highest + jnp.log(total)
            heads = jnp.dot(prob, pair[1, s], preferred_element_type=full).astype(low)
            for half in range(2):
                part = slice(half * 128, half * 128 + 128)
                head = step * 2 + half
                run = pl.ds(pl.multiple_of(step * 256 + half * 128, 128), 128)
                mixed[here, run] = heads[part]
                r.log_sum[s * 8 + head] = row_of(logs[part])
                top = jnp.max(highest[part], axis=0, keepdims=True)
                peaks[head] = jnp.maximum(peaks[head], top)
            return carry

        lax.fori_loop(0, 4, two_heads, 0)
    for head in range(8):
        r.peaks[head : head + 1, :] = peaks[head]
    written.append(net.load(mixed, r.mixed))

    w_out, shares = fetch.w_out, r.shares

    def branch_step(step, carry):
        columns = pl.ds(pl.multiple_of(step * 256, 256), 256)
        made = contract_last(mixed[...], w_out[columns, :])
        shares[:, :, :, columns] = made.astype(low).reshape(3, 4, 32, 256)
        return carry

    lax.fori_loop(0, 8, branch_step, 0)
    after = r.after_sum
    ring = ring_reduce(
        net,
        me.at(y=me.y_by(1)),
        me.at(y=me.y_by(3)),
        lambda step, half: shares.at[:, me.y_by(step), :, pl.ds(half * 1024, 1024)],
        r.branch_slots,
        lambda half: after.at[:, :, pl.ds(half * 1024, 1024)],
    )
    for _ in ring:
        pass
    own_rows = pl.ds(pl.multiple_of(me.y * 32, 32), 32)
    for s in range(3):
        r.after[s * 32 : s * 32 + 32, :] = after[s] + hidden[s, own_rows, :].astype(full)
    for one in arrivals:
        one.wait_recv()
    own_grads.wait()
    for one in written:
        one.wait()
    net.finish()


def row_of(column):
    eye = lax.broadcasted_iota(jnp.int32, (128, 128), 0) == lax.broadcasted_iota(
        jnp.int32, (128, 128), 1
    )
    return jnp.sum(jnp.where(eye, column, 0.0), axis=0, keepdims=True)


def mask_bias(me, segments, s):
    spot = me.context * 128 + lax.broadcasted_iota(jnp.int32, (128, 1024), 0)
    own = segments[s : s + 1, pl.ds(pl.multiple_of(me.context * 128, 128), 128)]
    document = column_of(own.astype(jnp.float32))
    allowed = (document == segments[s : s + 1, :].astype(jnp.float32)) & (
        lax.broadcasted_iota(jnp.int32, (128, 1024), 1) <= spot
    )
    return jnp.where(allowed, 0.0, masked_value)


def front(far, near):
    low, full = jnp.bfloat16, jnp.float32
    rows = (2, 2, 4, 48, 2048)
    outs = dict(
        key_raw=jax.ShapeDtypeStruct((384, 128), full),
        log_sum=jax.ShapeDtypeStruct((24, 1, 128), full),
        peaks=jax.ShapeDtypeStruct((8, 128), full),
        after=jax.ShapeDtypeStruct((96, 2048), full),
        table=jax.ShapeDtypeStruct((768, 128), low),
        info_in=jax.ShapeDtypeStruct((2, 2, 4, 8, 128), full),
    )
    far_outs = dict(
        query=jax.ShapeDtypeStruct((384, 1024), low),
        query_raw=jax.ShapeDtypeStruct((384, 1024), full),
        pair=jax.ShapeDtypeStruct((2, 3, 1024, 128), low),
        mixed=jax.ShapeDtypeStruct((384, 1024), low),
        grads=jax.ShapeDtypeStruct(rows, low),
    )
    scratch = dict(
        gain_rows=pltpu.VMEM((1, 2048), full),
        hidden_held=pltpu.VMEM((3, 128, 2048), low),
        key_weight=pltpu.VMEM((2048, 128), low),
        value_weight=pltpu.VMEM((2048, 128), low),
        cosine_held=pltpu.VMEM((128, 128), full),
        sine_held=pltpu.VMEM((128, 128), full),
        query_weight=pltpu.VMEM((2048, 1024), low),
        cotangent_held=pltpu.VMEM((3, 32, 2048), low),
        out_weight=pltpu.VMEM((2048, 1024), low),
        normed=pltpu.VMEM((384, 2048), low),
        pair_held=pltpu.VMEM((2, 3, 1024, 128), low),
        info=pltpu.VMEM((2, 2, 4, 8, 128), full),
        rows=pltpu.VMEM((128, 2048), low),
        sending=pltpu.VMEM(rows, low),
        query_held=pltpu.VMEM((384, 1024), low),
        query_raw_held=pltpu.VMEM((384, 1024), full),
        bias=pltpu.VMEM((128, 1024), full),
        peak_rows=pltpu.VMEM((8, 1, 128), full),
        mixed_held=pltpu.VMEM((384, 1024), low),
        shares=pltpu.VMEM((3, 4, 32, 2048), low),
        branch_slots=pltpu.VMEM((6, 3, 32, 1024), low),
        after_sum=pltpu.VMEM((3, 32, 2048), full),
        send=pltpu.SemaphoreType.DMA((46,)),
        recv=pltpu.SemaphoreType.DMA((46,)),
        here=pltpu.SemaphoreType.DMA((16,)),
    )
    return call(front_kernel, 2, far, near, outs, far_outs, scratch)


def finish_kernel(names, *refs):
    r = types.SimpleNamespace(**dict(zip(names, refs, strict=True)))
    r.layer_out[...] = r.after[...] + r.moe_out[...]
    r.input_grad[...] = r.after_grad[...] + r.normed_out[...].reshape(96, 2048)
    r.gate_w[...] = r.gate_part[...]
    r.up_w[...] = r.up_part[...]
    r.down_w[...] = r.down_part[...]
    r.query_w[...] = r.query_part[...]
    r.out_w[...] = r.out_part[...]
    r.gate_grad[...] = r.gate_grad_part[...]
    r.key_w[...] = r.pair_w[:, :128]
    r.value_w[...] = r.pair_w[:, 128:]
    r.attn_gain[...] = r.small[:16]
    r.moe_gain[...] = r.small[16:32]
    r.query_gain[...] = r.small[32:33]
    r.key_gain[...] = r.small[33:34]
    diagonal = lax.broadcasted_iota(jnp.int32, (8, 128), 0) == lax.broadcasted_iota(
        jnp.int32, (8, 128), 1
    )
    peaks = jnp.sum(jnp.where(diagonal, r.small[40:], 0.0), axis=0, keepdims=True)
    r.clip[...] = (clip_limit / jnp.maximum(peaks, clip_limit))[:, :8]


def finish(near):
    outs = dict(
        layer_out=(96, 2048),
        input_grad=(96, 2048),
        gate_w=(256, 768),
        up_w=(256, 768),
        down_w=(256, 768),
        query_w=(64, 1024),
        out_w=(64, 1024),
        gate_grad=(3, 8, 32),
        key_w=(64, 128),
        value_w=(64, 128),
        attn_gain=(16, 128),
        moe_gain=(16, 128),
        query_gain=(1, 128),
        key_gain=(1, 128),
        clip=(1, 8),
    )
    results = pl.pallas_call(
        functools.partial(finish_kernel, list(near) + list(outs)),
        out_shape=[jax.ShapeDtypeStruct(size, jnp.float32) for size in outs.values()],
        in_specs=[VMEM] * len(near),
        out_specs=[VMEM] * len(outs),
        compiler_params=pltpu.CompilerParams(vmem_limit_bytes=62 << 20),
        name="finish",
    )(*near.values())
    return types.SimpleNamespace(**dict(zip(outs, results, strict=True)))


def shards(
    hidden_in,
    segments,
    attn_gain,
    query_gain,
    key_gain,
    w_query,
    key_weight_matrix,
    value_weight_matrix,
    w_out,
    moe_gain,
    expert_ids,
    gate_values,
    capacity,
    w_gate,
    w_up,
    w_down,
    cotangent,
):
    attn_wide, moe_wide = attn_gain.reshape(16, 128), moe_gain.reshape(16, 128)
    query_row, key_row = query_gain[None], key_gain[None]
    ids, gates = expert_ids.swapaxes(1, 2), gate_values.swapaxes(1, 2)
    cosine, sine = rotary()
    first = front(
        dict(
            hidden=hidden_in,
            w_key=key_weight_matrix,
            w_value=value_weight_matrix,
            cosine=cosine,
            sine=sine,
            w_query=w_query,
            cotangent=cotangent,
            w_out=w_out,
        ),
        dict(
            attn_gain=attn_wide,
            query_gain=query_row,
            key_gain=key_row,
            segments=segments,
            ids=ids,
            gates=gates,
            capacity=capacity,
        ),
    )
    second = moe(
        dict(w_gate=w_gate[0], w_up=w_up[0], w_down=w_down[0], grads=first.grads),
        dict(
            after=first.after,
            cotangent=cotangent,
            moe_gain=moe_wide,
            ids=ids,
            table=first.table,
            info_in=first.info_in,
        ),
    )
    done = back(
        dict(
            branch=second.branch,
            w_out=w_out,
            w_query=w_query,
            gate=second.full_gate.reshape(4, 2, 256, 768),
            up=second.full_up.reshape(4, 2, 256, 768),
            down=second.full_down.reshape(4, 2, 256, 768),
            produced=second.produced,
            gate_begun=second.gate_slots,
            up_begun=second.up_slots,
            hidden=hidden_in,
            mixed=first.mixed,
            query=first.query,
            query_raw=first.query_raw,
            pair=first.pair,
            cosine=cosine,
            sine=sine,
            w_key=key_weight_matrix,
            w_value=value_weight_matrix,
        ),
        dict(
            table=first.table,
            key_raw=first.key_raw,
            log_sum=first.log_sum,
            segments=segments,
            attn_gain=attn_wide,
            query_gain=query_row,
            key_gain=key_row,
            moe_gain_part=second.gain_part,
            peaks=first.peaks,
        ),
    )
    last = finish(
        dict(
            after=first.after,
            moe_out=done.moe_out,
            after_grad=second.after_grad,
            normed_out=done.normed_out,
            small=done.small_out,
            pair_w=done.pair_w_out,
            gate_part=done.gate_out,
            up_part=done.up_out,
            down_part=done.down_out,
            query_part=done.query_w_out,
            out_part=done.out_w_out,
            gate_grad_part=second.gate_grad,
        )
    )
    layer_out = last.layer_out.reshape(cotangent.shape)
    input_grad = last.input_grad.reshape(cotangent.shape)
    gate_grad = last.gate_grad.swapaxes(1, 2)
    w_key_grad, w_value_grad = last.key_w, last.value_w
    w_query_grad, w_out_grad = last.query_w, last.out_w
    w_gate_grad, w_up_grad, w_down_grad = last.gate_w[None], last.up_w[None], last.down_w[None]
    attn_gain_grad, moe_gain_grad = last.attn_gain.reshape(2048), last.moe_gain.reshape(2048)
    query_gain_grad, key_gain_grad = last.query_gain.reshape(128), last.key_gain.reshape(128)
    head_clip_scale = last.clip.reshape(8)
    return (
        layer_out,
        input_grad,
        attn_gain_grad,
        query_gain_grad,
        key_gain_grad,
        w_query_grad,
        w_key_grad,
        w_value_grad,
        w_out_grad,
        moe_gain_grad,
        gate_grad,
        w_gate_grad,
        w_up_grad,
        w_down_grad,
        head_clip_scale,
    )


def solution(mesh):
    in_specs = (
        P("dp", "context", None),
        P("dp", None),
        P(),
        P(),
        P(),
        P(None, "experts"),
        P(None, "experts"),
        P(None, "experts"),
        P(None, "experts"),
        P(),
        P("dp", ("context", "experts"), None),
        P("dp", ("context", "experts"), None),
        P(),
        P(("dp", "experts"), None, None),
        P(("dp", "experts"), None, None),
        P(("dp", "experts"), None, None),
        P("dp", ("context", "experts"), None),
    )
    out_specs = (
        P("dp", ("context", "experts"), None),
        P("dp", ("context", "experts"), None),
        P(),
        P(),
        P(),
        P(("dp", "context"), "experts"),
        P(("dp", "context"), "experts"),
        P(("dp", "context"), "experts"),
        P(("dp", "context"), "experts"),
        P(),
        P("dp", ("context", "experts"), None),
        P(("dp", "experts"), "context", None),
        P(("dp", "experts"), "context", None),
        P(("dp", "experts"), "context", None),
        P("experts"),
    )
    return jax.shard_map(shards, mesh=mesh, in_specs=in_specs, out_specs=out_specs, check_vma=False)
```

```python
import functools
import itertools
import types

import jax
import jax.numpy as jnp
import numpy as np
from jax import lax
from jax.experimental import pallas as pl
from jax.experimental.pallas import tpu as pltpu
from jax.sharding import PartitionSpec as P

HEAD_SIZE = 128
MESH = pl.DeviceIdType.MESH
VMEM = pl.BlockSpec(memory_space=pltpu.VMEM)
ANY = pl.BlockSpec(memory_space=pl.ANY)
SMEM = pl.BlockSpec(memory_space=pltpu.SMEM)


epsilon = 1e-06
rope_base = 1000000.0
clip_limit = 1.0
masked_value = -1e30


def rotary():
    inverse = 1.0 / rope_base ** (np.arange(0, HEAD_SIZE, 2) / HEAD_SIZE)
    angle = np.arange(1024)[:, None] * inverse[None, :]
    cosine = np.concatenate([np.cos(angle), np.cos(angle)], axis=-1)
    sine = np.concatenate([-np.sin(angle), np.sin(angle)], axis=-1)
    shape = (8, 128, HEAD_SIZE)
    return (
        jnp.asarray(cosine.reshape(shape), jnp.float32),
        jnp.asarray(sine.reshape(shape), jnp.float32),
    )


def contract_last(left, right):
    return lax.dot_general(
        left, right, (((1,), (1,)), ((), ())), preferred_element_type=jnp.float32
    )


def contract_first(left, right):
    return lax.dot_general(
        left, right, (((0,), (0,)), ((), ())), preferred_element_type=jnp.float32
    )


class Place:
    def __init__(self):
        dp = lax.axis_index("dp")
        context = lax.axis_index("context")
        self.dp, self.context, self.y = dp, context, lax.axis_index("experts")
        self.core, self.z_hi = lax.rem(dp, 2), dp // 2
        self.x, self.z_lo = context // 2, lax.rem(context, 2)
        self.z = self.z_hi * 2 + self.z_lo
        self.spot = (self.core, self.z_hi, self.y)

    def at(self, x=None, y=None, z=None, core=None):
        x = self.x if x is None else x
        y = self.y if y is None else y
        z = self.z if z is None else z
        core = self.core if core is None else core
        return (z // 2 * 2 + core, x * 2 + lax.rem(z, 2), y)

    def x_by(self, step):
        return lax.rem(self.x + step, 4)

    def y_by(self, step):
        return lax.rem(self.y + step, 4)

    def z_by(self, step):
        return lax.rem(self.z + step, 4)


class Net:
    def __init__(self, send, recv, here=None):
        self.send, self.recv, self.copies = send, recv, []
        self.here, self.loads = here, 0

    def copy(self, src, dst, device):
        spot = len(self.copies)
        made = pltpu.make_async_remote_copy(
            src_ref=src,
            dst_ref=dst,
            send_sem=self.send.at[spot],
            recv_sem=self.recv.at[spot],
            device_id=device,
            device_id_type=MESH,
        )
        made.start()
        self.copies.append(made)
        return made

    def load(self, src, dst):
        made = pltpu.make_async_copy(src, dst, self.here.at[self.loads])
        self.loads += 1
        made.start()
        return made

    def sent(self, made):
        made.wait_send()
        self.copies = [None if one is made else one for one in self.copies]

    def finish(self):
        for made in self.copies:
            if made is not None:
                made.wait_send()


def greet(devices):
    barrier = pltpu.get_barrier_semaphore()
    for device in devices:
        pl.semaphore_signal(barrier, inc=1, device_id=device, device_id_type=MESH)
    return lambda: pl.semaphore_wait(barrier, len(devices))


def wide(ref):
    values = ref[...].astype(jnp.float32)
    return jnp.concatenate([values[step : step + 1] for step in range(16)], axis=1)


def add_into(target, parts, block=32):
    rows = target.shape[-2]
    block = min(block, rows)
    for lead in itertools.product(*[range(size) for size in target.shape[:-2]]):

        def body(step, carry, lead=lead):
            spot = lead + (pl.ds(pl.multiple_of(step * block, block), block),)
            total = parts[0][spot].astype(jnp.float32)
            for part in parts[1:]:
                total = total + part[spot].astype(jnp.float32)
            target[spot] = total.astype(target.dtype)
            return carry

        lax.fori_loop(0, rows // block, body, 0)


def ring_reduce(net, plus, minus, own, slots, target, held=None, begun=None):
    held = own if held is None else held
    done = 0 if begun is None else begun.shape[0]
    if done == 4:
        loads = [net.load(begun, slots.at[pl.ds(0, 4)])]
    elif done == 2:
        loads = [net.load(begun.at[step], slots.at[step * 2]) for step in range(2)]
    else:
        first_plus = net.copy(own(2, 0), slots.at[0], plus)
        first_minus = net.copy(own(2, 1), slots.at[2], minus)
    if done != 4:
        side_plus = net.copy(own(1, 1), slots.at[1], plus)
        side_minus = net.copy(own(3, 0), slots.at[3], minus)
    yield
    if done:
        for load in loads:
            load.wait()
    else:
        first_plus.wait_recv()
        first_minus.wait_recv()
    add_into(slots.at[0], [slots.at[0], held(1, 0)])
    last_plus = net.copy(slots.at[0], slots.at[4], plus)
    add_into(slots.at[2], [slots.at[2], held(3, 1)])
    last_minus = net.copy(slots.at[2], slots.at[5], minus)
    yield
    if done != 4:
        side_minus.wait_recv()
        side_plus.wait_recv()
    last_plus.wait_recv()
    add_into(target(0), [held(0, 0), slots.at[3], slots.at[4]])
    last_minus.wait_recv()
    add_into(target(1), [held(0, 1), slots.at[1], slots.at[5]])


def x_first(net, me, source, slots, middle, other, out, held=None, begun=None):
    staged = None
    if held is not None:
        order = {(1, 0): 0, (3, 1): 1, (0, 0): 2, (0, 1): 3}
        loads = [
            net.load(source.at[me.x_by(step), half], held.at[spot])
            for (step, half), spot in order.items()
        ]

        def staged(step, half):
            return held.at[order[step, half]]

    ring = ring_reduce(
        net,
        me.at(x=me.x_by(1)),
        me.at(x=me.x_by(3)),
        lambda step, half: source.at[me.x_by(step), half],
        slots,
        lambda half: middle.at[half],
        staged,
        begun,
    )
    next(ring)
    yield
    if held is not None:
        for load in loads:
            load.wait()
    yield from ring
    across = net.copy(middle.at[1 - me.z_lo], other, me.at(z=me.z + 1 - 2 * me.z_lo))
    yield
    across.wait_recv()
    add_into(out, [middle.at[me.z_lo], other])


def core_pair(net, me, sending, other, middle):
    across = net.copy(sending, other, me.at(core=1 - me.core))
    yield
    net.sent(across)
    across.wait_recv()
    add_into(middle, [middle, other])


def dense_x_first(net, me, sending, other, middle, slots, corner, last, out):
    yield from core_pair(net, me, sending, other, middle)
    yield from ring_reduce(
        net,
        me.at(x=me.x_by(1)),
        me.at(x=me.x_by(3)),
        lambda step, half: middle.at[half, me.x_by(step)],
        slots,
        lambda half: corner.at[half],
    )
    half_rows = corner.shape[2] // 2
    yield from ring_reduce(
        net,
        me.at(z=me.z_by(1)),
        me.at(z=me.z_by(3)),
        lambda step, half: corner.at[
            me.z_by(step) // 2, lax.rem(me.z_by(step), 2), pl.ds(half * half_rows, half_rows)
        ],
        last,
        lambda half: out.at[pl.ds(half * half_rows, half_rows)],
    )


def dense_z_first(net, me, sending, other, middle, slots, corner, last, out):
    yield from core_pair(net, me, sending, other, middle)
    yield from ring_reduce(
        net,
        me.at(z=me.z_by(1)),
        me.at(z=me.z_by(3)),
        lambda step, half: middle.at[
            me.z_by(step) // 2, pl.ds(half * 2, 2), lax.rem(me.z_by(step), 2)
        ],
        slots,
        lambda half: corner.at[pl.ds(half * 2, 2)],
    )
    half_rows = corner.shape[1] // 2
    yield from ring_reduce(
        net,
        me.at(x=me.x_by(1)),
        me.at(x=me.x_by(3)),
        lambda step, half: corner.at[me.x_by(step), pl.ds(half * half_rows, half_rows)],
        last,
        lambda half: out.at[pl.ds(half * half_rows, half_rows)],
    )


def all_sum(net, devices, spot, own, slots, most):
    slots[spot] = own[...]
    sent = [net.copy(own, slots.at[spot], device) for device in devices]
    yield
    for made in sent:
        made.wait_recv()
    count = slots.shape[0]
    total = slots[0]
    peak = slots[0, most:]
    for step in range(1, count):
        total = total + slots[step]
        peak = jnp.maximum(peak, slots[step, most:])
    for made in sent:
        net.sent(made)
    own[:most] = total[:most]
    own[most:] = peak


def all_small(net, me, working, by_core, by_x, by_z, by_y, out):
    yield from all_sum(net, [me.at(core=1 - me.core)], me.core, working, by_core, 40)
    yield from all_sum(net, [me.at(x=me.x_by(s)) for s in (1, 2, 3)], me.x, working, by_x, 40)
    yield from all_sum(net, [me.at(z=me.z_by(s)) for s in (1, 2, 3)], me.z, working, by_z, 40)
    out[40:] = working[40:]
    yield from all_sum(net, [me.at(y=me.y_by(s)) for s in (1, 2, 3)], me.y, working, by_y, 40)
    out[:40] = working[:40]


OFFSETS = [(a, b) for a in (2, 0, 3, 1) for b in (0, 1, 3, 2) if a or b]


def peer(me, a, b):
    z = me.z if a < 2 else lax.rem(me.z + 2, 4)
    core = me.core if a % 2 == 0 else 1 - me.core
    y = me.y_by(b)
    return (core, z // 2, y), me.at(z=z, core=core, y=y)


def peers(me):
    return [peer(me, a, b)[1] for a, b in OFFSETS]


def gather_rows(table, home, store):
    def body(step, carry):
        columns = pl.ds(pl.multiple_of(step * 256, 256), 256)
        rows = home[:, :, :, :, columns].reshape(768, 256)
        total = contract_first(table[...], rows)
        store(columns, total[:96])
        return carry

    lax.fori_loop(0, home.shape[4] // 256, body, 0)


def turned(values):
    return pltpu.roll(values, 64, 1)


def column_of(row):
    eye = lax.broadcasted_iota(jnp.int32, (128, 128), 0) == lax.broadcasted_iota(
        jnp.int32, (128, 128), 1
    )
    return jnp.sum(jnp.where(eye, row, 0.0), axis=1, keepdims=True)


def norm_back(gradient, raw, gain):
    inverse = lax.rsqrt(jnp.mean(raw * raw, axis=-1, keepdims=True) + epsilon)
    normal = raw * inverse
    scaled = gradient * gain
    result = inverse * (scaled - normal * jnp.mean(scaled * normal, axis=-1, keepdims=True))
    return result, jnp.sum(gradient * normal, axis=0, keepdims=True)


def back_kernel(names, *refs):
    r = types.SimpleNamespace(**dict(zip(names, refs, strict=True)))
    low, full = jnp.bfloat16, jnp.float32
    score_scale = HEAD_SIZE ** (-0.5)
    me = Place()
    net = Net(r.send, r.recv, r.here)
    fetch = Fetch(net)
    fetch.start("hidden", r.hidden, r.hidden_held)
    greeted = greet(
        [
            me.at(x=me.x_by(1)),
            me.at(x=me.x_by(3)),
            me.at(z=me.z_by(1)),
            me.at(z=me.z_by(3)),
            me.at(x=me.x_by(2)),
        ]
        + peers(me)
    )
    gains = r.gain_rows
    gains[...] = wide(r.attn_gain)
    greeted()

    branch, whole = r.branch, r.whole
    above, below = me.at(y=me.y_by(1)), me.at(y=me.y_by(3))
    to_above = net.copy(branch, whole.at[:, me.y], above)
    to_below = net.copy(branch, whole.at[:, me.y], below)
    own_branch = net.load(branch, whole.at[:, me.y])
    weight = r.weight
    load_out = net.load(r.w_out, weight)
    gate = x_first(
        net, me, r.gate, r.gate_slots, r.gate_middle, r.gate_other, r.gate_out, r.gate_held,
        r.gate_begun,
    )
    up = x_first(
        net, me, r.up, r.up_slots, r.up_middle, r.up_other, r.up_out, r.up_held, r.up_begun
    )
    down = x_first(
        net, me, r.down, r.down_slots, r.down_middle, r.down_other, r.down_out, r.down_held
    )
    next(gate)
    next(gate)
    next(up)
    produced, home, table = r.produced, r.home, r.table
    start = me.core * 384 + me.z_hi * 192 + me.y * 48
    mine = pl.ds(pl.multiple_of(start, 16), 48)
    home_came = []

    def bring_home(offsets):
        for a, b in offsets:
            device = peer(me, a, b)[1]
            home_came.append(net.copy(produced.at[SLOTS[a, b]], home.at[mine], device))

    straight = [(2, 0), (3, 0)]
    bring_home(straight)
    home_own = net.load(produced.at[0, 0], home.at[mine])
    next(up)
    fetch.start("pair", r.pair, r.pair_held)
    fetch.start("query", r.query, r.query_held)
    fetch.start("query_raw", r.query_raw, r.query_raw_held)
    fetch.start("cosine", r.cosine.at[me.context], r.cosine_held)
    fetch.start("sine", r.sine.at[me.context], r.sine_held)
    fetch.start("mixed", r.mixed, r.mixed_held)
    fetch.start("w_key", r.w_key, r.key_weight)
    fetch.start("w_value", r.w_value, r.value_weight)

    hidden, inverse = fetch.hidden, r.inverse
    for s in range(3):
        rows = slice(s * 128, s * 128 + 128)
        values = hidden[s].astype(full)
        root = lax.rsqrt(jnp.mean(values * values, axis=-1, keepdims=True) + epsilon)
        inverse[rows, :] = jnp.broadcast_to(root, (128, 128))
        for step in range(8):
            run = slice(step * 256, step * 256 + 256)
            tile = hidden[s, :, run].astype(full) * root * gains[:, run]
            r.normed[run, rows] = tile.T.astype(low)

    first, second = pl.ds(0, 1024), pl.ds(1024, 1024)
    to_above.wait_recv()
    passed = whole.at[:, me.y_by(3), :, first]
    far_above = net.copy(passed, passed, above)
    to_below.wait_recv()
    passed = whole.at[:, me.y_by(1), :, second]
    far_below = net.copy(passed, passed, below)
    own_branch.wait()
    load_out.wait()
    next(gate)
    far_above.wait_recv()
    far_below.wait_recv()

    bring_home([offset for offset in OFFSETS if offset not in straight])

    heads_grad = r.heads_grad

    def heads_step(step, carry):
        columns = pl.ds(pl.multiple_of(step * 256, 256), 256)
        heads_grad[:, columns] = jnp.dot(
            whole[...].reshape(384, 2048), weight[:, columns], preferred_element_type=full
        ).astype(low)
        return carry

    lax.fori_loop(0, 4, heads_step, 0)
    load_query = net.load(r.w_query, weight)

    query_low = heads_grad

    def own_input(columns):
        return hidden[:, :, columns].reshape(384, 256).astype(full)

    def normed(columns, right):
        return jnp.dot(r.normed[columns, :], right, preferred_element_type=full)

    def whole_part(columns):
        return whole[:, :, :, columns].reshape(384, 256)

    def branch_weight(columns, right):
        return contract_first(whole_part(columns), right)

    def weigh(core, left, right, target):
        def body(step, carry):
            z_hi, part = step // 2, lax.rem(step, 2)
            columns = pl.ds(pl.multiple_of((z_hi * 2 + core) * 512 + part * 256, 256), 256)
            made = left(columns, right[...]).astype(low)
            target[z_hi, pl.ds(part * 2, 2)] = made.reshape(2, 2, 64, right.shape[1])
            return carry

        lax.fori_loop(0, 4, body, 0)

    def dense(order, left, right, sending, other, middle, *more):
        weigh(1 - me.core, left, right, sending)
        task = order(net, me, sending, other, middle, *more)
        next(task)
        weigh(me.core, left, right, middle)
        return task

    out_w = dense(
        dense_z_first, branch_weight, fetch.mixed, r.sending, r.out_w_other, r.out_w_middle,
        r.out_w_slots, r.out_w_corner, r.out_w_last, r.out_w_out,
    )
    next(down)

    query, query_raw, pair = fetch.query, fetch.query_raw, fetch.pair
    cosine, sine = fetch.cosine, fetch.sine
    gain_query, gain_key = r.query_gain[...].astype(full), r.key_gain[...].astype(full)
    bias, key_sum, value_sum = r.bias, r.key_sum, r.value_sum
    pair_grad, gain_part = r.pair_grad, r.gain_part
    gain_part[...] = jnp.zeros((8, 128), full)

    def rope_back(gradient):
        return gradient * cosine[...] - turned(gradient) * sine[...]

    def attend(s):
        here = pl.ds(s * 128, 128)
        bias[...] = mask_bias(me, r.segments, s)
        key_sum[...] = jnp.zeros_like(key_sum)
        value_sum[...] = jnp.zeros_like(value_sum)

        def two_heads(step, carry):
            columns = pl.ds(pl.multiple_of(step * 256, 256), 256)

            def stacked(ref):
                both = ref[here, columns]
                return jnp.concatenate([both[:, :128], both[:, 128:]], axis=0)

            q, d = stacked(query), stacked(heads_grad)
            keys, values = pair[0, s], pair[1, s]
            lines = r.log_sum
            logs = jnp.concatenate(
                [column_of(lines[s * 8 + step * 2]), column_of(lines[s * 8 + step * 2 + 1])], axis=0
            )
            score = contract_last(q, keys) * score_scale
            score = score + jnp.concatenate([bias[...], bias[...]], axis=0)
            prob = jnp.exp(score - logs)
            prob_grad = contract_last(d, values)
            delta = jnp.sum(prob * prob_grad, axis=-1, keepdims=True)
            score_grad = (prob * (prob_grad - delta)).astype(low)
            value_sum[...] += contract_first(prob.astype(low), d)
            key_sum[...] += contract_first(score_grad, q)
            turned_grad = jnp.dot(score_grad, keys, preferred_element_type=full) * score_scale
            for half in range(2):
                run = pl.ds(pl.multiple_of(step * 256 + half * 128, 128), 128)
                grad, part = norm_back(
                    rope_back(turned_grad[half * 128 : half * 128 + 128]),
                    query_raw[here, run],
                    gain_query,
                )
                heads_grad[here, run] = grad.astype(low)
                gain_part[0:1, :] += part
            return carry

        lax.fori_loop(0, 4, two_heads, 0)
        pair_grad[s, :, :, 0] = (key_sum[...] * score_scale).astype(low).reshape(4, 2, 128, 128)
        pair_grad[s, :, :, 1] = value_sum[...].astype(low).reshape(4, 2, 128, 128)
        return x_first(
            net, me, pair_grad.at[s], r.pair_slots.at[s], r.pair_middle.at[s], r.pair_other.at[s],
            r.pair_out.at[s],
        )

    pairs = [attend(0)]
    next(pairs[0])
    next(out_w)
    pairs.append(attend(1))
    next(pairs[1])
    next(pairs[0])
    next(up)
    pairs.append(attend(2))
    next(pairs[2])
    next(pairs[1])
    next(pairs[0])

    query_w = dense(
        dense_x_first, normed, query_low, r.sending, r.query_w_other, r.query_w_middle,
        r.query_w_slots, r.query_w_corner, r.query_w_last, r.query_w_out,
    )
    next(pairs[2])
    next(pairs[1])
    next(query_w)
    next(pairs[2])

    load_query.wait()
    net.sent(far_above)
    net.sent(far_below)

    def query_step(step, carry):
        columns = pl.ds(pl.multiple_of(step * 256, 256), 256)
        made = contract_last(query_low[...], weight[columns, :])
        whole[:, :, :, columns] = made.astype(low).reshape(3, 4, 32, 256)
        return carry

    lax.fori_loop(0, 8, query_step, 0)
    next(down)

    pair_out, key_raw, pair_low = r.pair_out, r.key_raw, r.pair_low
    for s in range(3):
        next(pairs[s], None)
        rows = slice(s * 128, s * 128 + 128)
        grad, part = norm_back(rope_back(pair_out[s, 0]), key_raw[rows, :], gain_key)
        gain_part[1:2, :] += part
        pair_low[rows, :128] = grad.astype(low)
        pair_low[rows, 128:] = pair_out[s, 1].astype(low)

    w_key, w_value = fetch.w_key, fetch.w_value
    small = r.small
    normed_part = r.normed_part

    def normed_step(step, carry):
        columns = pl.ds(pl.multiple_of(step * 256, 256), 256)
        made = whole_part(columns).astype(full)
        made = made + contract_last(pair_low[:, :128], w_key[columns, :])
        made = made + contract_last(pair_low[:, 128:], w_value[columns, :])
        normal = own_input(columns) * inverse[:, 0:1]
        normed_part[:, columns] = jnp.sum(made * normal, axis=0, keepdims=True)
        whole[:, :, :, columns] = made.astype(low).reshape(3, 4, 32, 256)
        return carry

    lax.fori_loop(0, 8, normed_step, 0)
    normed_out = r.normed_out
    normed_sum = ring_reduce(
        net,
        above,
        below,
        lambda step, half: whole.at[:, me.y_by(step), :, pl.ds(half * 1024, 1024)],
        r.normed_slots,
        lambda half: normed_out.at[:, :, pl.ds(half * 1024, 1024)],
    )
    next(normed_sum)
    for step in range(16):
        run = slice(step * 128, step * 128 + 128)
        small[step : step + 1, :] = normed_part[:, run]
        small[16 + step : 17 + step, :] = r.moe_gain_part[:, run]
    small[32:40, :] = gain_part[...]
    small[40:, :] = r.peaks[...]
    smalls = all_small(
        net, me, small, r.by_core, r.by_x, r.by_z, r.by_y, r.small_out
    )
    pair_w = dense(
        dense_x_first, normed, pair_low, r.pair_sending, r.pair_w_other, r.pair_w_middle,
        r.pair_w_slots, r.pair_w_corner, r.pair_w_last, r.pair_w_out,
    )
    next(out_w)

    for made in home_came:
        made.wait_recv()
    home_own.wait()
    home_loads = [
        net.load(home.at[:, pl.ds(half * 1024, 1024)], weight.at[pl.ds(half * 768, 768)])
        for half in range(2)
    ]
    next(pair_w)
    next(smalls)
    moe_out = r.moe_out
    for half in range(2):
        home_loads[half].wait()

        def gather(step, carry, half=half):
            columns = pl.ds(pl.multiple_of(step * 256, 256), 256)
            total = contract_first(table[...], weight[half * 768 : half * 768 + 768, columns])
            moe_out[:, pl.ds(pl.multiple_of(half * 1024 + step * 256, 256), 256)] = total[:96]
            return carry

        lax.fori_loop(0, 4, gather, 0)

    def rest(*tasks):
        for task in tasks:
            next(task, None)

    rest(normed_sum, query_w, out_w, down, smalls)

    next(normed_sum, None)
    for s in range(3):
        rows = pl.ds(pl.multiple_of(me.y * 32, 32), 32)
        grad, _ = norm_back(normed_out[s], hidden[s, rows, :].astype(full), gains[...])
        normed_out[s] = grad

    rest(pair_w, out_w, query_w, down, smalls, gate, up)
    rest(pair_w, out_w, query_w, smalls)
    tasks = [pair_w, out_w, smalls, query_w, gate, up, down]
    while tasks:
        for task in list(tasks):
            if next(task, "end") == "end":
                tasks.remove(task)
    net.finish()


def dense_slots(columns, corner):
    low = jnp.bfloat16
    return [
        pltpu.VMEM((2, 4, 2, 64, columns), low),
        pltpu.VMEM((2, 4, 2, 64, columns), low),
        pltpu.VMEM((6, 2, 64, columns), low),
        pltpu.VMEM(corner + (64, columns), low),
        pltpu.VMEM((6, 32, columns), low),
    ]


def back(far, near):
    low, full = jnp.bfloat16, jnp.float32
    outs = dict(
        gate_out=(256, 768),
        up_out=(256, 768),
        down_out=(256, 768),
        query_w_out=(64, 1024),
        pair_w_out=(64, 256),
        out_w_out=(64, 1024),
        small_out=(48, 128),
        normed_out=(3, 32, 2048),
        moe_out=(96, 2048),
    )
    scratch = dict(
        gain_rows=pltpu.VMEM((1, 2048), full),
        hidden_held=pltpu.VMEM((3, 128, 2048), low),
        pair_held=pltpu.VMEM((2, 3, 1024, 128), low),
        query_held=pltpu.VMEM((384, 1024), low),
        query_raw_held=pltpu.VMEM((384, 1024), full),
        cosine_held=pltpu.VMEM((128, 128), full),
        sine_held=pltpu.VMEM((128, 128), full),
        mixed_held=pltpu.VMEM((384, 1024), low),
        key_weight=pltpu.VMEM((2048, 128), low),
        value_weight=pltpu.VMEM((2048, 128), low),
        whole=pltpu.VMEM((3, 4, 32, 2048), low),
        weight=pltpu.VMEM((2048, 1024), low),
        inverse=pltpu.VMEM((384, 128), full),
        normed=pltpu.VMEM((2048, 384), low),
        heads_grad=pltpu.VMEM((384, 1024), low),
        bias=pltpu.VMEM((128, 1024), full),
        key_sum=pltpu.VMEM((1024, 128), full),
        value_sum=pltpu.VMEM((1024, 128), full),
        pair_grad=pltpu.VMEM((3, 4, 2, 2, 128, 128), low),
        pair_slots=pltpu.VMEM((3, 6, 2, 128, 128), low),
        pair_middle=pltpu.VMEM((3, 2, 2, 128, 128), low),
        pair_other=pltpu.VMEM((3, 2, 128, 128), low),
        pair_out=pltpu.VMEM((3, 2, 128, 128), full),
        pair_low=pltpu.VMEM((384, 256), low),
        gain_part=pltpu.VMEM((8, 128), full),
        normed_part=pltpu.VMEM((1, 2048), full),
        normed_slots=pltpu.VMEM((6, 3, 32, 1024), low),
        small=pltpu.VMEM((48, 128), full),
        by_core=pltpu.VMEM((2, 48, 128), full),
        by_x=pltpu.VMEM((4, 48, 128), full),
        by_z=pltpu.VMEM((4, 48, 128), full),
        by_y=pltpu.VMEM((4, 48, 128), full),
        down_slots=pltpu.VMEM((6, 256, 768), low),
        down_middle=pltpu.VMEM((2, 256, 768), low),
        down_other=pltpu.VMEM((256, 768), low),
        down_held=pltpu.VMEM((4, 256, 768), low),
        gate_slots=pltpu.VMEM((6, 256, 768), low),
        gate_middle=pltpu.VMEM((2, 256, 768), low),
        gate_other=pltpu.VMEM((256, 768), low),
        gate_held=pltpu.VMEM((4, 256, 768), low),
        up_slots=pltpu.VMEM((6, 256, 768), low),
        up_middle=pltpu.VMEM((2, 256, 768), low),
        up_other=pltpu.VMEM((256, 768), low),
        up_held=pltpu.VMEM((4, 256, 768), low),
        sending=pltpu.VMEM((2, 4, 2, 64, 1024), low),
        pair_sending=pltpu.VMEM((2, 4, 2, 64, 256), low),
        query_w_other=None,
        query_w_middle=None,
        query_w_slots=None,
        query_w_corner=None,
        query_w_last=None,
        pair_w_other=None,
        pair_w_middle=None,
        pair_w_slots=None,
        pair_w_corner=None,
        pair_w_last=None,
        out_w_other=None,
        out_w_middle=None,
        out_w_slots=None,
        out_w_corner=None,
        out_w_last=None,
        send=pltpu.SemaphoreType.DMA((116,)),
        recv=pltpu.SemaphoreType.DMA((116,)),
        here=pltpu.SemaphoreType.DMA((34,)),
    )
    dense = dense_slots(1024, (2, 2)) + dense_slots(256, (2, 2)) + dense_slots(1024, (4,))
    scratch = {name: one or dense.pop(0) for name, one in scratch.items()}
    outs = {name: jax.ShapeDtypeStruct(size, full) for name, size in outs.items()}
    far_outs = dict(home=jax.ShapeDtypeStruct((768, 2048), low))
    return call(back_kernel, 0, far, near, outs, far_outs, scratch)


class Fetch:
    def __init__(self, net):
        self.net, self.waiting, self.held = net, {}, {}

    def start(self, name, source, target):
        self.waiting[name] = self.net.load(source, target)
        self.held[name] = target

    def __getattr__(self, name):
        if name in self.waiting:
            self.waiting.pop(name).wait()
        return self.held[name]


def token_table(ids, gates, capacity, table, info):
    low, full = jnp.bfloat16, jnp.float32
    expert = lax.broadcasted_iota(jnp.int32, (16, 32), 0)
    chosen, share = [], []
    for s in range(3):
        chosen_here = jnp.zeros((16, 32), full)
        share_here = jnp.zeros((16, 32), full)
        for k in range(8):
            named = ids[s, k : k + 1, :] == expert
            chosen_here = chosen_here + jnp.where(named, 1.0, 0.0)
            share_here = share_here + jnp.where(named, gates[s, k : k + 1, :], 0.0)
        chosen.append(chosen_here)
        share.append(share_here)
    none = jnp.zeros((16, 32), full)
    chosen = jnp.concatenate(chosen + [none], axis=1)
    share = jnp.concatenate(share + [none], axis=1)
    row = lax.broadcasted_iota(jnp.int32, (16, 128), 0)
    limit = jnp.zeros((16, 128), full)
    for e in range(16):
        limit = jnp.where(row == e, capacity[e].astype(full), limit)
    earlier = lax.broadcasted_iota(jnp.int32, (128, 128), 0) < lax.broadcasted_iota(
        jnp.int32, (128, 128), 1
    )
    before = jnp.dot(
        chosen.astype(low), jnp.where(earlier, 1.0, 0.0).astype(low), preferred_element_type=full
    )
    slot = jnp.where((chosen > 0.0) & (before < limit), before, -1.0)
    spot = lax.broadcasted_iota(jnp.int32, (48, 128), 0).astype(full)
    for place in range(16):
        core, z_hi, y = place // 8, place // 4 % 2, place % 4
        e = (z_hi * 2 + core) * 4 + y
        mask = jnp.where(slot[e : e + 1, :] == spot, 1.0, 0.0)
        table[place * 48 : place * 48 + 48, :] = mask.astype(low)
        info[core, z_hi, y] = jnp.concatenate(
            [slot[e : e + 1, :], share[e : e + 1, :], jnp.zeros((6, 128), full)], axis=0
        )


PHASES = (
    [(0, 0), (0, 1), (0, 3), (2, 0), (1, 0), (1, 1), (1, 3), (3, 0)],
    [(0, 2), (2, 1), (2, 3), (2, 2), (1, 2), (3, 1), (3, 3), (3, 2)],
)
SLOTS = {offset: (phase, spot) for phase in (0, 1) for spot, offset in enumerate(PHASES[phase])}


def spread(net, me, everyone, source, came):
    above, below = me.at(y=me.y_by(1)), me.at(y=me.y_by(3))
    sibling = me.at(core=1 - me.core)
    a, z_hi = (2, 1 - me.z_hi) if source is None else (0, me.z_hi)

    def block(b):
        return everyone.at[me.core, z_hi, me.y_by(b)]

    def half(b, part):
        return block(b).at[:, pl.ds(part * 16, 16)]

    def forward(view, device):
        return net.copy(view, view, device)

    source = block(0) if source is None else source
    up = net.copy(source, block(0), above)
    down = net.copy(source, block(0), below)
    came[a + 1, 0] = net.copy(source, block(0), sibling)
    yield
    up.wait_recv()
    far_up = forward(half(3, 0), above)
    came[a + 1, 3] = forward(block(3), sibling)
    down.wait_recv()
    far_down = forward(half(1, 1), below)
    came[a + 1, 1] = forward(block(1), sibling)
    yield
    far_up.wait_recv()
    far_down.wait_recv()
    came[a + 1, 2] = forward(block(2), sibling)
    yield


def moe_kernel(names, *refs):
    r = types.SimpleNamespace(**dict(zip(names, refs, strict=True)))
    low, full = jnp.bfloat16, jnp.float32
    me = Place()
    net = Net(r.send, r.recv, r.here)
    fetch = Fetch(net)
    fetch.start("w_gate", r.w_gate, r.gate_weight)
    fetch.start("w_up", r.w_up, r.up_weight)
    fetch.start("cots", r.cots, r.cots_held)
    fetch.start("w_down", r.w_down, r.down_weight)
    greeted = greet(peers(me) + [me.at(x=me.x_by(1)), me.at(x=me.x_by(3))])
    everyone, local, table = r.everyone, r.local, r.table
    values = r.after[...]
    inverse = lax.rsqrt(jnp.mean(values * values, axis=-1, keepdims=True) + epsilon)
    gain = wide(r.moe_gain)
    everyone[me.spot] = (values * inverse * gain).astype(low).reshape(3, 32, 2048)

    greeted()
    came = {}
    own_rows = everyone.at[me.spot]
    here_rows = spread(net, me, everyone, own_rows, came)
    next(here_rows)
    from_across = net.copy(own_rows, own_rows, me.at(z=me.z_by(2)))

    act, gate_back, up_back, back, home = r.act, r.gate_back, r.up_back, r.back, r.home
    grads = r.grads_held
    iota = lax.broadcasted_iota(jnp.int32, (48, 128), 0).astype(full)

    def slots_of(offset):
        core, z_hi, y = peer(me, *offset)[0]
        mask = r.info_in[core, z_hi, y, 0:1, :] == iota
        share = jnp.where(mask, r.info_in[core, z_hi, y, 1:2, :], 0.0)
        return mask, jnp.sum(share, axis=1, keepdims=True)

    def select(source, offset):
        mask, share = slots_of(offset)
        named = jnp.where(mask, 1.0, 0.0).astype(low)[:, :96]
        rows = source[peer(me, *offset)[0]].reshape(96, 2048)
        return jnp.dot(named, rows, preferred_element_type=full), share

    cots = fetch.cots
    for offset, slot in SLOTS.items():
        picked, share = select(cots, offset)
        r.raw_held[slot] = picked.astype(low)
        grads[slot] = (picked * share).astype(low)

    w_gate, w_up, w_down = fetch.w_gate, fetch.w_up, fetch.w_down
    back_came, dots_came, round_x, written = {}, {}, [], []
    right, left = me.at(x=me.x_by(1)), me.at(x=me.x_by(3))

    def weigh(entered, given, target):
        def body(step, carry):
            columns = pl.ds(pl.multiple_of(step * 256, 256), 256)
            left = entered[:, :, :, columns].reshape(768, 256)
            target[columns, :] = contract_first(left, given[...].reshape(768, 768)).astype(low)
            return carry

        lax.fori_loop(0, 8, body, 0)

    def chunk(target, step, half):
        start = (me.x_by(step) * 2 + half) * 256
        return target.at[pl.ds(pl.multiple_of(start, 256), 256)]

    for first in (0, 1):
        group = first
        if first == 0:
            next(here_rows)
            from_across.wait_recv()
            other_rows = spread(net, me, everyone, None, came)
            next(other_rows)
        masks, shares = [], []
        for offset in PHASES[first]:
            if offset in came:
                came[offset].wait_recv()
            picked, share = select(everyone, offset)
            local[SLOTS[offset]] = picked.astype(low)
            masks.append(slots_of(offset)[0])
            shares.append(share)
        shared = jnp.concatenate(shares, axis=0)

        def inner(step, carry, group=group, shared=shared):
            columns = pl.ds(pl.multiple_of(step * 256, 256), 256)
            entered = local[group].reshape(384, 2048)
            gate_pre = jnp.dot(entered, w_gate[:, columns], preferred_element_type=full)
            up_pre = jnp.dot(entered, w_up[:, columns], preferred_element_type=full)
            act_back = jnp.dot(
                grads[group].reshape(384, 2048), w_down[:, columns], preferred_element_type=full
            )
            sigmoid = 1.0 / (1.0 + jnp.exp(-gate_pre))
            silu = gate_pre * sigmoid
            act[group, :, columns] = (silu * up_pre).astype(low)
            gate_back[group, :, columns] = (
                act_back * up_pre * sigmoid * (1.0 + gate_pre * (1.0 - sigmoid))
            ).astype(low)
            up_back[group, :, columns] = (act_back * silu).astype(low)
            return carry

        def outer(step, dot, group=group, shared=shared):
            columns = pl.ds(pl.multiple_of(step * 256, 256), 256)
            row_back = contract_last(gate_back[group], w_gate[columns, :]) + contract_last(
                up_back[group], w_up[columns, :]
            )
            back[group, :, :, columns] = row_back.astype(low).reshape(8, 48, 256)
            return dot

        def finals(step, dot, group=group, shared=shared):
            columns = pl.ds(pl.multiple_of(step * 256, 256), 256)
            made = contract_last(act[group], w_down[columns, :]).astype(low).astype(full)
            r.produced_held[group, :, :, columns] = (made * shared).astype(low).reshape(8, 48, 256)
            incoming = r.raw_held[group, :, :, columns].reshape(384, 256).astype(full)
            return dot + jnp.sum(made * incoming, axis=1, keepdims=True)

        lax.fori_loop(0, 3, inner, 0)
        if first == 0:
            next(here_rows)
        lax.fori_loop(0, 8, outer, 0)
        if first == 0:
            next(other_rows)
        sources = [offset for offset in OFFSETS if offset in PHASES[first]]
        for offset in sources:
            device = peer(me, *offset)[1]
            back_came[offset] = net.copy(back.at[SLOTS[offset]], home.at[me.spot], device)
        if first == 1:
            weigh(local, gate_back, r.gate_held)
            round_x += [
                net.copy(chunk(r.gate_held, 2, 0), r.gate_slots.at[0], right),
                net.copy(chunk(r.gate_held, 2, 1), r.gate_slots.at[2], left),
                net.copy(chunk(r.gate_held, 1, 1), r.gate_slots.at[1], right),
                net.copy(chunk(r.gate_held, 3, 0), r.gate_slots.at[3], left),
            ]
            written.append(net.load(r.gate_held, r.full_gate))
            weigh(local, up_back, r.up_held)
            round_x += [
                net.copy(chunk(r.up_held, 2, 0), r.up_slots.at[0], right),
                net.copy(chunk(r.up_held, 2, 1), r.up_slots.at[1], left),
            ]
            written.append(net.load(r.up_held, r.full_up))
        dot = lax.fori_loop(0, 8, finals, jnp.zeros((384, 1), full))
        for place in range(8):
            line = jnp.where(masks[place], dot[place * 48 : place * 48 + 48], 0.0)
            line = jnp.sum(line, axis=0, keepdims=True)
            r.dots[group, place] = jnp.broadcast_to(line, (8, 128))
        for offset in sources:
            device = peer(me, *offset)[1]
            dots_came[offset] = net.copy(r.dots.at[SLOTS[offset]], r.dots_in.at[me.spot], device)
        if first == 0:
            next(other_rows)
    weigh(grads, act, r.down_held)
    written.append(net.load(r.produced_held, r.produced))
    written.append(net.load(r.down_held, r.full_down))
    home[me.spot] = back[0, 0]
    r.dots_in[me.spot] = r.dots[0, 0]

    for offset in OFFSETS:
        dots_came[offset].wait_recv()
    lines = [r.dots_in[e // 4 % 2, e // 8, e % 4, 0:1, :] for e in range(16)]
    lines = jnp.concatenate(lines, axis=0)
    expert = lax.broadcasted_iota(jnp.int32, (16, 32), 0)
    for s in range(3):
        dots = lines[:, s * 32 : s * 32 + 32]
        for k in range(8):
            named = r.ids[s, k : k + 1, :] == expert
            r.gate_grad[s, k : k + 1, :] = jnp.sum(
                jnp.where(named, dots, 0.0), axis=0, keepdims=True
            )

    for offset in OFFSETS:
        back_came[offset].wait_recv()
    after_grad = r.after_grad

    def keep(columns, total):
        after_grad[:, columns] = total

    gather_rows(table, home, keep)
    gradient = after_grad[...]
    moe_part, gain_part = norm_back(gradient, r.after[...], gain)
    r.gain_part[...] = gain_part
    result = r.cotangent[...].reshape(96, 2048).astype(full) + moe_part
    after_grad[...] = result
    r.branch[...] = result.astype(low).reshape(3, 32, 2048)
    for one in written:
        one.wait()
    for one in round_x:
        one.wait_recv()
    net.finish()


def moe(far, near):
    low, full = jnp.bfloat16, jnp.float32
    rows, home = (2, 8, 48, 2048), (2, 2, 4, 48, 2048)
    outs = dict(
        after_grad=jax.ShapeDtypeStruct((96, 2048), full),
        branch=jax.ShapeDtypeStruct((3, 32, 2048), low),
        gain_part=jax.ShapeDtypeStruct((1, 2048), full),
        gate_grad=jax.ShapeDtypeStruct((3, 8, 32), full),
    )
    far_outs = dict(
        produced=jax.ShapeDtypeStruct(rows, low),
        full_gate=jax.ShapeDtypeStruct((2048, 768), low),
        full_up=jax.ShapeDtypeStruct((2048, 768), low),
        full_down=jax.ShapeDtypeStruct((2048, 768), low),
        gate_slots=jax.ShapeDtypeStruct((4, 256, 768), low),
        up_slots=jax.ShapeDtypeStruct((2, 256, 768), low),
    )
    scratch = dict(
        everyone=pltpu.VMEM((2, 2, 4, 3, 32, 2048), low),
        local=pltpu.VMEM(rows, low),
        cots_held=pltpu.VMEM((2, 2, 4, 3, 32, 2048), low),
        raw_held=pltpu.VMEM(rows, low),
        grads_held=pltpu.VMEM(rows, low),
        produced_held=pltpu.VMEM(rows, low),
        back=pltpu.VMEM(rows, low),
        home=pltpu.VMEM(home, low),
        gate_weight=pltpu.VMEM((2048, 768), low),
        up_weight=pltpu.VMEM((2048, 768), low),
        down_weight=pltpu.VMEM((2048, 768), low),
        gate_held=pltpu.VMEM((2048, 768), low),
        up_held=pltpu.VMEM((2048, 768), low),
        down_held=pltpu.VMEM((2048, 768), low),
        act=pltpu.VMEM((2, 384, 768), low),
        gate_back=pltpu.VMEM((2, 384, 768), low),
        up_back=pltpu.VMEM((2, 384, 768), low),
        dots=pltpu.VMEM((2, 8, 8, 128), full),
        dots_in=pltpu.VMEM((2, 2, 4, 8, 128), full),
        send=pltpu.SemaphoreType.DMA((54,)),
        recv=pltpu.SemaphoreType.DMA((54,)),
        here=pltpu.SemaphoreType.DMA((8,)),
    )
    return call(moe_kernel, 1, far, near, outs, far_outs, scratch)


def call(kernel, number, far, near, outs, far_outs, scratch):
    names = list(far) + list(near) + list(outs) + list(far_outs) + list(scratch)
    shapes = {**outs, **far_outs}
    results = pl.pallas_call(
        functools.partial(kernel, names),
        out_shape=list(shapes.values()),
        in_specs=[ANY] * len(far)
        + [SMEM if one.ndim == 1 else VMEM for one in near.values()],
        out_specs=[VMEM] * len(outs) + [ANY] * len(far_outs),
        scratch_shapes=list(scratch.values()),
        compiler_params=pltpu.CompilerParams(
            collective_id=number, has_side_effects=True, vmem_limit_bytes=63 << 20
        ),
        name=kernel.__name__,
    )(*far.values(), *near.values())
    return types.SimpleNamespace(**dict(zip(shapes, results, strict=True)))


def front_kernel(names, *refs):
    r = types.SimpleNamespace(**dict(zip(names, refs, strict=True)))
    low, full = jnp.bfloat16, jnp.float32
    score_scale = HEAD_SIZE ** (-0.5)
    me = Place()
    net = Net(r.send, r.recv, r.here)
    fetch = Fetch(net)
    fetch.start("hidden", r.hidden, r.hidden_held)
    fetch.start("w_pair", r.w_key, r.key_weight)
    fetch.start("w_value", r.w_value, r.value_weight)
    fetch.start("cosine", r.cosine.at[me.context], r.cosine_held)
    fetch.start("sine", r.sine.at[me.context], r.sine_held)
    fetch.start("w_query", r.w_query, r.query_weight)
    fetch.start("w_out", r.w_out, r.out_weight)
    beside = me.at(z=me.z + 1 - 2 * me.z_lo)
    right, left = me.at(x=me.x_by(1)), me.at(x=me.x_by(3))
    greeted = greet([right, left, beside] + peers(me))
    gains = r.gain_rows
    gains[...] = wide(r.attn_gain)

    above, below = me.at(y=me.y_by(1)), me.at(y=me.y_by(3))
    across, came, told = me.at(z=me.z_by(2)), {}, []
    greeted()
    own_cot = net.load(r.cotangent, r.cots.at[me.spot])
    here_cot = spread(net, me, r.cots, r.cotangent, came)
    next(here_cot)
    from_across = net.copy(r.cotangent, r.cots.at[me.spot], across)

    hidden, normed = fetch.hidden, r.normed
    for s in range(3):
        values = hidden[s].astype(full)
        root = lax.rsqrt(jnp.mean(values * values, axis=-1, keepdims=True) + epsilon)
        normed[s * 128 : s * 128 + 128, :] = (values * root * gains[...]).astype(low)

    def rope(values):
        cosine = jnp.concatenate([fetch.cosine[...]] * 3, axis=0)
        sine = jnp.concatenate([fetch.sine[...]] * 3, axis=0)
        return values * cosine + turned(values) * sine

    def head_norm(raw, gain):
        return raw * lax.rsqrt(jnp.mean(raw * raw, axis=-1, keepdims=True) + epsilon) * gain

    pair, key_raw = r.pair_held, r.key_raw
    made = jnp.dot(normed[...], fetch.w_pair[...], preferred_element_type=full)
    key_raw[...] = made
    keys = rope(head_norm(made, r.key_gain[...].astype(full))).astype(low)
    values = jnp.dot(normed[...], fetch.w_value[...], preferred_element_type=full).astype(low)
    own = pl.ds(pl.multiple_of(me.context * 128, 128), 128)
    pair[0, :, own, :] = keys.reshape(3, 128, 128)
    pair[1, :, own, :] = values.reshape(3, 128, 128)

    def block(x, z_lo):
        return pl.ds(pl.multiple_of((x * 2 + z_lo) * 128, 128), 128)

    def piece(s, x, z_lo, half=None):
        rows = block(x, z_lo)
        return pair.at[:, s, rows, :] if half is None else pair.at[half, s, rows, :]

    def pass_on(view, device):
        return net.copy(view, view, device)

    own_z, other_z = me.z_lo, 1 - me.z_lo

    def bring_pair(s):
        from_z = pass_on(piece(s, me.x, own_z), beside)
        came = [(pass_on(piece(s, me.x, own_z), right), pass_on(piece(s, me.x, own_z), left))]
        yield
        from_z.wait_recv()
        came.append((pass_on(piece(s, me.x, other_z), right), pass_on(piece(s, me.x, other_z), left)))
        yield
        far = []
        for zs, (from_left, from_right) in zip((own_z, other_z), came, strict=True):
            from_left.wait_recv()
            far.append(pass_on(piece(s, me.x_by(3), zs, 0), right))
            from_right.wait_recv()
            far.append(pass_on(piece(s, me.x_by(1), zs, 1), left))
            yield
        for one in far:
            one.wait_recv()
        yield

    brought = [bring_pair(s) for s in range(3)]
    for s in range(3):
        next(brought[s])

    token_table(r.ids, r.gates, r.capacity, r.table, r.info)
    r.info_in[me.spot] = r.info[me.spot]
    for a, b in OFFSETS:
        spot, device = peer(me, a, b)
        told.append(net.copy(r.info.at[spot], r.info_in.at[me.spot], device))

    w_query, query, query_raw = fetch.w_query, r.query_held, r.query_raw_held

    def project(step, carry):
        columns = pl.ds(pl.multiple_of(step * 256, 256), 256)
        made = jnp.dot(normed[...], w_query[:, columns], preferred_element_type=full)
        query_raw[:, columns] = made
        for half in range(2):
            run = pl.ds(pl.multiple_of(step * 256 + half * 128, 128), 128)
            one = head_norm(made[:, half * 128 : half * 128 + 128], r.query_gain[...].astype(full))
            query[:, run] = rope(one).astype(low)
        return carry

    lax.fori_loop(0, 4, project, 0)
    written = [net.load(query, r.query), net.load(query_raw, r.query_raw)]
    for s in range(3):
        next(brought[s])
    next(here_cot)
    from_across.wait_recv()
    other_cot = spread(net, me, r.cots, None, came)
    next(other_cot)
    next(brought[0])
    next(brought[1])
    next(brought[0])
    next(brought[2])
    next(brought[1])

    bias, peaks, mixed = r.bias, r.peak_rows, r.mixed_held
    peaks[...] = jnp.full((8, 1, 128), -jnp.inf, full)

    def attend(s):
        here = pl.ds(s * 128, 128)
        bias[...] = mask_bias(me, r.segments, s)

        def two_heads(step, carry):
            columns = pl.ds(pl.multiple_of(step * 256, 256), 256)
            both = query[here, columns]
            q = jnp.concatenate([both[:, :128], both[:, 128:]], axis=0)
            score = contract_last(q, pair[0, s]) * score_scale
            score = score + jnp.concatenate([bias[...], bias[...]], axis=0)
            highest = jnp.max(score, axis=-1, keepdims=True)
            weight = jnp.exp(score - highest)
            total = jnp.sum(weight, axis=-1, keepdims=True)
            prob = (weight * (1.0 / total)).astype(low)
            logs = highest + jnp.log(total)
            heads = jnp.dot(prob, pair[1, s], preferred_element_type=full).astype(low)
            for half in range(2):
                part = slice(half * 128, half * 128 + 128)
                head = step * 2 + half
                run = pl.ds(pl.multiple_of(step * 256 + half * 128, 128), 128)
                mixed[here, run] = heads[part]
                r.log_sum[s * 8 + head] = row_of(logs[part])
                top = jnp.max(highest[part], axis=0, keepdims=True)
                peaks[head] = jnp.maximum(peaks[head], top)
            return carry

        lax.fori_loop(0, 4, two_heads, 0)
    shares, after = r.shares, r.after_sum

    def branch(s):
        w_out = fetch.w_out

        def body(step, carry):
            columns = pl.ds(pl.multiple_of(step * 256, 256), 256)
            made = contract_last(mixed[pl.ds(s * 128, 128), :], w_out[columns, :])
            shares[s, :, :, columns] = made.astype(low).reshape(4, 32, 256)
            return carry

        lax.fori_loop(0, 8, body, 0)
        return ring_reduce(
            net,
            above,
            below,
            lambda step, half: shares.at[s, me.y_by(step), :, pl.ds(half * 1024, 1024)],
            r.branch_slots.at[s],
            lambda half: after.at[s, :, pl.ds(half * 1024, 1024)],
        )

    next(brought[0])
    attend(0)
    next(brought[2])
    first = branch(0)
    next(first)
    next(brought[1])
    attend(1)
    next(other_cot)
    second = branch(1)
    next(second)
    next(first)
    next(brought[2])
    attend(2)
    third = branch(2)
    next(third)
    next(second)
    next(here_cot)
    written.append(net.load(pair, r.pair))
    written.append(net.load(mixed, r.mixed))
    for head in range(8):
        r.peaks[head : head + 1, :] = peaks[head]
    next(first, None)
    next(third)
    next(other_cot)
    next(second, None)
    next(third, None)
    own_rows = pl.ds(pl.multiple_of(me.y * 32, 32), 32)
    for s in range(3):
        r.after[s * 32 : s * 32 + 32, :] = after[s] + hidden[s, own_rows, :].astype(full)
    for one in list(came.values()) + told:
        one.wait_recv()
    own_cot.wait()
    for one in written:
        one.wait()
    net.finish()


def row_of(column):
    eye = lax.broadcasted_iota(jnp.int32, (128, 128), 0) == lax.broadcasted_iota(
        jnp.int32, (128, 128), 1
    )
    return jnp.sum(jnp.where(eye, column, 0.0), axis=0, keepdims=True)


def mask_bias(me, segments, s):
    spot = me.context * 128 + lax.broadcasted_iota(jnp.int32, (128, 1024), 0)
    own = segments[s : s + 1, pl.ds(pl.multiple_of(me.context * 128, 128), 128)]
    document = column_of(own.astype(jnp.float32))
    allowed = (document == segments[s : s + 1, :].astype(jnp.float32)) & (
        lax.broadcasted_iota(jnp.int32, (128, 1024), 1) <= spot
    )
    return jnp.where(allowed, 0.0, masked_value)


def front(far, near):
    low, full = jnp.bfloat16, jnp.float32
    outs = dict(
        key_raw=jax.ShapeDtypeStruct((384, 128), full),
        log_sum=jax.ShapeDtypeStruct((24, 1, 128), full),
        peaks=jax.ShapeDtypeStruct((8, 128), full),
        after=jax.ShapeDtypeStruct((96, 2048), full),
        table=jax.ShapeDtypeStruct((768, 128), low),
        info_in=jax.ShapeDtypeStruct((2, 2, 4, 8, 128), full),
    )
    far_outs = dict(
        query=jax.ShapeDtypeStruct((384, 1024), low),
        query_raw=jax.ShapeDtypeStruct((384, 1024), full),
        pair=jax.ShapeDtypeStruct((2, 3, 1024, 128), low),
        mixed=jax.ShapeDtypeStruct((384, 1024), low),
        cots=jax.ShapeDtypeStruct((2, 2, 4, 3, 32, 2048), low),
    )
    scratch = dict(
        gain_rows=pltpu.VMEM((1, 2048), full),
        hidden_held=pltpu.VMEM((3, 128, 2048), low),
        key_weight=pltpu.VMEM((2048, 128), low),
        value_weight=pltpu.VMEM((2048, 128), low),
        cosine_held=pltpu.VMEM((128, 128), full),
        sine_held=pltpu.VMEM((128, 128), full),
        query_weight=pltpu.VMEM((2048, 1024), low),
        out_weight=pltpu.VMEM((2048, 1024), low),
        normed=pltpu.VMEM((384, 2048), low),
        pair_held=pltpu.VMEM((2, 3, 1024, 128), low),
        info=pltpu.VMEM((2, 2, 4, 8, 128), full),
        query_held=pltpu.VMEM((384, 1024), low),
        query_raw_held=pltpu.VMEM((384, 1024), full),
        bias=pltpu.VMEM((128, 1024), full),
        peak_rows=pltpu.VMEM((8, 1, 128), full),
        mixed_held=pltpu.VMEM((384, 1024), low),
        shares=pltpu.VMEM((3, 4, 32, 2048), low),
        branch_slots=pltpu.VMEM((3, 6, 32, 1024), low),
        after_sum=pltpu.VMEM((3, 32, 2048), full),
        send=pltpu.SemaphoreType.DMA((84,)),
        recv=pltpu.SemaphoreType.DMA((84,)),
        here=pltpu.SemaphoreType.DMA((16,)),
    )
    return call(front_kernel, 2, far, near, outs, far_outs, scratch)


def finish_kernel(names, *refs):
    r = types.SimpleNamespace(**dict(zip(names, refs, strict=True)))
    r.layer_out[...] = r.after[...] + r.moe_out[...]
    r.input_grad[...] = r.after_grad[...] + r.normed_out[...].reshape(96, 2048)
    r.gate_w[...] = r.gate_part[...]
    r.up_w[...] = r.up_part[...]
    r.down_w[...] = r.down_part[...]
    r.query_w[...] = r.query_part[...]
    r.out_w[...] = r.out_part[...]
    r.gate_grad[...] = r.gate_grad_part[...]
    r.key_w[...] = r.pair_w[:, :128]
    r.value_w[...] = r.pair_w[:, 128:]
    r.attn_gain[...] = r.small[:16]
    r.moe_gain[...] = r.small[16:32]
    r.query_gain[...] = r.small[32:33]
    r.key_gain[...] = r.small[33:34]
    diagonal = lax.broadcasted_iota(jnp.int32, (8, 128), 0) == lax.broadcasted_iota(
        jnp.int32, (8, 128), 1
    )
    peaks = jnp.sum(jnp.where(diagonal, r.small[40:], 0.0), axis=0, keepdims=True)
    r.clip[...] = (clip_limit / jnp.maximum(peaks, clip_limit))[:, :8]


def finish(near):
    outs = dict(
        layer_out=(96, 2048),
        input_grad=(96, 2048),
        gate_w=(256, 768),
        up_w=(256, 768),
        down_w=(256, 768),
        query_w=(64, 1024),
        out_w=(64, 1024),
        gate_grad=(3, 8, 32),
        key_w=(64, 128),
        value_w=(64, 128),
        attn_gain=(16, 128),
        moe_gain=(16, 128),
        query_gain=(1, 128),
        key_gain=(1, 128),
        clip=(1, 8),
    )
    results = pl.pallas_call(
        functools.partial(finish_kernel, list(near) + list(outs)),
        out_shape=[jax.ShapeDtypeStruct(size, jnp.float32) for size in outs.values()],
        in_specs=[VMEM] * len(near),
        out_specs=[VMEM] * len(outs),
        compiler_params=pltpu.CompilerParams(vmem_limit_bytes=62 << 20),
        name="finish",
    )(*near.values())
    return types.SimpleNamespace(**dict(zip(outs, results, strict=True)))


def shards(
    hidden_in,
    segments,
    attn_gain,
    query_gain,
    key_gain,
    w_query,
    key_weight_matrix,
    value_weight_matrix,
    w_out,
    moe_gain,
    expert_ids,
    gate_values,
    capacity,
    w_gate,
    w_up,
    w_down,
    cotangent,
):
    attn_wide, moe_wide = attn_gain.reshape(16, 128), moe_gain.reshape(16, 128)
    query_row, key_row = query_gain[None], key_gain[None]
    ids, gates = expert_ids.swapaxes(1, 2), gate_values.swapaxes(1, 2)
    cosine, sine = rotary()
    first = front(
        dict(
            hidden=hidden_in,
            w_key=key_weight_matrix,
            w_value=value_weight_matrix,
            cosine=cosine,
            sine=sine,
            w_query=w_query,
            cotangent=cotangent,
            w_out=w_out,
        ),
        dict(
            attn_gain=attn_wide,
            query_gain=query_row,
            key_gain=key_row,
            segments=segments,
            ids=ids,
            gates=gates,
            capacity=capacity,
        ),
    )
    second = moe(
        dict(w_gate=w_gate[0], w_up=w_up[0], w_down=w_down[0], cots=first.cots),
        dict(
            after=first.after,
            cotangent=cotangent,
            moe_gain=moe_wide,
            ids=ids,
            table=first.table,
            info_in=first.info_in,
        ),
    )
    done = back(
        dict(
            branch=second.branch,
            w_out=w_out,
            w_query=w_query,
            gate=second.full_gate.reshape(4, 2, 256, 768),
            up=second.full_up.reshape(4, 2, 256, 768),
            down=second.full_down.reshape(4, 2, 256, 768),
            produced=second.produced,
            gate_begun=second.gate_slots,
            up_begun=second.up_slots,
            hidden=hidden_in,
            mixed=first.mixed,
            query=first.query,
            query_raw=first.query_raw,
            pair=first.pair,
            cosine=cosine,
            sine=sine,
            w_key=key_weight_matrix,
            w_value=value_weight_matrix,
        ),
        dict(
            table=first.table,
            key_raw=first.key_raw,
            log_sum=first.log_sum,
            segments=segments,
            attn_gain=attn_wide,
            query_gain=query_row,
            key_gain=key_row,
            moe_gain_part=second.gain_part,
            peaks=first.peaks,
        ),
    )
    last = finish(
        dict(
            after=first.after,
            moe_out=done.moe_out,
            after_grad=second.after_grad,
            normed_out=done.normed_out,
            small=done.small_out,
            pair_w=done.pair_w_out,
            gate_part=done.gate_out,
            up_part=done.up_out,
            down_part=done.down_out,
            query_part=done.query_w_out,
            out_part=done.out_w_out,
            gate_grad_part=second.gate_grad,
        )
    )
    layer_out = last.layer_out.reshape(cotangent.shape)
    input_grad = last.input_grad.reshape(cotangent.shape)
    gate_grad = last.gate_grad.swapaxes(1, 2)
    w_key_grad, w_value_grad = last.key_w, last.value_w
    w_query_grad, w_out_grad = last.query_w, last.out_w
    w_gate_grad, w_up_grad, w_down_grad = last.gate_w[None], last.up_w[None], last.down_w[None]
    attn_gain_grad, moe_gain_grad = last.attn_gain.reshape(2048), last.moe_gain.reshape(2048)
    query_gain_grad, key_gain_grad = last.query_gain.reshape(128), last.key_gain.reshape(128)
    head_clip_scale = last.clip.reshape(8)
    return (
        layer_out,
        input_grad,
        attn_gain_grad,
        query_gain_grad,
        key_gain_grad,
        w_query_grad,
        w_key_grad,
        w_value_grad,
        w_out_grad,
        moe_gain_grad,
        gate_grad,
        w_gate_grad,
        w_up_grad,
        w_down_grad,
        head_clip_scale,
    )


def solution(mesh):
    in_specs = (
        P("dp", "context", None),
        P("dp", None),
        P(),
        P(),
        P(),
        P(None, "experts"),
        P(None, "experts"),
        P(None, "experts"),
        P(None, "experts"),
        P(),
        P("dp", ("context", "experts"), None),
        P("dp", ("context", "experts"), None),
        P(),
        P(("dp", "experts"), None, None),
        P(("dp", "experts"), None, None),
        P(("dp", "experts"), None, None),
        P("dp", ("context", "experts"), None),
    )
    out_specs = (
        P("dp", ("context", "experts"), None),
        P("dp", ("context", "experts"), None),
        P(),
        P(),
        P(),
        P(("dp", "context"), "experts"),
        P(("dp", "context"), "experts"),
        P(("dp", "context"), "experts"),
        P(("dp", "context"), "experts"),
        P(),
        P("dp", ("context", "experts"), None),
        P(("dp", "experts"), "context", None),
        P(("dp", "experts"), "context", None),
        P(("dp", "experts"), "context", None),
        P("experts"),
    )
    return jax.shard_map(shards, mesh=mesh, in_specs=in_specs, out_specs=out_specs, check_vma=False)
```

```python
import functools
import itertools
import types

import jax
import jax.numpy as jnp
import numpy as np
from jax import lax
from jax.experimental import pallas as pl
from jax.experimental.pallas import tpu as pltpu
from jax.sharding import PartitionSpec as P

HEAD_SIZE = 128
MESH = pl.DeviceIdType.MESH
VMEM = pl.BlockSpec(memory_space=pltpu.VMEM)
ANY = pl.BlockSpec(memory_space=pl.ANY)
SMEM = pl.BlockSpec(memory_space=pltpu.SMEM)


epsilon = 1e-06
rope_base = 1000000.0
clip_limit = 1.0
masked_value = -1e30


def rotary():
    inverse = 1.0 / rope_base ** (np.arange(0, HEAD_SIZE, 2) / HEAD_SIZE)
    angle = np.arange(1024)[:, None] * inverse[None, :]
    cosine = np.concatenate([np.cos(angle), np.cos(angle)], axis=-1)
    sine = np.concatenate([-np.sin(angle), np.sin(angle)], axis=-1)
    shape = (8, 128, HEAD_SIZE)
    return (
        jnp.asarray(cosine.reshape(shape), jnp.float32),
        jnp.asarray(sine.reshape(shape), jnp.float32),
    )


def contract_last(left, right):
    return lax.dot_general(
        left, right, (((1,), (1,)), ((), ())), preferred_element_type=jnp.float32
    )


def contract_first(left, right):
    return lax.dot_general(
        left, right, (((0,), (0,)), ((), ())), preferred_element_type=jnp.float32
    )


class Place:
    def __init__(self):
        dp = lax.axis_index("dp")
        context = lax.axis_index("context")
        self.dp, self.context, self.y = dp, context, lax.axis_index("experts")
        self.core, self.z_hi = lax.rem(dp, 2), dp // 2
        self.x, self.z_lo = context // 2, lax.rem(context, 2)
        self.z = self.z_hi * 2 + self.z_lo
        self.spot = (self.core, self.z_hi, self.y)

    def at(self, x=None, y=None, z=None, core=None):
        x = self.x if x is None else x
        y = self.y if y is None else y
        z = self.z if z is None else z
        core = self.core if core is None else core
        return (z // 2 * 2 + core, x * 2 + lax.rem(z, 2), y)

    def x_by(self, step):
        return lax.rem(self.x + step, 4)

    def y_by(self, step):
        return lax.rem(self.y + step, 4)

    def z_by(self, step):
        return lax.rem(self.z + step, 4)


class Net:
    def __init__(self, send, recv, here=None):
        self.send, self.recv, self.copies = send, recv, []
        self.here, self.loads = here, 0

    def copy(self, src, dst, device):
        spot = len(self.copies)
        made = pltpu.make_async_remote_copy(
            src_ref=src,
            dst_ref=dst,
            send_sem=self.send.at[spot],
            recv_sem=self.recv.at[spot],
            device_id=device,
            device_id_type=MESH,
        )
        made.start()
        self.copies.append(made)
        return made

    def load(self, src, dst):
        made = pltpu.make_async_copy(src, dst, self.here.at[self.loads])
        self.loads += 1
        made.start()
        return made

    def sent(self, made):
        made.wait_send()
        self.copies = [None if one is made else one for one in self.copies]

    def finish(self):
        for made in self.copies:
            if made is not None:
                made.wait_send()


def greet(devices):
    barrier = pltpu.get_barrier_semaphore()
    for device in devices:
        pl.semaphore_signal(barrier, inc=1, device_id=device, device_id_type=MESH)
    return lambda: pl.semaphore_wait(barrier, len(devices))


def wide(ref):
    values = ref[...].astype(jnp.float32)
    return jnp.concatenate([values[step : step + 1] for step in range(16)], axis=1)


def add_into(target, parts, block=32):
    rows = target.shape[-2]
    block = min(block, rows)
    for lead in itertools.product(*[range(size) for size in target.shape[:-2]]):

        def body(step, carry, lead=lead):
            spot = lead + (pl.ds(pl.multiple_of(step * block, block), block),)
            total = parts[0][spot].astype(jnp.float32)
            for part in parts[1:]:
                total = total + part[spot].astype(jnp.float32)
            target[spot] = total.astype(target.dtype)
            return carry

        lax.fori_loop(0, rows // block, body, 0)


def ring_reduce(net, plus, minus, own, slots, target, held=None, begun=None):
    held = own if held is None else held
    done = 0 if begun is None else begun.shape[0]
    if done == 4:
        loads = [net.load(begun, slots.at[pl.ds(0, 4)])]
    elif done == 2:
        loads = [net.load(begun.at[step], slots.at[step * 2]) for step in range(2)]
    else:
        first_plus = net.copy(own(2, 0), slots.at[0], plus)
        first_minus = net.copy(own(2, 1), slots.at[2], minus)
    if done != 4:
        side_plus = net.copy(own(1, 1), slots.at[1], plus)
        side_minus = net.copy(own(3, 0), slots.at[3], minus)
    yield
    if done:
        for load in loads:
            load.wait()
    else:
        first_plus.wait_recv()
        first_minus.wait_recv()
    add_into(slots.at[0], [slots.at[0], held(1, 0)])
    last_plus = net.copy(slots.at[0], slots.at[4], plus)
    add_into(slots.at[2], [slots.at[2], held(3, 1)])
    last_minus = net.copy(slots.at[2], slots.at[5], minus)
    yield
    if done != 4:
        side_minus.wait_recv()
        side_plus.wait_recv()
    last_plus.wait_recv()
    add_into(target(0), [held(0, 0), slots.at[3], slots.at[4]])
    last_minus.wait_recv()
    add_into(target(1), [held(0, 1), slots.at[1], slots.at[5]])


def x_first(net, me, source, slots, middle, other, out, held=None, begun=None):
    staged = None
    if held is not None:
        order = {(1, 0): 0, (3, 1): 1, (0, 0): 2, (0, 1): 3}
        loads = [
            net.load(source.at[me.x_by(step), half], held.at[spot])
            for (step, half), spot in order.items()
        ]

        def staged(step, half):
            return held.at[order[step, half]]

    ring = ring_reduce(
        net,
        me.at(x=me.x_by(1)),
        me.at(x=me.x_by(3)),
        lambda step, half: source.at[me.x_by(step), half],
        slots,
        lambda half: middle.at[half],
        staged,
        begun,
    )
    next(ring)
    yield
    if held is not None:
        for load in loads:
            load.wait()
    yield from ring
    across = net.copy(middle.at[1 - me.z_lo], other, me.at(z=me.z + 1 - 2 * me.z_lo))
    yield
    across.wait_recv()
    add_into(out, [middle.at[me.z_lo], other])


def core_pair(net, me, sending, other, middle):
    across = net.copy(sending, other, me.at(core=1 - me.core))
    yield
    net.sent(across)
    across.wait_recv()
    add_into(middle, [middle, other])


def dense_x_first(net, me, sending, other, middle, slots, corner, last, out):
    yield from core_pair(net, me, sending, other, middle)
    yield from ring_reduce(
        net,
        me.at(x=me.x_by(1)),
        me.at(x=me.x_by(3)),
        lambda step, half: middle.at[half, me.x_by(step)],
        slots,
        lambda half: corner.at[half],
    )
    half_rows = corner.shape[2] // 2
    yield from ring_reduce(
        net,
        me.at(z=me.z_by(1)),
        me.at(z=me.z_by(3)),
        lambda step, half: corner.at[
            me.z_by(step) // 2, lax.rem(me.z_by(step), 2), pl.ds(half * half_rows, half_rows)
        ],
        last,
        lambda half: out.at[pl.ds(half * half_rows, half_rows)],
    )


def dense_z_first(net, me, sending, other, middle, slots, corner, last, out):
    yield from core_pair(net, me, sending, other, middle)
    yield from ring_reduce(
        net,
        me.at(z=me.z_by(1)),
        me.at(z=me.z_by(3)),
        lambda step, half: middle.at[
            me.z_by(step) // 2, pl.ds(half * 2, 2), lax.rem(me.z_by(step), 2)
        ],
        slots,
        lambda half: corner.at[pl.ds(half * 2, 2)],
    )
    half_rows = corner.shape[1] // 2
    yield from ring_reduce(
        net,
        me.at(x=me.x_by(1)),
        me.at(x=me.x_by(3)),
        lambda step, half: corner.at[me.x_by(step), pl.ds(half * half_rows, half_rows)],
        last,
        lambda half: out.at[pl.ds(half * half_rows, half_rows)],
    )


def all_sum(net, devices, spot, own, slots, most):
    slots[spot] = own[...]
    sent = [net.copy(own, slots.at[spot], device) for device in devices]
    yield
    for made in sent:
        made.wait_recv()
    count = slots.shape[0]
    total = slots[0]
    peak = slots[0, most:]
    for step in range(1, count):
        total = total + slots[step]
        peak = jnp.maximum(peak, slots[step, most:])
    for made in sent:
        net.sent(made)
    own[:most] = total[:most]
    own[most:] = peak


def all_small(net, me, working, by_core, by_x, by_z, by_y, out):
    yield from all_sum(net, [me.at(core=1 - me.core)], me.core, working, by_core, 40)
    yield from all_sum(net, [me.at(x=me.x_by(s)) for s in (1, 2, 3)], me.x, working, by_x, 40)
    yield from all_sum(net, [me.at(z=me.z_by(s)) for s in (1, 2, 3)], me.z, working, by_z, 40)
    out[40:] = working[40:]
    yield from all_sum(net, [me.at(y=me.y_by(s)) for s in (1, 2, 3)], me.y, working, by_y, 40)
    out[:40] = working[:40]


OFFSETS = [(a, b) for a in (2, 0, 3, 1) for b in (0, 1, 3, 2) if a or b]


def peer(me, a, b):
    z = me.z if a < 2 else lax.rem(me.z + 2, 4)
    core = me.core if a % 2 == 0 else 1 - me.core
    y = me.y_by(b)
    return (core, z // 2, y), me.at(z=z, core=core, y=y)


def peers(me):
    return [peer(me, a, b)[1] for a, b in OFFSETS]


def gather_rows(table, home, store):
    def body(step, carry):
        columns = pl.ds(pl.multiple_of(step * 256, 256), 256)
        rows = home[:, :, :, :, columns].reshape(768, 256)
        total = contract_first(table[...], rows)
        store(columns, total[:96])
        return carry

    lax.fori_loop(0, home.shape[4] // 256, body, 0)


def turned(values):
    return pltpu.roll(values, 64, 1)


def column_of(row):
    eye = lax.broadcasted_iota(jnp.int32, (128, 128), 0) == lax.broadcasted_iota(
        jnp.int32, (128, 128), 1
    )
    return jnp.sum(jnp.where(eye, row, 0.0), axis=1, keepdims=True)


def norm_back(gradient, raw, gain):
    inverse = lax.rsqrt(jnp.mean(raw * raw, axis=-1, keepdims=True) + epsilon)
    normal = raw * inverse
    scaled = gradient * gain
    result = inverse * (scaled - normal * jnp.mean(scaled * normal, axis=-1, keepdims=True))
    return result, jnp.sum(gradient * normal, axis=0, keepdims=True)


def back_kernel(names, *refs):
    r = types.SimpleNamespace(**dict(zip(names, refs, strict=True)))
    low, full = jnp.bfloat16, jnp.float32
    score_scale = HEAD_SIZE ** (-0.5)
    me = Place()
    net = Net(r.send, r.recv, r.here)
    fetch = Fetch(net)
    fetch.start("hidden", r.hidden, r.hidden_held)
    greeted = greet(
        [
            me.at(x=me.x_by(1)),
            me.at(x=me.x_by(3)),
            me.at(z=me.z_by(1)),
            me.at(z=me.z_by(3)),
            me.at(x=me.x_by(2)),
        ]
        + peers(me)
    )
    gains = r.gain_rows
    gains[...] = wide(r.attn_gain)
    greeted()

    branch, whole = r.branch, r.whole
    above, below = me.at(y=me.y_by(1)), me.at(y=me.y_by(3))
    to_above = net.copy(branch, whole.at[:, me.y], above)
    to_below = net.copy(branch, whole.at[:, me.y], below)
    own_branch = net.load(branch, whole.at[:, me.y])
    weight = r.weight
    load_out = net.load(r.w_out, weight)
    gate = x_first(
        net, me, r.gate, r.gate_slots, r.gate_middle, r.gate_other, r.gate_out, r.gate_held,
        r.gate_begun,
    )
    up = x_first(
        net, me, r.up, r.up_slots, r.up_middle, r.up_other, r.up_out, r.up_held, r.up_begun
    )
    down = x_first(
        net, me, r.down, r.down_slots, r.down_middle, r.down_other, r.down_out, r.down_held
    )
    next(gate)
    next(gate)
    next(up)
    produced, home, table = r.produced, r.home, r.table
    start = me.core * 384 + me.z_hi * 192 + me.y * 48
    mine = pl.ds(pl.multiple_of(start, 16), 48)
    home_came = []

    def bring_home(offsets):
        for a, b in offsets:
            device = peer(me, a, b)[1]
            home_came.append(net.copy(produced.at[SLOTS[a, b]], home.at[mine], device))

    straight = [(2, 0), (3, 0)]
    bring_home(straight)
    home_own = net.load(produced.at[0, 0], home.at[mine])
    next(up)
    fetch.start("pair", r.pair, r.pair_held)
    fetch.start("query", r.query, r.query_held)
    fetch.start("query_raw", r.query_raw, r.query_raw_held)
    fetch.start("cosine", r.cosine.at[me.context], r.cosine_held)
    fetch.start("sine", r.sine.at[me.context], r.sine_held)
    fetch.start("mixed", r.mixed, r.mixed_held)
    fetch.start("w_key", r.w_key, r.key_weight)
    fetch.start("w_value", r.w_value, r.value_weight)

    hidden, inverse = fetch.hidden, r.inverse
    for s in range(3):
        rows = slice(s * 128, s * 128 + 128)
        values = hidden[s].astype(full)
        root = lax.rsqrt(jnp.mean(values * values, axis=-1, keepdims=True) + epsilon)
        inverse[rows, :] = jnp.broadcast_to(root, (128, 128))
        for step in range(8):
            run = slice(step * 256, step * 256 + 256)
            tile = hidden[s, :, run].astype(full) * root * gains[:, run]
            r.normed[run, rows] = tile.T.astype(low)

    first, second = pl.ds(0, 1024), pl.ds(1024, 1024)
    to_above.wait_recv()
    passed = whole.at[:, me.y_by(3), :, first]
    far_above = net.copy(passed, passed, above)
    to_below.wait_recv()
    passed = whole.at[:, me.y_by(1), :, second]
    far_below = net.copy(passed, passed, below)
    own_branch.wait()
    load_out.wait()
    next(gate)
    far_above.wait_recv()
    far_below.wait_recv()

    bring_home([offset for offset in OFFSETS if offset not in straight])

    heads_grad = r.heads_grad

    def heads_step(step, carry):
        columns = pl.ds(pl.multiple_of(step * 256, 256), 256)
        heads_grad[:, columns] = jnp.dot(
            whole[...].reshape(384, 2048), weight[:, columns], preferred_element_type=full
        ).astype(low)
        return carry

    lax.fori_loop(0, 4, heads_step, 0)
    load_query = net.load(r.w_query, weight)

    query_low = heads_grad

    def own_input(columns):
        return hidden[:, :, columns].reshape(384, 256).astype(full)

    def normed(columns, right):
        return jnp.dot(r.normed[columns, :], right, preferred_element_type=full)

    def whole_part(columns):
        return whole[:, :, :, columns].reshape(384, 256)

    def branch_weight(columns, right):
        return contract_first(whole_part(columns), right)

    def weigh(core, left, right, target):
        def body(step, carry):
            z_hi, part = step // 2, lax.rem(step, 2)
            columns = pl.ds(pl.multiple_of((z_hi * 2 + core) * 512 + part * 256, 256), 256)
            made = left(columns, right[...]).astype(low)
            target[z_hi, pl.ds(part * 2, 2)] = made.reshape(2, 2, 64, right.shape[1])
            return carry

        lax.fori_loop(0, 4, body, 0)

    def dense(order, left, right, sending, other, middle, *more):
        weigh(1 - me.core, left, right, sending)
        task = order(net, me, sending, other, middle, *more)
        next(task)
        weigh(me.core, left, right, middle)
        return task

    out_w = dense(
        dense_z_first, branch_weight, fetch.mixed, r.sending, r.out_w_other, r.out_w_middle,
        r.out_w_slots, r.out_w_corner, r.out_w_last, r.out_w_out,
    )
    next(down)

    query, query_raw, pair = fetch.query, fetch.query_raw, fetch.pair
    cosine, sine = fetch.cosine, fetch.sine
    gain_query, gain_key = r.query_gain[...].astype(full), r.key_gain[...].astype(full)
    bias, key_sum, value_sum = r.bias, r.key_sum, r.value_sum
    pair_grad, gain_part = r.pair_grad, r.gain_part
    gain_part[...] = jnp.zeros((8, 128), full)

    def rope_back(gradient):
        return gradient * cosine[...] - turned(gradient) * sine[...]

    def attend(s):
        here = pl.ds(s * 128, 128)
        bias[...] = mask_bias(me, r.segments, s)
        key_sum[...] = jnp.zeros_like(key_sum)
        value_sum[...] = jnp.zeros_like(value_sum)

        def two_heads(step, carry):
            columns = pl.ds(pl.multiple_of(step * 256, 256), 256)

            def stacked(ref):
                both = ref[here, columns]
                return jnp.concatenate([both[:, :128], both[:, 128:]], axis=0)

            q, d = stacked(query), stacked(heads_grad)
            keys, values = pair[0, s], pair[1, s]
            lines = r.log_sum
            logs = jnp.concatenate(
                [column_of(lines[s * 8 + step * 2]), column_of(lines[s * 8 + step * 2 + 1])], axis=0
            )
            score = contract_last(q, keys) * score_scale
            score = score + jnp.concatenate([bias[...], bias[...]], axis=0)
            prob = jnp.exp(score - logs)
            prob_grad = contract_last(d, values)
            delta = jnp.sum(prob * prob_grad, axis=-1, keepdims=True)
            score_grad = (prob * (prob_grad - delta)).astype(low)
            value_sum[...] += contract_first(prob.astype(low), d)
            key_sum[...] += contract_first(score_grad, q)
            turned_grad = jnp.dot(score_grad, keys, preferred_element_type=full) * score_scale
            for half in range(2):
                run = pl.ds(pl.multiple_of(step * 256 + half * 128, 128), 128)
                grad, part = norm_back(
                    rope_back(turned_grad[half * 128 : half * 128 + 128]),
                    query_raw[here, run],
                    gain_query,
                )
                heads_grad[here, run] = grad.astype(low)
                gain_part[0:1, :] += part
            return carry

        lax.fori_loop(0, 4, two_heads, 0)
        pair_grad[s, :, :, 0] = (key_sum[...] * score_scale).astype(low).reshape(4, 2, 128, 128)
        pair_grad[s, :, :, 1] = value_sum[...].astype(low).reshape(4, 2, 128, 128)
        return x_first(
            net, me, pair_grad.at[s], r.pair_slots.at[s], r.pair_middle.at[s], r.pair_other.at[s],
            r.pair_out.at[s],
        )

    pairs = [attend(0)]
    next(pairs[0])
    next(out_w)
    pairs.append(attend(1))
    next(pairs[1])
    next(pairs[0])
    next(up)
    pairs.append(attend(2))
    next(pairs[2])
    next(pairs[1])
    next(pairs[0])

    query_w = dense(
        dense_x_first, normed, query_low, r.sending, r.query_w_other, r.query_w_middle,
        r.query_w_slots, r.query_w_corner, r.query_w_last, r.query_w_out,
    )
    next(pairs[2])
    next(pairs[1])
    next(query_w)
    next(pairs[2])

    load_query.wait()
    net.sent(far_above)
    net.sent(far_below)

    def query_step(step, carry):
        columns = pl.ds(pl.multiple_of(step * 256, 256), 256)
        made = contract_last(query_low[...], weight[columns, :])
        whole[:, :, :, columns] = made.astype(low).reshape(3, 4, 32, 256)
        return carry

    lax.fori_loop(0, 8, query_step, 0)
    next(down)

    pair_out, key_raw, pair_low = r.pair_out, r.key_raw, r.pair_low
    for s in range(3):
        next(pairs[s], None)
        rows = slice(s * 128, s * 128 + 128)
        grad, part = norm_back(rope_back(pair_out[s, 0]), key_raw[rows, :], gain_key)
        gain_part[1:2, :] += part
        pair_low[rows, :128] = grad.astype(low)
        pair_low[rows, 128:] = pair_out[s, 1].astype(low)

    w_key, w_value = fetch.w_key, fetch.w_value
    small = r.small
    normed_part = r.normed_part

    def normed_step(step, carry):
        columns = pl.ds(pl.multiple_of(step * 256, 256), 256)
        made = whole_part(columns).astype(full)
        made = made + contract_last(pair_low[:, :128], w_key[columns, :])
        made = made + contract_last(pair_low[:, 128:], w_value[columns, :])
        normal = own_input(columns) * inverse[:, 0:1]
        normed_part[:, columns] = jnp.sum(made * normal, axis=0, keepdims=True)
        whole[:, :, :, columns] = made.astype(low).reshape(3, 4, 32, 256)
        return carry

    lax.fori_loop(0, 8, normed_step, 0)
    normed_out = r.normed_out
    normed_sum = ring_reduce(
        net,
        above,
        below,
        lambda step, half: whole.at[:, me.y_by(step), :, pl.ds(half * 1024, 1024)],
        r.normed_slots,
        lambda half: normed_out.at[:, :, pl.ds(half * 1024, 1024)],
    )
    next(normed_sum)
    for step in range(16):
        run = slice(step * 128, step * 128 + 128)
        small[step : step + 1, :] = normed_part[:, run]
        small[16 + step : 17 + step, :] = r.moe_gain_part[:, run]
    small[32:40, :] = gain_part[...]
    small[40:, :] = r.peaks[...]
    smalls = all_small(
        net, me, small, r.by_core, r.by_x, r.by_z, r.by_y, r.small_out
    )
    pair_w = dense(
        dense_x_first, normed, pair_low, r.pair_sending, r.pair_w_other, r.pair_w_middle,
        r.pair_w_slots, r.pair_w_corner, r.pair_w_last, r.pair_w_out,
    )
    next(out_w)

    for made in home_came:
        made.wait_recv()
    home_own.wait()
    home_loads = [
        net.load(home.at[:, pl.ds(half * 1024, 1024)], weight.at[pl.ds(half * 768, 768)])
        for half in range(2)
    ]
    next(pair_w)
    next(smalls)
    moe_out = r.moe_out
    for half in range(2):
        home_loads[half].wait()

        def gather(step, carry, half=half):
            columns = pl.ds(pl.multiple_of(step * 256, 256), 256)
            total = contract_first(table[...], weight[half * 768 : half * 768 + 768, columns])
            moe_out[:, pl.ds(pl.multiple_of(half * 1024 + step * 256, 256), 256)] = total[:96]
            return carry

        lax.fori_loop(0, 4, gather, 0)

    def rest(*tasks):
        for task in tasks:
            next(task, None)

    rest(normed_sum, query_w, out_w, down, smalls)

    next(normed_sum, None)
    for s in range(3):
        rows = pl.ds(pl.multiple_of(me.y * 32, 32), 32)
        grad, _ = norm_back(normed_out[s], hidden[s, rows, :].astype(full), gains[...])
        normed_out[s] = grad

    rest(pair_w, out_w, query_w, down, smalls, gate, up)
    rest(pair_w, out_w, query_w, smalls)
    tasks = [pair_w, out_w, smalls, query_w, gate, up, down]
    while tasks:
        for task in list(tasks):
            if next(task, "end") == "end":
                tasks.remove(task)
    net.finish()


def dense_slots(columns, corner):
    low = jnp.bfloat16
    return [
        pltpu.VMEM((2, 4, 2, 64, columns), low),
        pltpu.VMEM((2, 4, 2, 64, columns), low),
        pltpu.VMEM((6, 2, 64, columns), low),
        pltpu.VMEM(corner + (64, columns), low),
        pltpu.VMEM((6, 32, columns), low),
    ]


def back(far, near):
    low, full = jnp.bfloat16, jnp.float32
    outs = dict(
        gate_out=(256, 768),
        up_out=(256, 768),
        down_out=(256, 768),
        query_w_out=(64, 1024),
        pair_w_out=(64, 256),
        out_w_out=(64, 1024),
        small_out=(48, 128),
        normed_out=(3, 32, 2048),
        moe_out=(96, 2048),
    )
    scratch = dict(
        gain_rows=pltpu.VMEM((1, 2048), full),
        hidden_held=pltpu.VMEM((3, 128, 2048), low),
        pair_held=pltpu.VMEM((2, 3, 1024, 128), low),
        query_held=pltpu.VMEM((384, 1024), low),
        query_raw_held=pltpu.VMEM((384, 1024), full),
        cosine_held=pltpu.VMEM((128, 128), full),
        sine_held=pltpu.VMEM((128, 128), full),
        mixed_held=pltpu.VMEM((384, 1024), low),
        key_weight=pltpu.VMEM((2048, 128), low),
        value_weight=pltpu.VMEM((2048, 128), low),
        whole=pltpu.VMEM((3, 4, 32, 2048), low),
        weight=pltpu.VMEM((2048, 1024), low),
        inverse=pltpu.VMEM((384, 128), full),
        normed=pltpu.VMEM((2048, 384), low),
        heads_grad=pltpu.VMEM((384, 1024), low),
        bias=pltpu.VMEM((128, 1024), full),
        key_sum=pltpu.VMEM((1024, 128), full),
        value_sum=pltpu.VMEM((1024, 128), full),
        pair_grad=pltpu.VMEM((3, 4, 2, 2, 128, 128), low),
        pair_slots=pltpu.VMEM((3, 6, 2, 128, 128), low),
        pair_middle=pltpu.VMEM((3, 2, 2, 128, 128), low),
        pair_other=pltpu.VMEM((3, 2, 128, 128), low),
        pair_out=pltpu.VMEM((3, 2, 128, 128), full),
        pair_low=pltpu.VMEM((384, 256), low),
        gain_part=pltpu.VMEM((8, 128), full),
        normed_part=pltpu.VMEM((1, 2048), full),
        normed_slots=pltpu.VMEM((6, 3, 32, 1024), low),
        small=pltpu.VMEM((48, 128), full),
        by_core=pltpu.VMEM((2, 48, 128), full),
        by_x=pltpu.VMEM((4, 48, 128), full),
        by_z=pltpu.VMEM((4, 48, 128), full),
        by_y=pltpu.VMEM((4, 48, 128), full),
        down_slots=pltpu.VMEM((6, 256, 768), low),
        down_middle=pltpu.VMEM((2, 256, 768), low),
        down_other=pltpu.VMEM((256, 768), low),
        down_held=pltpu.VMEM((4, 256, 768), low),
        gate_slots=pltpu.VMEM((6, 256, 768), low),
        gate_middle=pltpu.VMEM((2, 256, 768), low),
        gate_other=pltpu.VMEM((256, 768), low),
        gate_held=pltpu.VMEM((4, 256, 768), low),
        up_slots=pltpu.VMEM((6, 256, 768), low),
        up_middle=pltpu.VMEM((2, 256, 768), low),
        up_other=pltpu.VMEM((256, 768), low),
        up_held=pltpu.VMEM((4, 256, 768), low),
        sending=pltpu.VMEM((2, 4, 2, 64, 1024), low),
        pair_sending=pltpu.VMEM((2, 4, 2, 64, 256), low),
        query_w_other=None,
        query_w_middle=None,
        query_w_slots=None,
        query_w_corner=None,
        query_w_last=None,
        pair_w_other=None,
        pair_w_middle=None,
        pair_w_slots=None,
        pair_w_corner=None,
        pair_w_last=None,
        out_w_other=None,
        out_w_middle=None,
        out_w_slots=None,
        out_w_corner=None,
        out_w_last=None,
        send=pltpu.SemaphoreType.DMA((116,)),
        recv=pltpu.SemaphoreType.DMA((116,)),
        here=pltpu.SemaphoreType.DMA((34,)),
    )
    dense = dense_slots(1024, (2, 2)) + dense_slots(256, (2, 2)) + dense_slots(1024, (4,))
    scratch = {name: one or dense.pop(0) for name, one in scratch.items()}
    outs = {name: jax.ShapeDtypeStruct(size, full) for name, size in outs.items()}
    far_outs = dict(home=jax.ShapeDtypeStruct((768, 2048), low))
    return call(back_kernel, 0, far, near, outs, far_outs, scratch)


class Fetch:
    def __init__(self, net):
        self.net, self.waiting, self.held = net, {}, {}

    def start(self, name, source, target):
        self.waiting[name] = self.net.load(source, target)
        self.held[name] = target

    def __getattr__(self, name):
        if name in self.waiting:
            self.waiting.pop(name).wait()
        return self.held[name]


def token_table(ids, gates, capacity, table, info):
    low, full = jnp.bfloat16, jnp.float32
    expert = lax.broadcasted_iota(jnp.int32, (16, 32), 0)
    chosen, share = [], []
    for s in range(3):
        chosen_here = jnp.zeros((16, 32), full)
        share_here = jnp.zeros((16, 32), full)
        for k in range(8):
            named = ids[s, k : k + 1, :] == expert
            chosen_here = chosen_here + jnp.where(named, 1.0, 0.0)
            share_here = share_here + jnp.where(named, gates[s, k : k + 1, :], 0.0)
        chosen.append(chosen_here)
        share.append(share_here)
    none = jnp.zeros((16, 32), full)
    chosen = jnp.concatenate(chosen + [none], axis=1)
    share = jnp.concatenate(share + [none], axis=1)
    row = lax.broadcasted_iota(jnp.int32, (16, 128), 0)
    limit = jnp.zeros((16, 128), full)
    for e in range(16):
        limit = jnp.where(row == e, capacity[e].astype(full), limit)
    earlier = lax.broadcasted_iota(jnp.int32, (128, 128), 0) < lax.broadcasted_iota(
        jnp.int32, (128, 128), 1
    )
    before = jnp.dot(
        chosen.astype(low), jnp.where(earlier, 1.0, 0.0).astype(low), preferred_element_type=full
    )
    slot = jnp.where((chosen > 0.0) & (before < limit), before, -1.0)
    spot = lax.broadcasted_iota(jnp.int32, (48, 128), 0).astype(full)
    for place in range(16):
        core, z_hi, y = place // 8, place // 4 % 2, place % 4
        e = (z_hi * 2 + core) * 4 + y
        mask = jnp.where(slot[e : e + 1, :] == spot, 1.0, 0.0)
        table[place * 48 : place * 48 + 48, :] = mask.astype(low)
        info[core, z_hi, y] = jnp.concatenate(
            [slot[e : e + 1, :], share[e : e + 1, :], jnp.zeros((6, 128), full)], axis=0
        )


PHASES = (
    [(0, 0), (0, 1), (0, 3), (2, 0), (1, 0), (1, 1), (1, 3), (3, 0)],
    [(0, 2), (1, 2), (2, 1), (2, 3), (3, 1), (3, 3), (2, 2), (3, 2)],
)
SLOTS = {offset: (phase, spot) for phase in (0, 1) for spot, offset in enumerate(PHASES[phase])}


def spread(net, me, everyone, source, came):
    above, below = me.at(y=me.y_by(1)), me.at(y=me.y_by(3))
    sibling = me.at(core=1 - me.core)
    a, z_hi = (2, 1 - me.z_hi) if source is None else (0, me.z_hi)

    def block(b):
        return everyone.at[me.core, z_hi, me.y_by(b)]

    def half(b, part):
        return block(b).at[:, pl.ds(part * 16, 16)]

    def forward(view, device):
        return net.copy(view, view, device)

    source = block(0) if source is None else source
    up = net.copy(source, block(0), above)
    down = net.copy(source, block(0), below)
    came[a + 1, 0] = net.copy(source, block(0), sibling)
    yield
    up.wait_recv()
    far_up = forward(half(3, 0), above)
    came[a + 1, 3] = forward(block(3), sibling)
    down.wait_recv()
    far_down = forward(half(1, 1), below)
    came[a + 1, 1] = forward(block(1), sibling)
    yield
    far_up.wait_recv()
    far_down.wait_recv()
    came[a + 1, 2] = forward(block(2), sibling)
    yield


def moe_kernel(names, *refs):
    r = types.SimpleNamespace(**dict(zip(names, refs, strict=True)))
    low, full = jnp.bfloat16, jnp.float32
    me = Place()
    net = Net(r.send, r.recv, r.here)
    fetch = Fetch(net)
    fetch.start("w_gate", r.w_gate, r.gate_weight)
    fetch.start("w_up", r.w_up, r.up_weight)
    fetch.start("cots", r.cots, r.cots_held)
    fetch.start("w_down", r.w_down, r.down_weight)
    greeted = greet(peers(me) + [me.at(x=me.x_by(1)), me.at(x=me.x_by(3))])
    everyone, local, table = r.everyone, r.local, r.table
    values = r.after[...]
    inverse = lax.rsqrt(jnp.mean(values * values, axis=-1, keepdims=True) + epsilon)
    gain = wide(r.moe_gain)
    everyone[me.spot] = (values * inverse * gain).astype(low).reshape(3, 32, 2048)

    greeted()
    came = {}
    own_rows = everyone.at[me.spot]
    here_rows = spread(net, me, everyone, own_rows, came)
    next(here_rows)
    from_across = net.copy(own_rows, own_rows, me.at(z=me.z_by(2)))

    act, gate_back, up_back, back, home = r.act, r.gate_back, r.up_back, r.back, r.home
    grads = r.grads_held
    iota = lax.broadcasted_iota(jnp.int32, (48, 128), 0).astype(full)

    def slots_of(offset):
        core, z_hi, y = peer(me, *offset)[0]
        mask = r.info_in[core, z_hi, y, 0:1, :] == iota
        share = jnp.where(mask, r.info_in[core, z_hi, y, 1:2, :], 0.0)
        return mask, jnp.sum(share, axis=1, keepdims=True)

    def select(source, offset):
        mask, share = slots_of(offset)
        named = jnp.where(mask, 1.0, 0.0).astype(low)[:, :96]
        rows = source[peer(me, *offset)[0]].reshape(96, 2048)
        return jnp.dot(named, rows, preferred_element_type=full), share

    cots = fetch.cots
    for offset, slot in SLOTS.items():
        picked, share = select(cots, offset)
        r.raw_held[slot] = picked.astype(low)
        grads[slot] = (picked * share).astype(low)

    w_gate, w_up, w_down = fetch.w_gate, fetch.w_up, fetch.w_down
    back_came, dots_came, round_x, written = {}, {}, [], []
    right, left = me.at(x=me.x_by(1)), me.at(x=me.x_by(3))

    def weigh(entered, given, target):
        def body(step, carry):
            columns = pl.ds(pl.multiple_of(step * 256, 256), 256)
            left = entered[:, :, :, columns].reshape(768, 256)
            target[columns, :] = contract_first(left, given[...].reshape(768, 768)).astype(low)
            return carry

        lax.fori_loop(0, 8, body, 0)

    def chunk(target, step, half):
        start = (me.x_by(step) * 2 + half) * 256
        return target.at[pl.ds(pl.multiple_of(start, 256), 256)]

    def send_back(offsets):
        for offset in offsets:
            device = peer(me, *offset)[1]
            back_came[offset] = net.copy(back.at[SLOTS[offset]], home.at[me.spot], device)

    def through(group, low_slot, high_slot, between):
        run = slice(low_slot * 48, high_slot * 48)
        slots, rows = slice(low_slot, high_slot), (high_slot - low_slot) * 48
        for offset in PHASES[group][slots]:
            if offset in came:
                came[offset].wait_recv()
            local[SLOTS[offset]] = select(everyone, offset)[0].astype(low)

        def inner(step, carry):
            columns = pl.ds(pl.multiple_of(step * 256, 256), 256)
            entered = local[group, slots].reshape(rows, 2048)
            gate_pre = jnp.dot(entered, w_gate[:, columns], preferred_element_type=full)
            up_pre = jnp.dot(entered, w_up[:, columns], preferred_element_type=full)
            act_back = jnp.dot(
                grads[group, slots].reshape(rows, 2048),
                w_down[:, columns],
                preferred_element_type=full,
            )
            sigmoid = 1.0 / (1.0 + jnp.exp(-gate_pre))
            silu = gate_pre * sigmoid
            act[group, run, columns] = (silu * up_pre).astype(low)
            gate_back[group, run, columns] = (
                act_back * up_pre * sigmoid * (1.0 + gate_pre * (1.0 - sigmoid))
            ).astype(low)
            up_back[group, run, columns] = (act_back * silu).astype(low)
            return carry

        def outer(step, carry):
            columns = pl.ds(pl.multiple_of(step * 256, 256), 256)
            row_back = contract_last(gate_back[group, run, :], w_gate[columns, :]) + contract_last(
                up_back[group, run, :], w_up[columns, :]
            )
            back[group, slots, :, columns] = row_back.astype(low).reshape(rows // 48, 48, 256)
            return carry

        lax.fori_loop(0, 3, inner, 0)
        between()
        lax.fori_loop(0, 8, outer, 0)

    def results(group):
        given = [slots_of(offset) for offset in PHASES[group]]
        shared = jnp.concatenate([share for _, share in given], axis=0)

        def finals(step, dot):
            columns = pl.ds(pl.multiple_of(step * 256, 256), 256)
            made = contract_last(act[group], w_down[columns, :]).astype(low).astype(full)
            r.produced_held[group, :, :, columns] = (made * shared).astype(low).reshape(8, 48, 256)
            incoming = r.raw_held[group, :, :, columns].reshape(384, 256).astype(full)
            return dot + jnp.sum(made * incoming, axis=1, keepdims=True)

        dot = lax.fori_loop(0, 8, finals, jnp.zeros((384, 1), full))
        for spot, offset in enumerate(PHASES[group]):
            line = jnp.where(given[spot][0], dot[spot * 48 : spot * 48 + 48], 0.0)
            line = jnp.sum(line, axis=0, keepdims=True)
            r.dots[group, spot] = jnp.broadcast_to(line, (8, 128))
            if offset != (0, 0):
                device = peer(me, *offset)[1]
                dots_came[offset] = net.copy(
                    r.dots.at[group, spot], r.dots_in.at[me.spot], device
                )

    next(here_rows)
    from_across.wait_recv()
    other_rows = spread(net, me, everyone, None, came)
    next(other_rows)
    through(0, 0, 8, lambda: next(here_rows))
    next(other_rows)
    send_back([offset for offset in PHASES[0] if offset != (0, 0)])
    through(1, 0, 6, lambda: next(other_rows))
    send_back(PHASES[1][:6])
    through(1, 6, 8, lambda: None)
    send_back(PHASES[1][6:])
    weigh(local, gate_back, r.gate_held)
    round_x += [
        net.copy(chunk(r.gate_held, 2, 0), r.gate_slots.at[0], right),
        net.copy(chunk(r.gate_held, 2, 1), r.gate_slots.at[2], left),
        net.copy(chunk(r.gate_held, 1, 1), r.gate_slots.at[1], right),
        net.copy(chunk(r.gate_held, 3, 0), r.gate_slots.at[3], left),
    ]
    written.append(net.load(r.gate_held, r.full_gate))
    weigh(local, up_back, r.up_held)
    round_x += [
        net.copy(chunk(r.up_held, 2, 0), r.up_slots.at[0], right),
        net.copy(chunk(r.up_held, 2, 1), r.up_slots.at[1], left),
    ]
    written.append(net.load(r.up_held, r.full_up))
    results(0)
    results(1)
    weigh(grads, act, r.down_held)
    written.append(net.load(r.produced_held, r.produced))
    written.append(net.load(r.down_held, r.full_down))
    home[me.spot] = back[0, 0]
    r.dots_in[me.spot] = r.dots[0, 0]

    for offset in OFFSETS:
        dots_came[offset].wait_recv()
    lines = [r.dots_in[e // 4 % 2, e // 8, e % 4, 0:1, :] for e in range(16)]
    lines = jnp.concatenate(lines, axis=0)
    expert = lax.broadcasted_iota(jnp.int32, (16, 32), 0)
    for s in range(3):
        dots = lines[:, s * 32 : s * 32 + 32]
        for k in range(8):
            named = r.ids[s, k : k + 1, :] == expert
            r.gate_grad[s, k : k + 1, :] = jnp.sum(
                jnp.where(named, dots, 0.0), axis=0, keepdims=True
            )

    for offset in OFFSETS:
        back_came[offset].wait_recv()
    after_grad = r.after_grad

    def keep(columns, total):
        after_grad[:, columns] = total

    gather_rows(table, home, keep)
    gradient = after_grad[...]
    moe_part, gain_part = norm_back(gradient, r.after[...], gain)
    r.gain_part[...] = gain_part
    result = r.cotangent[...].reshape(96, 2048).astype(full) + moe_part
    after_grad[...] = result
    r.branch[...] = result.astype(low).reshape(3, 32, 2048)
    for one in written:
        one.wait()
    for one in round_x:
        one.wait_recv()
    net.finish()


def moe(far, near):
    low, full = jnp.bfloat16, jnp.float32
    rows, home = (2, 8, 48, 2048), (2, 2, 4, 48, 2048)
    outs = dict(
        after_grad=jax.ShapeDtypeStruct((96, 2048), full),
        branch=jax.ShapeDtypeStruct((3, 32, 2048), low),
        gain_part=jax.ShapeDtypeStruct((1, 2048), full),
        gate_grad=jax.ShapeDtypeStruct((3, 8, 32), full),
    )
    far_outs = dict(
        produced=jax.ShapeDtypeStruct(rows, low),
        full_gate=jax.ShapeDtypeStruct((2048, 768), low),
        full_up=jax.ShapeDtypeStruct((2048, 768), low),
        full_down=jax.ShapeDtypeStruct((2048, 768), low),
        gate_slots=jax.ShapeDtypeStruct((4, 256, 768), low),
        up_slots=jax.ShapeDtypeStruct((2, 256, 768), low),
    )
    scratch = dict(
        everyone=pltpu.VMEM((2, 2, 4, 3, 32, 2048), low),
        local=pltpu.VMEM(rows, low),
        cots_held=pltpu.VMEM((2, 2, 4, 3, 32, 2048), low),
        raw_held=pltpu.VMEM(rows, low),
        grads_held=pltpu.VMEM(rows, low),
        produced_held=pltpu.VMEM(rows, low),
        back=pltpu.VMEM(rows, low),
        home=pltpu.VMEM(home, low),
        gate_weight=pltpu.VMEM((2048, 768), low),
        up_weight=pltpu.VMEM((2048, 768), low),
        down_weight=pltpu.VMEM((2048, 768), low),
        gate_held=pltpu.VMEM((2048, 768), low),
        up_held=pltpu.VMEM((2048, 768), low),
        down_held=pltpu.VMEM((2048, 768), low),
        act=pltpu.VMEM((2, 384, 768), low),
        gate_back=pltpu.VMEM((2, 384, 768), low),
        up_back=pltpu.VMEM((2, 384, 768), low),
        dots=pltpu.VMEM((2, 8, 8, 128), full),
        dots_in=pltpu.VMEM((2, 2, 4, 8, 128), full),
        send=pltpu.SemaphoreType.DMA((54,)),
        recv=pltpu.SemaphoreType.DMA((54,)),
        here=pltpu.SemaphoreType.DMA((8,)),
    )
    return call(moe_kernel, 1, far, near, outs, far_outs, scratch)


def call(kernel, number, far, near, outs, far_outs, scratch):
    names = list(far) + list(near) + list(outs) + list(far_outs) + list(scratch)
    shapes = {**outs, **far_outs}
    results = pl.pallas_call(
        functools.partial(kernel, names),
        out_shape=list(shapes.values()),
        in_specs=[ANY] * len(far)
        + [SMEM if one.ndim == 1 else VMEM for one in near.values()],
        out_specs=[VMEM] * len(outs) + [ANY] * len(far_outs),
        scratch_shapes=list(scratch.values()),
        compiler_params=pltpu.CompilerParams(
            collective_id=number, has_side_effects=True, vmem_limit_bytes=63 << 20
        ),
        name=kernel.__name__,
    )(*far.values(), *near.values())
    return types.SimpleNamespace(**dict(zip(shapes, results, strict=True)))


def front_kernel(names, *refs):
    r = types.SimpleNamespace(**dict(zip(names, refs, strict=True)))
    low, full = jnp.bfloat16, jnp.float32
    score_scale = HEAD_SIZE ** (-0.5)
    me = Place()
    net = Net(r.send, r.recv, r.here)
    fetch = Fetch(net)
    fetch.start("hidden", r.hidden, r.hidden_held)
    fetch.start("w_pair", r.w_key, r.key_weight)
    fetch.start("w_value", r.w_value, r.value_weight)
    fetch.start("cosine", r.cosine.at[me.context], r.cosine_held)
    fetch.start("sine", r.sine.at[me.context], r.sine_held)
    fetch.start("w_query", r.w_query, r.query_weight)
    fetch.start("w_out", r.w_out, r.out_weight)
    beside = me.at(z=me.z + 1 - 2 * me.z_lo)
    right, left = me.at(x=me.x_by(1)), me.at(x=me.x_by(3))
    greeted = greet([right, left, beside] + peers(me))
    gains = r.gain_rows
    gains[...] = wide(r.attn_gain)

    above, below = me.at(y=me.y_by(1)), me.at(y=me.y_by(3))
    across, came, told = me.at(z=me.z_by(2)), {}, []
    greeted()
    own_cot = net.load(r.cotangent, r.cots.at[me.spot])
    here_cot = spread(net, me, r.cots, r.cotangent, came)
    next(here_cot)
    from_across = net.copy(r.cotangent, r.cots.at[me.spot], across)

    hidden, normed = fetch.hidden, r.normed
    for s in range(3):
        values = hidden[s].astype(full)
        root = lax.rsqrt(jnp.mean(values * values, axis=-1, keepdims=True) + epsilon)
        normed[s * 128 : s * 128 + 128, :] = (values * root * gains[...]).astype(low)

    def rope(values):
        cosine = jnp.concatenate([fetch.cosine[...]] * 3, axis=0)
        sine = jnp.concatenate([fetch.sine[...]] * 3, axis=0)
        return values * cosine + turned(values) * sine

    def head_norm(raw, gain):
        return raw * lax.rsqrt(jnp.mean(raw * raw, axis=-1, keepdims=True) + epsilon) * gain

    pair, key_raw = r.pair_held, r.key_raw
    made = jnp.dot(normed[...], fetch.w_pair[...], preferred_element_type=full)
    key_raw[...] = made
    keys = rope(head_norm(made, r.key_gain[...].astype(full))).astype(low)
    values = jnp.dot(normed[...], fetch.w_value[...], preferred_element_type=full).astype(low)
    own = pl.ds(pl.multiple_of(me.context * 128, 128), 128)
    pair[0, :, own, :] = keys.reshape(3, 128, 128)
    pair[1, :, own, :] = values.reshape(3, 128, 128)

    def block(x, z_lo):
        return pl.ds(pl.multiple_of((x * 2 + z_lo) * 128, 128), 128)

    def piece(s, x, z_lo, half=None):
        rows = block(x, z_lo)
        return pair.at[:, s, rows, :] if half is None else pair.at[half, s, rows, :]

    def pass_on(view, device):
        return net.copy(view, view, device)

    own_z, other_z = me.z_lo, 1 - me.z_lo

    def bring_pair(s):
        from_z = pass_on(piece(s, me.x, own_z), beside)
        came = [(pass_on(piece(s, me.x, own_z), right), pass_on(piece(s, me.x, own_z), left))]
        yield
        from_z.wait_recv()
        came.append((pass_on(piece(s, me.x, other_z), right), pass_on(piece(s, me.x, other_z), left)))
        yield
        far = []
        for zs, (from_left, from_right) in zip((own_z, other_z), came, strict=True):
            from_left.wait_recv()
            far.append(pass_on(piece(s, me.x_by(3), zs, 0), right))
            from_right.wait_recv()
            far.append(pass_on(piece(s, me.x_by(1), zs, 1), left))
            yield
        for one in far:
            one.wait_recv()
        yield

    brought = [bring_pair(s) for s in range(3)]
    for s in range(3):
        next(brought[s])

    token_table(r.ids, r.gates, r.capacity, r.table, r.info)
    r.info_in[me.spot] = r.info[me.spot]
    for a, b in OFFSETS:
        spot, device = peer(me, a, b)
        told.append(net.copy(r.info.at[spot], r.info_in.at[me.spot], device))

    w_query, query, query_raw = fetch.w_query, r.query_held, r.query_raw_held

    def project(step, carry):
        columns = pl.ds(pl.multiple_of(step * 256, 256), 256)
        made = jnp.dot(normed[...], w_query[:, columns], preferred_element_type=full)
        query_raw[:, columns] = made
        for half in range(2):
            run = pl.ds(pl.multiple_of(step * 256 + half * 128, 128), 128)
            one = head_norm(made[:, half * 128 : half * 128 + 128], r.query_gain[...].astype(full))
            query[:, run] = rope(one).astype(low)
        return carry

    lax.fori_loop(0, 4, project, 0)
    written = [net.load(query, r.query), net.load(query_raw, r.query_raw)]
    for s in range(3):
        next(brought[s])
    next(here_cot)
    from_across.wait_recv()
    other_cot = spread(net, me, r.cots, None, came)
    next(other_cot)
    next(brought[0])
    next(brought[1])
    next(brought[0])
    next(brought[2])
    next(brought[1])

    bias, peaks, mixed = r.bias, r.peak_rows, r.mixed_held
    peaks[...] = jnp.full((8, 1, 128), -jnp.inf, full)

    def attend(s):
        here = pl.ds(s * 128, 128)
        bias[...] = mask_bias(me, r.segments, s)

        def two_heads(step, carry):
            columns = pl.ds(pl.multiple_of(step * 256, 256), 256)
            both = query[here, columns]
            q = jnp.concatenate([both[:, :128], both[:, 128:]], axis=0)
            score = contract_last(q, pair[0, s]) * score_scale
            score = score + jnp.concatenate([bias[...], bias[...]], axis=0)
            highest = jnp.max(score, axis=-1, keepdims=True)
            weight = jnp.exp(score - highest)
            total = jnp.sum(weight, axis=-1, keepdims=True)
            prob = (weight * (1.0 / total)).astype(low)
            logs = highest + jnp.log(total)
            heads = jnp.dot(prob, pair[1, s], preferred_element_type=full).astype(low)
            for half in range(2):
                part = slice(half * 128, half * 128 + 128)
                head = step * 2 + half
                run = pl.ds(pl.multiple_of(step * 256 + half * 128, 128), 128)
                mixed[here, run] = heads[part]
                r.log_sum[s * 8 + head] = row_of(logs[part])
                top = jnp.max(highest[part], axis=0, keepdims=True)
                peaks[head] = jnp.maximum(peaks[head], top)
            return carry

        lax.fori_loop(0, 4, two_heads, 0)
    shares, after = r.shares, r.after_sum

    def branch(s):
        w_out = fetch.w_out

        def body(step, carry):
            columns = pl.ds(pl.multiple_of(step * 256, 256), 256)
            made = contract_last(mixed[pl.ds(s * 128, 128), :], w_out[columns, :])
            shares[s, :, :, columns] = made.astype(low).reshape(4, 32, 256)
            return carry

        lax.fori_loop(0, 8, body, 0)
        return ring_reduce(
            net,
            above,
            below,
            lambda step, half: shares.at[s, me.y_by(step), :, pl.ds(half * 1024, 1024)],
            r.branch_slots.at[s],
            lambda half: after.at[s, :, pl.ds(half * 1024, 1024)],
        )

    next(brought[0])
    attend(0)
    next(brought[2])
    first = branch(0)
    next(first)
    next(brought[1])
    attend(1)
    next(other_cot)
    second = branch(1)
    next(second)
    next(first)
    next(brought[2])
    attend(2)
    third = branch(2)
    next(third)
    next(second)
    next(here_cot)
    written.append(net.load(pair, r.pair))
    written.append(net.load(mixed, r.mixed))
    for head in range(8):
        r.peaks[head : head + 1, :] = peaks[head]
    next(first, None)
    next(third)
    next(other_cot)
    next(second, None)
    next(third, None)
    own_rows = pl.ds(pl.multiple_of(me.y * 32, 32), 32)
    for s in range(3):
        r.after[s * 32 : s * 32 + 32, :] = after[s] + hidden[s, own_rows, :].astype(full)
    for one in list(came.values()) + told:
        one.wait_recv()
    own_cot.wait()
    for one in written:
        one.wait()
    net.finish()


def row_of(column):
    eye = lax.broadcasted_iota(jnp.int32, (128, 128), 0) == lax.broadcasted_iota(
        jnp.int32, (128, 128), 1
    )
    return jnp.sum(jnp.where(eye, column, 0.0), axis=0, keepdims=True)


def mask_bias(me, segments, s):
    spot = me.context * 128 + lax.broadcasted_iota(jnp.int32, (128, 1024), 0)
    own = segments[s : s + 1, pl.ds(pl.multiple_of(me.context * 128, 128), 128)]
    document = column_of(own.astype(jnp.float32))
    allowed = (document == segments[s : s + 1, :].astype(jnp.float32)) & (
        lax.broadcasted_iota(jnp.int32, (128, 1024), 1) <= spot
    )
    return jnp.where(allowed, 0.0, masked_value)


def front(far, near):
    low, full = jnp.bfloat16, jnp.float32
    outs = dict(
        key_raw=jax.ShapeDtypeStruct((384, 128), full),
        log_sum=jax.ShapeDtypeStruct((24, 1, 128), full),
        peaks=jax.ShapeDtypeStruct((8, 128), full),
        after=jax.ShapeDtypeStruct((96, 2048), full),
        table=jax.ShapeDtypeStruct((768, 128), low),
        info_in=jax.ShapeDtypeStruct((2, 2, 4, 8, 128), full),
    )
    far_outs = dict(
        query=jax.ShapeDtypeStruct((384, 1024), low),
        query_raw=jax.ShapeDtypeStruct((384, 1024), full),
        pair=jax.ShapeDtypeStruct((2, 3, 1024, 128), low),
        mixed=jax.ShapeDtypeStruct((384, 1024), low),
        cots=jax.ShapeDtypeStruct((2, 2, 4, 3, 32, 2048), low),
    )
    scratch = dict(
        gain_rows=pltpu.VMEM((1, 2048), full),
        hidden_held=pltpu.VMEM((3, 128, 2048), low),
        key_weight=pltpu.VMEM((2048, 128), low),
        value_weight=pltpu.VMEM((2048, 128), low),
        cosine_held=pltpu.VMEM((128, 128), full),
        sine_held=pltpu.VMEM((128, 128), full),
        query_weight=pltpu.VMEM((2048, 1024), low),
        out_weight=pltpu.VMEM((2048, 1024), low),
        normed=pltpu.VMEM((384, 2048), low),
        pair_held=pltpu.VMEM((2, 3, 1024, 128), low),
        info=pltpu.VMEM((2, 2, 4, 8, 128), full),
        query_held=pltpu.VMEM((384, 1024), low),
        query_raw_held=pltpu.VMEM((384, 1024), full),
        bias=pltpu.VMEM((128, 1024), full),
        peak_rows=pltpu.VMEM((8, 1, 128), full),
        mixed_held=pltpu.VMEM((384, 1024), low),
        shares=pltpu.VMEM((3, 4, 32, 2048), low),
        branch_slots=pltpu.VMEM((3, 6, 32, 1024), low),
        after_sum=pltpu.VMEM((3, 32, 2048), full),
        send=pltpu.SemaphoreType.DMA((84,)),
        recv=pltpu.SemaphoreType.DMA((84,)),
        here=pltpu.SemaphoreType.DMA((16,)),
    )
    return call(front_kernel, 2, far, near, outs, far_outs, scratch)


def finish_kernel(names, *refs):
    r = types.SimpleNamespace(**dict(zip(names, refs, strict=True)))
    r.layer_out[...] = r.after[...] + r.moe_out[...]
    r.input_grad[...] = r.after_grad[...] + r.normed_out[...].reshape(96, 2048)
    r.gate_w[...] = r.gate_part[...]
    r.up_w[...] = r.up_part[...]
    r.down_w[...] = r.down_part[...]
    r.query_w[...] = r.query_part[...]
    r.out_w[...] = r.out_part[...]
    r.gate_grad[...] = r.gate_grad_part[...]
    r.key_w[...] = r.pair_w[:, :128]
    r.value_w[...] = r.pair_w[:, 128:]
    r.attn_gain[...] = r.small[:16]
    r.moe_gain[...] = r.small[16:32]
    r.query_gain[...] = r.small[32:33]
    r.key_gain[...] = r.small[33:34]
    diagonal = lax.broadcasted_iota(jnp.int32, (8, 128), 0) == lax.broadcasted_iota(
        jnp.int32, (8, 128), 1
    )
    peaks = jnp.sum(jnp.where(diagonal, r.small[40:], 0.0), axis=0, keepdims=True)
    r.clip[...] = (clip_limit / jnp.maximum(peaks, clip_limit))[:, :8]


def finish(near):
    outs = dict(
        layer_out=(96, 2048),
        input_grad=(96, 2048),
        gate_w=(256, 768),
        up_w=(256, 768),
        down_w=(256, 768),
        query_w=(64, 1024),
        out_w=(64, 1024),
        gate_grad=(3, 8, 32),
        key_w=(64, 128),
        value_w=(64, 128),
        attn_gain=(16, 128),
        moe_gain=(16, 128),
        query_gain=(1, 128),
        key_gain=(1, 128),
        clip=(1, 8),
    )
    results = pl.pallas_call(
        functools.partial(finish_kernel, list(near) + list(outs)),
        out_shape=[jax.ShapeDtypeStruct(size, jnp.float32) for size in outs.values()],
        in_specs=[VMEM] * len(near),
        out_specs=[VMEM] * len(outs),
        compiler_params=pltpu.CompilerParams(vmem_limit_bytes=62 << 20),
        name="finish",
    )(*near.values())
    return types.SimpleNamespace(**dict(zip(outs, results, strict=True)))


def shards(
    hidden_in,
    segments,
    attn_gain,
    query_gain,
    key_gain,
    w_query,
    key_weight_matrix,
    value_weight_matrix,
    w_out,
    moe_gain,
    expert_ids,
    gate_values,
    capacity,
    w_gate,
    w_up,
    w_down,
    cotangent,
):
    attn_wide, moe_wide = attn_gain.reshape(16, 128), moe_gain.reshape(16, 128)
    query_row, key_row = query_gain[None], key_gain[None]
    ids, gates = expert_ids.swapaxes(1, 2), gate_values.swapaxes(1, 2)
    cosine, sine = rotary()
    first = front(
        dict(
            hidden=hidden_in,
            w_key=key_weight_matrix,
            w_value=value_weight_matrix,
            cosine=cosine,
            sine=sine,
            w_query=w_query,
            cotangent=cotangent,
            w_out=w_out,
        ),
        dict(
            attn_gain=attn_wide,
            query_gain=query_row,
            key_gain=key_row,
            segments=segments,
            ids=ids,
            gates=gates,
            capacity=capacity,
        ),
    )
    second = moe(
        dict(w_gate=w_gate[0], w_up=w_up[0], w_down=w_down[0], cots=first.cots),
        dict(
            after=first.after,
            cotangent=cotangent,
            moe_gain=moe_wide,
            ids=ids,
            table=first.table,
            info_in=first.info_in,
        ),
    )
    done = back(
        dict(
            branch=second.branch,
            w_out=w_out,
            w_query=w_query,
            gate=second.full_gate.reshape(4, 2, 256, 768),
            up=second.full_up.reshape(4, 2, 256, 768),
            down=second.full_down.reshape(4, 2, 256, 768),
            produced=second.produced,
            gate_begun=second.gate_slots,
            up_begun=second.up_slots,
            hidden=hidden_in,
            mixed=first.mixed,
            query=first.query,
            query_raw=first.query_raw,
            pair=first.pair,
            cosine=cosine,
            sine=sine,
            w_key=key_weight_matrix,
            w_value=value_weight_matrix,
        ),
        dict(
            table=first.table,
            key_raw=first.key_raw,
            log_sum=first.log_sum,
            segments=segments,
            attn_gain=attn_wide,
            query_gain=query_row,
            key_gain=key_row,
            moe_gain_part=second.gain_part,
            peaks=first.peaks,
        ),
    )
    last = finish(
        dict(
            after=first.after,
            moe_out=done.moe_out,
            after_grad=second.after_grad,
            normed_out=done.normed_out,
            small=done.small_out,
            pair_w=done.pair_w_out,
            gate_part=done.gate_out,
            up_part=done.up_out,
            down_part=done.down_out,
            query_part=done.query_w_out,
            out_part=done.out_w_out,
            gate_grad_part=second.gate_grad,
        )
    )
    layer_out = last.layer_out.reshape(cotangent.shape)
    input_grad = last.input_grad.reshape(cotangent.shape)
    gate_grad = last.gate_grad.swapaxes(1, 2)
    w_key_grad, w_value_grad = last.key_w, last.value_w
    w_query_grad, w_out_grad = last.query_w, last.out_w
    w_gate_grad, w_up_grad, w_down_grad = last.gate_w[None], last.up_w[None], last.down_w[None]
    attn_gain_grad, moe_gain_grad = last.attn_gain.reshape(2048), last.moe_gain.reshape(2048)
    query_gain_grad, key_gain_grad = last.query_gain.reshape(128), last.key_gain.reshape(128)
    head_clip_scale = last.clip.reshape(8)
    return (
        layer_out,
        input_grad,
        attn_gain_grad,
        query_gain_grad,
        key_gain_grad,
        w_query_grad,
        w_key_grad,
        w_value_grad,
        w_out_grad,
        moe_gain_grad,
        gate_grad,
        w_gate_grad,
        w_up_grad,
        w_down_grad,
        head_clip_scale,
    )


def solution(mesh):
    in_specs = (
        P("dp", "context", None),
        P("dp", None),
        P(),
        P(),
        P(),
        P(None, "experts"),
        P(None, "experts"),
        P(None, "experts"),
        P(None, "experts"),
        P(),
        P("dp", ("context", "experts"), None),
        P("dp", ("context", "experts"), None),
        P(),
        P(("dp", "experts"), None, None),
        P(("dp", "experts"), None, None),
        P(("dp", "experts"), None, None),
        P("dp", ("context", "experts"), None),
    )
    out_specs = (
        P("dp", ("context", "experts"), None),
        P("dp", ("context", "experts"), None),
        P(),
        P(),
        P(),
        P(("dp", "context"), "experts"),
        P(("dp", "context"), "experts"),
        P(("dp", "context"), "experts"),
        P(("dp", "context"), "experts"),
        P(),
        P("dp", ("context", "experts"), None),
        P(("dp", "experts"), "context", None),
        P(("dp", "experts"), "context", None),
        P(("dp", "experts"), "context", None),
        P("experts"),
    )
    return jax.shard_map(shards, mesh=mesh, in_specs=in_specs, out_specs=out_specs, check_vma=False)
```

```python
import functools
import itertools
import types

import jax
import jax.numpy as jnp
import numpy as np
from jax import lax
from jax.experimental import pallas as pl
from jax.experimental.pallas import tpu as pltpu
from jax.sharding import PartitionSpec as P

HEAD_SIZE = 128
MESH = pl.DeviceIdType.MESH
VMEM = pl.BlockSpec(memory_space=pltpu.VMEM)
ANY = pl.BlockSpec(memory_space=pl.ANY)
SMEM = pl.BlockSpec(memory_space=pltpu.SMEM)


epsilon = 1e-06
rope_base = 1000000.0
clip_limit = 1.0
masked_value = -1e30


def rotary():
    inverse = 1.0 / rope_base ** (np.arange(0, HEAD_SIZE, 2) / HEAD_SIZE)
    angle = np.arange(1024)[:, None] * inverse[None, :]
    cosine = np.concatenate([np.cos(angle), np.cos(angle)], axis=-1)
    sine = np.concatenate([-np.sin(angle), np.sin(angle)], axis=-1)
    shape = (8, 128, HEAD_SIZE)
    return (
        jnp.asarray(cosine.reshape(shape), jnp.float32),
        jnp.asarray(sine.reshape(shape), jnp.float32),
    )


def contract_last(left, right):
    return lax.dot_general(
        left, right, (((1,), (1,)), ((), ())), preferred_element_type=jnp.float32
    )


def contract_first(left, right):
    return lax.dot_general(
        left, right, (((0,), (0,)), ((), ())), preferred_element_type=jnp.float32
    )


class Place:
    def __init__(self):
        dp = lax.axis_index("dp")
        context = lax.axis_index("context")
        self.dp, self.context, self.y = dp, context, lax.axis_index("experts")
        self.core, self.z_hi = lax.rem(dp, 2), dp // 2
        self.x, self.z_lo = context // 2, lax.rem(context, 2)
        self.z = self.z_hi * 2 + self.z_lo
        self.spot = (self.core, self.z_hi, self.y)

    def at(self, x=None, y=None, z=None, core=None):
        x = self.x if x is None else x
        y = self.y if y is None else y
        z = self.z if z is None else z
        core = self.core if core is None else core
        return (z // 2 * 2 + core, x * 2 + lax.rem(z, 2), y)

    def x_by(self, step):
        return lax.rem(self.x + step, 4)

    def y_by(self, step):
        return lax.rem(self.y + step, 4)

    def z_by(self, step):
        return lax.rem(self.z + step, 4)


class Net:
    def __init__(self, send, recv, here=None):
        self.send, self.recv, self.copies = send, recv, []
        self.here, self.loads = here, 0

    def copy(self, src, dst, device):
        spot = len(self.copies)
        made = pltpu.make_async_remote_copy(
            src_ref=src,
            dst_ref=dst,
            send_sem=self.send.at[spot],
            recv_sem=self.recv.at[spot],
            device_id=device,
            device_id_type=MESH,
        )
        made.start()
        self.copies.append(made)
        return made

    def load(self, src, dst):
        made = pltpu.make_async_copy(src, dst, self.here.at[self.loads])
        self.loads += 1
        made.start()
        return made

    def sent(self, made):
        made.wait_send()
        self.copies = [None if one is made else one for one in self.copies]

    def finish(self):
        for made in self.copies:
            if made is not None:
                made.wait_send()


def greet(devices):
    barrier = pltpu.get_barrier_semaphore()
    for device in devices:
        pl.semaphore_signal(barrier, inc=1, device_id=device, device_id_type=MESH)
    return lambda: pl.semaphore_wait(barrier, len(devices))


def wide(ref):
    values = ref[...].astype(jnp.float32)
    return jnp.concatenate([values[step : step + 1] for step in range(16)], axis=1)


def add_into(target, parts, block=32):
    rows = target.shape[-2]
    block = min(block, rows)
    for lead in itertools.product(*[range(size) for size in target.shape[:-2]]):

        def body(step, carry, lead=lead):
            spot = lead + (pl.ds(pl.multiple_of(step * block, block), block),)
            total = parts[0][spot].astype(jnp.float32)
            for part in parts[1:]:
                total = total + part[spot].astype(jnp.float32)
            target[spot] = total.astype(target.dtype)
            return carry

        lax.fori_loop(0, rows // block, body, 0)


def ring_reduce(net, plus, minus, own, slots, target, held=None, begun=None):
    held = own if held is None else held
    done = 0 if begun is None else begun.shape[0]
    if done == 4:
        loads = [net.load(begun, slots.at[pl.ds(0, 4)])]
    elif done == 2:
        loads = [net.load(begun.at[step], slots.at[step * 2]) for step in range(2)]
    else:
        first_plus = net.copy(own(2, 0), slots.at[0], plus)
        first_minus = net.copy(own(2, 1), slots.at[2], minus)
    if done != 4:
        side_plus = net.copy(own(1, 1), slots.at[1], plus)
        side_minus = net.copy(own(3, 0), slots.at[3], minus)
    yield
    if done:
        for load in loads:
            load.wait()
    else:
        first_plus.wait_recv()
        first_minus.wait_recv()
    add_into(slots.at[0], [slots.at[0], held(1, 0)])
    last_plus = net.copy(slots.at[0], slots.at[4], plus)
    add_into(slots.at[2], [slots.at[2], held(3, 1)])
    last_minus = net.copy(slots.at[2], slots.at[5], minus)
    yield
    if done != 4:
        side_minus.wait_recv()
        side_plus.wait_recv()
    last_plus.wait_recv()
    add_into(target(0), [held(0, 0), slots.at[3], slots.at[4]])
    last_minus.wait_recv()
    add_into(target(1), [held(0, 1), slots.at[1], slots.at[5]])


def x_first(net, me, source, slots, middle, other, out, held=None, begun=None):
    staged = None
    if held is not None:
        order = {(1, 0): 0, (3, 1): 1, (0, 0): 2, (0, 1): 3}
        loads = [
            net.load(source.at[me.x_by(step), half], held.at[spot])
            for (step, half), spot in order.items()
        ]

        def staged(step, half):
            return held.at[order[step, half]]

    ring = ring_reduce(
        net,
        me.at(x=me.x_by(1)),
        me.at(x=me.x_by(3)),
        lambda step, half: source.at[me.x_by(step), half],
        slots,
        lambda half: middle.at[half],
        staged,
        begun,
    )
    next(ring)
    yield
    if held is not None:
        for load in loads:
            load.wait()
    yield from ring
    across = net.copy(middle.at[1 - me.z_lo], other, me.at(z=me.z + 1 - 2 * me.z_lo))
    yield
    across.wait_recv()
    add_into(out, [middle.at[me.z_lo], other])


def core_pair(net, me, sending, other, middle):
    across = net.copy(sending, other, me.at(core=1 - me.core))
    yield
    net.sent(across)
    across.wait_recv()
    add_into(middle, [middle, other])


def dense_x_first(net, me, sending, other, middle, slots, corner, last, out):
    yield from core_pair(net, me, sending, other, middle)
    yield from ring_reduce(
        net,
        me.at(x=me.x_by(1)),
        me.at(x=me.x_by(3)),
        lambda step, half: middle.at[half, me.x_by(step)],
        slots,
        lambda half: corner.at[half],
    )
    half_rows = corner.shape[2] // 2
    yield from ring_reduce(
        net,
        me.at(z=me.z_by(1)),
        me.at(z=me.z_by(3)),
        lambda step, half: corner.at[
            me.z_by(step) // 2, lax.rem(me.z_by(step), 2), pl.ds(half * half_rows, half_rows)
        ],
        last,
        lambda half: out.at[pl.ds(half * half_rows, half_rows)],
    )


def dense_z_first(net, me, sending, other, middle, slots, corner, last, out):
    yield from core_pair(net, me, sending, other, middle)
    yield from ring_reduce(
        net,
        me.at(z=me.z_by(1)),
        me.at(z=me.z_by(3)),
        lambda step, half: middle.at[
            me.z_by(step) // 2, pl.ds(half * 2, 2), lax.rem(me.z_by(step), 2)
        ],
        slots,
        lambda half: corner.at[pl.ds(half * 2, 2)],
    )
    half_rows = corner.shape[1] // 2
    yield from ring_reduce(
        net,
        me.at(x=me.x_by(1)),
        me.at(x=me.x_by(3)),
        lambda step, half: corner.at[me.x_by(step), pl.ds(half * half_rows, half_rows)],
        last,
        lambda half: out.at[pl.ds(half * half_rows, half_rows)],
    )


def all_sum(net, devices, spot, own, slots, most):
    slots[spot] = own[...]
    sent = [net.copy(own, slots.at[spot], device) for device in devices]
    yield
    for made in sent:
        made.wait_recv()
    count = slots.shape[0]
    total = slots[0]
    peak = slots[0, most:]
    for step in range(1, count):
        total = total + slots[step]
        peak = jnp.maximum(peak, slots[step, most:])
    for made in sent:
        net.sent(made)
    own[:most] = total[:most]
    own[most:] = peak


def all_small(net, me, working, by_core, by_x, by_z, by_y, out):
    yield from all_sum(net, [me.at(core=1 - me.core)], me.core, working, by_core, 40)
    yield from all_sum(net, [me.at(x=me.x_by(s)) for s in (1, 2, 3)], me.x, working, by_x, 40)
    yield from all_sum(net, [me.at(z=me.z_by(s)) for s in (1, 2, 3)], me.z, working, by_z, 40)
    out[40:] = working[40:]
    yield from all_sum(net, [me.at(y=me.y_by(s)) for s in (1, 2, 3)], me.y, working, by_y, 40)
    out[:40] = working[:40]


OFFSETS = [(a, b) for a in (2, 0, 3, 1) for b in (0, 1, 3, 2) if a or b]


def peer(me, a, b):
    z = me.z if a < 2 else lax.rem(me.z + 2, 4)
    core = me.core if a % 2 == 0 else 1 - me.core
    y = me.y_by(b)
    return (core, z // 2, y), me.at(z=z, core=core, y=y)


def peers(me):
    return [peer(me, a, b)[1] for a, b in OFFSETS]


def gather_rows(table, home, store):
    def body(step, carry):
        columns = pl.ds(pl.multiple_of(step * 256, 256), 256)
        rows = home[:, :, :, :, columns].reshape(768, 256)
        total = contract_first(table[...], rows)
        store(columns, total[:96])
        return carry

    lax.fori_loop(0, home.shape[4] // 256, body, 0)


def turned(values):
    return pltpu.roll(values, 64, 1)


def column_of(row):
    eye = lax.broadcasted_iota(jnp.int32, (128, 128), 0) == lax.broadcasted_iota(
        jnp.int32, (128, 128), 1
    )
    return jnp.sum(jnp.where(eye, row, 0.0), axis=1, keepdims=True)


def norm_back(gradient, raw, gain):
    inverse = lax.rsqrt(jnp.mean(raw * raw, axis=-1, keepdims=True) + epsilon)
    normal = raw * inverse
    scaled = gradient * gain
    result = inverse * (scaled - normal * jnp.mean(scaled * normal, axis=-1, keepdims=True))
    return result, jnp.sum(gradient * normal, axis=0, keepdims=True)


def back_kernel(names, *refs):
    r = types.SimpleNamespace(**dict(zip(names, refs, strict=True)))
    low, full = jnp.bfloat16, jnp.float32
    score_scale = HEAD_SIZE ** (-0.5)
    me = Place()
    net = Net(r.send, r.recv, r.here)
    fetch = Fetch(net)
    fetch.start("hidden", r.hidden, r.hidden_held)
    greeted = greet(
        [
            me.at(x=me.x_by(1)),
            me.at(x=me.x_by(3)),
            me.at(z=me.z_by(1)),
            me.at(z=me.z_by(3)),
            me.at(x=me.x_by(2)),
        ]
        + peers(me)
    )
    gains = r.gain_rows
    gains[...] = wide(r.attn_gain)
    greeted()

    branch, whole = r.branch, r.whole
    above, below = me.at(y=me.y_by(1)), me.at(y=me.y_by(3))
    to_above = net.copy(branch, whole.at[:, me.y], above)
    to_below = net.copy(branch, whole.at[:, me.y], below)
    own_branch = net.load(branch, whole.at[:, me.y])
    weight = r.weight
    load_out = net.load(r.w_out, weight)
    gate = x_first(
        net, me, r.gate, r.gate_slots, r.gate_middle, r.gate_other, r.gate_out, r.gate_held,
        r.gate_begun,
    )
    up = x_first(
        net, me, r.up, r.up_slots, r.up_middle, r.up_other, r.up_out, r.up_held, r.up_begun
    )
    down = x_first(
        net, me, r.down, r.down_slots, r.down_middle, r.down_other, r.down_out, r.down_held
    )
    next(gate)
    next(gate)
    next(up)
    produced, home, table = r.produced, r.home, r.table
    start = me.core * 384 + me.z_hi * 192 + me.y * 48
    mine = pl.ds(pl.multiple_of(start, 16), 48)
    home_came = []

    def bring_home(offsets):
        for a, b in offsets:
            device = peer(me, a, b)[1]
            home_came.append(net.copy(produced.at[SLOTS[a, b]], home.at[mine], device))

    straight = [(2, 0), (3, 0)]
    bring_home(straight)
    home_own = net.load(produced.at[0, 0], home.at[mine])
    next(up)
    fetch.start("pair", r.pair, r.pair_held)
    fetch.start("query", r.query, r.query_held)
    fetch.start("query_raw", r.query_raw, r.query_raw_held)
    fetch.start("cosine", r.cosine.at[me.context], r.cosine_held)
    fetch.start("sine", r.sine.at[me.context], r.sine_held)
    fetch.start("mixed", r.mixed, r.mixed_held)
    fetch.start("w_key", r.w_key, r.key_weight)
    fetch.start("w_value", r.w_value, r.value_weight)

    hidden, inverse = fetch.hidden, r.inverse
    for s in range(3):
        rows = slice(s * 128, s * 128 + 128)
        values = hidden[s].astype(full)
        root = lax.rsqrt(jnp.mean(values * values, axis=-1, keepdims=True) + epsilon)
        inverse[rows, :] = jnp.broadcast_to(root, (128, 128))
        for step in range(8):
            run = slice(step * 256, step * 256 + 256)
            tile = hidden[s, :, run].astype(full) * root * gains[:, run]
            r.normed[run, rows] = tile.T.astype(low)

    first, second = pl.ds(0, 1024), pl.ds(1024, 1024)
    to_above.wait_recv()
    passed = whole.at[:, me.y_by(3), :, first]
    far_above = net.copy(passed, passed, above)
    to_below.wait_recv()
    passed = whole.at[:, me.y_by(1), :, second]
    far_below = net.copy(passed, passed, below)
    own_branch.wait()
    load_out.wait()
    next(gate)
    far_above.wait_recv()
    far_below.wait_recv()

    bring_home([offset for offset in OFFSETS if offset not in straight])

    heads_grad = r.heads_grad

    def heads_step(step, carry):
        columns = pl.ds(pl.multiple_of(step * 256, 256), 256)
        heads_grad[:, columns] = jnp.dot(
            whole[...].reshape(384, 2048), weight[:, columns], preferred_element_type=full
        ).astype(low)
        return carry

    lax.fori_loop(0, 4, heads_step, 0)
    load_query = net.load(r.w_query, weight)

    query_low = heads_grad

    def own_input(columns):
        return hidden[:, :, columns].reshape(384, 256).astype(full)

    def normed(columns, right):
        return jnp.dot(r.normed[columns, :], right, preferred_element_type=full)

    def whole_part(columns):
        return whole[:, :, :, columns].reshape(384, 256)

    def branch_weight(columns, right):
        return contract_first(whole_part(columns), right)

    def weigh(core, left, right, target):
        def body(step, carry):
            z_hi, part = step // 2, lax.rem(step, 2)
            columns = pl.ds(pl.multiple_of((z_hi * 2 + core) * 512 + part * 256, 256), 256)
            made = left(columns, right[...]).astype(low)
            target[z_hi, pl.ds(part * 2, 2)] = made.reshape(2, 2, 64, right.shape[1])
            return carry

        lax.fori_loop(0, 4, body, 0)

    def dense(order, left, right, sending, other, middle, *more):
        weigh(1 - me.core, left, right, sending)
        task = order(net, me, sending, other, middle, *more)
        next(task)
        weigh(me.core, left, right, middle)
        return task

    out_w = dense(
        dense_z_first, branch_weight, fetch.mixed, r.sending, r.out_w_other, r.out_w_middle,
        r.out_w_slots, r.out_w_corner, r.out_w_last, r.out_w_out,
    )
    next(down)

    query, query_raw, pair = fetch.query, fetch.query_raw, fetch.pair
    cosine, sine = fetch.cosine, fetch.sine
    gain_query, gain_key = r.query_gain[...].astype(full), r.key_gain[...].astype(full)
    bias, key_sum, value_sum = r.bias, r.key_sum, r.value_sum
    pair_grad, gain_part = r.pair_grad, r.gain_part
    gain_part[...] = jnp.zeros((8, 128), full)

    def rope_back(gradient):
        return gradient * cosine[...] - turned(gradient) * sine[...]

    def attend(s):
        here = pl.ds(s * 128, 128)
        bias[...] = mask_bias(me, r.segments, s)
        key_sum[...] = jnp.zeros_like(key_sum)
        value_sum[...] = jnp.zeros_like(value_sum)

        def two_heads(step, carry):
            columns = pl.ds(pl.multiple_of(step * 256, 256), 256)

            def stacked(ref):
                both = ref[here, columns]
                return jnp.concatenate([both[:, :128], both[:, 128:]], axis=0)

            q, d = stacked(query), stacked(heads_grad)
            keys, values = pair[0, s], pair[1, s]
            lines = r.log_sum
            logs = jnp.concatenate(
                [column_of(lines[s * 8 + step * 2]), column_of(lines[s * 8 + step * 2 + 1])], axis=0
            )
            score = contract_last(q, keys) * score_scale
            score = score + jnp.concatenate([bias[...], bias[...]], axis=0)
            prob = jnp.exp(score - logs)
            prob_grad = contract_last(d, values)
            delta = jnp.sum(prob * prob_grad, axis=-1, keepdims=True)
            score_grad = (prob * (prob_grad - delta)).astype(low)
            value_sum[...] += contract_first(prob.astype(low), d)
            key_sum[...] += contract_first(score_grad, q)
            turned_grad = jnp.dot(score_grad, keys, preferred_element_type=full) * score_scale
            for half in range(2):
                run = pl.ds(pl.multiple_of(step * 256 + half * 128, 128), 128)
                grad, part = norm_back(
                    rope_back(turned_grad[half * 128 : half * 128 + 128]),
                    query_raw[here, run],
                    gain_query,
                )
                heads_grad[here, run] = grad.astype(low)
                gain_part[0:1, :] += part
            return carry

        lax.fori_loop(0, 4, two_heads, 0)
        pair_grad[s, :, :, 0] = (key_sum[...] * score_scale).astype(low).reshape(4, 2, 128, 128)
        pair_grad[s, :, :, 1] = value_sum[...].astype(low).reshape(4, 2, 128, 128)
        return x_first(
            net, me, pair_grad.at[s], r.pair_slots.at[s], r.pair_middle.at[s], r.pair_other.at[s],
            r.pair_out.at[s],
        )

    pairs = [attend(0)]
    next(pairs[0])
    next(out_w)
    pairs.append(attend(1))
    next(pairs[1])
    next(pairs[0])
    next(up)
    pairs.append(attend(2))
    next(pairs[2])
    next(pairs[1])
    next(pairs[0])

    query_w = dense(
        dense_x_first, normed, query_low, r.sending, r.query_w_other, r.query_w_middle,
        r.query_w_slots, r.query_w_corner, r.query_w_last, r.query_w_out,
    )
    next(pairs[2])
    next(pairs[1])
    next(query_w)
    next(pairs[2])

    load_query.wait()
    net.sent(far_above)
    net.sent(far_below)

    def query_step(step, carry):
        columns = pl.ds(pl.multiple_of(step * 256, 256), 256)
        made = contract_last(query_low[...], weight[columns, :])
        whole[:, :, :, columns] = made.astype(low).reshape(3, 4, 32, 256)
        return carry

    lax.fori_loop(0, 8, query_step, 0)
    next(down)

    pair_out, key_raw, pair_low = r.pair_out, r.key_raw, r.pair_low
    for s in range(3):
        next(pairs[s], None)
        rows = slice(s * 128, s * 128 + 128)
        grad, part = norm_back(rope_back(pair_out[s, 0]), key_raw[rows, :], gain_key)
        gain_part[1:2, :] += part
        pair_low[rows, :128] = grad.astype(low)
        pair_low[rows, 128:] = pair_out[s, 1].astype(low)

    w_key, w_value = fetch.w_key, fetch.w_value
    small = r.small
    normed_part = r.normed_part

    def normed_step(step, carry):
        columns = pl.ds(pl.multiple_of(step * 256, 256), 256)
        made = whole_part(columns).astype(full)
        made = made + contract_last(pair_low[:, :128], w_key[columns, :])
        made = made + contract_last(pair_low[:, 128:], w_value[columns, :])
        normal = own_input(columns) * inverse[:, 0:1]
        normed_part[:, columns] = jnp.sum(made * normal, axis=0, keepdims=True)
        whole[:, :, :, columns] = made.astype(low).reshape(3, 4, 32, 256)
        return carry

    lax.fori_loop(0, 8, normed_step, 0)
    normed_out = r.normed_out
    normed_sum = ring_reduce(
        net,
        above,
        below,
        lambda step, half: whole.at[:, me.y_by(step), :, pl.ds(half * 1024, 1024)],
        r.normed_slots,
        lambda half: normed_out.at[:, :, pl.ds(half * 1024, 1024)],
    )
    next(normed_sum)
    for step in range(16):
        run = slice(step * 128, step * 128 + 128)
        small[step : step + 1, :] = normed_part[:, run]
        small[16 + step : 17 + step, :] = r.moe_gain_part[:, run]
    small[32:40, :] = gain_part[...]
    small[40:, :] = r.peaks[...]
    smalls = all_small(
        net, me, small, r.by_core, r.by_x, r.by_z, r.by_y, r.small_out
    )
    pair_w = dense(
        dense_x_first, normed, pair_low, r.pair_sending, r.pair_w_other, r.pair_w_middle,
        r.pair_w_slots, r.pair_w_corner, r.pair_w_last, r.pair_w_out,
    )
    next(out_w)

    for made in home_came:
        made.wait_recv()
    home_own.wait()
    home_loads = [
        net.load(home.at[:, pl.ds(half * 1024, 1024)], weight.at[pl.ds(half * 768, 768)])
        for half in range(2)
    ]
    next(pair_w)
    next(smalls)
    moe_out = r.moe_out
    for half in range(2):
        home_loads[half].wait()

        def gather(step, carry, half=half):
            columns = pl.ds(pl.multiple_of(step * 256, 256), 256)
            total = contract_first(table[...], weight[half * 768 : half * 768 + 768, columns])
            moe_out[:, pl.ds(pl.multiple_of(half * 1024 + step * 256, 256), 256)] = total[:96]
            return carry

        lax.fori_loop(0, 4, gather, 0)

    def rest(*tasks):
        for task in tasks:
            next(task, None)

    rest(normed_sum, query_w, out_w, down, smalls)

    next(normed_sum, None)
    for s in range(3):
        rows = pl.ds(pl.multiple_of(me.y * 32, 32), 32)
        grad, _ = norm_back(normed_out[s], hidden[s, rows, :].astype(full), gains[...])
        normed_out[s] = grad

    rest(pair_w, out_w, query_w, down, smalls, gate, up)
    rest(pair_w, out_w, query_w, smalls)
    tasks = [pair_w, out_w, smalls, query_w, gate, up, down]
    while tasks:
        for task in list(tasks):
            if next(task, "end") == "end":
                tasks.remove(task)
    net.finish()


def dense_slots(columns, corner):
    low = jnp.bfloat16
    return [
        pltpu.VMEM((2, 4, 2, 64, columns), low),
        pltpu.VMEM((2, 4, 2, 64, columns), low),
        pltpu.VMEM((6, 2, 64, columns), low),
        pltpu.VMEM(corner + (64, columns), low),
        pltpu.VMEM((6, 32, columns), low),
    ]


def back(far, near):
    low, full = jnp.bfloat16, jnp.float32
    outs = dict(
        gate_out=(256, 768),
        up_out=(256, 768),
        down_out=(256, 768),
        query_w_out=(64, 1024),
        pair_w_out=(64, 256),
        out_w_out=(64, 1024),
        small_out=(48, 128),
        normed_out=(3, 32, 2048),
        moe_out=(96, 2048),
    )
    scratch = dict(
        gain_rows=pltpu.VMEM((1, 2048), full),
        hidden_held=pltpu.VMEM((3, 128, 2048), low),
        pair_held=pltpu.VMEM((2, 3, 1024, 128), low),
        query_held=pltpu.VMEM((384, 1024), low),
        query_raw_held=pltpu.VMEM((384, 1024), full),
        cosine_held=pltpu.VMEM((128, 128), full),
        sine_held=pltpu.VMEM((128, 128), full),
        mixed_held=pltpu.VMEM((384, 1024), low),
        key_weight=pltpu.VMEM((2048, 128), low),
        value_weight=pltpu.VMEM((2048, 128), low),
        whole=pltpu.VMEM((3, 4, 32, 2048), low),
        weight=pltpu.VMEM((2048, 1024), low),
        inverse=pltpu.VMEM((384, 128), full),
        normed=pltpu.VMEM((2048, 384), low),
        heads_grad=pltpu.VMEM((384, 1024), low),
        bias=pltpu.VMEM((128, 1024), full),
        key_sum=pltpu.VMEM((1024, 128), full),
        value_sum=pltpu.VMEM((1024, 128), full),
        pair_grad=pltpu.VMEM((3, 4, 2, 2, 128, 128), low),
        pair_slots=pltpu.VMEM((3, 6, 2, 128, 128), low),
        pair_middle=pltpu.VMEM((3, 2, 2, 128, 128), low),
        pair_other=pltpu.VMEM((3, 2, 128, 128), low),
        pair_out=pltpu.VMEM((3, 2, 128, 128), full),
        pair_low=pltpu.VMEM((384, 256), low),
        gain_part=pltpu.VMEM((8, 128), full),
        normed_part=pltpu.VMEM((1, 2048), full),
        normed_slots=pltpu.VMEM((6, 3, 32, 1024), low),
        small=pltpu.VMEM((48, 128), full),
        by_core=pltpu.VMEM((2, 48, 128), full),
        by_x=pltpu.VMEM((4, 48, 128), full),
        by_z=pltpu.VMEM((4, 48, 128), full),
        by_y=pltpu.VMEM((4, 48, 128), full),
        down_slots=pltpu.VMEM((6, 256, 768), low),
        down_middle=pltpu.VMEM((2, 256, 768), low),
        down_other=pltpu.VMEM((256, 768), low),
        down_held=pltpu.VMEM((4, 256, 768), low),
        gate_slots=pltpu.VMEM((6, 256, 768), low),
        gate_middle=pltpu.VMEM((2, 256, 768), low),
        gate_other=pltpu.VMEM((256, 768), low),
        gate_held=pltpu.VMEM((4, 256, 768), low),
        up_slots=pltpu.VMEM((6, 256, 768), low),
        up_middle=pltpu.VMEM((2, 256, 768), low),
        up_other=pltpu.VMEM((256, 768), low),
        up_held=pltpu.VMEM((4, 256, 768), low),
        sending=pltpu.VMEM((2, 4, 2, 64, 1024), low),
        pair_sending=pltpu.VMEM((2, 4, 2, 64, 256), low),
        query_w_other=None,
        query_w_middle=None,
        query_w_slots=None,
        query_w_corner=None,
        query_w_last=None,
        pair_w_other=None,
        pair_w_middle=None,
        pair_w_slots=None,
        pair_w_corner=None,
        pair_w_last=None,
        out_w_other=None,
        out_w_middle=None,
        out_w_slots=None,
        out_w_corner=None,
        out_w_last=None,
        send=pltpu.SemaphoreType.DMA((116,)),
        recv=pltpu.SemaphoreType.DMA((116,)),
        here=pltpu.SemaphoreType.DMA((34,)),
    )
    dense = dense_slots(1024, (2, 2)) + dense_slots(256, (2, 2)) + dense_slots(1024, (4,))
    scratch = {name: one or dense.pop(0) for name, one in scratch.items()}
    outs = {name: jax.ShapeDtypeStruct(size, full) for name, size in outs.items()}
    far_outs = dict(home=jax.ShapeDtypeStruct((768, 2048), low))
    return call(back_kernel, 0, far, near, outs, far_outs, scratch)


class Fetch:
    def __init__(self, net):
        self.net, self.waiting, self.held = net, {}, {}

    def start(self, name, source, target):
        self.waiting[name] = self.net.load(source, target)
        self.held[name] = target

    def __getattr__(self, name):
        if name in self.waiting:
            self.waiting.pop(name).wait()
        return self.held[name]


def token_table(ids, gates, capacity, table, info):
    low, full = jnp.bfloat16, jnp.float32
    expert = lax.broadcasted_iota(jnp.int32, (16, 32), 0)
    chosen, share = [], []
    for s in range(3):
        chosen_here = jnp.zeros((16, 32), full)
        share_here = jnp.zeros((16, 32), full)
        for k in range(8):
            named = ids[s, k : k + 1, :] == expert
            chosen_here = chosen_here + jnp.where(named, 1.0, 0.0)
            share_here = share_here + jnp.where(named, gates[s, k : k + 1, :], 0.0)
        chosen.append(chosen_here)
        share.append(share_here)
    none = jnp.zeros((16, 32), full)
    chosen = jnp.concatenate(chosen + [none], axis=1)
    share = jnp.concatenate(share + [none], axis=1)
    row = lax.broadcasted_iota(jnp.int32, (16, 128), 0)
    limit = jnp.zeros((16, 128), full)
    for e in range(16):
        limit = jnp.where(row == e, capacity[e].astype(full), limit)
    earlier = lax.broadcasted_iota(jnp.int32, (128, 128), 0) < lax.broadcasted_iota(
        jnp.int32, (128, 128), 1
    )
    before = jnp.dot(
        chosen.astype(low), jnp.where(earlier, 1.0, 0.0).astype(low), preferred_element_type=full
    )
    slot = jnp.where((chosen > 0.0) & (before < limit), before, -1.0)
    spot = lax.broadcasted_iota(jnp.int32, (48, 128), 0).astype(full)
    for place in range(16):
        core, z_hi, y = place // 8, place // 4 % 2, place % 4
        e = (z_hi * 2 + core) * 4 + y
        mask = jnp.where(slot[e : e + 1, :] == spot, 1.0, 0.0)
        table[place * 48 : place * 48 + 48, :] = mask.astype(low)
        info[core, z_hi, y] = jnp.concatenate(
            [slot[e : e + 1, :], share[e : e + 1, :], jnp.zeros((6, 128), full)], axis=0
        )


PHASES = (
    [(0, 0), (0, 1), (0, 3), (2, 0), (1, 0), (1, 1), (1, 3), (3, 0)],
    [(0, 2), (1, 2), (2, 1), (2, 3), (3, 1), (3, 3), (2, 2), (3, 2)],
)
SLOTS = {offset: (phase, spot) for phase in (0, 1) for spot, offset in enumerate(PHASES[phase])}


def spread(net, me, everyone, source, came, crossed):
    above, below = me.at(y=me.y_by(1)), me.at(y=me.y_by(3))
    sibling, across = me.at(core=1 - me.core), me.at(z=me.z_by(2))
    own = source is not None
    a, z_hi = (0, me.z_hi) if own else (2, 1 - me.z_hi)

    def block(b):
        return everyone.at[me.core, z_hi, me.y_by(b)]

    def half(b, part):
        return block(b).at[:, pl.ds(part * 16, 16)]

    def quarter(b, part):
        return block(b).at[:, pl.ds(0, 16), pl.ds(part * 1024, 1024)]

    def forward(view, device):
        return net.copy(view, view, device)

    def pass_on(b):
        if own:
            crossed[b] = forward(half(b, 1), across)
        else:
            crossed[b].wait_recv()
        came[a + 1, b] = forward(block(b), sibling)

    piece = half if own else quarter
    if own:
        up = net.copy(source, block(0), above)
        down = net.copy(source, block(0), below)
        came[a + 1, 0] = net.copy(source, block(0), sibling)
    else:
        up = forward(half(0, 0), above)
        down = forward(half(0, 0), below)
        came[a + 1, 0] = forward(block(0), sibling)
    yield
    up.wait_recv()
    far_up = forward(piece(3, 0), above)
    down.wait_recv()
    far_down = forward(piece(1, 1), below)
    pass_on(3)
    pass_on(1)
    yield
    far_up.wait_recv()
    far_down.wait_recv()
    pass_on(2)
    yield


def moe_kernel(names, *refs):
    r = types.SimpleNamespace(**dict(zip(names, refs, strict=True)))
    low, full = jnp.bfloat16, jnp.float32
    me = Place()
    net = Net(r.send, r.recv, r.here)
    fetch = Fetch(net)
    fetch.start("w_gate", r.w_gate, r.gate_weight)
    fetch.start("w_up", r.w_up, r.up_weight)
    fetch.start("cots", r.cots, r.cots_held)
    fetch.start("w_down", r.w_down, r.down_weight)
    greeted = greet(peers(me) + [me.at(x=me.x_by(1)), me.at(x=me.x_by(3))])
    everyone, local, table = r.everyone, r.local, r.table
    values = r.after[...]
    inverse = lax.rsqrt(jnp.mean(values * values, axis=-1, keepdims=True) + epsilon)
    gain = wide(r.moe_gain)
    everyone[me.spot] = (values * inverse * gain).astype(low).reshape(3, 32, 2048)

    greeted()
    came, crossed = {}, {}
    own_rows = everyone.at[me.spot]
    here_rows = spread(net, me, everyone, own_rows, came, crossed)
    next(here_rows)
    from_across = net.copy(own_rows, own_rows, me.at(z=me.z_by(2)))

    act, gate_back, up_back, back, home = r.act, r.gate_back, r.up_back, r.back, r.home
    grads = r.grads_held
    iota = lax.broadcasted_iota(jnp.int32, (48, 128), 0).astype(full)

    def slots_of(offset):
        core, z_hi, y = peer(me, *offset)[0]
        mask = r.info_in[core, z_hi, y, 0:1, :] == iota
        share = jnp.where(mask, r.info_in[core, z_hi, y, 1:2, :], 0.0)
        return mask, jnp.sum(share, axis=1, keepdims=True)

    def select(source, offset):
        mask, share = slots_of(offset)
        named = jnp.where(mask, 1.0, 0.0).astype(low)[:, :96]
        rows = source[peer(me, *offset)[0]].reshape(96, 2048)
        return jnp.dot(named, rows, preferred_element_type=full), share

    cots = fetch.cots
    for offset, slot in SLOTS.items():
        picked, share = select(cots, offset)
        r.raw_held[slot] = picked.astype(low)
        grads[slot] = (picked * share).astype(low)

    w_gate, w_up, w_down = fetch.w_gate, fetch.w_up, fetch.w_down
    back_came, dots_came, round_x, written = {}, {}, [], []
    right, left = me.at(x=me.x_by(1)), me.at(x=me.x_by(3))

    def weigh(entered, given, target):
        def body(step, carry):
            columns = pl.ds(pl.multiple_of(step * 256, 256), 256)
            left = entered[:, :, :, columns].reshape(768, 256)
            target[columns, :] = contract_first(left, given[...].reshape(768, 768)).astype(low)
            return carry

        lax.fori_loop(0, 8, body, 0)

    def chunk(target, step, half):
        start = (me.x_by(step) * 2 + half) * 256
        return target.at[pl.ds(pl.multiple_of(start, 256), 256)]

    def send_back(offsets):
        for offset in offsets:
            device = peer(me, *offset)[1]
            back_came[offset] = net.copy(back.at[SLOTS[offset]], home.at[me.spot], device)

    def through(group, low_slot, high_slot, between):
        run = slice(low_slot * 48, high_slot * 48)
        slots, rows = slice(low_slot, high_slot), (high_slot - low_slot) * 48
        for offset in PHASES[group][slots]:
            if offset in came:
                came[offset].wait_recv()
            local[SLOTS[offset]] = select(everyone, offset)[0].astype(low)

        def inner(step, carry):
            columns = pl.ds(pl.multiple_of(step * 256, 256), 256)
            entered = local[group, slots].reshape(rows, 2048)
            gate_pre = jnp.dot(entered, w_gate[:, columns], preferred_element_type=full)
            up_pre = jnp.dot(entered, w_up[:, columns], preferred_element_type=full)
            act_back = jnp.dot(
                grads[group, slots].reshape(rows, 2048),
                w_down[:, columns],
                preferred_element_type=full,
            )
            sigmoid = 1.0 / (1.0 + jnp.exp(-gate_pre))
            silu = gate_pre * sigmoid
            act[group, run, columns] = (silu * up_pre).astype(low)
            gate_back[group, run, columns] = (
                act_back * up_pre * sigmoid * (1.0 + gate_pre * (1.0 - sigmoid))
            ).astype(low)
            up_back[group, run, columns] = (act_back * silu).astype(low)
            return carry

        def outer(step, carry):
            columns = pl.ds(pl.multiple_of(step * 256, 256), 256)
            row_back = contract_last(gate_back[group, run, :], w_gate[columns, :]) + contract_last(
                up_back[group, run, :], w_up[columns, :]
            )
            back[group, slots, :, columns] = row_back.astype(low).reshape(rows // 48, 48, 256)
            return carry

        lax.fori_loop(0, 3, inner, 0)
        between()
        lax.fori_loop(0, 8, outer, 0)

    def results(group):
        given = [slots_of(offset) for offset in PHASES[group]]
        shared = jnp.concatenate([share for _, share in given], axis=0)

        def finals(step, dot):
            columns = pl.ds(pl.multiple_of(step * 256, 256), 256)
            made = contract_last(act[group], w_down[columns, :]).astype(low).astype(full)
            r.produced_held[group, :, :, columns] = (made * shared).astype(low).reshape(8, 48, 256)
            incoming = r.raw_held[group, :, :, columns].reshape(384, 256).astype(full)
            return dot + jnp.sum(made * incoming, axis=1, keepdims=True)

        dot = lax.fori_loop(0, 8, finals, jnp.zeros((384, 1), full))
        for spot, offset in enumerate(PHASES[group]):
            line = jnp.where(given[spot][0], dot[spot * 48 : spot * 48 + 48], 0.0)
            line = jnp.sum(line, axis=0, keepdims=True)
            r.dots[group, spot] = jnp.broadcast_to(line, (8, 128))
            if offset != (0, 0):
                device = peer(me, *offset)[1]
                dots_came[offset] = net.copy(
                    r.dots.at[group, spot], r.dots_in.at[me.spot], device
                )

    next(here_rows)
    from_across.wait_recv()
    other_rows = spread(net, me, everyone, None, came, crossed)
    next(other_rows)
    through(0, 0, 8, lambda: next(here_rows))
    next(other_rows)
    send_back([offset for offset in PHASES[0] if offset != (0, 0)])
    through(1, 0, 6, lambda: next(other_rows))
    send_back(PHASES[1][:6])
    through(1, 6, 8, lambda: None)
    send_back(PHASES[1][6:])
    weigh(local, gate_back, r.gate_held)
    round_x += [
        net.copy(chunk(r.gate_held, 2, 0), r.gate_slots.at[0], right),
        net.copy(chunk(r.gate_held, 2, 1), r.gate_slots.at[2], left),
        net.copy(chunk(r.gate_held, 1, 1), r.gate_slots.at[1], right),
        net.copy(chunk(r.gate_held, 3, 0), r.gate_slots.at[3], left),
    ]
    written.append(net.load(r.gate_held, r.full_gate))
    weigh(local, up_back, r.up_held)
    round_x += [
        net.copy(chunk(r.up_held, 2, 0), r.up_slots.at[0], right),
        net.copy(chunk(r.up_held, 2, 1), r.up_slots.at[1], left),
    ]
    written.append(net.load(r.up_held, r.full_up))
    results(0)
    results(1)
    weigh(grads, act, r.down_held)
    written.append(net.load(r.produced_held, r.produced))
    written.append(net.load(r.down_held, r.full_down))
    home[me.spot] = back[0, 0]
    r.dots_in[me.spot] = r.dots[0, 0]

    for offset in OFFSETS:
        dots_came[offset].wait_recv()
    lines = [r.dots_in[e // 4 % 2, e // 8, e % 4, 0:1, :] for e in range(16)]
    lines = jnp.concatenate(lines, axis=0)
    expert = lax.broadcasted_iota(jnp.int32, (16, 32), 0)
    for s in range(3):
        dots = lines[:, s * 32 : s * 32 + 32]
        for k in range(8):
            named = r.ids[s, k : k + 1, :] == expert
            r.gate_grad[s, k : k + 1, :] = jnp.sum(
                jnp.where(named, dots, 0.0), axis=0, keepdims=True
            )

    for offset in OFFSETS:
        back_came[offset].wait_recv()
    after_grad = r.after_grad

    def keep(columns, total):
        after_grad[:, columns] = total

    gather_rows(table, home, keep)
    gradient = after_grad[...]
    moe_part, gain_part = norm_back(gradient, r.after[...], gain)
    r.gain_part[...] = gain_part
    result = r.cotangent[...].reshape(96, 2048).astype(full) + moe_part
    after_grad[...] = result
    r.branch[...] = result.astype(low).reshape(3, 32, 2048)
    for one in written:
        one.wait()
    for one in round_x:
        one.wait_recv()
    net.finish()


def moe(far, near):
    low, full = jnp.bfloat16, jnp.float32
    rows, home = (2, 8, 48, 2048), (2, 2, 4, 48, 2048)
    outs = dict(
        after_grad=jax.ShapeDtypeStruct((96, 2048), full),
        branch=jax.ShapeDtypeStruct((3, 32, 2048), low),
        gain_part=jax.ShapeDtypeStruct((1, 2048), full),
        gate_grad=jax.ShapeDtypeStruct((3, 8, 32), full),
    )
    far_outs = dict(
        produced=jax.ShapeDtypeStruct(rows, low),
        full_gate=jax.ShapeDtypeStruct((2048, 768), low),
        full_up=jax.ShapeDtypeStruct((2048, 768), low),
        full_down=jax.ShapeDtypeStruct((2048, 768), low),
        gate_slots=jax.ShapeDtypeStruct((4, 256, 768), low),
        up_slots=jax.ShapeDtypeStruct((2, 256, 768), low),
    )
    scratch = dict(
        everyone=pltpu.VMEM((2, 2, 4, 3, 32, 2048), low),
        local=pltpu.VMEM(rows, low),
        cots_held=pltpu.VMEM((2, 2, 4, 3, 32, 2048), low),
        raw_held=pltpu.VMEM(rows, low),
        grads_held=pltpu.VMEM(rows, low),
        produced_held=pltpu.VMEM(rows, low),
        back=pltpu.VMEM(rows, low),
        home=pltpu.VMEM(home, low),
        gate_weight=pltpu.VMEM((2048, 768), low),
        up_weight=pltpu.VMEM((2048, 768), low),
        down_weight=pltpu.VMEM((2048, 768), low),
        gate_held=pltpu.VMEM((2048, 768), low),
        up_held=pltpu.VMEM((2048, 768), low),
        down_held=pltpu.VMEM((2048, 768), low),
        act=pltpu.VMEM((2, 384, 768), low),
        gate_back=pltpu.VMEM((2, 384, 768), low),
        up_back=pltpu.VMEM((2, 384, 768), low),
        dots=pltpu.VMEM((2, 8, 8, 128), full),
        dots_in=pltpu.VMEM((2, 2, 4, 8, 128), full),
        send=pltpu.SemaphoreType.DMA((58,)),
        recv=pltpu.SemaphoreType.DMA((58,)),
        here=pltpu.SemaphoreType.DMA((8,)),
    )
    return call(moe_kernel, 1, far, near, outs, far_outs, scratch)


def call(kernel, number, far, near, outs, far_outs, scratch):
    names = list(far) + list(near) + list(outs) + list(far_outs) + list(scratch)
    shapes = {**outs, **far_outs}
    results = pl.pallas_call(
        functools.partial(kernel, names),
        out_shape=list(shapes.values()),
        in_specs=[ANY] * len(far)
        + [SMEM if one.ndim == 1 else VMEM for one in near.values()],
        out_specs=[VMEM] * len(outs) + [ANY] * len(far_outs),
        scratch_shapes=list(scratch.values()),
        compiler_params=pltpu.CompilerParams(
            collective_id=number, has_side_effects=True, vmem_limit_bytes=63 << 20
        ),
        name=kernel.__name__,
    )(*far.values(), *near.values())
    return types.SimpleNamespace(**dict(zip(shapes, results, strict=True)))


def front_kernel(names, *refs):
    r = types.SimpleNamespace(**dict(zip(names, refs, strict=True)))
    low, full = jnp.bfloat16, jnp.float32
    score_scale = HEAD_SIZE ** (-0.5)
    me = Place()
    net = Net(r.send, r.recv, r.here)
    fetch = Fetch(net)
    fetch.start("hidden", r.hidden, r.hidden_held)
    fetch.start("w_pair", r.w_key, r.key_weight)
    fetch.start("w_value", r.w_value, r.value_weight)
    fetch.start("cosine", r.cosine.at[me.context], r.cosine_held)
    fetch.start("sine", r.sine.at[me.context], r.sine_held)
    fetch.start("w_query", r.w_query, r.query_weight)
    fetch.start("w_out", r.w_out, r.out_weight)
    beside = me.at(z=me.z + 1 - 2 * me.z_lo)
    right, left = me.at(x=me.x_by(1)), me.at(x=me.x_by(3))
    greeted = greet([right, left, beside] + peers(me))
    gains = r.gain_rows
    gains[...] = wide(r.attn_gain)

    above, below = me.at(y=me.y_by(1)), me.at(y=me.y_by(3))
    across, came, crossed, told = me.at(z=me.z_by(2)), {}, {}, []
    greeted()
    own_cot = net.load(r.cotangent, r.cots.at[me.spot])
    here_cot = spread(net, me, r.cots, r.cotangent, came, crossed)
    next(here_cot)
    from_across = net.copy(r.cotangent, r.cots.at[me.spot], across)

    hidden, normed = fetch.hidden, r.normed
    for s in range(3):
        values = hidden[s].astype(full)
        root = lax.rsqrt(jnp.mean(values * values, axis=-1, keepdims=True) + epsilon)
        normed[s * 128 : s * 128 + 128, :] = (values * root * gains[...]).astype(low)

    def rope(values):
        cosine = jnp.concatenate([fetch.cosine[...]] * 3, axis=0)
        sine = jnp.concatenate([fetch.sine[...]] * 3, axis=0)
        return values * cosine + turned(values) * sine

    def head_norm(raw, gain):
        return raw * lax.rsqrt(jnp.mean(raw * raw, axis=-1, keepdims=True) + epsilon) * gain

    pair, key_raw = r.pair_held, r.key_raw
    made = jnp.dot(normed[...], fetch.w_pair[...], preferred_element_type=full)
    key_raw[...] = made
    keys = rope(head_norm(made, r.key_gain[...].astype(full))).astype(low)
    values = jnp.dot(normed[...], fetch.w_value[...], preferred_element_type=full).astype(low)
    own = pl.ds(pl.multiple_of(me.context * 128, 128), 128)
    pair[0, :, own, :] = keys.reshape(3, 128, 128)
    pair[1, :, own, :] = values.reshape(3, 128, 128)

    def block(x, z_lo):
        return pl.ds(pl.multiple_of((x * 2 + z_lo) * 128, 128), 128)

    def piece(s, x, z_lo, half=None):
        rows = block(x, z_lo)
        return pair.at[:, s, rows, :] if half is None else pair.at[half, s, rows, :]

    def pass_on(view, device):
        return net.copy(view, view, device)

    own_z, other_z = me.z_lo, 1 - me.z_lo

    def bring_pair(s):
        from_z = pass_on(piece(s, me.x, own_z), beside)
        came = [(pass_on(piece(s, me.x, own_z), right), pass_on(piece(s, me.x, own_z), left))]
        yield
        from_z.wait_recv()
        came.append((pass_on(piece(s, me.x, other_z), right), pass_on(piece(s, me.x, other_z), left)))
        yield
        far = []
        for zs, (from_left, from_right) in zip((own_z, other_z), came, strict=True):
            from_left.wait_recv()
            far.append(pass_on(piece(s, me.x_by(3), zs, 0), right))
            from_right.wait_recv()
            far.append(pass_on(piece(s, me.x_by(1), zs, 1), left))
            yield
        for one in far:
            one.wait_recv()
        yield

    brought = [bring_pair(s) for s in range(3)]
    for s in range(3):
        next(brought[s])

    w_query, query, query_raw = fetch.w_query, r.query_held, r.query_raw_held

    def project(step, carry):
        columns = pl.ds(pl.multiple_of(step * 256, 256), 256)
        made = jnp.dot(normed[...], w_query[:, columns], preferred_element_type=full)
        query_raw[:, columns] = made
        for half in range(2):
            run = pl.ds(pl.multiple_of(step * 256 + half * 128, 128), 128)
            one = head_norm(made[:, half * 128 : half * 128 + 128], r.query_gain[...].astype(full))
            query[:, run] = rope(one).astype(low)
        return carry

    lax.fori_loop(0, 2, project, 0)
    for s in range(3):
        next(brought[s])
    next(here_cot)
    from_across.wait_recv()
    other_cot = spread(net, me, r.cots, None, came, crossed)
    next(other_cot)
    lax.fori_loop(2, 4, project, 0)
    written = [net.load(query, r.query), net.load(query_raw, r.query_raw)]
    next(brought[0])
    next(brought[1])
    next(brought[0])
    next(brought[2])
    next(brought[1])

    bias, peaks, mixed = r.bias, r.peak_rows, r.mixed_held
    peaks[...] = jnp.full((8, 1, 128), -jnp.inf, full)

    def attend(s):
        here = pl.ds(s * 128, 128)
        bias[...] = mask_bias(me, r.segments, s)

        def two_heads(step, carry):
            columns = pl.ds(pl.multiple_of(step * 256, 256), 256)
            both = query[here, columns]
            q = jnp.concatenate([both[:, :128], both[:, 128:]], axis=0)
            score = contract_last(q, pair[0, s]) * score_scale
            score = score + jnp.concatenate([bias[...], bias[...]], axis=0)
            highest = jnp.max(score, axis=-1, keepdims=True)
            weight = jnp.exp(score - highest)
            total = jnp.sum(weight, axis=-1, keepdims=True)
            prob = (weight * (1.0 / total)).astype(low)
            logs = highest + jnp.log(total)
            heads = jnp.dot(prob, pair[1, s], preferred_element_type=full).astype(low)
            for half in range(2):
                part = slice(half * 128, half * 128 + 128)
                head = step * 2 + half
                run = pl.ds(pl.multiple_of(step * 256 + half * 128, 128), 128)
                mixed[here, run] = heads[part]
                r.log_sum[s * 8 + head] = row_of(logs[part])
                top = jnp.max(highest[part], axis=0, keepdims=True)
                peaks[head] = jnp.maximum(peaks[head], top)
            return carry

        lax.fori_loop(0, 4, two_heads, 0)
    shares, after = r.shares, r.after_sum

    def branch(s):
        w_out = fetch.w_out

        def body(step, carry):
            columns = pl.ds(pl.multiple_of(step * 256, 256), 256)
            made = contract_last(mixed[pl.ds(s * 128, 128), :], w_out[columns, :])
            shares[s, :, :, columns] = made.astype(low).reshape(4, 32, 256)
            return carry

        lax.fori_loop(0, 8, body, 0)
        return ring_reduce(
            net,
            above,
            below,
            lambda step, half: shares.at[s, me.y_by(step), :, pl.ds(half * 1024, 1024)],
            r.branch_slots.at[s],
            lambda half: after.at[s, :, pl.ds(half * 1024, 1024)],
        )

    next(brought[0])
    attend(0)
    next(brought[2])
    first = branch(0)
    next(first)
    next(brought[1])
    attend(1)
    next(here_cot)
    next(other_cot)
    second = branch(1)
    next(second)
    next(first)
    next(brought[2])
    attend(2)
    third = branch(2)
    next(third)

    token_table(r.ids, r.gates, r.capacity, r.table, r.info)
    r.info_in[me.spot] = r.info[me.spot]
    for a, b in OFFSETS:
        spot, device = peer(me, a, b)
        told.append(net.copy(r.info.at[spot], r.info_in.at[me.spot], device))

    next(second)
    written.append(net.load(pair, r.pair))
    written.append(net.load(mixed, r.mixed))
    for head in range(8):
        r.peaks[head : head + 1, :] = peaks[head]
    next(first, None)
    next(third)
    next(other_cot)
    next(second, None)
    next(third, None)
    own_rows = pl.ds(pl.multiple_of(me.y * 32, 32), 32)
    for s in range(3):
        r.after[s * 32 : s * 32 + 32, :] = after[s] + hidden[s, own_rows, :].astype(full)
    for one in list(came.values()) + told:
        one.wait_recv()
    own_cot.wait()
    for one in written:
        one.wait()
    net.finish()


def row_of(column):
    eye = lax.broadcasted_iota(jnp.int32, (128, 128), 0) == lax.broadcasted_iota(
        jnp.int32, (128, 128), 1
    )
    return jnp.sum(jnp.where(eye, column, 0.0), axis=0, keepdims=True)


def mask_bias(me, segments, s):
    spot = me.context * 128 + lax.broadcasted_iota(jnp.int32, (128, 1024), 0)
    own = segments[s : s + 1, pl.ds(pl.multiple_of(me.context * 128, 128), 128)]
    document = column_of(own.astype(jnp.float32))
    allowed = (document == segments[s : s + 1, :].astype(jnp.float32)) & (
        lax.broadcasted_iota(jnp.int32, (128, 1024), 1) <= spot
    )
    return jnp.where(allowed, 0.0, masked_value)


def front(far, near):
    low, full = jnp.bfloat16, jnp.float32
    outs = dict(
        key_raw=jax.ShapeDtypeStruct((384, 128), full),
        log_sum=jax.ShapeDtypeStruct((24, 1, 128), full),
        peaks=jax.ShapeDtypeStruct((8, 128), full),
        after=jax.ShapeDtypeStruct((96, 2048), full),
        table=jax.ShapeDtypeStruct((768, 128), low),
        info_in=jax.ShapeDtypeStruct((2, 2, 4, 8, 128), full),
    )
    far_outs = dict(
        query=jax.ShapeDtypeStruct((384, 1024), low),
        query_raw=jax.ShapeDtypeStruct((384, 1024), full),
        pair=jax.ShapeDtypeStruct((2, 3, 1024, 128), low),
        mixed=jax.ShapeDtypeStruct((384, 1024), low),
        cots=jax.ShapeDtypeStruct((2, 2, 4, 3, 32, 2048), low),
    )
    scratch = dict(
        gain_rows=pltpu.VMEM((1, 2048), full),
        hidden_held=pltpu.VMEM((3, 128, 2048), low),
        key_weight=pltpu.VMEM((2048, 128), low),
        value_weight=pltpu.VMEM((2048, 128), low),
        cosine_held=pltpu.VMEM((128, 128), full),
        sine_held=pltpu.VMEM((128, 128), full),
        query_weight=pltpu.VMEM((2048, 1024), low),
        out_weight=pltpu.VMEM((2048, 1024), low),
        normed=pltpu.VMEM((384, 2048), low),
        pair_held=pltpu.VMEM((2, 3, 1024, 128), low),
        info=pltpu.VMEM((2, 2, 4, 8, 128), full),
        query_held=pltpu.VMEM((384, 1024), low),
        query_raw_held=pltpu.VMEM((384, 1024), full),
        bias=pltpu.VMEM((128, 1024), full),
        peak_rows=pltpu.VMEM((8, 1, 128), full),
        mixed_held=pltpu.VMEM((384, 1024), low),
        shares=pltpu.VMEM((3, 4, 32, 2048), low),
        branch_slots=pltpu.VMEM((3, 6, 32, 1024), low),
        after_sum=pltpu.VMEM((3, 32, 2048), full),
        send=pltpu.SemaphoreType.DMA((84,)),
        recv=pltpu.SemaphoreType.DMA((84,)),
        here=pltpu.SemaphoreType.DMA((16,)),
    )
    return call(front_kernel, 2, far, near, outs, far_outs, scratch)


def finish_kernel(names, *refs):
    r = types.SimpleNamespace(**dict(zip(names, refs, strict=True)))
    r.layer_out[...] = r.after[...] + r.moe_out[...]
    r.input_grad[...] = r.after_grad[...] + r.normed_out[...].reshape(96, 2048)
    r.gate_w[...] = r.gate_part[...]
    r.up_w[...] = r.up_part[...]
    r.down_w[...] = r.down_part[...]
    r.query_w[...] = r.query_part[...]
    r.out_w[...] = r.out_part[...]
    r.gate_grad[...] = r.gate_grad_part[...]
    r.key_w[...] = r.pair_w[:, :128]
    r.value_w[...] = r.pair_w[:, 128:]
    r.attn_gain[...] = r.small[:16]
    r.moe_gain[...] = r.small[16:32]
    r.query_gain[...] = r.small[32:33]
    r.key_gain[...] = r.small[33:34]
    diagonal = lax.broadcasted_iota(jnp.int32, (8, 128), 0) == lax.broadcasted_iota(
        jnp.int32, (8, 128), 1
    )
    peaks = jnp.sum(jnp.where(diagonal, r.small[40:], 0.0), axis=0, keepdims=True)
    r.clip[...] = (clip_limit / jnp.maximum(peaks, clip_limit))[:, :8]


def finish(near):
    outs = dict(
        layer_out=(96, 2048),
        input_grad=(96, 2048),
        gate_w=(256, 768),
        up_w=(256, 768),
        down_w=(256, 768),
        query_w=(64, 1024),
        out_w=(64, 1024),
        gate_grad=(3, 8, 32),
        key_w=(64, 128),
        value_w=(64, 128),
        attn_gain=(16, 128),
        moe_gain=(16, 128),
        query_gain=(1, 128),
        key_gain=(1, 128),
        clip=(1, 8),
    )
    results = pl.pallas_call(
        functools.partial(finish_kernel, list(near) + list(outs)),
        out_shape=[jax.ShapeDtypeStruct(size, jnp.float32) for size in outs.values()],
        in_specs=[VMEM] * len(near),
        out_specs=[VMEM] * len(outs),
        compiler_params=pltpu.CompilerParams(vmem_limit_bytes=62 << 20),
        name="finish",
    )(*near.values())
    return types.SimpleNamespace(**dict(zip(outs, results, strict=True)))


def shards(
    hidden_in,
    segments,
    attn_gain,
    query_gain,
    key_gain,
    w_query,
    key_weight_matrix,
    value_weight_matrix,
    w_out,
    moe_gain,
    expert_ids,
    gate_values,
    capacity,
    w_gate,
    w_up,
    w_down,
    cotangent,
):
    attn_wide, moe_wide = attn_gain.reshape(16, 128), moe_gain.reshape(16, 128)
    query_row, key_row = query_gain[None], key_gain[None]
    ids, gates = expert_ids.swapaxes(1, 2), gate_values.swapaxes(1, 2)
    cosine, sine = rotary()
    first = front(
        dict(
            hidden=hidden_in,
            w_key=key_weight_matrix,
            w_value=value_weight_matrix,
            cosine=cosine,
            sine=sine,
            w_query=w_query,
            cotangent=cotangent,
            w_out=w_out,
        ),
        dict(
            attn_gain=attn_wide,
            query_gain=query_row,
            key_gain=key_row,
            segments=segments,
            ids=ids,
            gates=gates,
            capacity=capacity,
        ),
    )
    second = moe(
        dict(w_gate=w_gate[0], w_up=w_up[0], w_down=w_down[0], cots=first.cots),
        dict(
            after=first.after,
            cotangent=cotangent,
            moe_gain=moe_wide,
            ids=ids,
            table=first.table,
            info_in=first.info_in,
        ),
    )
    done = back(
        dict(
            branch=second.branch,
            w_out=w_out,
            w_query=w_query,
            gate=second.full_gate.reshape(4, 2, 256, 768),
            up=second.full_up.reshape(4, 2, 256, 768),
            down=second.full_down.reshape(4, 2, 256, 768),
            produced=second.produced,
            gate_begun=second.gate_slots,
            up_begun=second.up_slots,
            hidden=hidden_in,
            mixed=first.mixed,
            query=first.query,
            query_raw=first.query_raw,
            pair=first.pair,
            cosine=cosine,
            sine=sine,
            w_key=key_weight_matrix,
            w_value=value_weight_matrix,
        ),
        dict(
            table=first.table,
            key_raw=first.key_raw,
            log_sum=first.log_sum,
            segments=segments,
            attn_gain=attn_wide,
            query_gain=query_row,
            key_gain=key_row,
            moe_gain_part=second.gain_part,
            peaks=first.peaks,
        ),
    )
    last = finish(
        dict(
            after=first.after,
            moe_out=done.moe_out,
            after_grad=second.after_grad,
            normed_out=done.normed_out,
            small=done.small_out,
            pair_w=done.pair_w_out,
            gate_part=done.gate_out,
            up_part=done.up_out,
            down_part=done.down_out,
            query_part=done.query_w_out,
            out_part=done.out_w_out,
            gate_grad_part=second.gate_grad,
        )
    )
    layer_out = last.layer_out.reshape(cotangent.shape)
    input_grad = last.input_grad.reshape(cotangent.shape)
    gate_grad = last.gate_grad.swapaxes(1, 2)
    w_key_grad, w_value_grad = last.key_w, last.value_w
    w_query_grad, w_out_grad = last.query_w, last.out_w
    w_gate_grad, w_up_grad, w_down_grad = last.gate_w[None], last.up_w[None], last.down_w[None]
    attn_gain_grad, moe_gain_grad = last.attn_gain.reshape(2048), last.moe_gain.reshape(2048)
    query_gain_grad, key_gain_grad = last.query_gain.reshape(128), last.key_gain.reshape(128)
    head_clip_scale = last.clip.reshape(8)
    return (
        layer_out,
        input_grad,
        attn_gain_grad,
        query_gain_grad,
        key_gain_grad,
        w_query_grad,
        w_key_grad,
        w_value_grad,
        w_out_grad,
        moe_gain_grad,
        gate_grad,
        w_gate_grad,
        w_up_grad,
        w_down_grad,
        head_clip_scale,
    )


def solution(mesh):
    in_specs = (
        P("dp", "context", None),
        P("dp", None),
        P(),
        P(),
        P(),
        P(None, "experts"),
        P(None, "experts"),
        P(None, "experts"),
        P(None, "experts"),
        P(),
        P("dp", ("context", "experts"), None),
        P("dp", ("context", "experts"), None),
        P(),
        P(("dp", "experts"), None, None),
        P(("dp", "experts"), None, None),
        P(("dp", "experts"), None, None),
        P("dp", ("context", "experts"), None),
    )
    out_specs = (
        P("dp", ("context", "experts"), None),
        P("dp", ("context", "experts"), None),
        P(),
        P(),
        P(),
        P(("dp", "context"), "experts"),
        P(("dp", "context"), "experts"),
        P(("dp", "context"), "experts"),
        P(("dp", "context"), "experts"),
        P(),
        P("dp", ("context", "experts"), None),
        P(("dp", "experts"), "context", None),
        P(("dp", "experts"), "context", None),
        P(("dp", "experts"), "context", None),
        P("experts"),
    )
    return jax.shard_map(shards, mesh=mesh, in_specs=in_specs, out_specs=out_specs, check_vma=False)
```

```python
import functools
import itertools
import types

import jax
import jax.numpy as jnp
import numpy as np
from jax import lax
from jax.experimental import pallas as pl
from jax.experimental.pallas import tpu as pltpu
from jax.sharding import PartitionSpec as P

HEAD_SIZE = 128
MESH = pl.DeviceIdType.MESH
VMEM = pl.BlockSpec(memory_space=pltpu.VMEM)
ANY = pl.BlockSpec(memory_space=pl.ANY)
SMEM = pl.BlockSpec(memory_space=pltpu.SMEM)


epsilon = 1e-06
rope_base = 1000000.0
clip_limit = 1.0
masked_value = -1e30


def rotary():
    inverse = 1.0 / rope_base ** (np.arange(0, HEAD_SIZE, 2) / HEAD_SIZE)
    angle = np.arange(1024)[:, None] * inverse[None, :]
    cosine = np.concatenate([np.cos(angle), np.cos(angle)], axis=-1)
    sine = np.concatenate([-np.sin(angle), np.sin(angle)], axis=-1)
    shape = (8, 128, HEAD_SIZE)
    return (
        jnp.asarray(cosine.reshape(shape), jnp.float32),
        jnp.asarray(sine.reshape(shape), jnp.float32),
    )


def contract_last(left, right):
    return lax.dot_general(
        left, right, (((1,), (1,)), ((), ())), preferred_element_type=jnp.float32
    )


def contract_first(left, right):
    return lax.dot_general(
        left, right, (((0,), (0,)), ((), ())), preferred_element_type=jnp.float32
    )


class Place:
    def __init__(self):
        dp = lax.axis_index("dp")
        context = lax.axis_index("context")
        self.dp, self.context, self.y = dp, context, lax.axis_index("experts")
        self.core, self.z_hi = lax.rem(dp, 2), dp // 2
        self.x, self.z_lo = context // 2, lax.rem(context, 2)
        self.z = self.z_hi * 2 + self.z_lo
        self.spot = (self.core, self.z_hi, self.y)

    def at(self, x=None, y=None, z=None, core=None):
        x = self.x if x is None else x
        y = self.y if y is None else y
        z = self.z if z is None else z
        core = self.core if core is None else core
        return (z // 2 * 2 + core, x * 2 + lax.rem(z, 2), y)

    def x_by(self, step):
        return lax.rem(self.x + step, 4)

    def y_by(self, step):
        return lax.rem(self.y + step, 4)

    def z_by(self, step):
        return lax.rem(self.z + step, 4)


class Net:
    def __init__(self, send, recv, here=None):
        self.send, self.recv, self.copies = send, recv, []
        self.here, self.loads = here, 0

    def copy(self, src, dst, device):
        spot = len(self.copies)
        made = pltpu.make_async_remote_copy(
            src_ref=src,
            dst_ref=dst,
            send_sem=self.send.at[spot],
            recv_sem=self.recv.at[spot],
            device_id=device,
            device_id_type=MESH,
        )
        made.start()
        self.copies.append(made)
        return made

    def load(self, src, dst):
        made = pltpu.make_async_copy(src, dst, self.here.at[self.loads])
        self.loads += 1
        made.start()
        return made

    def sent(self, made):
        made.wait_send()
        self.copies = [None if one is made else one for one in self.copies]

    def finish(self):
        for made in self.copies:
            if made is not None:
                made.wait_send()


def greet(devices):
    barrier = pltpu.get_barrier_semaphore()
    for device in devices:
        pl.semaphore_signal(barrier, inc=1, device_id=device, device_id_type=MESH)
    return lambda: pl.semaphore_wait(barrier, len(devices))


def wide(ref):
    values = ref[...].astype(jnp.float32)
    return jnp.concatenate([values[step : step + 1] for step in range(16)], axis=1)


def add_into(target, parts, block=32):
    rows = target.shape[-2]
    block = min(block, rows)
    for lead in itertools.product(*[range(size) for size in target.shape[:-2]]):

        def body(step, carry, lead=lead):
            spot = lead + (pl.ds(pl.multiple_of(step * block, block), block),)
            total = parts[0][spot].astype(jnp.float32)
            for part in parts[1:]:
                total = total + part[spot].astype(jnp.float32)
            target[spot] = total.astype(target.dtype)
            return carry

        lax.fori_loop(0, rows // block, body, 0)


def ring_reduce(net, plus, minus, own, slots, target, held=None, begun=None):
    held = own if held is None else held
    done = 0 if begun is None else begun.shape[0]
    if done == 4:
        loads = [net.load(begun, slots.at[pl.ds(0, 4)])]
    elif done == 2:
        loads = [net.load(begun.at[step], slots.at[step * 2]) for step in range(2)]
    else:
        first_plus = net.copy(own(2, 0), slots.at[0], plus)
        first_minus = net.copy(own(2, 1), slots.at[2], minus)
    if done != 4:
        side_plus = net.copy(own(1, 1), slots.at[1], plus)
        side_minus = net.copy(own(3, 0), slots.at[3], minus)
    yield
    if done:
        for load in loads:
            load.wait()
    else:
        first_plus.wait_recv()
        first_minus.wait_recv()
    add_into(slots.at[0], [slots.at[0], held(1, 0)])
    last_plus = net.copy(slots.at[0], slots.at[4], plus)
    add_into(slots.at[2], [slots.at[2], held(3, 1)])
    last_minus = net.copy(slots.at[2], slots.at[5], minus)
    yield
    if done != 4:
        side_minus.wait_recv()
        side_plus.wait_recv()
    last_plus.wait_recv()
    add_into(target(0), [held(0, 0), slots.at[3], slots.at[4]])
    last_minus.wait_recv()
    add_into(target(1), [held(0, 1), slots.at[1], slots.at[5]])


def x_first(net, me, source, slots, middle, other, out, held=None, begun=None):
    staged = None
    if held is not None:
        order = {(1, 0): 0, (3, 1): 1, (0, 0): 2, (0, 1): 3}
        loads = [
            net.load(source.at[me.x_by(step), half], held.at[spot])
            for (step, half), spot in order.items()
        ]

        def staged(step, half):
            return held.at[order[step, half]]

    ring = ring_reduce(
        net,
        me.at(x=me.x_by(1)),
        me.at(x=me.x_by(3)),
        lambda step, half: source.at[me.x_by(step), half],
        slots,
        lambda half: middle.at[half],
        staged,
        begun,
    )
    next(ring)
    yield
    if held is not None:
        for load in loads:
            load.wait()
    yield from ring
    across = net.copy(middle.at[1 - me.z_lo], other, me.at(z=me.z + 1 - 2 * me.z_lo))
    yield
    across.wait_recv()
    add_into(out, [middle.at[me.z_lo], other])


def core_pair(net, me, sending, other, middle):
    across = net.copy(sending, other, me.at(core=1 - me.core))
    yield
    net.sent(across)
    across.wait_recv()
    add_into(middle, [middle, other])


def dense_x_first(net, me, sending, other, middle, slots, corner, last, out):
    yield from core_pair(net, me, sending, other, middle)
    yield from ring_reduce(
        net,
        me.at(x=me.x_by(1)),
        me.at(x=me.x_by(3)),
        lambda step, half: middle.at[half, me.x_by(step)],
        slots,
        lambda half: corner.at[half],
    )
    half_rows = corner.shape[2] // 2
    yield from ring_reduce(
        net,
        me.at(z=me.z_by(1)),
        me.at(z=me.z_by(3)),
        lambda step, half: corner.at[
            me.z_by(step) // 2, lax.rem(me.z_by(step), 2), pl.ds(half * half_rows, half_rows)
        ],
        last,
        lambda half: out.at[pl.ds(half * half_rows, half_rows)],
    )


def dense_z_first(net, me, sending, other, middle, slots, corner, last, out):
    yield from core_pair(net, me, sending, other, middle)
    yield from ring_reduce(
        net,
        me.at(z=me.z_by(1)),
        me.at(z=me.z_by(3)),
        lambda step, half: middle.at[
            me.z_by(step) // 2, pl.ds(half * 2, 2), lax.rem(me.z_by(step), 2)
        ],
        slots,
        lambda half: corner.at[pl.ds(half * 2, 2)],
    )
    half_rows = corner.shape[1] // 2
    yield from ring_reduce(
        net,
        me.at(x=me.x_by(1)),
        me.at(x=me.x_by(3)),
        lambda step, half: corner.at[me.x_by(step), pl.ds(half * half_rows, half_rows)],
        last,
        lambda half: out.at[pl.ds(half * half_rows, half_rows)],
    )


def all_sum(net, devices, spot, own, slots, most):
    slots[spot] = own[...]
    sent = [net.copy(own, slots.at[spot], device) for device in devices]
    yield
    for made in sent:
        made.wait_recv()
    count = slots.shape[0]
    total = slots[0]
    peak = slots[0, most:]
    for step in range(1, count):
        total = total + slots[step]
        peak = jnp.maximum(peak, slots[step, most:])
    for made in sent:
        net.sent(made)
    own[:most] = total[:most]
    own[most:] = peak


def all_small(net, me, working, by_core, by_x, by_z, by_y, out):
    yield from all_sum(net, [me.at(core=1 - me.core)], me.core, working, by_core, 40)
    yield from all_sum(net, [me.at(x=me.x_by(s)) for s in (1, 2, 3)], me.x, working, by_x, 40)
    yield from all_sum(net, [me.at(z=me.z_by(s)) for s in (1, 2, 3)], me.z, working, by_z, 40)
    out[40:] = working[40:]
    yield from all_sum(net, [me.at(y=me.y_by(s)) for s in (1, 2, 3)], me.y, working, by_y, 40)
    out[:40] = working[:40]


OFFSETS = [(a, b) for a in (2, 0, 3, 1) for b in (0, 1, 3, 2) if a or b]


def peer(me, a, b):
    z = me.z if a < 2 else lax.rem(me.z + 2, 4)
    core = me.core if a % 2 == 0 else 1 - me.core
    y = me.y_by(b)
    return (core, z // 2, y), me.at(z=z, core=core, y=y)


def peers(me):
    return [peer(me, a, b)[1] for a, b in OFFSETS]


def gather_rows(table, home, store):
    def body(step, carry):
        columns = pl.ds(pl.multiple_of(step * 256, 256), 256)
        rows = home[:, :, :, :, columns].reshape(768, 256)
        total = contract_first(table[...], rows)
        store(columns, total[:96])
        return carry

    lax.fori_loop(0, home.shape[4] // 256, body, 0)


def turned(values):
    return pltpu.roll(values, 64, 1)


def column_of(row):
    eye = lax.broadcasted_iota(jnp.int32, (128, 128), 0) == lax.broadcasted_iota(
        jnp.int32, (128, 128), 1
    )
    return jnp.sum(jnp.where(eye, row, 0.0), axis=1, keepdims=True)


def norm_back(gradient, raw, gain):
    inverse = lax.rsqrt(jnp.mean(raw * raw, axis=-1, keepdims=True) + epsilon)
    normal = raw * inverse
    scaled = gradient * gain
    result = inverse * (scaled - normal * jnp.mean(scaled * normal, axis=-1, keepdims=True))
    return result, jnp.sum(gradient * normal, axis=0, keepdims=True)


def back_kernel(names, *refs):
    r = types.SimpleNamespace(**dict(zip(names, refs, strict=True)))
    low, full = jnp.bfloat16, jnp.float32
    score_scale = HEAD_SIZE ** (-0.5)
    me = Place()
    net = Net(r.send, r.recv, r.here)
    fetch = Fetch(net)
    fetch.start("hidden", r.hidden, r.hidden_held)
    greeted = greet(
        [
            me.at(x=me.x_by(1)),
            me.at(x=me.x_by(3)),
            me.at(z=me.z_by(1)),
            me.at(z=me.z_by(3)),
            me.at(x=me.x_by(2)),
        ]
        + peers(me)
    )
    gains = r.gain_rows
    gains[...] = wide(r.attn_gain)
    greeted()

    branch, whole = r.branch, r.whole
    above, below = me.at(y=me.y_by(1)), me.at(y=me.y_by(3))
    to_above = net.copy(branch, whole.at[:, me.y], above)
    to_below = net.copy(branch, whole.at[:, me.y], below)
    own_branch = net.load(branch, whole.at[:, me.y])
    weight = r.weight
    load_out = net.load(r.w_out, weight)
    gate = x_first(
        net, me, r.gate, r.gate_slots, r.gate_middle, r.gate_other, r.gate_out, r.gate_held,
        r.gate_begun,
    )
    up = x_first(
        net, me, r.up, r.up_slots, r.up_middle, r.up_other, r.up_out, r.up_held, r.up_begun
    )
    down = x_first(
        net, me, r.down, r.down_slots, r.down_middle, r.down_other, r.down_out, r.down_held
    )
    next(gate)
    next(gate)
    next(up)
    produced, home, table = r.produced, r.home, r.table
    start = me.core * 384 + me.z_hi * 192 + me.y * 48
    mine = pl.ds(pl.multiple_of(start, 16), 48)
    home_came = []

    def bring_home(offsets):
        for a, b in offsets:
            device = peer(me, a, b)[1]
            home_came.append(net.copy(produced.at[SLOTS[a, b]], home.at[mine], device))

    straight = [(2, 0), (3, 0)]
    bring_home(straight)
    home_own = net.load(produced.at[0, 0], home.at[mine])
    next(up)
    fetch.start("pair", r.pair, r.pair_held)
    fetch.start("query", r.query, r.query_held)
    fetch.start("query_raw", r.query_raw, r.query_raw_held)
    fetch.start("cosine", r.cosine.at[me.context], r.cosine_held)
    fetch.start("sine", r.sine.at[me.context], r.sine_held)
    fetch.start("mixed", r.mixed, r.mixed_held)
    fetch.start("w_key", r.w_key, r.key_weight)
    fetch.start("w_value", r.w_value, r.value_weight)

    hidden, inverse = fetch.hidden, r.inverse
    for s in range(3):
        rows = slice(s * 128, s * 128 + 128)
        values = hidden[s].astype(full)
        root = lax.rsqrt(jnp.mean(values * values, axis=-1, keepdims=True) + epsilon)
        inverse[rows, :] = jnp.broadcast_to(root, (128, 128))
        for step in range(8):
            run = slice(step * 256, step * 256 + 256)
            tile = hidden[s, :, run].astype(full) * root * gains[:, run]
            r.normed[run, rows] = tile.T.astype(low)

    first, second = pl.ds(0, 1024), pl.ds(1024, 1024)
    to_above.wait_recv()
    passed = whole.at[:, me.y_by(3), :, first]
    far_above = net.copy(passed, passed, above)
    to_below.wait_recv()
    passed = whole.at[:, me.y_by(1), :, second]
    far_below = net.copy(passed, passed, below)
    own_branch.wait()
    load_out.wait()
    next(gate)
    far_above.wait_recv()
    far_below.wait_recv()

    bring_home([offset for offset in OFFSETS if offset not in straight])
    next(down)

    heads_grad = r.heads_grad

    def heads_step(step, carry):
        columns = pl.ds(pl.multiple_of(step * 256, 256), 256)
        heads_grad[:, columns] = jnp.dot(
            whole[...].reshape(384, 2048), weight[:, columns], preferred_element_type=full
        ).astype(low)
        return carry

    lax.fori_loop(0, 4, heads_step, 0)
    load_query = net.load(r.w_query, weight)

    query_low = heads_grad

    def own_input(columns):
        return hidden[:, :, columns].reshape(384, 256).astype(full)

    def normed(columns, right):
        return jnp.dot(r.normed[columns, :], right, preferred_element_type=full)

    def whole_part(columns):
        return whole[:, :, :, columns].reshape(384, 256)

    def branch_weight(columns, right):
        return contract_first(whole_part(columns), right)

    def weigh(core, left, right, target):
        def body(step, carry):
            z_hi, part = step // 2, lax.rem(step, 2)
            columns = pl.ds(pl.multiple_of((z_hi * 2 + core) * 512 + part * 256, 256), 256)
            made = left(columns, right[...]).astype(low)
            target[z_hi, pl.ds(part * 2, 2)] = made.reshape(2, 2, 64, right.shape[1])
            return carry

        lax.fori_loop(0, 4, body, 0)

    def dense(order, left, right, sending, other, middle, *more):
        weigh(1 - me.core, left, right, sending)
        task = order(net, me, sending, other, middle, *more)
        next(task)
        weigh(me.core, left, right, middle)
        return task

    out_w = dense(
        dense_z_first, branch_weight, fetch.mixed, r.sending, r.out_w_other, r.out_w_middle,
        r.out_w_slots, r.out_w_corner, r.out_w_last, r.out_w_out,
    )

    query, query_raw, pair = fetch.query, fetch.query_raw, fetch.pair
    cosine, sine = fetch.cosine, fetch.sine
    gain_query, gain_key = r.query_gain[...].astype(full), r.key_gain[...].astype(full)
    bias, key_sum, value_sum = r.bias, r.key_sum, r.value_sum
    pair_grad, gain_part = r.pair_grad, r.gain_part
    gain_part[...] = jnp.zeros((8, 128), full)

    def rope_back(gradient):
        return gradient * cosine[...] - turned(gradient) * sine[...]

    def attend(s):
        here = pl.ds(s * 128, 128)
        bias[...] = mask_bias(me, r.segments, s)
        key_sum[...] = jnp.zeros_like(key_sum)
        value_sum[...] = jnp.zeros_like(value_sum)

        def two_heads(step, carry):
            columns = pl.ds(pl.multiple_of(step * 256, 256), 256)

            def stacked(ref):
                both = ref[here, columns]
                return jnp.concatenate([both[:, :128], both[:, 128:]], axis=0)

            q, d = stacked(query), stacked(heads_grad)
            keys, values = pair[0, s], pair[1, s]
            lines = r.log_sum
            logs = jnp.concatenate(
                [column_of(lines[s * 8 + step * 2]), column_of(lines[s * 8 + step * 2 + 1])], axis=0
            )
            score = contract_last(q, keys) * score_scale
            score = score + jnp.concatenate([bias[...], bias[...]], axis=0)
            prob = jnp.exp(score - logs)
            prob_grad = contract_last(d, values)
            delta = jnp.sum(prob * prob_grad, axis=-1, keepdims=True)
            score_grad = (prob * (prob_grad - delta)).astype(low)
            value_sum[...] += contract_first(prob.astype(low), d)
            key_sum[...] += contract_first(score_grad, q)
            turned_grad = jnp.dot(score_grad, keys, preferred_element_type=full) * score_scale
            for half in range(2):
                run = pl.ds(pl.multiple_of(step * 256 + half * 128, 128), 128)
                grad, part = norm_back(
                    rope_back(turned_grad[half * 128 : half * 128 + 128]),
                    query_raw[here, run],
                    gain_query,
                )
                heads_grad[here, run] = grad.astype(low)
                gain_part[0:1, :] += part
            return carry

        lax.fori_loop(0, 4, two_heads, 0)
        pair_grad[s, :, :, 0] = (key_sum[...] * score_scale).astype(low).reshape(4, 2, 128, 128)
        pair_grad[s, :, :, 1] = value_sum[...].astype(low).reshape(4, 2, 128, 128)
        return x_first(
            net, me, pair_grad.at[s], r.pair_slots.at[s], r.pair_middle.at[s], r.pair_other.at[s],
            r.pair_out.at[s],
        )

    pairs = [attend(0)]
    next(pairs[0])
    next(out_w)
    pairs.append(attend(1))
    next(pairs[1])
    next(pairs[0])
    next(up)
    pairs.append(attend(2))
    next(pairs[2])
    next(pairs[1])
    next(pairs[0])

    query_w = dense(
        dense_x_first, normed, query_low, r.sending, r.query_w_other, r.query_w_middle,
        r.query_w_slots, r.query_w_corner, r.query_w_last, r.query_w_out,
    )
    next(pairs[2])
    next(pairs[1])
    next(query_w)
    next(pairs[2])

    load_query.wait()
    net.sent(far_above)
    net.sent(far_below)

    def query_step(step, carry):
        columns = pl.ds(pl.multiple_of(step * 256, 256), 256)
        made = contract_last(query_low[...], weight[columns, :])
        whole[:, :, :, columns] = made.astype(low).reshape(3, 4, 32, 256)
        return carry

    lax.fori_loop(0, 8, query_step, 0)
    next(down)

    pair_out, key_raw, pair_low = r.pair_out, r.key_raw, r.pair_low
    for s in range(3):
        next(pairs[s], None)
        rows = slice(s * 128, s * 128 + 128)
        grad, part = norm_back(rope_back(pair_out[s, 0]), key_raw[rows, :], gain_key)
        gain_part[1:2, :] += part
        pair_low[rows, :128] = grad.astype(low)
        pair_low[rows, 128:] = pair_out[s, 1].astype(low)

    w_key, w_value = fetch.w_key, fetch.w_value
    small = r.small
    normed_part = r.normed_part

    def normed_step(step, carry):
        columns = pl.ds(pl.multiple_of(step * 256, 256), 256)
        made = whole_part(columns).astype(full)
        made = made + contract_last(pair_low[:, :128], w_key[columns, :])
        made = made + contract_last(pair_low[:, 128:], w_value[columns, :])
        normal = own_input(columns) * inverse[:, 0:1]
        normed_part[:, columns] = jnp.sum(made * normal, axis=0, keepdims=True)
        whole[:, :, :, columns] = made.astype(low).reshape(3, 4, 32, 256)
        return carry

    lax.fori_loop(0, 8, normed_step, 0)
    normed_out = r.normed_out
    normed_sum = ring_reduce(
        net,
        above,
        below,
        lambda step, half: whole.at[:, me.y_by(step), :, pl.ds(half * 1024, 1024)],
        r.normed_slots,
        lambda half: normed_out.at[:, :, pl.ds(half * 1024, 1024)],
    )
    next(normed_sum)
    for step in range(16):
        run = slice(step * 128, step * 128 + 128)
        small[step : step + 1, :] = normed_part[:, run]
        small[16 + step : 17 + step, :] = r.moe_gain_part[:, run]
    small[32:40, :] = gain_part[...]
    small[40:, :] = r.peaks[...]
    smalls = all_small(
        net, me, small, r.by_core, r.by_x, r.by_z, r.by_y, r.small_out
    )
    pair_w = dense(
        dense_x_first, normed, pair_low, r.pair_sending, r.pair_w_other, r.pair_w_middle,
        r.pair_w_slots, r.pair_w_corner, r.pair_w_last, r.pair_w_out,
    )
    next(out_w)

    for made in home_came:
        made.wait_recv()
    home_own.wait()
    home_loads = [
        net.load(home.at[:, pl.ds(half * 1024, 1024)], weight.at[pl.ds(half * 768, 768)])
        for half in range(2)
    ]
    next(pair_w)
    next(smalls)
    def rest(*tasks):
        for task in tasks:
            next(task, None)

    rest(query_w, normed_sum, pair_w, smalls, out_w, down, query_w, pair_w, smalls)
    moe_out = r.moe_out
    for half in range(2):
        home_loads[half].wait()

        def gather(step, carry, half=half):
            columns = pl.ds(pl.multiple_of(step * 256, 256), 256)
            total = contract_first(table[...], weight[half * 768 : half * 768 + 768, columns])
            moe_out[:, pl.ds(pl.multiple_of(half * 1024 + step * 256, 256), 256)] = total[:96]
            return carry

        lax.fori_loop(0, 4, gather, 0)

    next(normed_sum, None)
    for s in range(3):
        rows = pl.ds(pl.multiple_of(me.y * 32, 32), 32)
        grad, _ = norm_back(normed_out[s], hidden[s, rows, :].astype(full), gains[...])
        normed_out[s] = grad

    rest(out_w, query_w, pair_w, smalls, gate, up, down, out_w, query_w, pair_w)
    tasks = [pair_w, out_w, smalls, query_w, gate, up, down]
    while tasks:
        for task in list(tasks):
            if next(task, "end") == "end":
                tasks.remove(task)
    net.finish()


def dense_slots(columns, corner):
    low = jnp.bfloat16
    return [
        pltpu.VMEM((2, 4, 2, 64, columns), low),
        pltpu.VMEM((2, 4, 2, 64, columns), low),
        pltpu.VMEM((6, 2, 64, columns), low),
        pltpu.VMEM(corner + (64, columns), low),
        pltpu.VMEM((6, 32, columns), low),
    ]


def back(far, near):
    low, full = jnp.bfloat16, jnp.float32
    outs = dict(
        gate_out=(256, 768),
        up_out=(256, 768),
        down_out=(256, 768),
        query_w_out=(64, 1024),
        pair_w_out=(64, 256),
        out_w_out=(64, 1024),
        small_out=(48, 128),
        normed_out=(3, 32, 2048),
        moe_out=(96, 2048),
    )
    scratch = dict(
        gain_rows=pltpu.VMEM((1, 2048), full),
        hidden_held=pltpu.VMEM((3, 128, 2048), low),
        pair_held=pltpu.VMEM((2, 3, 1024, 128), low),
        query_held=pltpu.VMEM((384, 1024), low),
        query_raw_held=pltpu.VMEM((384, 1024), full),
        cosine_held=pltpu.VMEM((128, 128), full),
        sine_held=pltpu.VMEM((128, 128), full),
        mixed_held=pltpu.VMEM((384, 1024), low),
        key_weight=pltpu.VMEM((2048, 128), low),
        value_weight=pltpu.VMEM((2048, 128), low),
        whole=pltpu.VMEM((3, 4, 32, 2048), low),
        weight=pltpu.VMEM((2048, 1024), low),
        inverse=pltpu.VMEM((384, 128), full),
        normed=pltpu.VMEM((2048, 384), low),
        heads_grad=pltpu.VMEM((384, 1024), low),
        bias=pltpu.VMEM((128, 1024), full),
        key_sum=pltpu.VMEM((1024, 128), full),
        value_sum=pltpu.VMEM((1024, 128), full),
        pair_grad=pltpu.VMEM((3, 4, 2, 2, 128, 128), low),
        pair_slots=pltpu.VMEM((3, 6, 2, 128, 128), low),
        pair_middle=pltpu.VMEM((3, 2, 2, 128, 128), low),
        pair_other=pltpu.VMEM((3, 2, 128, 128), low),
        pair_out=pltpu.VMEM((3, 2, 128, 128), full),
        pair_low=pltpu.VMEM((384, 256), low),
        gain_part=pltpu.VMEM((8, 128), full),
        normed_part=pltpu.VMEM((1, 2048), full),
        normed_slots=pltpu.VMEM((6, 3, 32, 1024), low),
        small=pltpu.VMEM((48, 128), full),
        by_core=pltpu.VMEM((2, 48, 128), full),
        by_x=pltpu.VMEM((4, 48, 128), full),
        by_z=pltpu.VMEM((4, 48, 128), full),
        by_y=pltpu.VMEM((4, 48, 128), full),
        down_slots=pltpu.VMEM((6, 256, 768), low),
        down_middle=pltpu.VMEM((2, 256, 768), low),
        down_other=pltpu.VMEM((256, 768), low),
        down_held=pltpu.VMEM((4, 256, 768), low),
        gate_slots=pltpu.VMEM((6, 256, 768), low),
        gate_middle=pltpu.VMEM((2, 256, 768), low),
        gate_other=pltpu.VMEM((256, 768), low),
        gate_held=pltpu.VMEM((4, 256, 768), low),
        up_slots=pltpu.VMEM((6, 256, 768), low),
        up_middle=pltpu.VMEM((2, 256, 768), low),
        up_other=pltpu.VMEM((256, 768), low),
        up_held=pltpu.VMEM((4, 256, 768), low),
        sending=pltpu.VMEM((2, 4, 2, 64, 1024), low),
        pair_sending=pltpu.VMEM((2, 4, 2, 64, 256), low),
        query_w_other=None,
        query_w_middle=None,
        query_w_slots=None,
        query_w_corner=None,
        query_w_last=None,
        pair_w_other=None,
        pair_w_middle=None,
        pair_w_slots=None,
        pair_w_corner=None,
        pair_w_last=None,
        out_w_other=None,
        out_w_middle=None,
        out_w_slots=None,
        out_w_corner=None,
        out_w_last=None,
        send=pltpu.SemaphoreType.DMA((116,)),
        recv=pltpu.SemaphoreType.DMA((116,)),
        here=pltpu.SemaphoreType.DMA((34,)),
    )
    dense = dense_slots(1024, (2, 2)) + dense_slots(256, (2, 2)) + dense_slots(1024, (4,))
    scratch = {name: one or dense.pop(0) for name, one in scratch.items()}
    outs = {name: jax.ShapeDtypeStruct(size, full) for name, size in outs.items()}
    far_outs = dict(home=jax.ShapeDtypeStruct((768, 2048), low))
    return call(back_kernel, 0, far, near, outs, far_outs, scratch)


class Fetch:
    def __init__(self, net):
        self.net, self.waiting, self.held = net, {}, {}

    def start(self, name, source, target):
        self.waiting[name] = self.net.load(source, target)
        self.held[name] = target

    def __getattr__(self, name):
        if name in self.waiting:
            self.waiting.pop(name).wait()
        return self.held[name]


def token_table(ids, gates, capacity, table, info):
    low, full = jnp.bfloat16, jnp.float32
    expert = lax.broadcasted_iota(jnp.int32, (16, 32), 0)
    chosen, share = [], []
    for s in range(3):
        chosen_here = jnp.zeros((16, 32), full)
        share_here = jnp.zeros((16, 32), full)
        for k in range(8):
            named = ids[s, k : k + 1, :] == expert
            chosen_here = chosen_here + jnp.where(named, 1.0, 0.0)
            share_here = share_here + jnp.where(named, gates[s, k : k + 1, :], 0.0)
        chosen.append(chosen_here)
        share.append(share_here)
    none = jnp.zeros((16, 32), full)
    chosen = jnp.concatenate(chosen + [none], axis=1)
    share = jnp.concatenate(share + [none], axis=1)
    row = lax.broadcasted_iota(jnp.int32, (16, 128), 0)
    limit = jnp.zeros((16, 128), full)
    for e in range(16):
        limit = jnp.where(row == e, capacity[e].astype(full), limit)
    earlier = lax.broadcasted_iota(jnp.int32, (128, 128), 0) < lax.broadcasted_iota(
        jnp.int32, (128, 128), 1
    )
    before = jnp.dot(
        chosen.astype(low), jnp.where(earlier, 1.0, 0.0).astype(low), preferred_element_type=full
    )
    slot = jnp.where((chosen > 0.0) & (before < limit), before, -1.0)
    spot = lax.broadcasted_iota(jnp.int32, (48, 128), 0).astype(full)
    for place in range(16):
        core, z_hi, y = place // 8, place // 4 % 2, place % 4
        e = (z_hi * 2 + core) * 4 + y
        mask = jnp.where(slot[e : e + 1, :] == spot, 1.0, 0.0)
        table[place * 48 : place * 48 + 48, :] = mask.astype(low)
        info[core, z_hi, y] = jnp.concatenate(
            [slot[e : e + 1, :], share[e : e + 1, :], jnp.zeros((6, 128), full)], axis=0
        )


PHASES = (
    [(0, 0), (0, 1), (0, 3), (2, 0), (1, 0), (1, 1), (1, 3), (3, 0)],
    [(0, 2), (1, 2), (2, 1), (2, 3), (3, 1), (3, 3), (2, 2), (3, 2)],
)
SLOTS = {offset: (phase, spot) for phase in (0, 1) for spot, offset in enumerate(PHASES[phase])}


def spread(net, me, everyone, source, came, crossed):
    above, below = me.at(y=me.y_by(1)), me.at(y=me.y_by(3))
    sibling, across = me.at(core=1 - me.core), me.at(z=me.z_by(2))
    own = source is not None
    a, z_hi = (0, me.z_hi) if own else (2, 1 - me.z_hi)

    def block(b):
        return everyone.at[me.core, z_hi, me.y_by(b)]

    def half(b, part):
        return block(b).at[:, pl.ds(part * 16, 16)]

    def quarter(b, part):
        return block(b).at[:, pl.ds(0, 16), pl.ds(part * 1024, 1024)]

    def forward(view, device):
        return net.copy(view, view, device)

    def pass_on(b):
        if own:
            crossed[b] = forward(half(b, 1), across)
        else:
            crossed[b].wait_recv()
        came[a + 1, b] = forward(block(b), sibling)

    piece = half if own else quarter
    if own:
        up = net.copy(source, block(0), above)
        down = net.copy(source, block(0), below)
        came[a + 1, 0] = net.copy(source, block(0), sibling)
    else:
        up = forward(half(0, 0), above)
        down = forward(half(0, 0), below)
        came[a + 1, 0] = forward(block(0), sibling)
    yield
    up.wait_recv()
    far_up = forward(piece(3, 0), above)
    down.wait_recv()
    far_down = forward(piece(1, 1), below)
    pass_on(3)
    pass_on(1)
    yield
    far_up.wait_recv()
    far_down.wait_recv()
    pass_on(2)
    yield


def moe_kernel(names, *refs):
    r = types.SimpleNamespace(**dict(zip(names, refs, strict=True)))
    low, full = jnp.bfloat16, jnp.float32
    me = Place()
    net = Net(r.send, r.recv, r.here)
    fetch = Fetch(net)
    fetch.start("w_gate", r.w_gate, r.gate_weight)
    fetch.start("w_up", r.w_up, r.up_weight)
    fetch.start("cots", r.cots, r.cots_held)
    fetch.start("w_down", r.w_down, r.down_weight)
    greeted = greet(peers(me) + [me.at(x=me.x_by(1)), me.at(x=me.x_by(3))])
    everyone, local, table = r.everyone, r.local, r.table
    values = r.after[...]
    inverse = lax.rsqrt(jnp.mean(values * values, axis=-1, keepdims=True) + epsilon)
    gain = wide(r.moe_gain)
    everyone[me.spot] = (values * inverse * gain).astype(low).reshape(3, 32, 2048)

    greeted()
    came, crossed = {}, {}
    own_rows = everyone.at[me.spot]
    here_rows = spread(net, me, everyone, own_rows, came, crossed)
    next(here_rows)
    from_across = net.copy(own_rows, own_rows, me.at(z=me.z_by(2)))

    act, gate_back, up_back, back, home = r.act, r.gate_back, r.up_back, r.back, r.home
    grads = r.grads_held
    iota = lax.broadcasted_iota(jnp.int32, (48, 128), 0).astype(full)

    def slots_of(offset):
        core, z_hi, y = peer(me, *offset)[0]
        mask = r.info_in[core, z_hi, y, 0:1, :] == iota
        share = jnp.where(mask, r.info_in[core, z_hi, y, 1:2, :], 0.0)
        return mask, jnp.sum(share, axis=1, keepdims=True)

    def select(source, offset):
        mask, share = slots_of(offset)
        named = jnp.where(mask, 1.0, 0.0).astype(low)[:, :96]
        rows = source[peer(me, *offset)[0]].reshape(96, 2048)
        return jnp.dot(named, rows, preferred_element_type=full), share

    cots = fetch.cots
    for offset, slot in SLOTS.items():
        picked, share = select(cots, offset)
        r.raw_held[slot] = picked.astype(low)
        grads[slot] = (picked * share).astype(low)

    w_gate, w_up, w_down = fetch.w_gate, fetch.w_up, fetch.w_down
    back_came, dots_came, round_x, written = {}, {}, [], []
    right, left = me.at(x=me.x_by(1)), me.at(x=me.x_by(3))

    def weigh(entered, given, target):
        def body(step, carry):
            columns = pl.ds(pl.multiple_of(step * 256, 256), 256)
            left = entered[:, :, :, columns].reshape(768, 256)
            target[columns, :] = contract_first(left, given[...].reshape(768, 768)).astype(low)
            return carry

        lax.fori_loop(0, 8, body, 0)

    def chunk(target, step, half):
        start = (me.x_by(step) * 2 + half) * 256
        return target.at[pl.ds(pl.multiple_of(start, 256), 256)]

    def send_back(offsets):
        for offset in offsets:
            device = peer(me, *offset)[1]
            back_came[offset] = net.copy(back.at[SLOTS[offset]], home.at[me.spot], device)

    def through(group, low_slot, high_slot, between):
        run = slice(low_slot * 48, high_slot * 48)
        slots, rows = slice(low_slot, high_slot), (high_slot - low_slot) * 48
        for offset in PHASES[group][slots]:
            if offset in came:
                came[offset].wait_recv()
            local[SLOTS[offset]] = select(everyone, offset)[0].astype(low)

        def inner(step, carry):
            columns = pl.ds(pl.multiple_of(step * 256, 256), 256)
            entered = local[group, slots].reshape(rows, 2048)
            gate_pre = jnp.dot(entered, w_gate[:, columns], preferred_element_type=full)
            up_pre = jnp.dot(entered, w_up[:, columns], preferred_element_type=full)
            act_back = jnp.dot(
                grads[group, slots].reshape(rows, 2048),
                w_down[:, columns],
                preferred_element_type=full,
            )
            sigmoid = 1.0 / (1.0 + jnp.exp(-gate_pre))
            silu = gate_pre * sigmoid
            act[group, run, columns] = (silu * up_pre).astype(low)
            gate_back[group, run, columns] = (
                act_back * up_pre * sigmoid * (1.0 + gate_pre * (1.0 - sigmoid))
            ).astype(low)
            up_back[group, run, columns] = (act_back * silu).astype(low)
            return carry

        def outer(step, carry):
            columns = pl.ds(pl.multiple_of(step * 256, 256), 256)
            row_back = contract_last(gate_back[group, run, :], w_gate[columns, :]) + contract_last(
                up_back[group, run, :], w_up[columns, :]
            )
            back[group, slots, :, columns] = row_back.astype(low).reshape(rows // 48, 48, 256)
            return carry

        lax.fori_loop(0, 3, inner, 0)
        between()
        lax.fori_loop(0, 8, outer, 0)

    def results(group):
        given = [slots_of(offset) for offset in PHASES[group]]
        shared = jnp.concatenate([share for _, share in given], axis=0)

        def finals(step, dot):
            columns = pl.ds(pl.multiple_of(step * 256, 256), 256)
            made = contract_last(act[group], w_down[columns, :]).astype(low).astype(full)
            r.produced_held[group, :, :, columns] = (made * shared).astype(low).reshape(8, 48, 256)
            incoming = r.raw_held[group, :, :, columns].reshape(384, 256).astype(full)
            return dot + jnp.sum(made * incoming, axis=1, keepdims=True)

        dot = lax.fori_loop(0, 8, finals, jnp.zeros((384, 1), full))
        for spot, offset in enumerate(PHASES[group]):
            line = jnp.where(given[spot][0], dot[spot * 48 : spot * 48 + 48], 0.0)
            line = jnp.sum(line, axis=0, keepdims=True)
            r.dots[group, spot] = jnp.broadcast_to(line, (8, 128))
            if offset != (0, 0):
                device = peer(me, *offset)[1]
                dots_came[offset] = net.copy(
                    r.dots.at[group, spot], r.dots_in.at[me.spot], device
                )

    next(here_rows)
    from_across.wait_recv()
    other_rows = spread(net, me, everyone, None, came, crossed)
    next(other_rows)
    through(0, 0, 8, lambda: next(here_rows))
    next(other_rows)
    send_back([offset for offset in PHASES[0] if offset != (0, 0)])
    through(1, 0, 6, lambda: next(other_rows))
    send_back(PHASES[1][:6])
    through(1, 6, 8, lambda: None)
    send_back(PHASES[1][6:])
    weigh(local, gate_back, r.gate_held)
    round_x += [
        net.copy(chunk(r.gate_held, 2, 0), r.gate_slots.at[0], right),
        net.copy(chunk(r.gate_held, 2, 1), r.gate_slots.at[2], left),
        net.copy(chunk(r.gate_held, 1, 1), r.gate_slots.at[1], right),
        net.copy(chunk(r.gate_held, 3, 0), r.gate_slots.at[3], left),
    ]
    written.append(net.load(r.gate_held, r.full_gate))
    weigh(local, up_back, r.up_held)
    round_x += [
        net.copy(chunk(r.up_held, 2, 0), r.up_slots.at[0], right),
        net.copy(chunk(r.up_held, 2, 1), r.up_slots.at[1], left),
    ]
    written.append(net.load(r.up_held, r.full_up))
    results(0)
    results(1)
    weigh(grads, act, r.down_held)
    written.append(net.load(r.produced_held, r.produced))
    written.append(net.load(r.down_held, r.full_down))
    home[me.spot] = back[0, 0]
    r.dots_in[me.spot] = r.dots[0, 0]

    for offset in OFFSETS:
        dots_came[offset].wait_recv()
    lines = [r.dots_in[e // 4 % 2, e // 8, e % 4, 0:1, :] for e in range(16)]
    lines = jnp.concatenate(lines, axis=0)
    expert = lax.broadcasted_iota(jnp.int32, (16, 32), 0)
    for s in range(3):
        dots = lines[:, s * 32 : s * 32 + 32]
        for k in range(8):
            named = r.ids[s, k : k + 1, :] == expert
            r.gate_grad[s, k : k + 1, :] = jnp.sum(
                jnp.where(named, dots, 0.0), axis=0, keepdims=True
            )

    for offset in OFFSETS:
        back_came[offset].wait_recv()
    after_grad = r.after_grad

    def keep(columns, total):
        after_grad[:, columns] = total

    gather_rows(table, home, keep)
    gradient = after_grad[...]
    moe_part, gain_part = norm_back(gradient, r.after[...], gain)
    r.gain_part[...] = gain_part
    result = r.cotangent[...].reshape(96, 2048).astype(full) + moe_part
    after_grad[...] = result
    r.branch[...] = result.astype(low).reshape(3, 32, 2048)
    for one in written:
        one.wait()
    for one in round_x:
        one.wait_recv()
    net.finish()


def moe(far, near):
    low, full = jnp.bfloat16, jnp.float32
    rows, home = (2, 8, 48, 2048), (2, 2, 4, 48, 2048)
    outs = dict(
        after_grad=jax.ShapeDtypeStruct((96, 2048), full),
        branch=jax.ShapeDtypeStruct((3, 32, 2048), low),
        gain_part=jax.ShapeDtypeStruct((1, 2048), full),
        gate_grad=jax.ShapeDtypeStruct((3, 8, 32), full),
    )
    far_outs = dict(
        produced=jax.ShapeDtypeStruct(rows, low),
        full_gate=jax.ShapeDtypeStruct((2048, 768), low),
        full_up=jax.ShapeDtypeStruct((2048, 768), low),
        full_down=jax.ShapeDtypeStruct((2048, 768), low),
        gate_slots=jax.ShapeDtypeStruct((4, 256, 768), low),
        up_slots=jax.ShapeDtypeStruct((2, 256, 768), low),
    )
    scratch = dict(
        everyone=pltpu.VMEM((2, 2, 4, 3, 32, 2048), low),
        local=pltpu.VMEM(rows, low),
        cots_held=pltpu.VMEM((2, 2, 4, 3, 32, 2048), low),
        raw_held=pltpu.VMEM(rows, low),
        grads_held=pltpu.VMEM(rows, low),
        produced_held=pltpu.VMEM(rows, low),
        back=pltpu.VMEM(rows, low),
        home=pltpu.VMEM(home, low),
        gate_weight=pltpu.VMEM((2048, 768), low),
        up_weight=pltpu.VMEM((2048, 768), low),
        down_weight=pltpu.VMEM((2048, 768), low),
        gate_held=pltpu.VMEM((2048, 768), low),
        up_held=pltpu.VMEM((2048, 768), low),
        down_held=pltpu.VMEM((2048, 768), low),
        act=pltpu.VMEM((2, 384, 768), low),
        gate_back=pltpu.VMEM((2, 384, 768), low),
        up_back=pltpu.VMEM((2, 384, 768), low),
        dots=pltpu.VMEM((2, 8, 8, 128), full),
        dots_in=pltpu.VMEM((2, 2, 4, 8, 128), full),
        send=pltpu.SemaphoreType.DMA((58,)),
        recv=pltpu.SemaphoreType.DMA((58,)),
        here=pltpu.SemaphoreType.DMA((8,)),
    )
    return call(moe_kernel, 1, far, near, outs, far_outs, scratch)


def call(kernel, number, far, near, outs, far_outs, scratch):
    names = list(far) + list(near) + list(outs) + list(far_outs) + list(scratch)
    shapes = {**outs, **far_outs}
    results = pl.pallas_call(
        functools.partial(kernel, names),
        out_shape=list(shapes.values()),
        in_specs=[ANY] * len(far)
        + [SMEM if one.ndim == 1 else VMEM for one in near.values()],
        out_specs=[VMEM] * len(outs) + [ANY] * len(far_outs),
        scratch_shapes=list(scratch.values()),
        compiler_params=pltpu.CompilerParams(
            collective_id=number, has_side_effects=True, vmem_limit_bytes=63 << 20
        ),
        name=kernel.__name__,
    )(*far.values(), *near.values())
    return types.SimpleNamespace(**dict(zip(shapes, results, strict=True)))


def front_kernel(names, *refs):
    r = types.SimpleNamespace(**dict(zip(names, refs, strict=True)))
    low, full = jnp.bfloat16, jnp.float32
    score_scale = HEAD_SIZE ** (-0.5)
    me = Place()
    net = Net(r.send, r.recv, r.here)
    fetch = Fetch(net)
    fetch.start("hidden", r.hidden, r.hidden_held)
    fetch.start("w_pair", r.w_key, r.key_weight)
    fetch.start("w_value", r.w_value, r.value_weight)
    fetch.start("cosine", r.cosine.at[me.context], r.cosine_held)
    fetch.start("sine", r.sine.at[me.context], r.sine_held)
    fetch.start("w_query", r.w_query, r.query_weight)
    fetch.start("w_out", r.w_out, r.out_weight)
    beside = me.at(z=me.z + 1 - 2 * me.z_lo)
    right, left = me.at(x=me.x_by(1)), me.at(x=me.x_by(3))
    greeted = greet([right, left, beside] + peers(me))
    gains = r.gain_rows
    gains[...] = wide(r.attn_gain)

    above, below = me.at(y=me.y_by(1)), me.at(y=me.y_by(3))
    across, came, crossed, told = me.at(z=me.z_by(2)), {}, {}, []
    greeted()
    own_cot = net.load(r.cotangent, r.cots.at[me.spot])
    here_cot = spread(net, me, r.cots, r.cotangent, came, crossed)
    next(here_cot)
    from_across = net.copy(r.cotangent, r.cots.at[me.spot], across)

    hidden, normed = fetch.hidden, r.normed
    for s in range(3):
        values = hidden[s].astype(full)
        root = lax.rsqrt(jnp.mean(values * values, axis=-1, keepdims=True) + epsilon)
        normed[s * 128 : s * 128 + 128, :] = (values * root * gains[...]).astype(low)

    def rope(values):
        cosine = jnp.concatenate([fetch.cosine[...]] * 3, axis=0)
        sine = jnp.concatenate([fetch.sine[...]] * 3, axis=0)
        return values * cosine + turned(values) * sine

    def head_norm(raw, gain):
        return raw * lax.rsqrt(jnp.mean(raw * raw, axis=-1, keepdims=True) + epsilon) * gain

    pair, key_raw = r.pair_held, r.key_raw
    made = jnp.dot(normed[...], fetch.w_pair[...], preferred_element_type=full)
    key_raw[...] = made
    keys = rope(head_norm(made, r.key_gain[...].astype(full))).astype(low)
    values = jnp.dot(normed[...], fetch.w_value[...], preferred_element_type=full).astype(low)
    own = pl.ds(pl.multiple_of(me.context * 128, 128), 128)
    pair[0, :, own, :] = keys.reshape(3, 128, 128)
    pair[1, :, own, :] = values.reshape(3, 128, 128)

    def block(x, z_lo):
        return pl.ds(pl.multiple_of((x * 2 + z_lo) * 128, 128), 128)

    def piece(s, x, z_lo, half=None):
        rows = block(x, z_lo)
        return pair.at[:, s, rows, :] if half is None else pair.at[half, s, rows, :]

    def pass_on(view, device):
        return net.copy(view, view, device)

    own_z, other_z = me.z_lo, 1 - me.z_lo

    def bring_pair(s):
        from_z = pass_on(piece(s, me.x, own_z), beside)
        came = [(pass_on(piece(s, me.x, own_z), right), pass_on(piece(s, me.x, own_z), left))]
        yield
        from_z.wait_recv()
        came.append((pass_on(piece(s, me.x, other_z), right), pass_on(piece(s, me.x, other_z), left)))
        yield
        far = []
        for zs, (from_left, from_right) in zip((own_z, other_z), came, strict=True):
            from_left.wait_recv()
            far.append(pass_on(piece(s, me.x_by(3), zs, 0), right))
            from_right.wait_recv()
            far.append(pass_on(piece(s, me.x_by(1), zs, 1), left))
            yield
        for one in far:
            one.wait_recv()
        yield

    brought = [bring_pair(s) for s in range(3)]
    for s in range(3):
        next(brought[s])

    w_query, query, query_raw = fetch.w_query, r.query_held, r.query_raw_held

    def project(step, carry):
        columns = pl.ds(pl.multiple_of(step * 256, 256), 256)
        made = jnp.dot(normed[...], w_query[:, columns], preferred_element_type=full)
        query_raw[:, columns] = made
        for half in range(2):
            run = pl.ds(pl.multiple_of(step * 256 + half * 128, 128), 128)
            one = head_norm(made[:, half * 128 : half * 128 + 128], r.query_gain[...].astype(full))
            query[:, run] = rope(one).astype(low)
        return carry

    lax.fori_loop(0, 2, project, 0)
    for s in range(3):
        next(brought[s])
    next(here_cot)
    from_across.wait_recv()
    other_cot = spread(net, me, r.cots, None, came, crossed)
    next(other_cot)
    lax.fori_loop(2, 4, project, 0)
    written = [net.load(query, r.query), net.load(query_raw, r.query_raw)]
    next(brought[0])
    next(brought[1])
    next(brought[0])
    next(brought[2])
    next(brought[1])

    bias, peaks, mixed = r.bias, r.peak_rows, r.mixed_held
    peaks[...] = jnp.full((8, 1, 128), -jnp.inf, full)

    def attend(s):
        here = pl.ds(s * 128, 128)
        bias[...] = mask_bias(me, r.segments, s)

        def two_heads(step, carry):
            columns = pl.ds(pl.multiple_of(step * 256, 256), 256)
            both = query[here, columns]
            q = jnp.concatenate([both[:, :128], both[:, 128:]], axis=0)
            score = contract_last(q, pair[0, s]) * score_scale
            score = score + jnp.concatenate([bias[...], bias[...]], axis=0)
            highest = jnp.max(score, axis=-1, keepdims=True)
            weight = jnp.exp(score - highest)
            total = jnp.sum(weight, axis=-1, keepdims=True)
            prob = (weight * (1.0 / total)).astype(low)
            logs = highest + jnp.log(total)
            heads = jnp.dot(prob, pair[1, s], preferred_element_type=full).astype(low)
            for half in range(2):
                part = slice(half * 128, half * 128 + 128)
                head = step * 2 + half
                run = pl.ds(pl.multiple_of(step * 256 + half * 128, 128), 128)
                mixed[here, run] = heads[part]
                r.log_sum[s * 8 + head] = row_of(logs[part])
                top = jnp.max(highest[part], axis=0, keepdims=True)
                peaks[head] = jnp.maximum(peaks[head], top)
            return carry

        lax.fori_loop(0, 4, two_heads, 0)
    shares, after = r.shares, r.after_sum

    def branch(s):
        w_out = fetch.w_out

        def body(step, carry):
            columns = pl.ds(pl.multiple_of(step * 256, 256), 256)
            made = contract_last(mixed[pl.ds(s * 128, 128), :], w_out[columns, :])
            shares[s, :, :, columns] = made.astype(low).reshape(4, 32, 256)
            return carry

        lax.fori_loop(0, 8, body, 0)
        return ring_reduce(
            net,
            above,
            below,
            lambda step, half: shares.at[s, me.y_by(step), :, pl.ds(half * 1024, 1024)],
            r.branch_slots.at[s],
            lambda half: after.at[s, :, pl.ds(half * 1024, 1024)],
        )

    next(brought[0])
    attend(0)
    next(brought[2])
    first = branch(0)
    next(first)
    next(brought[1])
    attend(1)
    next(here_cot)
    next(other_cot)
    second = branch(1)
    next(second)
    next(first)
    next(brought[2])
    attend(2)
    third = branch(2)
    next(third)

    token_table(r.ids, r.gates, r.capacity, r.table, r.info)
    r.info_in[me.spot] = r.info[me.spot]
    for a, b in OFFSETS:
        spot, device = peer(me, a, b)
        told.append(net.copy(r.info.at[spot], r.info_in.at[me.spot], device))

    next(second)
    written.append(net.load(pair, r.pair))
    written.append(net.load(mixed, r.mixed))
    for head in range(8):
        r.peaks[head : head + 1, :] = peaks[head]
    next(first, None)
    next(third)
    next(other_cot)
    next(second, None)
    next(third, None)
    own_rows = pl.ds(pl.multiple_of(me.y * 32, 32), 32)
    for s in range(3):
        r.after[s * 32 : s * 32 + 32, :] = after[s] + hidden[s, own_rows, :].astype(full)
    for one in list(came.values()) + told:
        one.wait_recv()
    own_cot.wait()
    for one in written:
        one.wait()
    net.finish()


def row_of(column):
    eye = lax.broadcasted_iota(jnp.int32, (128, 128), 0) == lax.broadcasted_iota(
        jnp.int32, (128, 128), 1
    )
    return jnp.sum(jnp.where(eye, column, 0.0), axis=0, keepdims=True)


def mask_bias(me, segments, s):
    spot = me.context * 128 + lax.broadcasted_iota(jnp.int32, (128, 1024), 0)
    own = segments[s : s + 1, pl.ds(pl.multiple_of(me.context * 128, 128), 128)]
    document = column_of(own.astype(jnp.float32))
    allowed = (document == segments[s : s + 1, :].astype(jnp.float32)) & (
        lax.broadcasted_iota(jnp.int32, (128, 1024), 1) <= spot
    )
    return jnp.where(allowed, 0.0, masked_value)


def front(far, near):
    low, full = jnp.bfloat16, jnp.float32
    outs = dict(
        key_raw=jax.ShapeDtypeStruct((384, 128), full),
        log_sum=jax.ShapeDtypeStruct((24, 1, 128), full),
        peaks=jax.ShapeDtypeStruct((8, 128), full),
        after=jax.ShapeDtypeStruct((96, 2048), full),
        table=jax.ShapeDtypeStruct((768, 128), low),
        info_in=jax.ShapeDtypeStruct((2, 2, 4, 8, 128), full),
    )
    far_outs = dict(
        query=jax.ShapeDtypeStruct((384, 1024), low),
        query_raw=jax.ShapeDtypeStruct((384, 1024), full),
        pair=jax.ShapeDtypeStruct((2, 3, 1024, 128), low),
        mixed=jax.ShapeDtypeStruct((384, 1024), low),
        cots=jax.ShapeDtypeStruct((2, 2, 4, 3, 32, 2048), low),
    )
    scratch = dict(
        gain_rows=pltpu.VMEM((1, 2048), full),
        hidden_held=pltpu.VMEM((3, 128, 2048), low),
        key_weight=pltpu.VMEM((2048, 128), low),
        value_weight=pltpu.VMEM((2048, 128), low),
        cosine_held=pltpu.VMEM((128, 128), full),
        sine_held=pltpu.VMEM((128, 128), full),
        query_weight=pltpu.VMEM((2048, 1024), low),
        out_weight=pltpu.VMEM((2048, 1024), low),
        normed=pltpu.VMEM((384, 2048), low),
        pair_held=pltpu.VMEM((2, 3, 1024, 128), low),
        info=pltpu.VMEM((2, 2, 4, 8, 128), full),
        query_held=pltpu.VMEM((384, 1024), low),
        query_raw_held=pltpu.VMEM((384, 1024), full),
        bias=pltpu.VMEM((128, 1024), full),
        peak_rows=pltpu.VMEM((8, 1, 128), full),
        mixed_held=pltpu.VMEM((384, 1024), low),
        shares=pltpu.VMEM((3, 4, 32, 2048), low),
        branch_slots=pltpu.VMEM((3, 6, 32, 1024), low),
        after_sum=pltpu.VMEM((3, 32, 2048), full),
        send=pltpu.SemaphoreType.DMA((84,)),
        recv=pltpu.SemaphoreType.DMA((84,)),
        here=pltpu.SemaphoreType.DMA((16,)),
    )
    return call(front_kernel, 2, far, near, outs, far_outs, scratch)


def finish_kernel(names, *refs):
    r = types.SimpleNamespace(**dict(zip(names, refs, strict=True)))
    r.layer_out[...] = r.after[...] + r.moe_out[...]
    r.input_grad[...] = r.after_grad[...] + r.normed_out[...].reshape(96, 2048)
    r.gate_w[...] = r.gate_part[...]
    r.up_w[...] = r.up_part[...]
    r.down_w[...] = r.down_part[...]
    r.query_w[...] = r.query_part[...]
    r.out_w[...] = r.out_part[...]
    r.gate_grad[...] = r.gate_grad_part[...]
    r.key_w[...] = r.pair_w[:, :128]
    r.value_w[...] = r.pair_w[:, 128:]
    r.attn_gain[...] = r.small[:16]
    r.moe_gain[...] = r.small[16:32]
    r.query_gain[...] = r.small[32:33]
    r.key_gain[...] = r.small[33:34]
    diagonal = lax.broadcasted_iota(jnp.int32, (8, 128), 0) == lax.broadcasted_iota(
        jnp.int32, (8, 128), 1
    )
    peaks = jnp.sum(jnp.where(diagonal, r.small[40:], 0.0), axis=0, keepdims=True)
    r.clip[...] = (clip_limit / jnp.maximum(peaks, clip_limit))[:, :8]


def finish(near):
    outs = dict(
        layer_out=(96, 2048),
        input_grad=(96, 2048),
        gate_w=(256, 768),
        up_w=(256, 768),
        down_w=(256, 768),
        query_w=(64, 1024),
        out_w=(64, 1024),
        gate_grad=(3, 8, 32),
        key_w=(64, 128),
        value_w=(64, 128),
        attn_gain=(16, 128),
        moe_gain=(16, 128),
        query_gain=(1, 128),
        key_gain=(1, 128),
        clip=(1, 8),
    )
    results = pl.pallas_call(
        functools.partial(finish_kernel, list(near) + list(outs)),
        out_shape=[jax.ShapeDtypeStruct(size, jnp.float32) for size in outs.values()],
        in_specs=[VMEM] * len(near),
        out_specs=[VMEM] * len(outs),
        compiler_params=pltpu.CompilerParams(vmem_limit_bytes=62 << 20),
        name="finish",
    )(*near.values())
    return types.SimpleNamespace(**dict(zip(outs, results, strict=True)))


def shards(
    hidden_in,
    segments,
    attn_gain,
    query_gain,
    key_gain,
    w_query,
    key_weight_matrix,
    value_weight_matrix,
    w_out,
    moe_gain,
    expert_ids,
    gate_values,
    capacity,
    w_gate,
    w_up,
    w_down,
    cotangent,
):
    attn_wide, moe_wide = attn_gain.reshape(16, 128), moe_gain.reshape(16, 128)
    query_row, key_row = query_gain[None], key_gain[None]
    ids, gates = expert_ids.swapaxes(1, 2), gate_values.swapaxes(1, 2)
    cosine, sine = rotary()
    first = front(
        dict(
            hidden=hidden_in,
            w_key=key_weight_matrix,
            w_value=value_weight_matrix,
            cosine=cosine,
            sine=sine,
            w_query=w_query,
            cotangent=cotangent,
            w_out=w_out,
        ),
        dict(
            attn_gain=attn_wide,
            query_gain=query_row,
            key_gain=key_row,
            segments=segments,
            ids=ids,
            gates=gates,
            capacity=capacity,
        ),
    )
    second = moe(
        dict(w_gate=w_gate[0], w_up=w_up[0], w_down=w_down[0], cots=first.cots),
        dict(
            after=first.after,
            cotangent=cotangent,
            moe_gain=moe_wide,
            ids=ids,
            table=first.table,
            info_in=first.info_in,
        ),
    )
    done = back(
        dict(
            branch=second.branch,
            w_out=w_out,
            w_query=w_query,
            gate=second.full_gate.reshape(4, 2, 256, 768),
            up=second.full_up.reshape(4, 2, 256, 768),
            down=second.full_down.reshape(4, 2, 256, 768),
            produced=second.produced,
            gate_begun=second.gate_slots,
            up_begun=second.up_slots,
            hidden=hidden_in,
            mixed=first.mixed,
            query=first.query,
            query_raw=first.query_raw,
            pair=first.pair,
            cosine=cosine,
            sine=sine,
            w_key=key_weight_matrix,
            w_value=value_weight_matrix,
        ),
        dict(
            table=first.table,
            key_raw=first.key_raw,
            log_sum=first.log_sum,
            segments=segments,
            attn_gain=attn_wide,
            query_gain=query_row,
            key_gain=key_row,
            moe_gain_part=second.gain_part,
            peaks=first.peaks,
        ),
    )
    last = finish(
        dict(
            after=first.after,
            moe_out=done.moe_out,
            after_grad=second.after_grad,
            normed_out=done.normed_out,
            small=done.small_out,
            pair_w=done.pair_w_out,
            gate_part=done.gate_out,
            up_part=done.up_out,
            down_part=done.down_out,
            query_part=done.query_w_out,
            out_part=done.out_w_out,
            gate_grad_part=second.gate_grad,
        )
    )
    layer_out = last.layer_out.reshape(cotangent.shape)
    input_grad = last.input_grad.reshape(cotangent.shape)
    gate_grad = last.gate_grad.swapaxes(1, 2)
    w_key_grad, w_value_grad = last.key_w, last.value_w
    w_query_grad, w_out_grad = last.query_w, last.out_w
    w_gate_grad, w_up_grad, w_down_grad = last.gate_w[None], last.up_w[None], last.down_w[None]
    attn_gain_grad, moe_gain_grad = last.attn_gain.reshape(2048), last.moe_gain.reshape(2048)
    query_gain_grad, key_gain_grad = last.query_gain.reshape(128), last.key_gain.reshape(128)
    head_clip_scale = last.clip.reshape(8)
    return (
        layer_out,
        input_grad,
        attn_gain_grad,
        query_gain_grad,
        key_gain_grad,
        w_query_grad,
        w_key_grad,
        w_value_grad,
        w_out_grad,
        moe_gain_grad,
        gate_grad,
        w_gate_grad,
        w_up_grad,
        w_down_grad,
        head_clip_scale,
    )


def solution(mesh):
    in_specs = (
        P("dp", "context", None),
        P("dp", None),
        P(),
        P(),
        P(),
        P(None, "experts"),
        P(None, "experts"),
        P(None, "experts"),
        P(None, "experts"),
        P(),
        P("dp", ("context", "experts"), None),
        P("dp", ("context", "experts"), None),
        P(),
        P(("dp", "experts"), None, None),
        P(("dp", "experts"), None, None),
        P(("dp", "experts"), None, None),
        P("dp", ("context", "experts"), None),
    )
    out_specs = (
        P("dp", ("context", "experts"), None),
        P("dp", ("context", "experts"), None),
        P(),
        P(),
        P(),
        P(("dp", "context"), "experts"),
        P(("dp", "context"), "experts"),
        P(("dp", "context"), "experts"),
        P(("dp", "context"), "experts"),
        P(),
        P("dp", ("context", "experts"), None),
        P(("dp", "experts"), "context", None),
        P(("dp", "experts"), "context", None),
        P(("dp", "experts"), "context", None),
        P("experts"),
    )
    return jax.shard_map(shards, mesh=mesh, in_specs=in_specs, out_specs=out_specs, check_vma=False)
```
